32 devices in a mesh: dp: 8 (over z, y), head: 4 (over x, core).
Axes of the slice: x: 2, y: 2, z: 4, core: 2. Of those that a mesh axis runs over, the one named last changes fastest.
Arguments:
- token_ids: int32 [32768], P(('dp', 'head')), may hold values from 0 to 50687
- seq_lengths: int32 [128], P(('dp', 'head')), may hold values from 1 to 512, as said below
- teacher_hidden: bfloat16 [32768, 1024], P(('dp', 'head')), may hold values from -6 to 6
- teacher_weight: bfloat16 [1024, 3072], P(None, 'head'), may hold values from -0.1875 to 0.1875
- token_table: float32 [50688, 512], P(('dp', 'head')), may hold values from -6 to 6
- token_first: float32 [50688, 512], P(('dp', 'head')), may hold values from -9.313226e-09 to 9.313226e-09
- token_second: float32 [50688, 512], P(('dp', 'head')), may hold values from 1e-19 to 8e-19
- position_table: float32 [512, 512], P('dp', 'head'), may hold values from -3 to 3
- position_first: float32 [512, 512], P('dp', 'head'), may hold values from -3.7252903e-08 to 3.7252903e-08
- position_second: float32 [512, 512], P('dp', 'head'), may hold values from 1.25e-19 to 1e-18
- qkv_weight: float32 [2, 512, 1536], P(None, 'dp', 'head'), may hold values from -0.25 to 0.25
- qkv_first: float32 [2, 512, 1536], P(None, 'dp', 'head'), may hold values from -3.7252903e-08 to 3.7252903e-08
- qkv_second: float32 [2, 512, 1536], P(None, 'dp', 'head'), may hold values from 1.5e-18 to 1.2e-17
- proj_weight: float32 [1, 512, 512], P(None, 'dp', 'head'), may hold values from -0.25 to 0.25
- proj_first: float32 [1, 512, 512], P(None, 'dp', 'head'), may hold values from -3.7252903e-08 to 3.7252903e-08
- proj_second: float32 [1, 512, 512], P(None, 'dp', 'head'), may hold values from 1.5e-18 to 1.2e-17
- up_weight: float32 [1, 512, 2048], P(None, 'dp', 'head'), may hold values from -0.25 to 0.25
- up_first: float32 [1, 512, 2048], P(None, 'dp', 'head'), may hold values from -3.7252903e-08 to 3.7252903e-08
- up_second: float32 [1, 512, 2048], P(None, 'dp', 'head'), may hold values from 1.5e-18 to 1.2e-17
- down_weight: float32 [1, 2048, 512], P(None, 'dp', 'head'), may hold values from -0.125 to 0.125
- down_first: float32 [1, 2048, 512], P(None, 'dp', 'head'), may hold values from -3.7252903e-08 to 3.7252903e-08
- down_second: float32 [1, 2048, 512], P(None, 'dp', 'head'), may hold values from 1.5e-18 to 1.2e-17
- gains_biases: float32 [9216], P(('dp', 'head')), may hold values from -0.8 to 1.9
- gains_first: float32 [9216], P(('dp', 'head')), may hold values from -1.1920929e-07 to 1.1920929e-07
- gains_second: float32 [9216], P(('dp', 'head')), may hold values from 3e-16 to 2.4e-15
Outputs:
- token_table_new: float32 [50688, 512], P(('dp', 'head'))
- token_first_new: float32 [50688, 512], P(('dp', 'head'))
- token_second_new: float32 [50688, 512], P(('dp', 'head'))
- position_table_new: float32 [512, 512], P('dp', 'head')
- position_first_new: float32 [512, 512], P('dp', 'head')
- position_second_new: float32 [512, 512], P('dp', 'head')
- qkv_weight_new: float32 [2, 512, 1536], P(None, 'dp', 'head')
- qkv_first_new: float32 [2, 512, 1536], P(None, 'dp', 'head')
- qkv_second_new: float32 [2, 512, 1536], P(None, 'dp', 'head')
- proj_weight_new: float32 [1, 512, 512], P(None, 'dp', 'head')
- proj_first_new: float32 [1, 512, 512], P(None, 'dp', 'head')
- proj_second_new: float32 [1, 512, 512], P(None, 'dp', 'head')
- up_weight_new: float32 [1, 512, 2048], P(None, 'dp', 'head')
- up_first_new: float32 [1, 512, 2048], P(None, 'dp', 'head')
- up_second_new: float32 [1, 512, 2048], P(None, 'dp', 'head')
- down_weight_new: float32 [1, 2048, 512], P(None, 'dp', 'head')
- down_first_new: float32 [1, 2048, 512], P(None, 'dp', 'head')
- down_second_new: float32 [1, 2048, 512], P(None, 'dp', 'head')
- gains_biases_new: float32 [9216], P(('dp', 'head'))
- gains_first_new: float32 [9216], P(('dp', 'head'))
- gains_second_new: float32 [9216], P(('dp', 'head'))
- grad_norm: float32 [], replicated
- loss_parts: float32 [2], replicated
The draws below stay inside these ranges and needn't reach their ends.
Inputs may be any that keep to these rules, and one draw needn't show every extreme that they name: `seq_lengths`: each sequence's valid tokens are at least one and at most its bucket's length (128, 256 or 512).
All inputs are finite; a program needn't handle non-finite values.
Results may differ from the reference program's by a relative error of at most 0.017.
Values may be sent and summed in bfloat16 or wider, within the bound.
A program may use at most 256 MiB of HBM per device.

```python
import math
import jax
import jax.numpy as jnp
import numpy as np
from jax import lax

D = 512
HEADS = 8
HD = 64
FF = 2048
TD = 1024
THEADS = 16
THD = 64
REL = 64
VOCAB = 50688
MAXPOS = 512
LAYERS = 2
LA = 128
LB = 256
LC = 512
M = 1
STEP = 10
SEQ_DEV = 4
TOK_DEV = 1024
TOKENS = 32768
P_SMALL = 9216
N_DP = 8
N_HEAD = 4
DEVICES = 32


def draw_seq_lengths(key, part):
    seq_total = DEVICES * 4 * M
    position = jnp.arange(seq_total, dtype=jnp.int32)
    device = position // (4 * M)
    slot_idx = position % (4 * M)
    seq_len = jnp.where(slot_idx < 2 * M, LA, jnp.where(slot_idx < 3 * M, LB, LC))
    row_pos = device // N_HEAD
    col_pos = device % N_HEAD
    span_row = max(N_DP - 1, 1)
    span_col = max(N_HEAD - 1, 1)
    weight_num = span_row * span_col + row_pos * span_col + col_pos * span_row
    top_len = jnp.maximum(seq_len * weight_num // (3 * span_row * span_col), 1)
    low_len = jnp.maximum(top_len * 3 // 5, 1)
    drawn_len = jax.random.randint(key, (seq_total,), low_len, top_len + 1)
    chosen = jax.random.randint(jax.random.fold_in(key, 7), (), 0, M)
    forced = (device == DEVICES - 1) & (slot_idx == 3 * M + chosen)
    return jnp.where(forced, LC, drawn_len).astype(jnp.int32)


def draw_gains_biases(key, part):
    size_all = 2 * D + (LAYERS - 1) * (9 * D + FF) + 3 * D
    position = jnp.arange(size_all, dtype=jnp.int32)
    stride = 9 * D + FF
    within = (position - 2 * D) % stride
    in_layers = (position >= 2 * D) & (position < 2 * D + (LAYERS - 1) * stride)
    first_gain = (within >= 5 * D + FF) & (within < 6 * D + FF)
    second_gain = (within >= 7 * D + FF) & (within < 8 * D + FF)
    is_gain = (position < D) | in_layers & (first_gain | second_gain)
    feature = (position % D).astype(jnp.float32)
    rising = 0.5 + feature / D
    key_one = jax.random.fold_in(key, 1)
    key_two = jax.random.fold_in(key, 2)
    jitter = jax.random.uniform(key_one, (size_all,), jnp.float32, 0.8, 1.2)
    shifts = jnp.clip(jax.random.normal(key_two, (size_all,), jnp.float32), -4.0, 4.0) * 0.2
    return jnp.where(is_gain, rising * jitter, shifts).astype(jnp.float32)


def plant(values, stream_key, low, largest):
    spot = [jax.random.randint(jax.random.fold_in(stream_key, axis), (), 0, length) for axis, length in enumerate(values.shape)]
    main_axis = values.shape.index(max(values.shape))
    neighbour = spot[:main_axis] + [(spot[main_axis] + 1) % values.shape[main_axis]] + spot[main_axis + 1:]
    return values.at[tuple(spot)].set(low).at[tuple(neighbour)].set(largest)


def level_of(stream_key, extent, split, least, largest):
    def one(axis_at, blocks):
        heights = jax.random.uniform(jax.random.fold_in(jax.random.fold_in(stream_key, 6), axis_at), (blocks,), jnp.float32, least / len(split), largest / len(split))
        return jnp.repeat(jnp.exp(heights), extent[axis_at] // blocks).reshape((-1,) + (1,) * (len(extent) - axis_at - 1))

    level = one(*split[0])
    for cut in split[1:]:
        level = level * one(*cut)
    return level


def rank_table(number_of, skew):
    loads = [(1 << 20) // math.isqrt(rank ** skew) + 1 for rank in range(1, number_of + 1)]
    width = 1 + sum(loads) // (1 << 30)
    return np.cumsum(np.array([max(1, weight // width) for weight in loads]))


def ranked_ids(own_key, dims, number_of, skew):
    table = rank_table(number_of, skew)
    ticket = jax.random.randint(jax.random.fold_in(own_key, 1), dims, 0, int(table[number_of - 1]))
    standing = jnp.searchsorted(jnp.asarray(table, jnp.int32), ticket, side="right")
    return jax.random.permutation(jax.random.fold_in(own_key, 2), number_of)[standing].astype(jnp.int32)


def gaussian(stream_key, extent, scale, most, split=(), kind=jnp.bfloat16):
    gain = level_of(stream_key, extent, split, -0.22, 0.18) if split else 1.0
    entries = jax.random.normal(stream_key, extent, jnp.float32) * scale * gain
    return jnp.minimum(jnp.maximum(entries, -most), most).astype(kind)


def setup_inputs(seed: int = 0) -> dict:
    streams_of = jax.random.split(jax.random.key(seed), 26)
    return {
        "token_ids": plant(ranked_ids(streams_of[0], (TOKENS,), VOCAB, 2), jax.random.fold_in(streams_of[0], 3), 0, VOCAB - 1).astype(jnp.int32),
        "seq_lengths": draw_seq_lengths(jax.random.fold_in(streams_of[25], 71), 0),
        "teacher_hidden": gaussian(streams_of[2], (TOKENS, TD), 1.0, 6.0, ((0, 32),)),
        "teacher_weight": gaussian(streams_of[3], (TD, 3 * TD), TD ** -0.5, 0.1875, ((1, 4),)),
        "token_table": gaussian(streams_of[4], (VOCAB, D), 1.0, 6.0, ((0, 32),), jnp.float32),
        "token_first": gaussian(streams_of[5], (VOCAB, D), (1.5e-9), 9.313225746154785e-09, ((0, 32),), jnp.float32),
        "token_second": jnp.clip(jnp.exp(math.log(7.99999974612418e-19) - 2.0794415 * jax.random.uniform(streams_of[6], (VOCAB, D), jnp.float32) ** level_of(streams_of[6], (VOCAB, D), ((0, 32),), -0.2, 0.2)), 9.999999682655225e-20, 7.99999974612418e-19),
        "position_table": gaussian(streams_of[7], (MAXPOS, D), 0.5, 3.0, ((0, 8), (1, 4)), jnp.float32),
        "position_first": gaussian(streams_of[8], (MAXPOS, D), (6e-9), 3.725290298461914e-08, ((0, 8), (1, 4)), jnp.float32),
        "position_second": jnp.clip(jnp.exp(math.log(1.000000045813705e-18) - 2.0794415 * jax.random.uniform(streams_of[9], (MAXPOS, D), jnp.float32) ** level_of(streams_of[9], (MAXPOS, D), ((0, 8), (1, 4)), -0.2, 0.2)), 1.2500000572671312e-19, 1.000000045813705e-18),
        "qkv_weight": gaussian(streams_of[10], (LAYERS, D, 3 * D), D ** -0.5, 0.25, ((1, 8), (2, 4)), jnp.float32),
        "qkv_first": gaussian(streams_of[11], (LAYERS, D, 3 * D), (6e-9), 3.725290298461914e-08, ((1, 8), (2, 4)), jnp.float32),
        "qkv_second": jnp.clip(jnp.exp(math.log(1.2000000136174153e-17) - 2.0794415 * jax.random.uniform(streams_of[12], (LAYERS, D, 3 * D), jnp.float32) ** level_of(streams_of[12], (LAYERS, D, 3 * D), ((1, 8), (2, 4)), -0.2, 0.2)), 1.5000000170217692e-18, 1.2000000136174153e-17),
        "proj_weight": gaussian(streams_of[13], (LAYERS - 1, D, D), D ** -0.5, 0.25, ((1, 8), (2, 4)), jnp.float32),
        "proj_first": gaussian(streams_of[14], (LAYERS - 1, D, D), (6e-9), 3.725290298461914e-08, ((1, 8), (2, 4)), jnp.float32),
        "proj_second": jnp.clip(jnp.exp(math.log(1.2000000136174153e-17) - 2.0794415 * jax.random.uniform(streams_of[15], (LAYERS - 1, D, D), jnp.float32) ** level_of(streams_of[15], (LAYERS - 1, D, D), ((1, 8), (2, 4)), -0.2, 0.2)), 1.5000000170217692e-18, 1.2000000136174153e-17),
        "up_weight": gaussian(streams_of[16], (LAYERS - 1, D, FF), D ** -0.5, 0.25, ((1, 8), (2, 4)), jnp.float32),
        "up_first": gaussian(streams_of[17], (LAYERS - 1, D, FF), (6e-9), 3.725290298461914e-08, ((1, 8), (2, 4)), jnp.float32),
        "up_second": jnp.clip(jnp.exp(math.log(1.2000000136174153e-17) - 2.0794415 * jax.random.uniform(streams_of[18], (LAYERS - 1, D, FF), jnp.float32) ** level_of(streams_of[18], (LAYERS - 1, D, FF), ((1, 8), (2, 4)), -0.2, 0.2)), 1.5000000170217692e-18, 1.2000000136174153e-17),
        "down_weight": gaussian(streams_of[19], (LAYERS - 1, FF, D), FF ** -0.5, 0.125, ((1, 8), (2, 4)), jnp.float32),
        "down_first": gaussian(streams_of[20], (LAYERS - 1, FF, D), (6e-9), 3.725290298461914e-08, ((1, 8), (2, 4)), jnp.float32),
        "down_second": jnp.clip(jnp.exp(math.log(1.2000000136174153e-17) - 2.0794415 * jax.random.uniform(streams_of[21], (LAYERS - 1, FF, D), jnp.float32) ** level_of(streams_of[21], (LAYERS - 1, FF, D), ((1, 8), (2, 4)), -0.2, 0.2)), 1.5000000170217692e-18, 1.2000000136174153e-17),
        "gains_biases": draw_gains_biases(jax.random.fold_in(streams_of[25], 71), 0),
        "gains_first": gaussian(streams_of[23], (P_SMALL,), (2e-8), 1.1920928955078125e-07, ((0, 32),), jnp.float32),
        "gains_second": jnp.clip(jnp.exp(math.log(2.4000000934092797e-15) - 2.0794415 * jax.random.uniform(streams_of[24], (P_SMALL,), jnp.float32) ** level_of(streams_of[24], (P_SMALL,), ((0, 32),), -0.2, 0.2)), 3.0000001167615996e-16, 2.4000000934092797e-15),
    }


B_ONE = 0.9
B_TWO = 0.999
EPSILON = 1e-10
DECAY = 0.01
THRESHOLD = 0.0003
RATE_TABLE = 1.0
RATE_MATRIX = 0.1
RATE_SMALL = 2.0
HIGH = lax.Precision.HIGHEST

@jax.custom_vjp
def low(v):
    return lax.optimization_barrier(v.astype(jnp.bfloat16)).astype(jnp.float32)

@jax.custom_vjp
def low_back(v):
    return v

def low_keep(v):
    return (low(v), None)

def low_pass(kept, grad):
    return (grad,)

def back_keep(v):
    return (v, None)

def back_low(kept, grad):
    return (low(grad),)
low.defvjp(low_keep, low_pass)
low_back.defvjp(back_keep, back_low)

def matmul(left, right):
    return jnp.dot(left, right, precision=HIGH, preferred_element_type=jnp.float32)

def layer_norm(values, gain_vec, shift_vec):
    average = lax.optimization_barrier(jnp.mean(values, axis=-1, keepdims=True))
    centered = values - average
    variance = lax.optimization_barrier(jnp.mean(centered * centered, axis=-1, keepdims=True))
    return centered * lax.rsqrt(variance + 1e-05) * gain_vec + shift_vec

def bucket_shapes():
    return ((2 * M, LA), (M, LB), (M, LC))

def split_tokens(token_block):
    pieces = []
    offset = 0
    for seq_count, seq_len in bucket_shapes():
        pieces.append(token_block[offset:offset + seq_count * seq_len].reshape((seq_count, seq_len) + token_block.shape[1:]))
        offset = offset + seq_count * seq_len
    return pieces

def key_masks(seq_lengths):
    mask_list = []
    offset = 0
    for seq_count, seq_len in bucket_shapes():
        lengths_here = seq_lengths[offset:offset + seq_count]
        mask_list.append(jnp.arange(seq_len, dtype=jnp.int32)[None, :] < lengths_here[:, None])
        offset = offset + seq_count
    return mask_list

def positions():
    return jnp.concatenate([jnp.tile(jnp.arange(seq_len, dtype=jnp.int32), seq_count) for seq_count, seq_len in bucket_shapes()])

@jax.checkpoint
def attend(qkv_block, key_valid):
    seq_count, seq_len = (qkv_block.shape[0], qkv_block.shape[1])
    shaped = qkv_block.reshape(seq_count, seq_len, HEADS, 3, HD)
    scores = jnp.einsum('sqhe,skhe->shqk', shaped[:, :, :, 0], shaped[:, :, :, 1], precision=HIGH) / math.sqrt(HD)
    scores = jnp.where(key_valid[:, None, None, :], scores, -1e+30)
    attention = low(jax.nn.softmax(scores, axis=-1))
    context = jnp.einsum('shqk,skhe->sqhe', attention, shaped[:, :, :, 2], precision=HIGH)
    return context.reshape(seq_count * seq_len, D)

def log_relation(vectors, key_valid):
    scores = jnp.einsum('sire,sjre->srij', vectors, vectors, precision=HIGH) / math.sqrt(vectors.shape[-1])
    scores = jnp.where(key_valid[:, None, None, :], scores, -1e+30)
    return jax.nn.log_softmax(scores, axis=-1)

@jax.checkpoint
def relation_group(teacher_rel, student_rel, key_valid):
    teacher_log = log_relation(teacher_rel, key_valid)
    student_log = log_relation(student_rel, key_valid)
    inside = key_valid[:, None, None, :]
    diverge = lax.optimization_barrier(jnp.sum(jnp.where(inside, jnp.exp(teacher_log) * (teacher_log - student_log), 0.0), axis=-1))
    return jnp.sum(jnp.where(key_valid[:, None, :], diverge, 0.0))

def relation_loss(teacher_block, student_block, key_valid):
    seq_count, seq_len = key_valid.shape
    teacher_parts = teacher_block.reshape(seq_count, seq_len, THEADS, 3, THD)
    student_parts = student_block.reshape(seq_count, seq_len, HEADS, 3, HD)
    loss_total = jnp.zeros((), jnp.float32)
    for part_idx in range(3):
        teacher_rel = teacher_parts[:, :, :, part_idx].reshape(seq_count, seq_len, REL // 4, 4, TD // REL).transpose(2, 0, 1, 3, 4)
        student_rel = student_parts[:, :, :, part_idx].reshape(seq_count, seq_len, REL // 4, 4, D // REL).transpose(2, 0, 1, 3, 4)
        group_sums = lax.map(lambda rel_pair: relation_group(rel_pair[0], rel_pair[1], key_valid), (teacher_rel, student_rel))
        loss_total = loss_total + jnp.sum(group_sums)
    return loss_total / (3 * REL)

def student_layer(hidden, layer_idx, qkv_weight, proj_weight, up_weight, down_weight, gains_biases, mask_list):
    offset = 2 * D + layer_idx * (9 * D + FF)
    qkv_all = low(matmul(low(hidden), low(qkv_weight[layer_idx])) + gains_biases[offset:offset + 3 * D])
    context = jnp.concatenate([attend(qkv_piece, valid_keys) for qkv_piece, valid_keys in zip(split_tokens(qkv_all), mask_list)], axis=0)
    mixed = hidden + matmul(low(context), low(proj_weight[layer_idx])) + gains_biases[offset + 3 * D:offset + 4 * D]
    middle = layer_norm(mixed, gains_biases[offset + 5 * D + FF:offset + 6 * D + FF], gains_biases[offset + 6 * D + FF:offset + 7 * D + FF])
    inner_act = low(jax.nn.gelu(matmul(low(middle), low(up_weight[layer_idx])) + gains_biases[offset + 4 * D:offset + 4 * D + FF], approximate=False))
    output = middle + matmul(inner_act, low(down_weight[layer_idx])) + gains_biases[offset + 4 * D + FF:offset + 5 * D + FF]
    return layer_norm(output, gains_biases[offset + 7 * D + FF:offset + 8 * D + FF], gains_biases[offset + 8 * D + FF:offset + 9 * D + FF])

def device_forward(teacher_qkv, seq_lengths, token_rows, position_table, qkv_weight, proj_weight, up_weight, down_weight, gains_biases):
    mask_list = key_masks(seq_lengths)
    gains_low = low(gains_biases)
    hidden = layer_norm(low_back(token_rows) + low(position_table)[positions()], gains_low[0:D], gains_low[D:2 * D])
    for layer_idx in range(LAYERS - 1):
        hidden = student_layer(hidden, layer_idx, qkv_weight, proj_weight, up_weight, down_weight, gains_low, mask_list)
    offset = 2 * D + (LAYERS - 1) * (9 * D + FF)
    final_qkv = low(matmul(low(hidden), low(qkv_weight[LAYERS - 1])) + gains_low[offset:offset + 3 * D])
    loss_total = jnp.zeros((), jnp.float32)
    for teacher_piece, student_piece, valid_keys in zip(split_tokens(teacher_qkv), split_tokens(final_qkv), mask_list):
        loss_total = loss_total + relation_loss(teacher_piece, student_piece, valid_keys)
    return loss_total

def adam_update(master, first, second, grad_clip, rate):
    first_new = B_ONE * first + (1.0 - B_ONE) * grad_clip
    second_new = B_TWO * second + (1.0 - B_TWO) * grad_clip * grad_clip
    ascent = first_new / (1.0 - B_ONE ** STEP) / (jnp.sqrt(second_new / (1.0 - B_TWO ** STEP)) + EPSILON)
    return (master - rate * (ascent + DECAY * master), first_new, second_new)

def reference(token_ids, seq_lengths, teacher_hidden, teacher_weight, token_table, token_first, token_second, position_table, position_first, position_second, qkv_weight, qkv_first, qkv_second, proj_weight, proj_first, proj_second, up_weight, up_first, up_second, down_weight, down_first, down_second, gains_biases, gains_first, gains_second):
    masters = (token_table, position_table, qkv_weight, proj_weight, up_weight, down_weight, gains_biases)
    lowered = tuple((low(master) for master in masters))
    teacher_full = teacher_weight.astype(jnp.float32)
    id_blocks = token_ids.reshape(DEVICES, TOK_DEV)
    length_blocks = seq_lengths.reshape(DEVICES, SEQ_DEV)
    hidden_blocks = teacher_hidden.reshape(DEVICES, TOK_DEV, TD)

    def one_device(carried, inputs):
        ids_here, lengths_here, hidden_here = inputs
        teacher_qkv = low(matmul(hidden_here.astype(jnp.float32), teacher_full))

        def local_loss(table_in, position_in, qkv_in, proj_in, up_in, down_in, gains_in):
            return device_forward(teacher_qkv, lengths_here, table_in[ids_here], position_in, qkv_in, proj_in, up_in, down_in, gains_in)
        loss_here, backward = jax.vjp(local_loss, lowered[0], lowered[1], lowered[2], lowered[3], lowered[4], lowered[5], lowered[6])
        gradients = backward(jnp.ones((), jnp.float32))
        grad_sums, loss_sum = carried
        return ((tuple((total_grad + grad_here for total_grad, grad_here in zip(grad_sums, gradients))), loss_sum + loss_here), None)
    initial = (tuple((jnp.zeros(master.shape, jnp.float32) for master in masters)), jnp.zeros((), jnp.float32))
    (grad_sums, loss_sum), ignored = lax.scan(one_device, initial, (id_blocks, length_blocks, hidden_blocks))
    valid_total = jnp.sum(seq_lengths).astype(jnp.float32)
    scaled = tuple((total_grad / valid_total for total_grad in grad_sums))
    grad_norm = jnp.sqrt(sum((jnp.sum(grad_item * grad_item) for grad_item in scaled)))
    clip_factor = THRESHOLD / jnp.maximum(grad_norm, THRESHOLD)
    token_new = adam_update(token_table, token_first, token_second, scaled[0] * clip_factor, RATE_TABLE)
    position_new = adam_update(position_table, position_first, position_second, scaled[1] * clip_factor, RATE_TABLE)
    qkv_new = adam_update(qkv_weight, qkv_first, qkv_second, scaled[2] * clip_factor, RATE_MATRIX)
    proj_new = adam_update(proj_weight, proj_first, proj_second, scaled[3] * clip_factor, RATE_MATRIX)
    up_new = adam_update(up_weight, up_first, up_second, scaled[4] * clip_factor, RATE_MATRIX)
    down_new = adam_update(down_weight, down_first, down_second, scaled[5] * clip_factor, RATE_MATRIX)
    gains_new = adam_update(gains_biases, gains_first, gains_second, scaled[6] * clip_factor, RATE_SMALL)
    loss_parts = jnp.stack([loss_sum, valid_total])
    return (token_new[0], token_new[1], token_new[2], position_new[0], position_new[1], position_new[2], qkv_new[0], qkv_new[1], qkv_new[2], proj_new[0], proj_new[1], proj_new[2], up_new[0], up_new[1], up_new[2], down_new[0], down_new[1], down_new[2], gains_new[0], gains_new[1], gains_new[2], grad_norm, loss_parts)
```

```python
import math

import jax
import jax.numpy as jnp
from jax import lax
from jax.experimental import pallas as pl
from jax.experimental.pallas import tpu as pltpu
from jax.sharding import PartitionSpec as P

D = 512
HEADS = 8
HD = 64
FF = 2048
TD = 1024
THEADS = 16
THD = 64
REL = 64
LAYERS = 2
LA = 128
LB = 256
LC = 512
M = 1
STEP = 10


B_ONE = 0.9
B_TWO = 0.999
EPSILON = 1e-10
DECAY = 0.01
THRESHOLD = 0.0003
RATE_TABLE = 1.0
RATE_MATRIX = 0.1
RATE_SMALL = 2.0
HIGH = lax.Precision.HIGHEST


def round_value(value_in):
    return lax.optimization_barrier(value_in.astype(jnp.bfloat16)).astype(jnp.float32)


def same_value(value_in):
    return value_in


def round_keep(value_in):
    return (round_value(value_in), None)


def round_pass(kept, grad):
    return (grad,)


def same_keep(value_in):
    return (value_in, None)


def same_round(kept, grad):
    return (round_value(grad),)


def low(value_in):
    rounding = jax.custom_vjp(round_value)
    rounding.defvjp(round_keep, round_pass)
    return rounding(value_in)


def low_back(value_in):
    passing = jax.custom_vjp(same_value)
    passing.defvjp(same_keep, same_round)
    return passing(value_in)


def dot(left, right, dims=(((1,), (0,)), ((), ()))):
    return lax.dot_general(left, right, dims, preferred_element_type=jnp.float32)


NT = (((1,), (1,)), ((), ()))


@jax.custom_vjp
def matmul(left, right):
    return dot(left.astype(jnp.bfloat16), right)


def matmul_keep(left, right):
    left_low = left.astype(jnp.bfloat16)
    return (dot(left_low, right), (left_low, right))


def matmul_back(kept, grad):
    left_low, right = kept
    grad_low = grad.astype(jnp.bfloat16)
    return (
        dot(grad_low, right, NT),
        dot(left_low, grad_low, (((0,), (0,)), ((), ()))),
    )


matmul.defvjp(matmul_keep, matmul_back)


def layer_norm(values, gain_vec, shift_vec):
    average = jnp.mean(values, axis=-1, keepdims=True)
    centered = values - average
    variance = jnp.mean(centered * centered, axis=-1, keepdims=True)
    return centered * lax.rsqrt(variance + 1e-05) * gain_vec + shift_vec


def bucket_shapes():
    return ((2 * M, LA), (M, LB), (M, LC))


def split_tokens(token_block):
    pieces = []
    offset = 0
    for seq_count, seq_len in bucket_shapes():
        pieces.append(
            token_block[offset : offset + seq_count * seq_len].reshape(
                (seq_count, seq_len) + token_block.shape[1:]
            )
        )
        offset = offset + seq_count * seq_len
    return pieces


def key_masks(seq_lengths):
    mask_list = []
    offset = 0
    for seq_count, seq_len in bucket_shapes():
        lengths_here = seq_lengths[offset : offset + seq_count]
        mask_list.append(jnp.arange(seq_len, dtype=jnp.int32)[None, :] < lengths_here[:, None])
        offset = offset + seq_count
    return mask_list


def position_rows(table):
    pieces = []
    for seq_count, seq_len in bucket_shapes():
        pieces.extend([table[:seq_len]] * seq_count)
    return jnp.concatenate(pieces, axis=0)


def heads_first(block):
    return block.transpose(0, 2, 1, 3)


def attend_parts(qkv_low, key_valid):
    seq_count, seq_len = qkv_low.shape[:2]
    shaped = qkv_low.reshape(seq_count, seq_len, HEADS, 3, HD)
    query, key, value = (heads_first(shaped[:, :, :, part]) for part in range(3))
    scores = jnp.einsum("shqe,shke->shqk", query, key, preferred_element_type=jnp.float32)
    scores = jnp.where(key_valid[:, None, None, :], scores / math.sqrt(HD), -1e30)
    return query, key, value, jax.nn.softmax(scores, axis=-1)


def tokens_first(block):
    seq_count, heads, seq_len, size = block.shape
    return block.transpose(0, 2, 1, 3).reshape(seq_count, seq_len, heads * size)


@jax.custom_vjp
def attend(qkv_block, key_valid):
    return attend_keep(qkv_block, key_valid)[0]


def attend_keep(qkv_block, key_valid):
    qkv_low = qkv_block.astype(jnp.bfloat16)
    query, key, value, soft = attend_parts(qkv_low, key_valid)
    context = jnp.einsum(
        "shqk,shke->shqe", soft.astype(jnp.bfloat16), value, preferred_element_type=jnp.float32
    )
    return (tokens_first(context), (qkv_low, key_valid))


def attend_back(kept, grad):
    qkv_low, key_valid = kept
    seq_count, seq_len = qkv_low.shape[:2]
    query, key, value, soft = attend_parts(qkv_low, key_valid)
    grad_low = heads_first(grad.astype(jnp.bfloat16).reshape(seq_count, seq_len, HEADS, HD))
    soft_low = soft.astype(jnp.bfloat16)
    grad_value = jnp.einsum(
        "shqk,shqe->shke", soft_low, grad_low, preferred_element_type=jnp.float32
    )
    grad_soft = jnp.einsum(
        "shqe,shke->shqk", grad_low, value, preferred_element_type=jnp.float32
    )
    inner = jnp.sum(grad_soft * soft, axis=-1, keepdims=True)
    grad_scores = ((grad_soft - inner) * soft / math.sqrt(HD)).astype(jnp.bfloat16)
    grad_query = jnp.einsum(
        "shqk,shke->shqe", grad_scores, key, preferred_element_type=jnp.float32
    )
    grad_key = jnp.einsum(
        "shqk,shqe->shke", grad_scores, query, preferred_element_type=jnp.float32
    )
    grads = jnp.stack([grad_query, grad_key, grad_value], axis=3)
    grads = grads.transpose(0, 2, 1, 3, 4).reshape(seq_count, seq_len, 3 * D)
    return (grads, None)


attend.defvjp(attend_keep, attend_back)

LOG2E = 1.4426950408889634
LN2 = 0.6931471805599453
GROUPS = 4
S_WIDE = D // GROUPS
T_WIDE = TD // GROUPS
S_DIM = D // REL
T_DIM = TD // REL
FAST_LIMIT = 85.0
SEQS = ((0, LA), (LA, LA), (2 * LA, LB), (2 * LA + LB, LC))
TOKENS_HERE = 2 * LA + LB + LC


def relation_kernel(
    lens_ref, s_ref, t_ref, ds_ref, loss_ref, s_rows, t_rows, d_rows, s_exp, t_exp, s_keep, t_keep
):
    @pl.when((pl.program_id(0) == 0) & (pl.program_id(1) == 0))
    def _():
        loss_ref[...] = jnp.zeros_like(loss_ref)

    s_scale = LOG2E / math.sqrt(S_DIM)
    t_scale = LOG2E / math.sqrt(T_DIM)
    zero = jnp.zeros((), jnp.bfloat16)
    half_heads = 128 // T_DIM

    def prepare(seq):
        off, length = SEQS[seq]
        valid = lens_ref[seq]
        row_valid = lax.broadcasted_iota(jnp.int32, (length, 128), 0) < valid
        s_block = jnp.where(row_valid, s_ref[off : off + length, :], zero)
        s_keep[off : off + length, :] = s_block
        s_rows[:, off : off + length] = s_block.astype(jnp.float32).T
        for half in range(2):
            cols = slice(half * 128, half * 128 + 128)
            t_block = jnp.where(row_valid, t_ref[off : off + length, cols], zero)
            t_keep[half, off : off + length, :] = t_block
            t_rows[cols, off : off + length] = t_block.astype(jnp.float32).T
        s_here = s_rows[:, off : off + length]
        t_here = t_rows[:, off : off + length]
        s_square = jnp.sum((s_here * s_here).reshape(16, S_DIM, length), axis=1)
        t_square = jnp.sum((t_here * t_here).reshape(16, T_DIM, length), axis=1)
        valid_row = (lax.broadcasted_iota(jnp.int32, (8, length), 1) < valid).astype(jnp.float32)
        padded = (length - valid).astype(jnp.float32)
        return (
            jnp.max(s_square) * s_scale,
            jnp.max(t_square) * t_scale,
            valid_row,
            padded,
        )

    info = [prepare(seq) for seq in range(len(SEQS))]

    def fold_rows(value):
        total = value[0:8]
        for start in range(8, value.shape[0], 8):
            total = total + value[start : start + 8]
        return total

    def one_head(seq, half, head):
        off, length = SEQS[seq]
        lane = lax.broadcasted_iota(jnp.int32, (length, 128), 1)
        s_one = jnp.where(
            lane // S_DIM == half * half_heads + head, s_keep[off : off + length, :], zero
        )
        t_one = jnp.where(lane // T_DIM == head, t_keep[half, off : off + length, :], zero)
        return s_one, t_one

    def row_slices(seq, half, head):
        off, length = SEQS[seq]
        index = half * half_heads + head
        s_slice = pl.ds(pl.multiple_of(index * S_DIM, S_DIM), S_DIM)
        t_slice = pl.ds(pl.multiple_of(index * T_DIM, T_DIM), T_DIM)
        return s_slice, t_slice

    def fast_heads(work, half):
        sums = []
        for seq, head, slot in work:
            off, length = SEQS[seq]
            s_bound, t_bound, valid_row, padded = info[seq]
            s_one, t_one = one_head(seq, half, head)
            chunk = min(256, length)
            s_sum = jnp.zeros((8, length), jnp.float32)
            t_sum = jnp.zeros((8, length), jnp.float32)
            for start in range(0, length, chunk):
                rows = slice(off + start, off + start + chunk)
                here = slice(start, start + chunk)
                s_value = jnp.exp2(dot(s_keep[rows, :], s_one, NT) * s_scale - s_bound)
                s_sum = s_sum + fold_rows(s_value)
                s_exp[slot, here, 0:length] = s_value.astype(jnp.bfloat16)
                t_value = jnp.exp2(dot(t_keep[half, rows, :], t_one, NT) * t_scale - t_bound)
                t_sum = t_sum + fold_rows(t_value)
                t_exp[slot, here, 0:length] = t_value.astype(jnp.bfloat16)
            s_total = jnp.sum(s_sum, axis=0, keepdims=True) - padded * jnp.exp2(-s_bound)
            t_total = jnp.sum(t_sum, axis=0, keepdims=True) - padded * jnp.exp2(-t_bound)
            sums.append((s_total, t_total))
        loss_sum = jnp.zeros((8, 128), jnp.float32)
        for (seq, head, slot), (s_total, t_total) in zip(work, sums):
            off, length = SEQS[seq]
            s_bound, t_bound, valid_row, padded = info[seq]
            s_slice, t_slice = row_slices(seq, half, head)
            s_recip = valid_row / s_total
            t_recip = valid_row / t_total
            s_vec = s_rows[s_slice, off : off + length]
            t_vec = t_rows[t_slice, off : off + length]
            t_left = jnp.concatenate([s_vec, s_vec * t_recip, t_vec], axis=0).astype(jnp.bfloat16)
            s_left = jnp.concatenate([s_vec, s_vec * s_recip], axis=0).astype(jnp.bfloat16)
            t_out = dot(t_left, t_exp[slot, 0:length, 0:length])
            s_out = dot(s_left, s_exp[slot, 0:length, 0:length])
            d_rows[s_slice, off : off + length] = (
                s_out[0:8] * s_recip - t_out[0:8] * t_recip + (s_out[8:16] - t_out[8:16]) * valid_row
            )
            inner = t_vec * t_out[16:32]
            inner = (inner[0:8] + inner[8:16]) * t_scale - s_vec * t_out[0:8] * s_scale
            parts = inner * t_recip + (valid_row * 0.125) * (
                jnp.log2(s_total) + s_bound - jnp.log2(t_total) - t_bound
            )
            for start in range(0, length, 128):
                loss_sum = loss_sum + parts[:, start : start + 128]
        loss_ref[...] += loss_sum

    def exact_head(seq, half, head):
        off, length = SEQS[seq]
        valid = lens_ref[seq]
        s_one, t_one = one_head(seq, half, head)
        s_slice, t_slice = row_slices(seq, half, head)
        key_valid = lax.broadcasted_iota(jnp.int32, (length, 128), 0) < valid
        s_exp[0, 0:length, 0:128] = s_one
        t_exp[0, 0:length, 0:128] = t_one

        def log_soft(scores, scale):
            scaled = jnp.where(key_valid, scores * scale, -1e30)
            top = jnp.max(scaled, axis=0, keepdims=True)
            shifted = scaled - top
            total = jnp.sum(jnp.exp2(shifted), axis=0, keepdims=True)
            return shifted - jnp.log2(total)

        def queries(block, carry):
            start = pl.multiple_of(block * 128, 128)
            here = pl.ds(start, 128)
            query_valid = lax.broadcasted_iota(jnp.int32, (length, 128), 1) + start < valid
            both = key_valid & query_valid
            s_log = log_soft(
                dot(s_keep[off : off + length, :], s_exp[0, here, 0:128], NT), s_scale
            )
            t_log = log_soft(
                dot(t_keep[half, off : off + length, :], t_exp[0, here, 0:128], NT), t_scale
            )
            t_soft = jnp.exp2(t_log)
            change = jnp.where(both, jnp.exp2(s_log) - t_soft, 0.0)
            s_exp[1, 0:length, here] = change.astype(jnp.bfloat16)
            loss_ref[...] += fold_rows(jnp.where(both, t_soft * (t_log - s_log), 0.0))
            return carry

        lax.fori_loop(0, length // 128, queries, 0)
        s_vec = s_rows[s_slice, off : off + length]
        left = jnp.concatenate([s_vec, jnp.zeros_like(s_vec)], axis=0).astype(jnp.bfloat16)
        change = s_exp[1, 0:length, 0:length]
        d_rows[s_slice, off : off + length] = (dot(left, change) + dot(left, change, NT))[0:8]

    top_bound = info[0][0]
    for entry in info:
        top_bound = jnp.maximum(top_bound, jnp.maximum(entry[0], entry[1]))
    fast = top_bound < FAST_LIMIT

    @pl.when(fast)
    def _():
        for half in range(2):
            for seqs, at_once in (((3,), 2), ((2,), 4), ((0, 1), 4)):

                def body(step, carry, half=half, seqs=seqs, at_once=at_once):
                    fast_heads(
                        [
                            (seq, step * at_once + offset, offset * len(seqs) + place)
                            for offset in range(at_once)
                            for place, seq in enumerate(seqs)
                        ],
                        half,
                    )
                    return carry

                lax.fori_loop(0, half_heads // at_once, body, 0)

    @pl.when(jnp.logical_not(fast))
    def _():
        for half in range(2):
            for seq in range(len(SEQS)):

                def body(head, carry, half=half, seq=seq):
                    exact_head(seq, half, head)
                    return carry

                lax.fori_loop(0, half_heads, body, 0)

    for off, length in SEQS:
        ds_ref[off : off + length, :] = (
            d_rows[:, off : off + length].T * (1.0 / math.sqrt(S_DIM) / (3 * REL))
        ).astype(ds_ref.dtype)


def relation(seq_lengths, student, teacher):
    block_s = pl.BlockSpec((TOKENS_HERE, S_WIDE), lambda part, group: (0, part * GROUPS + group))
    block_t = pl.BlockSpec((TOKENS_HERE, T_WIDE), lambda part, group: (0, part * GROUPS + group))
    grads, loss = pl.pallas_call(
        relation_kernel,
        grid=(3, GROUPS),
        in_specs=[pl.BlockSpec(memory_space=pltpu.SMEM), block_s, block_t],
        out_specs=[block_s, pl.BlockSpec((8, 128), lambda part, group: (0, 0))],
        out_shape=[
            jax.ShapeDtypeStruct((TOKENS_HERE, 3 * D), jnp.bfloat16),
            jax.ShapeDtypeStruct((8, 128), jnp.float32),
        ],
        scratch_shapes=[
            pltpu.VMEM((S_WIDE, TOKENS_HERE), jnp.float32),
            pltpu.VMEM((T_WIDE, TOKENS_HERE), jnp.float32),
            pltpu.VMEM((S_WIDE, TOKENS_HERE), jnp.float32),
            pltpu.VMEM((8, LC, LC), jnp.bfloat16),
            pltpu.VMEM((8, LC, LC), jnp.bfloat16),
            pltpu.VMEM((TOKENS_HERE, 128), jnp.bfloat16),
            pltpu.VMEM((2, TOKENS_HERE, 128), jnp.bfloat16),
        ],
        compiler_params=pltpu.CompilerParams(vmem_limit_bytes=48 * 2**20),
    )(seq_lengths, student, teacher)
    return grads, jnp.sum(loss) * (LN2 / (3 * REL))


def by_part(columns, heads):
    lead = columns.shape[:-1]
    size = columns.shape[-1] // heads // 3
    shaped = columns.reshape(lead + (heads, 3, size))
    return jnp.moveaxis(shaped, -2, -3).reshape(columns.shape)


def by_head(columns, heads):
    lead = columns.shape[:-1]
    size = columns.shape[-1] // heads // 3
    shaped = columns.reshape(lead + (3, heads, size))
    return jnp.moveaxis(shaped, -2, -3).reshape(columns.shape)


def student_layer(
    hidden, qkv_weight, proj_weight, up_weight, down_weight, gains_biases, mask_list
):
    offset = 2 * D
    qkv_all = matmul(hidden, qkv_weight) + gains_biases[offset : offset + 3 * D]
    context = jnp.concatenate(
        [
            attend(qkv_piece, valid_keys).reshape(-1, D)
            for qkv_piece, valid_keys in zip(split_tokens(qkv_all), mask_list)
        ],
        axis=0,
    )
    mixed = (
        hidden + matmul(context, proj_weight) + gains_biases[offset + 3 * D : offset + 4 * D]
    )
    middle = layer_norm(
        mixed,
        gains_biases[offset + 5 * D + FF : offset + 6 * D + FF],
        gains_biases[offset + 6 * D + FF : offset + 7 * D + FF],
    )
    inner_act = jax.nn.gelu(
        matmul(middle, up_weight) + gains_biases[offset + 4 * D : offset + 4 * D + FF],
        approximate=False,
    )
    output = (
        middle
        + matmul(inner_act, down_weight)
        + gains_biases[offset + 4 * D + FF : offset + 5 * D + FF]
    )
    return layer_norm(
        output,
        gains_biases[offset + 7 * D + FF : offset + 8 * D + FF],
        gains_biases[offset + 8 * D + FF : offset + 9 * D + FF],
    )


def device_forward(
    seq_lengths, token_rows, position_table, qkv_first, qkv_last, proj_weight, up_weight, down_weight, gains_low
):
    mask_list = key_masks(seq_lengths)
    hidden = layer_norm(
        low_back(token_rows) + position_rows(position_table), gains_low[0:D], gains_low[D : 2 * D]
    )
    hidden = student_layer(
        hidden, qkv_first, proj_weight, up_weight, down_weight, gains_low, mask_list
    )
    offset = 2 * D + (LAYERS - 1) * (9 * D + FF)
    return matmul(hidden, qkv_last) + by_part(gains_low[offset : offset + 3 * D], HEADS)


def adam_update(master, first, second, grad_clip, rate):
    first_new = B_ONE * first + (1.0 - B_ONE) * grad_clip
    second_new = B_TWO * second + (1.0 - B_TWO) * grad_clip * grad_clip
    ascent = (
        first_new / (1.0 - B_ONE**STEP) / (jnp.sqrt(second_new / (1.0 - B_TWO**STEP)) + EPSILON)
    )
    return (master - rate * (ascent + DECAY * master), first_new, second_new)


def shards(
    token_ids,
    seq_lengths,
    teacher_hidden,
    teacher_weight,
    token_table,
    token_first,
    token_second,
    position_table,
    position_first,
    position_second,
    qkv_weight,
    qkv_first,
    qkv_second,
    proj_weight,
    proj_first,
    proj_second,
    up_weight,
    up_first,
    up_second,
    down_weight,
    down_first,
    down_second,
    gains_biases,
    gains_first,
    gains_second,
):
    head_index = lax.axis_index("head")
    head_count = lax.axis_size("head")
    local_count = jnp.sum(seq_lengths).astype(jnp.float32)
    valid_total = lax.psum(local_count, ("dp", "head"))
    group_ids = lax.all_gather(token_ids, "head", axis=0, tiled=True)
    col_parts = (
        lax.all_gather(qkv_weight.astype(jnp.bfloat16), "head", axis=2, tiled=True),
        lax.all_gather(proj_weight.astype(jnp.bfloat16), "head", axis=2, tiled=True),
        lax.all_gather(up_weight.astype(jnp.bfloat16), "head", axis=2, tiled=True),
        lax.all_gather(down_weight.astype(jnp.bfloat16), "head", axis=2, tiled=True),
        lax.all_gather(position_table.astype(jnp.bfloat16), "head", axis=1, tiled=True),
        lax.all_gather(gains_biases.astype(jnp.bfloat16), "head", axis=0, tiled=True),
    )
    full_parts = (
        lax.all_gather(col_parts[0], "dp", axis=1, tiled=True),
        lax.all_gather(col_parts[1], "dp", axis=1, tiled=True),
        lax.all_gather(col_parts[2], "dp", axis=1, tiled=True),
        lax.all_gather(col_parts[3], "dp", axis=1, tiled=True),
        lax.all_gather(col_parts[4], "dp", axis=0, tiled=True),
        lax.all_gather(col_parts[5], "dp", axis=0, tiled=True),
        lax.all_gather(token_table.astype(jnp.bfloat16), "dp", axis=0, tiled=True),
    )
    table_rows = full_parts[6]
    shard_rows = token_table.shape[0]
    block_ids = group_ids // shard_rows
    owned = block_ids % head_count == head_index
    local_rows = jnp.where(owned, block_ids // head_count * shard_rows + group_ids % shard_rows, 0)
    picked = jnp.where(owned[:, None], table_rows[local_rows], jnp.zeros((), jnp.bfloat16))
    token_rows = lax.psum_scatter(picked, "head", scatter_dimension=0, tiled=True).astype(
        jnp.float32
    )
    teacher_full = lax.all_gather(teacher_weight, "head", axis=1, tiled=True)
    teacher_qkv = dot(teacher_hidden, by_part(teacher_full, THEADS)).astype(jnp.bfloat16)
    last_parts = by_part(full_parts[0][LAYERS - 1], HEADS)
    final_qkv, backward = jax.vjp(
        lambda *values: device_forward(seq_lengths, *values),
        token_rows,
        full_parts[4].astype(jnp.float32),
        full_parts[0][0],
        last_parts,
        full_parts[1][0],
        full_parts[2][0],
        full_parts[3][0],
        full_parts[5].astype(jnp.float32),
    )
    final_grad, loss_local = relation(seq_lengths, final_qkv.astype(jnp.bfloat16), teacher_qkv)
    row_grad, position_grad, first_grad, last_grad, proj_grad, up_grad, down_grad, gains_grad = backward(
        final_grad.astype(jnp.float32)
    )
    qkv_grad = jnp.stack([first_grad, by_head(last_grad, HEADS)])
    proj_grad, up_grad, down_grad = proj_grad[None], up_grad[None], down_grad[None]
    spread_grads = lax.all_gather(row_grad.astype(jnp.bfloat16), "head", axis=0, tiled=True)
    table_grad = jax.ops.segment_sum(
        spread_grads.astype(jnp.float32),
        jnp.where(owned, local_rows, table_rows.shape[0]),
        num_segments=table_rows.shape[0] + 1,
    )[:-1]
    reduced_rows = (
        lax.psum_scatter(
            qkv_grad.astype(jnp.bfloat16), "dp", scatter_dimension=1, tiled=True
        ).astype(jnp.float32),
        lax.psum_scatter(
            proj_grad.astype(jnp.bfloat16), "dp", scatter_dimension=1, tiled=True
        ).astype(jnp.float32),
        lax.psum_scatter(
            up_grad.astype(jnp.bfloat16), "dp", scatter_dimension=1, tiled=True
        ).astype(jnp.float32),
        lax.psum_scatter(
            down_grad.astype(jnp.bfloat16), "dp", scatter_dimension=1, tiled=True
        ).astype(jnp.float32),
        lax.psum_scatter(
            position_grad.astype(jnp.bfloat16), "dp", scatter_dimension=0, tiled=True
        ).astype(jnp.float32),
        lax.psum_scatter(
            gains_grad.astype(jnp.bfloat16), "dp", scatter_dimension=0, tiled=True
        ).astype(jnp.float32),
        lax.psum_scatter(
            table_grad.astype(jnp.bfloat16), "dp", scatter_dimension=0, tiled=True
        ).astype(jnp.float32),
    )
    reduced = (
        lax.psum_scatter(
            reduced_rows[0].astype(jnp.bfloat16), "head", scatter_dimension=2, tiled=True
        ).astype(jnp.float32),
        lax.psum_scatter(
            reduced_rows[1].astype(jnp.bfloat16), "head", scatter_dimension=2, tiled=True
        ).astype(jnp.float32),
        lax.psum_scatter(
            reduced_rows[2].astype(jnp.bfloat16), "head", scatter_dimension=2, tiled=True
        ).astype(jnp.float32),
        lax.psum_scatter(
            reduced_rows[3].astype(jnp.bfloat16), "head", scatter_dimension=2, tiled=True
        ).astype(jnp.float32),
        lax.psum_scatter(
            reduced_rows[4].astype(jnp.bfloat16), "head", scatter_dimension=1, tiled=True
        ).astype(jnp.float32),
        lax.psum_scatter(
            reduced_rows[5].astype(jnp.bfloat16), "head", scatter_dimension=0, tiled=True
        ).astype(jnp.float32),
    )
    shard_grads = (
        reduced_rows[6],
        reduced[4],
        reduced[0],
        reduced[1],
        reduced[2],
        reduced[3],
        reduced[5],
    )
    squares = sum((jnp.sum(grad_item * grad_item) for grad_item in shard_grads))
    square_total, loss_total = lax.psum((squares, loss_local), ("dp", "head"))
    grad_norm = jnp.sqrt(square_total) / valid_total
    clip_factor = THRESHOLD / jnp.maximum(grad_norm, THRESHOLD)
    factor = clip_factor / valid_total
    token_new = adam_update(
        token_table, token_first, token_second, shard_grads[0] * factor, RATE_TABLE
    )
    position_new = adam_update(
        position_table, position_first, position_second, shard_grads[1] * factor, RATE_TABLE
    )
    qkv_new = adam_update(qkv_weight, qkv_first, qkv_second, shard_grads[2] * factor, RATE_MATRIX)
    proj_new = adam_update(
        proj_weight, proj_first, proj_second, shard_grads[3] * factor, RATE_MATRIX
    )
    up_new = adam_update(up_weight, up_first, up_second, shard_grads[4] * factor, RATE_MATRIX)
    down_new = adam_update(
        down_weight, down_first, down_second, shard_grads[5] * factor, RATE_MATRIX
    )
    gains_new = adam_update(
        gains_biases, gains_first, gains_second, shard_grads[6] * factor, RATE_SMALL
    )
    loss_parts = jnp.stack([loss_total, valid_total])
    return (
        token_new[0],
        token_new[1],
        token_new[2],
        position_new[0],
        position_new[1],
        position_new[2],
        qkv_new[0],
        qkv_new[1],
        qkv_new[2],
        proj_new[0],
        proj_new[1],
        proj_new[2],
        up_new[0],
        up_new[1],
        up_new[2],
        down_new[0],
        down_new[1],
        down_new[2],
        gains_new[0],
        gains_new[1],
        gains_new[2],
        grad_norm,
        loss_parts,
    )


def solution(mesh):
    placed = (
        P(("dp", "head")),
        P(("dp", "head")),
        P(("dp", "head"), None),
        P(None, "head"),
        P(("dp", "head"), None),
        P(("dp", "head"), None),
        P(("dp", "head"), None),
        P("dp", "head"),
        P("dp", "head"),
        P("dp", "head"),
        P(None, "dp", "head"),
        P(None, "dp", "head"),
        P(None, "dp", "head"),
        P(None, "dp", "head"),
        P(None, "dp", "head"),
        P(None, "dp", "head"),
        P(None, "dp", "head"),
        P(None, "dp", "head"),
        P(None, "dp", "head"),
        P(None, "dp", "head"),
        P(None, "dp", "head"),
        P(None, "dp", "head"),
        P(("dp", "head")),
        P(("dp", "head")),
        P(("dp", "head")),
    )
    return jax.shard_map(
        shards,
        mesh=mesh,
        in_specs=placed,
        out_specs=(
            P(("dp", "head"), None),
            P(("dp", "head"), None),
            P(("dp", "head"), None),
            P("dp", "head"),
            P("dp", "head"),
            P("dp", "head"),
            P(None, "dp", "head"),
            P(None, "dp", "head"),
            P(None, "dp", "head"),
            P(None, "dp", "head"),
            P(None, "dp", "head"),
            P(None, "dp", "head"),
            P(None, "dp", "head"),
            P(None, "dp", "head"),
            P(None, "dp", "head"),
            P(None, "dp", "head"),
            P(None, "dp", "head"),
            P(None, "dp", "head"),
            P(("dp", "head")),
            P(("dp", "head")),
            P(("dp", "head")),
            P(),
            P(),
        ),
        check_vma=False,
    )
```

```python
import functools
import math

import jax
import jax.numpy as jnp
from jax import lax
from jax.experimental import pallas as pl
from jax.experimental.pallas import tpu as pltpu
from jax.sharding import PartitionSpec as P

D = 512
HEADS = 8
HD = 64
FF = 2048
TD = 1024
THEADS = 16
THD = 64
REL = 64
LAYERS = 2
LA = 128
LB = 256
LC = 512
M = 1
STEP = 10


B_ONE = 0.9
B_TWO = 0.999
EPSILON = 1e-10
DECAY = 0.01
THRESHOLD = 0.0003
RATE_TABLE = 1.0
RATE_MATRIX = 0.1
RATE_SMALL = 2.0
HIGH = lax.Precision.HIGHEST


def round_value(value_in):
    return lax.optimization_barrier(value_in.astype(jnp.bfloat16)).astype(jnp.float32)


def same_value(value_in):
    return value_in


def round_keep(value_in):
    return (round_value(value_in), None)


def round_pass(kept, grad):
    return (grad,)


def same_keep(value_in):
    return (value_in, None)


def same_round(kept, grad):
    return (round_value(grad),)


def low(value_in):
    rounding = jax.custom_vjp(round_value)
    rounding.defvjp(round_keep, round_pass)
    return rounding(value_in)


def low_back(value_in):
    passing = jax.custom_vjp(same_value)
    passing.defvjp(same_keep, same_round)
    return passing(value_in)


def dot(left, right, dims=(((1,), (0,)), ((), ()))):
    return lax.dot_general(left, right, dims, preferred_element_type=jnp.float32)


NT = (((1,), (1,)), ((), ()))


@jax.custom_vjp
def matmul(left, right):
    return dot(left.astype(jnp.bfloat16), right)


def matmul_keep(left, right):
    left_low = left.astype(jnp.bfloat16)
    return (dot(left_low, right), (left_low, right))


def matmul_back(kept, grad):
    left_low, right = kept
    grad_low = grad.astype(jnp.bfloat16)
    return (
        dot(grad_low, right, NT),
        dot(left_low, grad_low, (((0,), (0,)), ((), ()))),
    )


matmul.defvjp(matmul_keep, matmul_back)


def layer_norm(values, gain_vec, shift_vec):
    average = jnp.mean(values, axis=-1, keepdims=True)
    centered = values - average
    variance = jnp.mean(centered * centered, axis=-1, keepdims=True)
    return centered * lax.rsqrt(variance + 1e-05) * gain_vec + shift_vec


def bucket_shapes():
    return ((2 * M, LA), (M, LB), (M, LC))


def split_tokens(token_block):
    pieces = []
    offset = 0
    for seq_count, seq_len in bucket_shapes():
        pieces.append(
            token_block[offset : offset + seq_count * seq_len].reshape(
                (seq_count, seq_len) + token_block.shape[1:]
            )
        )
        offset = offset + seq_count * seq_len
    return pieces


def key_masks(seq_lengths):
    mask_list = []
    offset = 0
    for seq_count, seq_len in bucket_shapes():
        lengths_here = seq_lengths[offset : offset + seq_count]
        mask_list.append(jnp.arange(seq_len, dtype=jnp.int32)[None, :] < lengths_here[:, None])
        offset = offset + seq_count
    return mask_list


def position_rows(table):
    pieces = []
    for seq_count, seq_len in bucket_shapes():
        pieces.extend([table[:seq_len]] * seq_count)
    return jnp.concatenate(pieces, axis=0)


def heads_first(block):
    return block.transpose(0, 2, 1, 3)


def attend_parts(parts, key_valid):
    query, key, value = parts
    scores = jnp.einsum("shqe,shke->shqk", query, key, preferred_element_type=jnp.float32)
    scores = jnp.where(key_valid[:, None, None, :], scores / math.sqrt(HD), -1e30)
    return jax.nn.softmax(scores, axis=-1)


def split_heads(block):
    seq_count, seq_len, width = block.shape
    return block.reshape(seq_count, seq_len, HEADS, HD).transpose(0, 2, 1, 3)


def join_heads(block):
    seq_count, heads, seq_len, size = block.shape
    return block.transpose(0, 2, 1, 3).reshape(seq_count, seq_len, heads * size)


@jax.custom_vjp
def attend(query, key, value, key_valid):
    return attend_keep(query, key, value, key_valid)[0]


def attend_keep(query, key, value, key_valid):
    parts = tuple(split_heads(part.astype(jnp.bfloat16)) for part in (query, key, value))
    soft = attend_parts(parts, key_valid)
    context = jnp.einsum(
        "shqk,shke->shqe", soft.astype(jnp.bfloat16), parts[2], preferred_element_type=jnp.float32
    )
    return (join_heads(context), (parts, key_valid))


def attend_back(kept, grad):
    parts, key_valid = kept
    query, key, value = parts
    soft = attend_parts(parts, key_valid)
    grad_low = split_heads(grad.astype(jnp.bfloat16))
    soft_low = soft.astype(jnp.bfloat16)
    grad_value = jnp.einsum(
        "shqk,shqe->shke", soft_low, grad_low, preferred_element_type=jnp.float32
    )
    grad_soft = jnp.einsum(
        "shqe,shke->shqk", grad_low, value, preferred_element_type=jnp.float32
    )
    inner = jnp.sum(grad_soft * soft, axis=-1, keepdims=True)
    grad_scores = ((grad_soft - inner) * soft / math.sqrt(HD)).astype(jnp.bfloat16)
    grad_query = jnp.einsum(
        "shqk,shke->shqe", grad_scores, key, preferred_element_type=jnp.float32
    )
    grad_key = jnp.einsum(
        "shqk,shqe->shke", grad_scores, query, preferred_element_type=jnp.float32
    )
    return (join_heads(grad_query), join_heads(grad_key), join_heads(grad_value), None)


attend.defvjp(attend_keep, attend_back)

LOG2E = 1.4426950408889634
LN2 = 0.6931471805599453
GROUPS = 4
S_WIDE = D // GROUPS
T_WIDE = TD // GROUPS
S_DIM = D // REL
T_DIM = TD // REL
FAST_LIMIT = 85.0
SEQS = ((0, LA), (LA, LA), (2 * LA, LB), (2 * LA + LB, LC))
TOKENS_HERE = 2 * LA + LB + LC


def relation_kernel(
    lens_ref, s_ref, t_ref, ds_ref, loss_ref, s_rows, t_rows, d_rows, s_exp, t_exp, s_keep, t_keep
):
    @pl.when((pl.program_id(0) == 0) & (pl.program_id(1) == 0))
    def _():
        loss_ref[...] = jnp.zeros_like(loss_ref)

    s_scale = LOG2E / math.sqrt(S_DIM)
    t_scale = LOG2E / math.sqrt(T_DIM)
    zero = jnp.zeros((), jnp.bfloat16)
    half_heads = 128 // T_DIM

    def prepare(seq):
        off, length = SEQS[seq]
        valid = lens_ref[seq]
        row_valid = lax.broadcasted_iota(jnp.int32, (length, 128), 0) < valid
        s_block = jnp.where(row_valid, s_ref[off : off + length, :], zero)
        s_keep[off : off + length, :] = s_block
        s_rows[:, off : off + length] = s_block.astype(jnp.float32).T
        for half in range(2):
            cols = slice(half * 128, half * 128 + 128)
            t_block = jnp.where(row_valid, t_ref[off : off + length, cols], zero)
            t_keep[half, off : off + length, :] = t_block
            t_rows[cols, off : off + length] = t_block.astype(jnp.float32).T
        s_here = s_rows[:, off : off + length]
        t_here = t_rows[:, off : off + length]
        s_square = jnp.sum((s_here * s_here).reshape(16, S_DIM, length), axis=1)
        t_square = jnp.sum((t_here * t_here).reshape(16, T_DIM, length), axis=1)
        valid_row = (lax.broadcasted_iota(jnp.int32, (8, length), 1) < valid).astype(jnp.float32)
        padded = (length - valid).astype(jnp.float32)
        return (
            jnp.max(s_square) * s_scale,
            jnp.max(t_square) * t_scale,
            valid_row,
            padded,
        )

    info = [prepare(seq) for seq in range(len(SEQS))]

    def fold_rows(value):
        total = value[0:8]
        for start in range(8, value.shape[0], 8):
            total = total + value[start : start + 8]
        return total

    def one_head(seq, half, head):
        off, length = SEQS[seq]
        lane = lax.broadcasted_iota(jnp.int32, (length, 128), 1)
        s_one = jnp.where(
            lane // S_DIM == half * half_heads + head, s_keep[off : off + length, :], zero
        )
        t_one = jnp.where(lane // T_DIM == head, t_keep[half, off : off + length, :], zero)
        return s_one, t_one

    def row_slices(seq, half, head):
        off, length = SEQS[seq]
        index = half * half_heads + head
        s_slice = pl.ds(pl.multiple_of(index * S_DIM, S_DIM), S_DIM)
        t_slice = pl.ds(pl.multiple_of(index * T_DIM, T_DIM), T_DIM)
        return s_slice, t_slice

    def fast_heads(work, half):
        sums = []
        for seq, head, slot in work:
            off, length = SEQS[seq]
            s_bound, t_bound, valid_row, padded = info[seq]
            s_one, t_one = one_head(seq, half, head)
            chunk = min(256, length)
            s_sum = jnp.zeros((8, length), jnp.float32)
            t_sum = jnp.zeros((8, length), jnp.float32)
            for start in range(0, length, chunk):
                rows = slice(off + start, off + start + chunk)
                here = slice(start, start + chunk)
                s_value = jnp.exp2(dot(s_keep[rows, :], s_one, NT) * s_scale - s_bound)
                s_sum = s_sum + fold_rows(s_value)
                s_exp[slot, here, 0:length] = s_value.astype(jnp.bfloat16)
                t_value = jnp.exp2(dot(t_keep[half, rows, :], t_one, NT) * t_scale - t_bound)
                t_sum = t_sum + fold_rows(t_value)
                t_exp[slot, here, 0:length] = t_value.astype(jnp.bfloat16)
            s_total = jnp.sum(s_sum, axis=0, keepdims=True) - padded * jnp.exp2(-s_bound)
            t_total = jnp.sum(t_sum, axis=0, keepdims=True) - padded * jnp.exp2(-t_bound)
            sums.append((s_total, t_total))
        loss_sum = jnp.zeros((8, 128), jnp.float32)
        for (seq, head, slot), (s_total, t_total) in zip(work, sums):
            off, length = SEQS[seq]
            s_bound, t_bound, valid_row, padded = info[seq]
            s_slice, t_slice = row_slices(seq, half, head)
            s_recip = valid_row / s_total
            t_recip = valid_row / t_total
            s_vec = s_rows[s_slice, off : off + length]
            t_vec = t_rows[t_slice, off : off + length]
            t_left = jnp.concatenate([s_vec, s_vec * t_recip, t_vec], axis=0).astype(jnp.bfloat16)
            s_left = jnp.concatenate([s_vec, s_vec * s_recip], axis=0).astype(jnp.bfloat16)
            t_out = dot(t_left, t_exp[slot, 0:length, 0:length])
            s_out = dot(s_left, s_exp[slot, 0:length, 0:length])
            d_rows[s_slice, off : off + length] = (
                s_out[0:8] * s_recip - t_out[0:8] * t_recip + (s_out[8:16] - t_out[8:16]) * valid_row
            )
            inner = t_vec * t_out[16:32]
            inner = (inner[0:8] + inner[8:16]) * t_scale - s_vec * t_out[0:8] * s_scale
            parts = inner * t_recip + (valid_row * 0.125) * (
                jnp.log2(s_total) + s_bound - jnp.log2(t_total) - t_bound
            )
            for start in range(0, length, 128):
                loss_sum = loss_sum + parts[:, start : start + 128]
        loss_ref[...] += loss_sum

    def exact_head(seq, half, head):
        off, length = SEQS[seq]
        valid = lens_ref[seq]
        s_one, t_one = one_head(seq, half, head)
        s_slice, t_slice = row_slices(seq, half, head)
        key_valid = lax.broadcasted_iota(jnp.int32, (length, 128), 0) < valid
        s_exp[0, 0:length, 0:128] = s_one
        t_exp[0, 0:length, 0:128] = t_one

        def log_soft(scores, scale):
            scaled = jnp.where(key_valid, scores * scale, -1e30)
            top = jnp.max(scaled, axis=0, keepdims=True)
            shifted = scaled - top
            total = jnp.sum(jnp.exp2(shifted), axis=0, keepdims=True)
            return shifted - jnp.log2(total)

        def queries(block, carry):
            start = pl.multiple_of(block * 128, 128)
            here = pl.ds(start, 128)
            query_valid = lax.broadcasted_iota(jnp.int32, (length, 128), 1) + start < valid
            both = key_valid & query_valid
            s_log = log_soft(
                dot(s_keep[off : off + length, :], s_exp[0, here, 0:128], NT), s_scale
            )
            t_log = log_soft(
                dot(t_keep[half, off : off + length, :], t_exp[0, here, 0:128], NT), t_scale
            )
            t_soft = jnp.exp2(t_log)
            change = jnp.where(both, jnp.exp2(s_log) - t_soft, 0.0)
            s_exp[1, 0:length, here] = change.astype(jnp.bfloat16)
            loss_ref[...] += fold_rows(jnp.where(both, t_soft * (t_log - s_log), 0.0))
            return carry

        lax.fori_loop(0, length // 128, queries, 0)
        s_vec = s_rows[s_slice, off : off + length]
        left = jnp.concatenate([s_vec, jnp.zeros_like(s_vec)], axis=0).astype(jnp.bfloat16)
        change = s_exp[1, 0:length, 0:length]
        d_rows[s_slice, off : off + length] = (dot(left, change) + dot(left, change, NT))[0:8]

    top_bound = info[0][0]
    for entry in info:
        top_bound = jnp.maximum(top_bound, jnp.maximum(entry[0], entry[1]))
    fast = top_bound < FAST_LIMIT

    @pl.when(fast)
    def _():
        for half in range(2):
            for seqs, at_once in (((3,), 2), ((2,), 4), ((0, 1), 4)):

                def body(step, carry, half=half, seqs=seqs, at_once=at_once):
                    fast_heads(
                        [
                            (seq, step * at_once + offset, offset * len(seqs) + place)
                            for offset in range(at_once)
                            for place, seq in enumerate(seqs)
                        ],
                        half,
                    )
                    return carry

                lax.fori_loop(0, half_heads // at_once, body, 0)

    @pl.when(jnp.logical_not(fast))
    def _():
        for half in range(2):
            for seq in range(len(SEQS)):

                def body(head, carry, half=half, seq=seq):
                    exact_head(seq, half, head)
                    return carry

                lax.fori_loop(0, half_heads, body, 0)

    for off, length in SEQS:
        ds_ref[off : off + length, :] = (
            d_rows[:, off : off + length].T * (1.0 / math.sqrt(S_DIM) / (3 * REL))
        ).astype(ds_ref.dtype)


def relation(seq_lengths, student, teacher):
    block_s = pl.BlockSpec((None, TOKENS_HERE, S_WIDE), lambda part, group: (part, 0, group))
    block_t = pl.BlockSpec((None, TOKENS_HERE, T_WIDE), lambda part, group: (part, 0, group))
    grads, loss = pl.pallas_call(
        relation_kernel,
        grid=(3, GROUPS),
        in_specs=[pl.BlockSpec(memory_space=pltpu.SMEM), block_s, block_t],
        out_specs=[block_s, pl.BlockSpec((8, 128), lambda part, group: (0, 0))],
        out_shape=[
            jax.ShapeDtypeStruct((3, TOKENS_HERE, D), jnp.bfloat16),
            jax.ShapeDtypeStruct((8, 128), jnp.float32),
        ],
        scratch_shapes=[
            pltpu.VMEM((S_WIDE, TOKENS_HERE), jnp.float32),
            pltpu.VMEM((T_WIDE, TOKENS_HERE), jnp.float32),
            pltpu.VMEM((S_WIDE, TOKENS_HERE), jnp.float32),
            pltpu.VMEM((8, LC, LC), jnp.bfloat16),
            pltpu.VMEM((8, LC, LC), jnp.bfloat16),
            pltpu.VMEM((TOKENS_HERE, 128), jnp.bfloat16),
            pltpu.VMEM((2, TOKENS_HERE, 128), jnp.bfloat16),
        ],
        compiler_params=pltpu.CompilerParams(vmem_limit_bytes=48 * 2**20),
    )(seq_lengths, student, teacher)
    return grads, jnp.sum(loss) * (LN2 / (3 * REL))


def by_part(columns, heads):
    lead = columns.shape[:-1]
    size = columns.shape[-1] // heads // 3
    shaped = columns.reshape(lead + (heads, 3, size))
    return jnp.moveaxis(shaped, -2, -3).reshape(columns.shape)


def by_head(columns, heads):
    lead = columns.shape[:-1]
    size = columns.shape[-1] // heads // 3
    shaped = columns.reshape(lead + (3, heads, size))
    return jnp.moveaxis(shaped, -2, -3).reshape(columns.shape)


def student_layer(
    hidden, qkv_weight, proj_weight, up_weight, down_weight, gains_biases, mask_list
):
    offset = 2 * D
    bias = by_part(gains_biases[offset : offset + 3 * D], HEADS).reshape(3, D)
    parts = [
        split_tokens(matmul(hidden, qkv_weight[part]) + bias[part]) for part in range(3)
    ]
    context = jnp.concatenate(
        [
            attend(query, key, value, valid_keys).reshape(-1, D)
            for query, key, value, valid_keys in zip(*parts, mask_list)
        ],
        axis=0,
    )
    mixed = (
        hidden + matmul(context, proj_weight) + gains_biases[offset + 3 * D : offset + 4 * D]
    )
    middle = layer_norm(
        mixed,
        gains_biases[offset + 5 * D + FF : offset + 6 * D + FF],
        gains_biases[offset + 6 * D + FF : offset + 7 * D + FF],
    )
    inner_act = jax.nn.gelu(
        matmul(middle, up_weight) + gains_biases[offset + 4 * D : offset + 4 * D + FF],
        approximate=False,
    )
    output = (
        middle
        + matmul(inner_act, down_weight)
        + gains_biases[offset + 4 * D + FF : offset + 5 * D + FF]
    )
    return layer_norm(
        output,
        gains_biases[offset + 7 * D + FF : offset + 8 * D + FF],
        gains_biases[offset + 8 * D + FF : offset + 9 * D + FF],
    )


def device_forward(
    seq_lengths, token_rows, position_table, qkv_first, qkv_last, proj_weight, up_weight, down_weight, gains_low
):
    mask_list = key_masks(seq_lengths)
    hidden = layer_norm(
        low_back(token_rows) + position_rows(position_table), gains_low[0:D], gains_low[D : 2 * D]
    )
    hidden = student_layer(
        hidden, qkv_first, proj_weight, up_weight, down_weight, gains_low, mask_list
    )
    offset = 2 * D + (LAYERS - 1) * (9 * D + FF)
    bias = by_part(gains_low[offset : offset + 3 * D], HEADS).reshape(3, D)
    return tuple(matmul(hidden, qkv_last[part]) + bias[part] for part in range(3))


MESH_IDS = pl.DeviceIdType.MESH


def barrier_all(rank, count, place):
    barrier = pltpu.get_barrier_semaphore()

    def greet(step, carry):
        pl.semaphore_signal(
            barrier, inc=1, device_id=place(lax.rem(rank + step, count)), device_id_type=MESH_IDS
        )
        return carry

    lax.fori_loop(1, count, greet, 0)
    pl.semaphore_wait(barrier, count - 1)


class Spot:
    def __init__(self, n_dp, n_head):
        self.n_dp, self.n_head = n_dp, n_head
        self.count = n_dp * n_head
        self.nz, self.nx = n_dp // 2, n_head // 2
        dp, head = lax.axis_index("dp"), lax.axis_index("head")
        self.rank = dp * n_head + head
        self.z, self.y = dp // 2, lax.rem(dp, 2)
        self.x, self.c = head // 2, lax.rem(head, 2)

    def place(self, rank):
        return (rank // self.n_head, lax.rem(rank, self.n_head))

    def device(self, z, y, x, c):
        return (z * 2 + y, x * 2 + c)


def remote(source, target, send_sem, recv_sem, device):
    return pltpu.make_async_remote_copy(
        src_ref=source,
        dst_ref=target,
        send_sem=send_sem,
        recv_sem=recv_sem,
        device_id=device,
        device_id_type=MESH_IDS,
    )


def start_all_to_all(spot, source, target, send_sems, recv_sems, local_sem):
    pltpu.make_async_copy(source.at[spot.rank], target.at[spot.rank], local_sem).start()

    def send(step, carry):
        peer = lax.rem(spot.rank + step, spot.count)
        remote(
            source.at[peer], target.at[spot.rank], send_sems.at[step], recv_sems.at[step], spot.place(peer)
        ).start()
        return carry

    lax.fori_loop(1, spot.count, send, 0)


def finish_all_to_all(spot, source, target, send_sems, recv_sems, local_sem):
    def take(step, carry):
        origin = lax.rem(spot.rank + spot.count - step, spot.count)
        copy = remote(
            source.at[origin], target.at[origin], send_sems.at[step], recv_sems.at[step], spot.place(origin)
        )
        copy.wait_recv()
        copy.wait_send()
        return carry

    lax.fori_loop(1, spot.count, take, 0)
    pltpu.make_async_copy(source.at[spot.rank], target.at[spot.rank], local_sem).wait()


def small_exchange_kernel(sizes, source, target, send_sems, recv_sems, local_sem):
    spot = Spot(*sizes)
    barrier_all(spot.rank, spot.count, spot.place)
    start_all_to_all(spot, source, target, send_sems, recv_sems, local_sem)
    finish_all_to_all(spot, source, target, send_sems, recv_sems, local_sem)


def small_exchange(sizes, messages, collective_id):
    count = sizes[0] * sizes[1]
    return pl.pallas_call(
        functools.partial(small_exchange_kernel, sizes),
        in_specs=[pl.BlockSpec(memory_space=pltpu.VMEM)],
        out_specs=pl.BlockSpec(memory_space=pltpu.VMEM),
        out_shape=jax.ShapeDtypeStruct(messages.shape, messages.dtype),
        scratch_shapes=[
            pltpu.SemaphoreType.DMA((count,)),
            pltpu.SemaphoreType.DMA((count,)),
            pltpu.SemaphoreType.DMA,
        ],
        compiler_params=pltpu.CompilerParams(collective_id=collective_id, has_side_effects=True),
    )(messages)


def gather_kernel(
    sizes,
    rows,
    shard,
    teach,
    rows_out,
    full,
    teach_full,
    row_send,
    row_recv,
    piece_send,
    piece_recv,
    teach_send,
    teach_recv,
    local_sems,
):
    spot = Spot(*sizes)
    z, y, x, c, nz, nx = spot.z, spot.y, spot.x, spot.c, spot.nz, spot.nx
    wide = teach.shape[2]
    barrier_all(spot.rank, spot.count, spot.place)
    own_copy = pltpu.make_async_copy(shard, full.at[z * 2 + y, x * 2 + c], local_sems.at[1])
    own_copy.start()

    def cols(head):
        return pl.ds(pl.multiple_of(head * wide, wide), wide)

    own_teach = pltpu.make_async_copy(teach, teach_full.at[:, :, cols(x * 2 + c)], local_sems.at[2])
    own_teach.start()
    sends = []

    def send_piece(source, piece, device):
        copy = remote(
            source,
            full.at[piece[0] * 2 + piece[1], piece[2] * 2 + piece[3]],
            piece_send.at[len(sends)],
            piece_recv.at[piece[0] * 2 + piece[1], piece[2] * 2 + piece[3]],
            device,
        )
        copy.start()
        sends.append(copy)

    def wait_piece(piece):
        here = full.at[piece[0] * 2 + piece[1], piece[2] * 2 + piece[3]]
        remote(
            here,
            here,
            piece_send.at[0],
            piece_recv.at[piece[0] * 2 + piece[1], piece[2] * 2 + piece[3]],
            spot.device(z, y, x, 1 - c),
        ).wait_recv()
        return here

    own = (z, y, x, c)
    others_x = [lax.rem(x + step, nx) for step in range(1, nx)]
    for step in range(1, nz):
        send_piece(shard, own, spot.device(lax.rem(z + step, nz), y, x, c))
    teach_sends = []

    def send_teach(source, head, device, slot):
        copy = remote(
            source, teach_full.at[:, :, cols(head)], teach_send.at[slot], teach_recv.at[head], device
        )
        copy.start()
        teach_sends.append(copy)

    for step, other in enumerate(others_x):
        send_piece(shard, own, spot.device(z, y, other, c))
        send_teach(teach, x * 2 + c, spot.device(z, y, other, c), step)
    send_piece(shard, own, spot.device(z, 1 - y, x, c))
    send_piece(shard, own, spot.device(z, y, x, 1 - c))
    send_teach(teach, x * 2 + c, spot.device(z, y, x, 1 - c), nx - 1)
    start_all_to_all(spot, rows, rows_out, row_send, row_recv, local_sems.at[0])
    for step in range(1, nz):
        piece = (lax.rem(z + nz - step, nz), y, x, c)
        here = wait_piece(piece)
        for other in others_x:
            send_piece(here, piece, spot.device(z, y, other, c))
        send_piece(here, piece, spot.device(z, 1 - y, x, c))
        send_piece(here, piece, spot.device(z, y, x, 1 - c))
    for step in range(nz):
        for other in others_x:
            piece = (lax.rem(z + nz - step, nz), y, other, c)
            here = wait_piece(piece)
            send_piece(here, piece, spot.device(z, 1 - y, x, c))
            send_piece(here, piece, spot.device(z, y, x, 1 - c))

    def wait_teach(head):
        here = teach_full.at[:, :, cols(head)]
        remote(
            here, here, teach_send.at[0], teach_recv.at[head], spot.device(z, y, x, 1 - c)
        ).wait_recv()
        return here

    for step, other in enumerate(others_x):
        here = wait_teach(other * 2 + c)
        send_teach(here, other * 2 + c, spot.device(z, y, x, 1 - c), nx + step)
    for step in range(nz):
        for column in [x] + others_x:
            piece = (lax.rem(z + nz - step, nz), 1 - y, column, c)
            here = wait_piece(piece)
            send_piece(here, piece, spot.device(z, y, x, 1 - c))
    for step in range(nz):
        for side in (y, 1 - y):
            for column in [x] + others_x:
                wait_piece((lax.rem(z + nz - step, nz), side, column, 1 - c))
    for column in [x] + others_x:
        wait_teach(column * 2 + 1 - c)
    for copy in sends + teach_sends:
        copy.wait_send()
    finish_all_to_all(spot, rows, rows_out, row_send, row_recv, local_sems.at[0])
    own_copy.wait()
    own_teach.wait()


def gather_weights(sizes, rows, shard, teach):
    n_dp, n_head = sizes
    count = n_dp * n_head
    nz, nx = n_dp // 2, n_head // 2
    sends = (nz - 1) + (nx - 1) + 2 + (nz - 1) * (nx + 1) + nz * (nx - 1) * 2 + nz * nx
    anywhere = pl.BlockSpec(memory_space=pl.ANY)
    return pl.pallas_call(
        functools.partial(gather_kernel, sizes),
        in_specs=[anywhere] * 3,
        out_specs=[anywhere] * 3,
        out_shape=[
            jax.ShapeDtypeStruct(rows.shape, rows.dtype),
            jax.ShapeDtypeStruct((n_dp, n_head) + shard.shape, shard.dtype),
            jax.ShapeDtypeStruct(teach.shape[:2] + (n_head * teach.shape[2],), teach.dtype),
        ],
        scratch_shapes=[
            pltpu.SemaphoreType.DMA((count,)),
            pltpu.SemaphoreType.DMA((count,)),
            pltpu.SemaphoreType.DMA((sends,)),
            pltpu.SemaphoreType.DMA((n_dp, n_head)),
            pltpu.SemaphoreType.DMA((2 * nx,)),
            pltpu.SemaphoreType.DMA((n_head,)),
            pltpu.SemaphoreType.DMA((3,)),
        ],
        compiler_params=pltpu.CompilerParams(collective_id=2, has_side_effects=True),
    )(rows, shard, teach)


def reduce_kernel(
    sizes,
    rows,
    pieces,
    rows_out,
    total,
    core_in,
    y_in,
    x_in,
    z_in,
    row_send,
    row_recv,
    core_send,
    core_recv,
    y_send,
    y_recv,
    x_send,
    x_recv,
    z_send,
    z_recv,
    local_sem,
):
    spot = Spot(*sizes)
    z, y, x, c, nz, nx = spot.z, spot.y, spot.x, spot.c, spot.nz, spot.nx
    depth = pieces.shape[2]
    chunk = 16
    barrier_all(spot.rank, spot.count, spot.place)
    sibling = spot.device(z, y, x, 1 - c)
    opposite = spot.device(z, 1 - y, x, c)

    def core_copy(deep, side, column):
        return remote(
            pieces.at[deep * 2 + side, column * 2 + 1 - c],
            core_in.at[deep, side, column],
            core_send.at[deep, side, column],
            core_recv.at[deep, side, column],
            sibling,
        )

    def y_copy(deep, column):
        return remote(
            core_in.at[deep, 1 - y, column],
            y_in.at[deep, column],
            y_send.at[deep, column],
            y_recv.at[deep, column],
            opposite,
        )

    def x_copy(step, deep):
        column = lax.rem(x + step, nx)
        return remote(
            y_in.at[deep, column],
            x_in.at[step - 1, deep],
            x_send.at[step - 1, deep],
            x_recv.at[step - 1, deep],
            spot.device(z, y, column, c),
        )

    def z_copy(step):
        deep = lax.rem(z + step, nz)
        return remote(
            y_in.at[deep, x],
            z_in.at[step - 1],
            z_send.at[step - 1],
            z_recv.at[step - 1],
            spot.device(deep, y, x, c),
        )

    def add_into(target, sources):
        def some(block, carry):
            here = pl.ds(pl.multiple_of(block * chunk, chunk), chunk)
            value = target[here, :].astype(jnp.float32)
            for source in sources:
                value = value + source[here, :].astype(jnp.float32)
            target[here, :] = value.astype(target.dtype)
            return carry

        lax.fori_loop(0, depth // chunk, some, 0, unroll=5 if depth // chunk % 5 == 0 else 1)

    depth_order = lambda step: lax.rem(z + 1 + step, nz)
    columns = [lax.rem(x + step, nx) for step in range(1, nx)] + [x]
    for side in (1 - y, y):
        for column in columns:

            def send_core(step, carry, side=side, column=column):
                core_copy(depth_order(step), side, column).start()
                return carry

            lax.fori_loop(0, nz, send_core, 0)
    start_all_to_all(spot, rows, rows_out, row_send, row_recv, local_sem)
    for side in (1 - y, y):
        for column in columns:

            def take_core(step, carry, side=side, column=column):
                deep = depth_order(step)
                core_copy(deep, side, column).wait_recv()
                add_into(core_in.at[deep, side, column], [pieces.at[deep * 2 + side, column * 2 + c]])
                return carry

            def send_y(step, carry, column=column):
                take_core(step, carry, 1 - y, column)
                y_copy(depth_order(step), column).start()
                return carry

            lax.fori_loop(0, nz, send_y if side is not y else take_core, 0)
    for step_x, column in enumerate(columns):

        def take_y(step, carry, step_x=step_x, column=column):
            deep = depth_order(step)
            y_copy(deep, column).wait_recv()
            add_into(y_in.at[deep, column], [core_in.at[deep, y, column]])
            if step_x + 1 < nx:
                x_copy(step_x + 1, deep).start()
            return carry

        lax.fori_loop(0, nz, take_y, 0)
    for step in range(nz):
        deep = depth_order(step)
        for step_x in range(1, nx):
            x_copy(step_x, deep).wait_recv()
        add_into(y_in.at[deep, x], [x_in.at[step_x, deep] for step_x in range(nx - 1)])
        if step + 1 < nz:
            z_copy(step + 1).start()
    for step in range(1, nz):
        z_copy(step).wait_recv()

    def finish(block, carry):
        here = pl.ds(pl.multiple_of(block * chunk, chunk), chunk)
        value = y_in[z, x, here, :].astype(jnp.float32)
        for step in range(nz - 1):
            value = value + z_in[step, here, :].astype(jnp.float32)
        total[here, :] = value
        return carry

    lax.fori_loop(0, depth // chunk, finish, 0)
    for side in (1 - y, y):
        for column in columns:

            def end_core(step, carry, side=side, column=column):
                core_copy(depth_order(step), side, column).wait_send()
                return carry

            lax.fori_loop(0, nz, end_core, 0)
    for column in columns:

        def end_y(step, carry, column=column):
            y_copy(depth_order(step), column).wait_send()
            return carry

        lax.fori_loop(0, nz, end_y, 0)
    for step_x in range(1, nx):

        def end_x(step, carry, step_x=step_x):
            x_copy(step_x, depth_order(step)).wait_send()
            return carry

        lax.fori_loop(0, nz, end_x, 0)
    for step in range(1, nz):
        z_copy(step).wait_send()
    finish_all_to_all(spot, rows, rows_out, row_send, row_recv, local_sem)


def reduce_grads(sizes, rows, pieces):
    n_dp, n_head = sizes
    count = n_dp * n_head
    nz, nx = n_dp // 2, n_head // 2
    one = pieces.shape[2:]
    dma = pltpu.SemaphoreType.DMA
    return pl.pallas_call(
        functools.partial(reduce_kernel, sizes),
        in_specs=[pl.BlockSpec(memory_space=pl.ANY), pl.BlockSpec(memory_space=pltpu.VMEM)],
        out_specs=[pl.BlockSpec(memory_space=pl.ANY), pl.BlockSpec(memory_space=pltpu.VMEM)],
        out_shape=[
            jax.ShapeDtypeStruct(rows.shape, rows.dtype),
            jax.ShapeDtypeStruct(one, jnp.float32),
        ],
        scratch_shapes=[
            pltpu.VMEM((nz, 2, nx) + one, pieces.dtype),
            pltpu.VMEM((nz, nx) + one, pieces.dtype),
            pltpu.VMEM((nx - 1, nz) + one, pieces.dtype),
            pltpu.VMEM((nz - 1,) + one, pieces.dtype),
            dma((count,)),
            dma((count,)),
            dma((nz, 2, nx)),
            dma((nz, 2, nx)),
            dma((nz, nx)),
            dma((nz, nx)),
            dma((nx - 1, nz)),
            dma((nx - 1, nz)),
            dma((nz - 1,)),
            dma((nz - 1,)),
            dma,
        ],
        compiler_params=pltpu.CompilerParams(
            collective_id=3, has_side_effects=True, vmem_limit_bytes=40 * 2**20
        ),
    )(rows, pieces)


def flat(block):
    return block.reshape(-1, 128)


def block_width(columns):
    return 128 if columns % 128 == 0 else columns


class Packing:
    def __init__(self, shapes, sizes):
        self.n_dp, self.n_head = sizes
        self.shapes = shapes
        self.widths = [shape[1] // 3 if kind else block_width(shape[1]) for kind, shape in shapes]
        self.rows = [shape[0] * shape[1] // 128 for kind, shape in shapes]

    def pack_shard(self, blocks, small):
        parts = []
        for (kind, shape), width, block in zip(self.shapes, self.widths, blocks):
            if kind:
                block = by_part(block, shape[1] // (3 * HD))
            parts.append(flat(block.reshape(shape[0], -1, width).transpose(1, 0, 2)))
        spare = -small.shape[0] % 128
        parts.append(flat(jnp.pad(small, (0, spare))))
        used = sum(part.shape[0] for part in parts)
        return jnp.pad(jnp.concatenate(parts, axis=0), ((0, -used % 16), (0, 0)))

    def unpack_full(self, full, small_size):
        start = 0
        outs = []
        for (kind, shape), width, rows in zip(self.shapes, self.widths, self.rows):
            piece = full[:, :, start : start + rows]
            start = start + rows
            piece = piece.reshape(self.n_dp, self.n_head, shape[1] // width, shape[0], width)
            if kind:
                piece = piece.transpose(2, 0, 3, 1, 4)
                outs.append(piece.reshape(3, self.n_dp * shape[0], self.n_head * width))
            else:
                piece = piece.transpose(0, 3, 1, 2, 4)
                outs.append(piece.reshape(self.n_dp * shape[0], self.n_head * shape[1]))
        piece = full[:, :, start : start + -(-small_size // 128)]
        piece = piece.reshape(self.n_dp * self.n_head, -1)[:, :small_size]
        return outs, piece.reshape(-1)

    def pack_full(self, grads, small):
        parts = []
        for (kind, shape), width, rows, grad in zip(self.shapes, self.widths, self.rows, grads):
            if kind:
                grad = grad.reshape(3, self.n_dp, shape[0], self.n_head, width)
                grad = grad.transpose(1, 3, 0, 2, 4)
            else:
                grad = grad.reshape(self.n_dp, shape[0], self.n_head, shape[1] // width, width)
                grad = grad.transpose(0, 2, 3, 1, 4)
            parts.append(grad.reshape(self.n_dp, self.n_head, rows, 128))
        small = small.reshape(self.n_dp * self.n_head, -1)
        small = jnp.pad(small, ((0, 0), (0, -small.shape[1] % 128)))
        parts.append(small.reshape(self.n_dp, self.n_head, -1, 128))
        used = sum(part.shape[2] for part in parts)
        return jnp.pad(jnp.concatenate(parts, axis=2), ((0, 0), (0, 0), (0, -used % 16), (0, 0)))

    def unpack_shard(self, total, small_size):
        start = 0
        outs = []
        for (kind, shape), width, rows in zip(self.shapes, self.widths, self.rows):
            block = total[start : start + rows].reshape(shape[1] // width, shape[0], width)
            start = start + rows
            block = block.transpose(1, 0, 2).reshape(shape)
            outs.append(by_head(block, shape[1] // (3 * HD)) if kind else block)
        small = total[start : start + -(-small_size // 128)].reshape(-1)[:small_size]
        return outs, small


def request_slots(token_ids, shard_rows, count, room):
    here = token_ids.shape[0]
    index = jnp.arange(here, dtype=jnp.int32)
    owner = token_ids // shard_rows
    equal = token_ids[:, None] == token_ids[None, :]
    first = jnp.min(jnp.where(equal, index[:, None], here), axis=0)
    is_first = first == index
    earlier = (owner[:, None] == owner[None, :]) & is_first[:, None] & (index[:, None] < index[None, :])
    order = jnp.sum(earlier.astype(jnp.int32), axis=0)
    overflow = jnp.any(is_first & (order >= room))
    slot_first = owner * room + order
    chosen = first[None, :] == index[:, None]
    slot = jnp.sum(jnp.where(chosen, slot_first[:, None], 0), axis=0)
    spots = jnp.arange(count * room, dtype=jnp.int32)
    asked = is_first[:, None] & (slot_first[:, None] == spots[None, :]) & (order < room)[:, None]
    request = jnp.sum(jnp.where(asked, (token_ids % shard_rows)[:, None], 0), axis=0)
    return slot, request, overflow


def one_hot(index, size):
    return (index[:, None] == jnp.arange(size, dtype=jnp.int32)[None, :]).astype(jnp.bfloat16)


def adam_update(master, first, second, grad_clip, rate):
    first_new = B_ONE * first + (1.0 - B_ONE) * grad_clip
    second_new = B_TWO * second + (1.0 - B_TWO) * grad_clip * grad_clip
    ascent = (
        first_new / (1.0 - B_ONE**STEP) / (jnp.sqrt(second_new / (1.0 - B_TWO**STEP)) + EPSILON)
    )
    return (master - rate * (ascent + DECAY * master), first_new, second_new)


def shards(
    token_ids,
    seq_lengths,
    teacher_hidden,
    teacher_weight,
    token_table,
    token_first,
    token_second,
    position_table,
    position_first,
    position_second,
    qkv_weight,
    qkv_first,
    qkv_second,
    proj_weight,
    proj_first,
    proj_second,
    up_weight,
    up_first,
    up_second,
    down_weight,
    down_first,
    down_second,
    gains_biases,
    gains_first,
    gains_second,
):
    n_dp, n_head = sizes = (lax.axis_size("dp"), lax.axis_size("head"))
    count = n_dp * n_head
    here, shard_rows = token_ids.shape[0], token_table.shape[0]
    room = 16 * -(-3 * here // (2 * count * 16))
    slot, request, overflow = request_slots(token_ids, shard_rows, count, room)
    notes = jnp.stack([overflow.astype(jnp.int32), jnp.sum(seq_lengths)])
    message = jnp.concatenate(
        [
            jnp.pad(request.reshape(count, 1, room), ((0, 0), (0, 0), (0, 128 - room))),
            jnp.broadcast_to(jnp.pad(notes, (0, 126)), (count, 1, 128)),
            jnp.zeros((count, 6, 128), jnp.int32),
        ],
        axis=1,
    )
    heard = small_exchange(sizes, message, 1)
    too_many = jnp.any(heard[:, 1, 0] > 0)
    valid_total = jnp.sum(heard[:, 1, 1]).astype(jnp.float32)
    wanted = heard[:, 0, :room].reshape(-1)
    table_low = token_table.astype(jnp.bfloat16)
    wanted_hot = one_hot(wanted, shard_rows)
    rows_out = dot(wanted_hot, table_low).astype(jnp.bfloat16).reshape(count, room, D)
    packing = Packing(
        [
            (True, qkv_weight.shape[1:]),
            (True, qkv_weight.shape[1:]),
            (False, proj_weight.shape[1:]),
            (False, up_weight.shape[1:]),
            (False, down_weight.shape[1:]),
            (False, position_table.shape),
        ],
        sizes,
    )
    shard = packing.pack_shard(
        [
            block.astype(jnp.bfloat16)
            for block in (
                qkv_weight[0], qkv_weight[1], proj_weight[0], up_weight[0], down_weight[0], position_table
            )
        ],
        gains_biases.astype(jnp.bfloat16),
    )
    teach = by_part(teacher_weight, teacher_weight.shape[1] // (3 * THD))
    teach = teach.reshape(TD, 3, -1).transpose(1, 0, 2)
    rows_in, full, teach_full = gather_weights(sizes, rows_out, shard, teach)
    blocks, gains_low = packing.unpack_full(full, gains_biases.shape[0])
    slot_hot = one_hot(slot, count * room)

    def owned_rows():
        group_ids = lax.all_gather(token_ids, "head", axis=0, tiled=True)
        block_ids = group_ids // shard_rows
        owned = block_ids % n_head == lax.axis_index("head")
        local = jnp.where(owned, block_ids // n_head * shard_rows + group_ids % shard_rows, 0)
        return owned, local

    def rows_by_owner():
        owned, local = owned_rows()
        rows_all = lax.all_gather(table_low, "dp", axis=0, tiled=True)
        picked = jnp.where(owned[:, None], rows_all[local], jnp.zeros((), jnp.bfloat16))
        return lax.psum_scatter(picked, "head", scatter_dimension=0, tiled=True)

    def rows_by_slot():
        return dot(slot_hot, rows_in.reshape(count * room, D)).astype(jnp.bfloat16)

    token_rows = lax.cond(too_many, rows_by_owner, rows_by_slot).astype(jnp.float32)
    teacher_qkv = jnp.stack(
        [dot(teacher_hidden, teach_full[part]).astype(jnp.bfloat16) for part in range(3)]
    )
    final_qkv, backward = jax.vjp(
        lambda *values: device_forward(seq_lengths, *values),
        token_rows,
        blocks[5].astype(jnp.float32),
        blocks[0],
        blocks[1],
        blocks[2],
        blocks[3],
        blocks[4],
        gains_low.astype(jnp.float32),
    )
    final_grad, loss_local = relation(
        seq_lengths, jnp.stack([part.astype(jnp.bfloat16) for part in final_qkv]), teacher_qkv
    )
    row_grad, position_grad, first_grad, last_grad, proj_grad, up_grad, down_grad, gains_grad = backward(
        tuple(final_grad[part].astype(jnp.float32) for part in range(3))
    )
    row_low = row_grad.astype(jnp.bfloat16)
    slot_grads = lax.dot_general(
        slot_hot, row_low, (((0,), (0,)), ((), ())), preferred_element_type=jnp.float32
    )
    pieces = packing.pack_full(
        [
            grad.astype(jnp.bfloat16)
            for grad in (first_grad, last_grad, proj_grad, up_grad, down_grad, position_grad)
        ],
        gains_grad.astype(jnp.bfloat16),
    )
    grads_in, total = reduce_grads(
        sizes, slot_grads.astype(jnp.bfloat16).reshape(count, room, D), pieces
    )

    def table_by_owner():
        owned, local = owned_rows()
        spread = lax.all_gather(row_low, "head", axis=0, tiled=True)
        table_grad = jax.ops.segment_sum(
            spread.astype(jnp.float32),
            jnp.where(owned, local, n_dp * shard_rows),
            num_segments=n_dp * shard_rows + 1,
        )[:-1]
        return lax.psum_scatter(
            table_grad.astype(jnp.bfloat16), "dp", scatter_dimension=0, tiled=True
        ).astype(jnp.float32)

    def table_by_slot():
        return lax.dot_general(
            wanted_hot,
            grads_in.reshape(count * room, D),
            (((0,), (0,)), ((), ())),
            preferred_element_type=jnp.float32,
        )

    table_grad = lax.cond(too_many, table_by_owner, table_by_slot)
    reduced, small_grad = packing.unpack_shard(total, gains_biases.shape[0])
    shard_grads = (
        table_grad,
        reduced[5],
        jnp.stack(reduced[:2]),
        reduced[2][None],
        reduced[3][None],
        reduced[4][None],
        small_grad,
    )
    squares = sum((jnp.sum(grad_item * grad_item) for grad_item in shard_grads))
    sums = jnp.pad(jnp.stack([squares, loss_local])[None], ((0, 7), (0, 126)))
    everyone = small_exchange(sizes, jnp.broadcast_to(sums, (count, 8, 128)), 4)
    square_total = jnp.sum(everyone[:, 0, 0])
    loss_total = jnp.sum(everyone[:, 0, 1])
    grad_norm = jnp.sqrt(square_total) / valid_total
    clip_factor = THRESHOLD / jnp.maximum(grad_norm, THRESHOLD)
    factor = clip_factor / valid_total
    token_new = adam_update(
        token_table, token_first, token_second, shard_grads[0] * factor, RATE_TABLE
    )
    position_new = adam_update(
        position_table, position_first, position_second, shard_grads[1] * factor, RATE_TABLE
    )
    qkv_new = adam_update(qkv_weight, qkv_first, qkv_second, shard_grads[2] * factor, RATE_MATRIX)
    proj_new = adam_update(
        proj_weight, proj_first, proj_second, shard_grads[3] * factor, RATE_MATRIX
    )
    up_new = adam_update(up_weight, up_first, up_second, shard_grads[4] * factor, RATE_MATRIX)
    down_new = adam_update(
        down_weight, down_first, down_second, shard_grads[5] * factor, RATE_MATRIX
    )
    gains_new = adam_update(
        gains_biases, gains_first, gains_second, shard_grads[6] * factor, RATE_SMALL
    )
    loss_parts = jnp.stack([loss_total, valid_total])
    return (
        token_new[0],
        token_new[1],
        token_new[2],
        position_new[0],
        position_new[1],
        position_new[2],
        qkv_new[0],
        qkv_new[1],
        qkv_new[2],
        proj_new[0],
        proj_new[1],
        proj_new[2],
        up_new[0],
        up_new[1],
        up_new[2],
        down_new[0],
        down_new[1],
        down_new[2],
        gains_new[0],
        gains_new[1],
        gains_new[2],
        grad_norm,
        loss_parts,
    )


def solution(mesh):
    placed = (
        P(("dp", "head")),
        P(("dp", "head")),
        P(("dp", "head"), None),
        P(None, "head"),
        P(("dp", "head"), None),
        P(("dp", "head"), None),
        P(("dp", "head"), None),
        P("dp", "head"),
        P("dp", "head"),
        P("dp", "head"),
        P(None, "dp", "head"),
        P(None, "dp", "head"),
        P(None, "dp", "head"),
        P(None, "dp", "head"),
        P(None, "dp", "head"),
        P(None, "dp", "head"),
        P(None, "dp", "head"),
        P(None, "dp", "head"),
        P(None, "dp", "head"),
        P(None, "dp", "head"),
        P(None, "dp", "head"),
        P(None, "dp", "head"),
        P(("dp", "head")),
        P(("dp", "head")),
        P(("dp", "head")),
    )
    return jax.shard_map(
        shards,
        mesh=mesh,
        in_specs=placed,
        out_specs=(
            P(("dp", "head"), None),
            P(("dp", "head"), None),
            P(("dp", "head"), None),
            P("dp", "head"),
            P("dp", "head"),
            P("dp", "head"),
            P(None, "dp", "head"),
            P(None, "dp", "head"),
            P(None, "dp", "head"),
            P(None, "dp", "head"),
            P(None, "dp", "head"),
            P(None, "dp", "head"),
            P(None, "dp", "head"),
            P(None, "dp", "head"),
            P(None, "dp", "head"),
            P(None, "dp", "head"),
            P(None, "dp", "head"),
            P(None, "dp", "head"),
            P(("dp", "head")),
            P(("dp", "head")),
            P(("dp", "head")),
            P(),
            P(),
        ),
        check_vma=False,
    )
```

```python
import functools
import math

import jax
import jax.numpy as jnp
from jax import lax
from jax.experimental import pallas as pl
from jax.experimental.pallas import tpu as pltpu
from jax.sharding import PartitionSpec as P

D = 512
HEADS = 8
HD = 64
FF = 2048
TD = 1024
THEADS = 16
THD = 64
REL = 64
LAYERS = 2
LA = 128
LB = 256
LC = 512
M = 1
STEP = 10


B_ONE = 0.9
B_TWO = 0.999
EPSILON = 1e-10
DECAY = 0.01
THRESHOLD = 0.0003
RATE_TABLE = 1.0
RATE_MATRIX = 0.1
RATE_SMALL = 2.0


def dot(left, right, dims=(((1,), (0,)), ((), ()))):
    return lax.dot_general(left, right, dims, preferred_element_type=jnp.float32)


NT = (((1,), (1,)), ((), ()))


LOG2E = 1.4426950408889634
LN2 = 0.6931471805599453
GROUPS = 4
S_WIDE = D // GROUPS
T_WIDE = TD // GROUPS
S_DIM = D // REL
T_DIM = TD // REL
FAST_LIMIT = 85.0
SEQS = ((0, LA), (LA, LA), (2 * LA, LB), (2 * LA + LB, LC))
TOKENS_HERE = 2 * LA + LB + LC


def relation_kernel(
    lens_ref, s_ref, t_ref, ds_ref, loss_ref, s_rows, t_rows, d_rows, s_exp, t_exp, s_keep, t_keep
):
    @pl.when((pl.program_id(0) == 0) & (pl.program_id(1) == 0))
    def _():
        loss_ref[...] = jnp.zeros_like(loss_ref)

    s_scale = LOG2E / math.sqrt(S_DIM)
    t_scale = LOG2E / math.sqrt(T_DIM)
    zero = jnp.zeros((), jnp.bfloat16)
    half_heads = 128 // T_DIM

    def prepare(seq):
        off, length = SEQS[seq]
        valid = lens_ref[seq]
        row_valid = lax.broadcasted_iota(jnp.int32, (length, 128), 0) < valid
        s_block = jnp.where(row_valid, s_ref[off : off + length, :], zero)
        s_keep[off : off + length, :] = s_block
        s_rows[:, off : off + length] = s_block.astype(jnp.float32).T
        for half in range(2):
            cols = slice(half * 128, half * 128 + 128)
            t_block = jnp.where(row_valid, t_ref[off : off + length, cols], zero)
            t_keep[half, off : off + length, :] = t_block
            t_rows[cols, off : off + length] = t_block.astype(jnp.float32).T
        s_here = s_rows[:, off : off + length]
        t_here = t_rows[:, off : off + length]
        s_square = jnp.sum((s_here * s_here).reshape(16, S_DIM, length), axis=1)
        t_square = jnp.sum((t_here * t_here).reshape(16, T_DIM, length), axis=1)
        valid_row = (lax.broadcasted_iota(jnp.int32, (8, length), 1) < valid).astype(jnp.float32)
        padded = (length - valid).astype(jnp.float32)
        return (
            jnp.max(s_square) * s_scale,
            jnp.max(t_square) * t_scale,
            valid_row,
            padded,
        )

    info = [prepare(seq) for seq in range(len(SEQS))]

    def fold_rows(value):
        total = value[0:8]
        for start in range(8, value.shape[0], 8):
            total = total + value[start : start + 8]
        return total

    def one_head(seq, half, head):
        off, length = SEQS[seq]
        lane = lax.broadcasted_iota(jnp.int32, (length, 128), 1)
        s_one = jnp.where(
            lane // S_DIM == half * half_heads + head, s_keep[off : off + length, :], zero
        )
        t_one = jnp.where(lane // T_DIM == head, t_keep[half, off : off + length, :], zero)
        return s_one, t_one

    def row_slices(seq, half, head):
        off, length = SEQS[seq]
        index = half * half_heads + head
        s_slice = pl.ds(pl.multiple_of(index * S_DIM, S_DIM), S_DIM)
        t_slice = pl.ds(pl.multiple_of(index * T_DIM, T_DIM), T_DIM)
        return s_slice, t_slice

    def fast_heads(work, half):
        sums = []
        for seq, head, slot in work:
            off, length = SEQS[seq]
            s_bound, t_bound, valid_row, padded = info[seq]
            s_one, t_one = one_head(seq, half, head)
            chunk = min(256, length)
            s_sum = jnp.zeros((8, length), jnp.float32)
            t_sum = jnp.zeros((8, length), jnp.float32)
            for start in range(0, length, chunk):
                rows = slice(off + start, off + start + chunk)
                here = slice(start, start + chunk)
                s_value = jnp.exp2(dot(s_keep[rows, :], s_one, NT) * s_scale - s_bound)
                s_sum = s_sum + fold_rows(s_value)
                s_exp[slot, here, 0:length] = s_value.astype(jnp.bfloat16)
                t_value = jnp.exp2(dot(t_keep[half, rows, :], t_one, NT) * t_scale - t_bound)
                t_sum = t_sum + fold_rows(t_value)
                t_exp[slot, here, 0:length] = t_value.astype(jnp.bfloat16)
            s_total = jnp.sum(s_sum, axis=0, keepdims=True) - padded * jnp.exp2(-s_bound)
            t_total = jnp.sum(t_sum, axis=0, keepdims=True) - padded * jnp.exp2(-t_bound)
            sums.append((s_total, t_total))
        loss_sum = jnp.zeros((8, 128), jnp.float32)
        for (seq, head, slot), (s_total, t_total) in zip(work, sums):
            off, length = SEQS[seq]
            s_bound, t_bound, valid_row, padded = info[seq]
            s_slice, t_slice = row_slices(seq, half, head)
            s_recip = valid_row / s_total
            t_recip = valid_row / t_total
            s_vec = s_rows[s_slice, off : off + length]
            t_vec = t_rows[t_slice, off : off + length]
            t_left = jnp.concatenate([s_vec, s_vec * t_recip, t_vec], axis=0).astype(jnp.bfloat16)
            s_left = jnp.concatenate([s_vec, s_vec * s_recip], axis=0).astype(jnp.bfloat16)
            t_out = dot(t_left, t_exp[slot, 0:length, 0:length])
            s_out = dot(s_left, s_exp[slot, 0:length, 0:length])
            d_rows[s_slice, off : off + length] = (
                s_out[0:8] * s_recip - t_out[0:8] * t_recip + (s_out[8:16] - t_out[8:16]) * valid_row
            )
            inner = t_vec * t_out[16:32]
            inner = (inner[0:8] + inner[8:16]) * t_scale - s_vec * t_out[0:8] * s_scale
            parts = inner * t_recip + (valid_row * 0.125) * (
                jnp.log2(s_total) + s_bound - jnp.log2(t_total) - t_bound
            )
            for start in range(0, length, 128):
                loss_sum = loss_sum + parts[:, start : start + 128]
        loss_ref[...] += loss_sum

    def exact_head(seq, half, head):
        off, length = SEQS[seq]
        valid = lens_ref[seq]
        s_one, t_one = one_head(seq, half, head)
        s_slice, t_slice = row_slices(seq, half, head)
        key_valid = lax.broadcasted_iota(jnp.int32, (length, 128), 0) < valid
        s_exp[0, 0:length, 0:128] = s_one
        t_exp[0, 0:length, 0:128] = t_one

        def log_soft(scores, scale):
            scaled = jnp.where(key_valid, scores * scale, -1e30)
            top = jnp.max(scaled, axis=0, keepdims=True)
            shifted = scaled - top
            total = jnp.sum(jnp.exp2(shifted), axis=0, keepdims=True)
            return shifted - jnp.log2(total)

        def queries(block, carry):
            start = pl.multiple_of(block * 128, 128)
            here = pl.ds(start, 128)
            query_valid = lax.broadcasted_iota(jnp.int32, (length, 128), 1) + start < valid
            both = key_valid & query_valid
            s_log = log_soft(
                dot(s_keep[off : off + length, :], s_exp[0, here, 0:128], NT), s_scale
            )
            t_log = log_soft(
                dot(t_keep[half, off : off + length, :], t_exp[0, here, 0:128], NT), t_scale
            )
            t_soft = jnp.exp2(t_log)
            change = jnp.where(both, jnp.exp2(s_log) - t_soft, 0.0)
            s_exp[1, 0:length, here] = change.astype(jnp.bfloat16)
            loss_ref[...] += fold_rows(jnp.where(both, t_soft * (t_log - s_log), 0.0))
            return carry

        lax.fori_loop(0, length // 128, queries, 0)
        s_vec = s_rows[s_slice, off : off + length]
        left = jnp.concatenate([s_vec, jnp.zeros_like(s_vec)], axis=0).astype(jnp.bfloat16)
        change = s_exp[1, 0:length, 0:length]
        d_rows[s_slice, off : off + length] = (dot(left, change) + dot(left, change, NT))[0:8]

    top_bound = info[0][0]
    for entry in info:
        top_bound = jnp.maximum(top_bound, jnp.maximum(entry[0], entry[1]))
    fast = top_bound < FAST_LIMIT

    @pl.when(fast)
    def _():
        for half in range(2):
            for seqs, at_once in (((3,), 2), ((2,), 4), ((0, 1), 4)):

                def body(step, carry, half=half, seqs=seqs, at_once=at_once):
                    fast_heads(
                        [
                            (seq, step * at_once + offset, offset * len(seqs) + place)
                            for offset in range(at_once)
                            for place, seq in enumerate(seqs)
                        ],
                        half,
                    )
                    return carry

                lax.fori_loop(0, half_heads // at_once, body, 0)

    @pl.when(jnp.logical_not(fast))
    def _():
        for half in range(2):
            for seq in range(len(SEQS)):

                def body(head, carry, half=half, seq=seq):
                    exact_head(seq, half, head)
                    return carry

                lax.fori_loop(0, half_heads, body, 0)

    for off, length in SEQS:
        ds_ref[off : off + length, :] = (
            d_rows[:, off : off + length].T * (1.0 / math.sqrt(S_DIM) / (3 * REL))
        ).astype(ds_ref.dtype)


def relation(seq_lengths, student, teacher):
    block_s = pl.BlockSpec((None, TOKENS_HERE, S_WIDE), lambda part, group: (part, 0, group))
    block_t = pl.BlockSpec((None, TOKENS_HERE, T_WIDE), lambda part, group: (part, 0, group))
    grads, loss = pl.pallas_call(
        relation_kernel,
        grid=(3, GROUPS),
        in_specs=[pl.BlockSpec(memory_space=pltpu.SMEM), block_s, block_t],
        out_specs=[block_s, pl.BlockSpec((8, 128), lambda part, group: (0, 0))],
        out_shape=[
            jax.ShapeDtypeStruct((3, TOKENS_HERE, D), jnp.bfloat16),
            jax.ShapeDtypeStruct((8, 128), jnp.float32),
        ],
        scratch_shapes=[
            pltpu.VMEM((S_WIDE, TOKENS_HERE), jnp.float32),
            pltpu.VMEM((T_WIDE, TOKENS_HERE), jnp.float32),
            pltpu.VMEM((S_WIDE, TOKENS_HERE), jnp.float32),
            pltpu.VMEM((8, LC, LC), jnp.bfloat16),
            pltpu.VMEM((8, LC, LC), jnp.bfloat16),
            pltpu.VMEM((TOKENS_HERE, 128), jnp.bfloat16),
            pltpu.VMEM((2, TOKENS_HERE, 128), jnp.bfloat16),
        ],
        compiler_params=pltpu.CompilerParams(vmem_limit_bytes=48 * 2**20),
    )(seq_lengths, student, teacher)
    return grads, jnp.sum(loss) * (LN2 / (3 * REL))


def by_part(columns, heads):
    lead = columns.shape[:-1]
    size = columns.shape[-1] // heads // 3
    shaped = columns.reshape(lead + (heads, 3, size))
    return jnp.moveaxis(shaped, -2, -3).reshape(columns.shape)


def by_head(columns, heads):
    lead = columns.shape[:-1]
    size = columns.shape[-1] // heads // 3
    shaped = columns.reshape(lead + (3, heads, size))
    return jnp.moveaxis(shaped, -2, -3).reshape(columns.shape)


POS_AT = 7
GAIN_ROWS = 18
ERF_TOP = (
    -2.72614225801306e-10,
    2.77068142495902e-08,
    -2.10102402082508e-06,
    -5.69250639462346e-05,
    -7.34990630326855e-04,
    -2.95459980854025e-03,
    -1.60960333262415e-02,
)
ERF_LOW = (
    -1.45660718464996e-05,
    -2.13374055278905e-04,
    -1.68282697438203e-03,
    -7.37332916720468e-03,
    -1.42647390514189e-02,
)
STEP_ROWS = 256


def erf(value):
    value = jnp.clip(value, -4.0, 4.0)
    square = value * value
    top = jnp.full_like(value, ERF_TOP[0])
    for factor in ERF_TOP[1:]:
        top = top * square + factor
    low_part = jnp.full_like(value, ERF_LOW[0])
    for factor in ERF_LOW[1:]:
        low_part = low_part * square + factor
    return value * top / low_part


def normal_cdf(value):
    return 0.5 + 0.5 * erf(value * math.sqrt(0.5))


def normalize(values):
    average = jnp.mean(values, axis=-1, keepdims=True)
    centered = values - average
    variance = jnp.mean(centered * centered, axis=-1, keepdims=True)
    scale = lax.rsqrt(variance + 1e-05)
    return centered * scale, scale


def low16(value):
    return value.astype(jnp.bfloat16)


def step_slice(step):
    return pl.ds(pl.multiple_of(step * STEP_ROWS, STEP_ROWS), STEP_ROWS)


def head_soft(q_pair, k_one, valid, length):
    scores = dot(q_pair, k_one, NT) * (1.0 / math.sqrt(HD))
    lane = lax.broadcasted_iota(jnp.int32, scores.shape, 1)
    scores = jnp.where(lane < valid, scores, -1e30)
    top = jnp.max(scores, axis=-1, keepdims=True)
    value = jnp.exp(scores - top)
    return value / jnp.sum(value, axis=-1, keepdims=True)


def forward_kernel(
    lens_ref,
    rows_ref,
    slot_ref,
    big,
    gains,
    s_out,
    hat0,
    hat1,
    hat2,
    scale0,
    scale1,
    scale2,
    hid_low,
    qkv_low,
    ctx_low,
    mid_low,
    pre_low,
    act_low,
    x_low,
    hidden_kept,
):
    steps = TOKENS_HERE // STEP_ROWS

    def embed(step, carry):
        here = step_slice(step)
        spots = lax.broadcasted_iota(jnp.int32, (STEP_ROWS, rows_ref.shape[0]), 1)
        chosen = low16(jnp.where(slot_ref[here, :] == spots, 1.0, 0.0))
        first = big[POS_AT, 0:STEP_ROWS, :].astype(jnp.float32)
        twice = jnp.concatenate([first[0:LA], first[0:LA]], axis=0)
        late = big[POS_AT, STEP_ROWS : 2 * STEP_ROWS, :].astype(jnp.float32)
        place = jnp.where(step == 0, twice, jnp.where(step == 3, late, first))
        hat, scale = normalize(dot(chosen, rows_ref[...]) + place)
        hat0[here, :] = low16(hat)
        scale0[here, :] = scale
        wide = hat * gains[0:1, :] + gains[1:2, :]
        hidden_kept[here, :] = wide
        hidden = low16(wide)
        hid_low[here, :] = hidden
        for part in range(3):
            qkv_low[part, here, :] = low16(dot(hidden, big[part]) + gains[2 + part : 3 + part, :])
        return carry

    lax.fori_loop(0, steps, embed, 0)
    zero = jnp.zeros((), jnp.bfloat16)
    for seq, (off, length) in enumerate(SEQS):

        def attend_pair(pair, carry, seq=seq, off=off, length=length):
            rows = slice(off, off + length)
            cols = pl.ds(pl.multiple_of(pair * 128, 128), 128)
            query, key, value = (qkv_low[part, rows, cols] for part in range(3))
            lane = lax.broadcasted_iota(jnp.int32, (length, 128), 1)
            total = jnp.zeros((length, 128), jnp.float32)
            for side in range(2):
                mine = lane // HD == side
                soft = head_soft(query, jnp.where(mine, key, zero), lens_ref[seq], length)
                total = total + dot(low16(soft), jnp.where(mine, value, zero))
            ctx_low[rows, cols] = low16(total)
            return carry

        lax.fori_loop(0, D // 128, attend_pair, 0)

    def rest(step, carry):
        here = step_slice(step)
        hat, scale = normalize(hidden_kept[here, :] + dot(ctx_low[here, :], big[6]) + gains[5:6, :])
        hat1[here, :] = low16(hat)
        scale1[here, :] = scale
        middle = hat * gains[11:12, :] + gains[12:13, :]
        middle_low = low16(middle)
        mid_low[here, :] = middle_low
        output = middle + gains[10:11, :]
        for block in range(4):
            cols = slice(block * D, block * D + D)
            pre = dot(middle_low, big[8 + block]) + gains[6 + block : 7 + block, :]
            act = low16(pre * normal_cdf(pre))
            pre_low[here, cols] = low16(pre)
            act_low[here, cols] = act
            output = output + dot(act, big[12 + block])
        hat, scale = normalize(output)
        hat2[here, :] = low16(hat)
        scale2[here, :] = scale
        final = low16(hat * gains[13:14, :] + gains[14:15, :])
        x_low[here, :] = final
        for part in range(3):
            s_out[part, here, :] = low16(dot(final, big[3 + part]) + gains[15 + part : 16 + part, :])
        return carry

    lax.fori_loop(0, steps, rest, 0)


def forward_layer(seq_lengths, rows, slot, big, gains):
    vmem = pl.BlockSpec(memory_space=pltpu.VMEM)
    shape = lambda *dims: jax.ShapeDtypeStruct(dims, jnp.float32)
    half = lambda *dims: jax.ShapeDtypeStruct(dims, jnp.bfloat16)
    tokens = TOKENS_HERE
    outs = [half(3, tokens, D)]
    outs += [half(tokens, D)] * 3 + [shape(tokens, 1)] * 3
    outs += [half(tokens, D), half(3, tokens, D), half(tokens, D), half(tokens, D)]
    outs += [half(tokens, FF), half(tokens, FF), half(tokens, D)]
    return pl.pallas_call(
        forward_kernel,
        in_specs=[pl.BlockSpec(memory_space=pltpu.SMEM)] + [vmem] * 4,
        out_specs=[vmem] * len(outs),
        out_shape=outs,
        scratch_shapes=[pltpu.VMEM((tokens, D), jnp.float32)],
        compiler_params=pltpu.CompilerParams(vmem_limit_bytes=56 * 2**20),
    )(seq_lengths, rows, slot[:, None], big, gains)


def backward_kernel(
    lens_ref,
    slot_ref,
    big,
    gains,
    ds_ref,
    hat0,
    hat1,
    hat2,
    scale0,
    scale1,
    scale2,
    hid_low,
    qkv_low,
    ctx_low,
    mid_low,
    pre_low,
    act_low,
    x_low,
    grads,
    small,
    slot_grads,
    row_low,
    flow,
    flow_low,
    wide_low,
    turned,
    dqkv_low,
):
    steps = TOKENS_HERE // STEP_ROWS
    small[...] = jnp.zeros_like(small)

    def add_small(row, value):
        small[row : row + 1, :] += jnp.sum(value, axis=0, keepdims=True)

    def norm_back(here, grad, hat_ref, scale_ref, row):
        hat = hat_ref[here, :].astype(jnp.float32)
        add_small(row, grad * hat)
        add_small(row + 1, grad)
        inner = grad * gains[row : row + 1, :]
        mean_inner = jnp.mean(inner, axis=-1, keepdims=True)
        mean_hat = jnp.mean(inner * hat, axis=-1, keepdims=True)
        return scale_ref[here, :] * (inner - mean_inner - hat * mean_hat)

    def turn(source, width):
        for start in range(0, TOKENS_HERE, STEP_ROWS):
            turned[0:width, start : start + STEP_ROWS] = source[start : start + STEP_ROWS, 0:width].T

    def weight_grads(pairs):
        for index, right in pairs:
            grads[index] = low16(dot(turned[0:D, :], right))

    def last(step, carry):
        here = step_slice(step)
        grad = jnp.zeros((STEP_ROWS, D), jnp.float32)
        for part in range(3):
            piece = ds_ref[part, here, :]
            add_small(15 + part, piece.astype(jnp.float32))
            grad = grad + dot(piece, big[3 + part], NT)
        grad = norm_back(here, grad, hat2, scale2, 13)
        add_small(10, grad)
        grad_low = low16(grad)
        flow_low[here, :] = grad_low
        total = grad
        for block in range(4):
            cols = slice(block * D, block * D + D)
            pre = pre_low[here, cols].astype(jnp.float32)
            slope = normal_cdf(pre) + pre * jnp.exp(pre * pre * -0.5) * (1.0 / math.sqrt(2.0 * math.pi))
            inner = dot(grad_low, big[12 + block], NT) * slope
            add_small(6 + block, inner)
            inner_low = low16(inner)
            wide_low[here, cols] = inner_low
            total = total + dot(inner_low, big[8 + block], NT)
        flow[here, :] = total
        return carry

    lax.fori_loop(0, steps, last, 0)
    turn(x_low, D)
    weight_grads([(3 + part, ds_ref[part]) for part in range(3)])
    for block in range(4):
        cols = slice(block * D, block * D + D)
        for start in range(0, TOKENS_HERE, STEP_ROWS):
            turned[:, start : start + STEP_ROWS] = act_low[start : start + STEP_ROWS, cols].T
        weight_grads([(12 + block, flow_low[...])])
    turn(mid_low, D)
    weight_grads([(8 + block, wide_low[:, block * D : block * D + D]) for block in range(4)])

    def middle(step, carry):
        here = step_slice(step)
        grad = norm_back(here, flow[here, :], hat1, scale1, 11)
        add_small(5, grad)
        flow[here, :] = grad
        grad_low = low16(grad)
        flow_low[here, :] = grad_low
        wide_low[here, 0:D] = low16(dot(grad_low, big[6], NT))
        return carry

    lax.fori_loop(0, steps, middle, 0)
    turn(ctx_low, D)
    weight_grads([(6, flow_low[...])])
    zero = jnp.zeros((), jnp.bfloat16)
    for seq, (off, length) in enumerate(SEQS):

        def attend_pair(pair, carry, seq=seq, off=off, length=length):
            rows = slice(off, off + length)
            cols = pl.ds(pl.multiple_of(pair * 128, 128), 128)
            query, key, value = (qkv_low[part, rows, cols] for part in range(3))
            out_grad = wide_low[rows, cols]
            lane = lax.broadcasted_iota(jnp.int32, (length, 128), 1)
            sums = [jnp.zeros((length, 128), jnp.float32)] * 3
            for side in range(2):
                mine = lane // HD == side
                key_one = jnp.where(mine, key, zero)
                soft = head_soft(query, key_one, lens_ref[seq], length)
                grad_one = jnp.where(mine, out_grad, zero)
                soft_grad = dot(grad_one, value, NT)
                inner = jnp.sum(soft_grad * soft, axis=-1, keepdims=True)
                score_grad = low16((soft_grad - inner) * soft * (1.0 / math.sqrt(HD)))
                query_one = jnp.where(mine, query, zero)
                sums[0] = sums[0] + dot(score_grad, key_one)
                sums[1] = sums[1] + dot(score_grad.T, query_one)
                sums[2] = sums[2] + dot(low16(soft).T, grad_one)
            for part in range(3):
                dqkv_low[part, rows, cols] = low16(sums[part])
            return carry

        lax.fori_loop(0, D // 128, attend_pair, 0)

    def first(step, carry):
        here = step_slice(step)
        grad = flow[here, :]
        for part in range(3):
            piece = dqkv_low[part, here, :]
            add_small(2 + part, piece.astype(jnp.float32))
            grad = grad + dot(piece, big[part], NT)
        grad = norm_back(here, grad, hat0, scale0, 0)
        flow[here, :] = grad
        row_low[here, :] = low16(grad)
        return carry

    lax.fori_loop(0, steps, first, 0)
    turn(hid_low, D)
    weight_grads([(part, dqkv_low[part]) for part in range(3)])
    near = flow[0:LA, :] + flow[LA : 2 * LA, :] + flow[2 * LA : 3 * LA, :] + flow[4 * LA : 5 * LA, :]
    grads[POS_AT, 0:LA, :] = low16(near)
    grads[POS_AT, LA:LB, :] = low16(flow[3 * LA : 4 * LA, :] + flow[5 * LA : 6 * LA, :])
    grads[POS_AT, LB:LC, :] = low16(flow[2 * LA + LB + LB :, :])
    places = slot_grads.shape[0]
    size = 512 if places % 512 == 0 else places

    def spread(block, carry):
        start = pl.multiple_of(block * size, size)
        spots = lax.broadcasted_iota(jnp.int32, (size, TOKENS_HERE), 0) + start
        chosen = low16(jnp.where(slot_ref[...] == spots, 1.0, 0.0))
        slot_grads[pl.ds(start, size), :] = low16(dot(chosen, row_low[...]))
        return carry

    lax.fori_loop(0, places // size, spread, 0)


def backward_layer(seq_lengths, slot, big, gains, final_grad, kept, places):
    vmem = pl.BlockSpec(memory_space=pltpu.VMEM)
    half = lambda *dims: jax.ShapeDtypeStruct(dims, jnp.bfloat16)
    tokens = TOKENS_HERE
    return pl.pallas_call(
        backward_kernel,
        in_specs=[pl.BlockSpec(memory_space=pltpu.SMEM)] + [vmem] * (4 + len(kept)),
        out_specs=[vmem] * 4,
        out_shape=[
            half(16, D, D),
            jax.ShapeDtypeStruct((GAIN_ROWS, D), jnp.float32),
            half(places, D),
            half(tokens, D),
        ],
        scratch_shapes=[
            pltpu.VMEM((tokens, D), jnp.float32),
            pltpu.VMEM((tokens, D), jnp.bfloat16),
            pltpu.VMEM((tokens, FF), jnp.bfloat16),
            pltpu.VMEM((D, tokens), jnp.bfloat16),
            pltpu.VMEM((3, tokens, D), jnp.bfloat16),
        ],
        compiler_params=pltpu.CompilerParams(vmem_limit_bytes=60 * 2**20),
    )(seq_lengths, slot[None, :], big, gains, final_grad, *kept)


def teacher_kernel(hidden, weight, out):
    out[...] = low16(dot(hidden[...], weight[...]))


def project_teacher(hidden, weight):
    tokens = hidden.shape[0]
    return pl.pallas_call(
        teacher_kernel,
        grid=(3, tokens // STEP_ROWS),
        in_specs=[
            pl.BlockSpec((STEP_ROWS, TD), lambda part, step: (step, 0)),
            pl.BlockSpec((None, TD, TD), lambda part, step: (part, 0, 0)),
        ],
        out_specs=pl.BlockSpec((None, STEP_ROWS, TD), lambda part, step: (part, step, 0)),
        out_shape=jax.ShapeDtypeStruct((3, tokens, TD), jnp.bfloat16),
        compiler_params=pltpu.CompilerParams(vmem_limit_bytes=32 * 2**20),
    )(hidden, weight)


MESH_IDS = pl.DeviceIdType.MESH


def barrier_all(rank, count, place):
    barrier = pltpu.get_barrier_semaphore()

    def greet(step, carry):
        pl.semaphore_signal(
            barrier, inc=1, device_id=place(lax.rem(rank + step, count)), device_id_type=MESH_IDS
        )
        return carry

    lax.fori_loop(1, count, greet, 0)
    pl.semaphore_wait(barrier, count - 1)


class Spot:
    def __init__(self, n_dp, n_head):
        self.n_dp, self.n_head = n_dp, n_head
        self.count = n_dp * n_head
        self.nz, self.nx = n_dp // 2, n_head // 2
        dp, head = lax.axis_index("dp"), lax.axis_index("head")
        self.rank = dp * n_head + head
        self.z, self.y = dp // 2, lax.rem(dp, 2)
        self.x, self.c = head // 2, lax.rem(head, 2)

    def place(self, rank):
        return (rank // self.n_head, lax.rem(rank, self.n_head))

    def device(self, z, y, x, c):
        return (z * 2 + y, x * 2 + c)


def remote(source, target, send_sem, recv_sem, device):
    return pltpu.make_async_remote_copy(
        src_ref=source,
        dst_ref=target,
        send_sem=send_sem,
        recv_sem=recv_sem,
        device_id=device,
        device_id_type=MESH_IDS,
    )


def start_all_to_all(spot, source, target, send_sems, recv_sems, local_sem):
    pltpu.make_async_copy(source.at[spot.rank], target.at[spot.rank], local_sem).start()

    def send(step, carry):
        peer = lax.rem(spot.rank + step, spot.count)
        remote(
            source.at[peer], target.at[spot.rank], send_sems.at[step], recv_sems.at[step], spot.place(peer)
        ).start()
        return carry

    lax.fori_loop(1, spot.count, send, 0)


def finish_all_to_all(spot, source, target, send_sems, recv_sems, local_sem):
    def take(step, carry):
        origin = lax.rem(spot.rank + spot.count - step, spot.count)
        copy = remote(
            source.at[origin], target.at[origin], send_sems.at[step], recv_sems.at[step], spot.place(origin)
        )
        copy.wait_recv()
        copy.wait_send()
        return carry

    lax.fori_loop(1, spot.count, take, 0)
    pltpu.make_async_copy(source.at[spot.rank], target.at[spot.rank], local_sem).wait()


def small_exchange_kernel(sizes, source, target, send_sems, recv_sems, local_sem):
    spot = Spot(*sizes)
    barrier_all(spot.rank, spot.count, spot.place)
    start_all_to_all(spot, source, target, send_sems, recv_sems, local_sem)
    finish_all_to_all(spot, source, target, send_sems, recv_sems, local_sem)


def small_exchange(sizes, messages, collective_id):
    count = sizes[0] * sizes[1]
    return pl.pallas_call(
        functools.partial(small_exchange_kernel, sizes),
        in_specs=[pl.BlockSpec(memory_space=pltpu.VMEM)],
        out_specs=pl.BlockSpec(memory_space=pltpu.VMEM),
        out_shape=jax.ShapeDtypeStruct(messages.shape, messages.dtype),
        scratch_shapes=[
            pltpu.SemaphoreType.DMA((count,)),
            pltpu.SemaphoreType.DMA((count,)),
            pltpu.SemaphoreType.DMA,
        ],
        compiler_params=pltpu.CompilerParams(collective_id=collective_id, has_side_effects=True),
    )(messages)


def is_direct(shape):
    return shape[1] % 16 == 0 and shape[2] % 128 == 0


def piece_of(whole, shape, dp, head):
    if not is_direct(shape):
        return whole.at[dp, head]
    rows = pl.ds(pl.multiple_of(dp * shape[1], shape[1]), shape[1])
    return whole.at[:, rows, pl.ds(pl.multiple_of(head * shape[2], shape[2]), shape[2])]


def whole_shape(sizes, shape):
    if not is_direct(shape):
        return sizes + shape
    return (shape[0], sizes[0] * shape[1], sizes[1] * shape[2])


def gather_kernel(
    sizes,
    rows,
    shard,
    teach,
    rows_out,
    full,
    teach_full,
    row_send,
    row_recv,
    piece_send,
    piece_recv,
    teach_send,
    teach_recv,
    local_sems,
):
    spot = Spot(*sizes)
    z, y, x, c, nz, nx = spot.z, spot.y, spot.x, spot.c, spot.nz, spot.nx
    wide = teach.shape[2]
    barrier_all(spot.rank, spot.count, spot.place)
    own_copy = pltpu.make_async_copy(
        shard, piece_of(full, shard.shape, z * 2 + y, x * 2 + c), local_sems.at[1]
    )
    own_copy.start()

    def cols(head):
        return pl.ds(pl.multiple_of(head * wide, wide), wide)

    own_teach = pltpu.make_async_copy(teach, teach_full.at[:, :, cols(x * 2 + c)], local_sems.at[2])
    own_teach.start()
    sends = []

    def send_piece(source, piece, device):
        copy = remote(
            source,
            piece_of(full, shard.shape, piece[0] * 2 + piece[1], piece[2] * 2 + piece[3]),
            piece_send.at[len(sends)],
            piece_recv.at[piece[0] * 2 + piece[1], piece[2] * 2 + piece[3]],
            device,
        )
        copy.start()
        sends.append(copy)

    def wait_piece(piece):
        here = piece_of(full, shard.shape, piece[0] * 2 + piece[1], piece[2] * 2 + piece[3])
        remote(
            here,
            here,
            piece_send.at[0],
            piece_recv.at[piece[0] * 2 + piece[1], piece[2] * 2 + piece[3]],
            spot.device(z, y, x, 1 - c),
        ).wait_recv()
        return here

    own = (z, y, x, c)
    others_x = [lax.rem(x + step, nx) for step in range(1, nx)]
    for step in range(1, nz):
        send_piece(shard, own, spot.device(lax.rem(z + step, nz), y, x, c))
    teach_sends = []

    def send_teach(source, head, device, slot):
        copy = remote(
            source, teach_full.at[:, :, cols(head)], teach_send.at[slot], teach_recv.at[head], device
        )
        copy.start()
        teach_sends.append(copy)

    for step, other in enumerate(others_x):
        send_piece(shard, own, spot.device(z, y, other, c))
        send_teach(teach, x * 2 + c, spot.device(z, y, other, c), step)
    send_piece(shard, own, spot.device(z, 1 - y, x, c))
    send_piece(shard, own, spot.device(z, y, x, 1 - c))
    send_teach(teach, x * 2 + c, spot.device(z, y, x, 1 - c), nx - 1)
    start_all_to_all(spot, rows, rows_out, row_send, row_recv, local_sems.at[0])
    for step in range(1, nz):
        piece = (lax.rem(z + nz - step, nz), y, x, c)
        here = wait_piece(piece)
        for other in others_x:
            send_piece(here, piece, spot.device(z, y, other, c))
        send_piece(here, piece, spot.device(z, 1 - y, x, c))
        send_piece(here, piece, spot.device(z, y, x, 1 - c))
    for step in range(nz):
        for other in others_x:
            piece = (lax.rem(z + nz - step, nz), y, other, c)
            here = wait_piece(piece)
            send_piece(here, piece, spot.device(z, 1 - y, x, c))
            send_piece(here, piece, spot.device(z, y, x, 1 - c))

    def wait_teach(head):
        here = teach_full.at[:, :, cols(head)]
        remote(
            here, here, teach_send.at[0], teach_recv.at[head], spot.device(z, y, x, 1 - c)
        ).wait_recv()
        return here

    for step, other in enumerate(others_x):
        here = wait_teach(other * 2 + c)
        send_teach(here, other * 2 + c, spot.device(z, y, x, 1 - c), nx + step)
    for step in range(nz):
        for column in [x] + others_x:
            piece = (lax.rem(z + nz - step, nz), 1 - y, column, c)
            here = wait_piece(piece)
            send_piece(here, piece, spot.device(z, y, x, 1 - c))
    for step in range(nz):
        for side in (y, 1 - y):
            for column in [x] + others_x:
                wait_piece((lax.rem(z + nz - step, nz), side, column, 1 - c))
    for column in [x] + others_x:
        wait_teach(column * 2 + 1 - c)
    for copy in sends + teach_sends:
        copy.wait_send()
    finish_all_to_all(spot, rows, rows_out, row_send, row_recv, local_sems.at[0])
    own_copy.wait()
    own_teach.wait()


def gather_weights(sizes, rows, shard, teach):
    n_dp, n_head = sizes
    count = n_dp * n_head
    nz, nx = n_dp // 2, n_head // 2
    sends = (nz - 1) + (nx - 1) + 2 + (nz - 1) * (nx + 1) + nz * (nx - 1) * 2 + nz * nx
    anywhere = pl.BlockSpec(memory_space=pl.ANY)
    return pl.pallas_call(
        functools.partial(gather_kernel, sizes),
        in_specs=[anywhere] * 3,
        out_specs=[anywhere] * 3,
        out_shape=[
            jax.ShapeDtypeStruct(rows.shape, rows.dtype),
            jax.ShapeDtypeStruct(whole_shape(sizes, shard.shape), shard.dtype),
            jax.ShapeDtypeStruct(teach.shape[:2] + (n_head * teach.shape[2],), teach.dtype),
        ],
        scratch_shapes=[
            pltpu.SemaphoreType.DMA((count,)),
            pltpu.SemaphoreType.DMA((count,)),
            pltpu.SemaphoreType.DMA((sends,)),
            pltpu.SemaphoreType.DMA((n_dp, n_head)),
            pltpu.SemaphoreType.DMA((2 * nx,)),
            pltpu.SemaphoreType.DMA((n_head,)),
            pltpu.SemaphoreType.DMA((3,)),
        ],
        compiler_params=pltpu.CompilerParams(collective_id=2, has_side_effects=True),
    )(rows, shard, teach)


def reduce_kernel(
    sizes,
    rows,
    pieces,
    rows_out,
    total,
    core_in,
    y_in,
    x_in,
    z_in,
    row_send,
    row_recv,
    core_send,
    core_recv,
    y_send,
    y_recv,
    x_send,
    x_recv,
    z_send,
    z_recv,
    local_sem,
):
    spot = Spot(*sizes)
    z, y, x, c, nz, nx = spot.z, spot.y, spot.x, spot.c, spot.nz, spot.nx
    shape = total.shape
    barrier_all(spot.rank, spot.count, spot.place)
    sibling = spot.device(z, y, x, 1 - c)
    opposite = spot.device(z, 1 - y, x, c)

    def core_copy(deep, side, column):
        return remote(
            piece_of(pieces, shape, deep * 2 + side, column * 2 + 1 - c),
            core_in.at[deep, side, column],
            core_send.at[deep, side, column],
            core_recv.at[deep, side, column],
            sibling,
        )

    def y_copy(deep, column):
        return remote(
            core_in.at[deep, 1 - y, column],
            y_in.at[deep, column],
            y_send.at[deep, column],
            y_recv.at[deep, column],
            opposite,
        )

    def x_copy(step, deep):
        column = lax.rem(x + step, nx)
        return remote(
            y_in.at[deep, column],
            x_in.at[step - 1, deep],
            x_send.at[step - 1, deep],
            x_recv.at[step - 1, deep],
            spot.device(z, y, column, c),
        )

    def z_copy(step):
        deep = lax.rem(z + step, nz)
        return remote(
            y_in.at[deep, x],
            z_in.at[step - 1],
            z_send.at[step - 1],
            z_recv.at[step - 1],
            spot.device(deep, y, x, c),
        )

    def add_into(target, sources):
        def some(block, carry):
            value = target[block].astype(jnp.float32)
            for source in sources:
                value = value + source[block].astype(jnp.float32)
            target[block] = value.astype(target.dtype)
            return carry

        lax.fori_loop(0, shape[0], some, 0)

    depth_order = lambda step: lax.rem(z + 1 + step, nz)
    columns = [lax.rem(x + step, nx) for step in range(1, nx)] + [x]
    for side in (1 - y, y):
        for column in columns:

            def send_core(step, carry, side=side, column=column):
                core_copy(depth_order(step), side, column).start()
                return carry

            lax.fori_loop(0, nz, send_core, 0)
    start_all_to_all(spot, rows, rows_out, row_send, row_recv, local_sem)
    for side in (1 - y, y):
        for column in columns:

            def take_core(step, carry, side=side, column=column):
                deep = depth_order(step)
                core_copy(deep, side, column).wait_recv()
                own = piece_of(pieces, shape, deep * 2 + side, column * 2 + c)
                add_into(core_in.at[deep, side, column], [own])
                return carry

            def send_y(step, carry, column=column):
                take_core(step, carry, 1 - y, column)
                y_copy(depth_order(step), column).start()
                return carry

            lax.fori_loop(0, nz, send_y if side is not y else take_core, 0)
    for step_x, column in enumerate(columns):

        def take_y(step, carry, step_x=step_x, column=column):
            deep = depth_order(step)
            y_copy(deep, column).wait_recv()
            add_into(y_in.at[deep, column], [core_in.at[deep, y, column]])
            if step_x + 1 < nx:
                x_copy(step_x + 1, deep).start()
            return carry

        lax.fori_loop(0, nz, take_y, 0)
    for step in range(nz):
        deep = depth_order(step)
        for step_x in range(1, nx):
            x_copy(step_x, deep).wait_recv()
        add_into(y_in.at[deep, x], [x_in.at[step_x, deep] for step_x in range(nx - 1)])
        if step + 1 < nz:
            z_copy(step + 1).start()
    for step in range(1, nz):
        z_copy(step).wait_recv()

    def finish(block, carry):
        value = y_in[z, x, block].astype(jnp.float32)
        for step in range(nz - 1):
            value = value + z_in[step, block].astype(jnp.float32)
        total[block] = value
        return carry

    lax.fori_loop(0, shape[0], finish, 0)
    for side in (1 - y, y):
        for column in columns:

            def end_core(step, carry, side=side, column=column):
                core_copy(depth_order(step), side, column).wait_send()
                return carry

            lax.fori_loop(0, nz, end_core, 0)
    for column in columns:

        def end_y(step, carry, column=column):
            y_copy(depth_order(step), column).wait_send()
            return carry

        lax.fori_loop(0, nz, end_y, 0)
    for step_x in range(1, nx):

        def end_x(step, carry, step_x=step_x):
            x_copy(step_x, depth_order(step)).wait_send()
            return carry

        lax.fori_loop(0, nz, end_x, 0)
    for step in range(1, nz):
        z_copy(step).wait_send()
    finish_all_to_all(spot, rows, rows_out, row_send, row_recv, local_sem)


def reduce_grads(sizes, rows, pieces, one):
    n_dp, n_head = sizes
    count = n_dp * n_head
    nz, nx = n_dp // 2, n_head // 2
    dma = pltpu.SemaphoreType.DMA
    return pl.pallas_call(
        functools.partial(reduce_kernel, sizes),
        in_specs=[pl.BlockSpec(memory_space=pl.ANY), pl.BlockSpec(memory_space=pltpu.VMEM)],
        out_specs=[pl.BlockSpec(memory_space=pl.ANY), pl.BlockSpec(memory_space=pltpu.VMEM)],
        out_shape=[
            jax.ShapeDtypeStruct(rows.shape, rows.dtype),
            jax.ShapeDtypeStruct(one, jnp.float32),
        ],
        scratch_shapes=[
            pltpu.VMEM((nz, 2, nx) + one, pieces.dtype),
            pltpu.VMEM((nz, nx) + one, pieces.dtype),
            pltpu.VMEM((nx - 1, nz) + one, pieces.dtype),
            pltpu.VMEM((nz - 1,) + one, pieces.dtype),
            dma((count,)),
            dma((count,)),
            dma((nz, 2, nx)),
            dma((nz, 2, nx)),
            dma((nz, nx)),
            dma((nz, nx)),
            dma((nx - 1, nz)),
            dma((nx - 1, nz)),
            dma((nz - 1,)),
            dma((nz - 1,)),
            dma,
        ],
        compiler_params=pltpu.CompilerParams(
            collective_id=3, has_side_effects=True, vmem_limit_bytes=40 * 2**20
        ),
    )(rows, pieces)


def stack_blocks(qkv_weight, proj_weight, up_weight, down_weight, position_table):
    depth, width = position_table.shape
    parts = by_part(qkv_weight, qkv_weight.shape[2] // (3 * HD))
    parts = parts.reshape(LAYERS, depth, 3, width).transpose(0, 2, 1, 3).reshape(6, depth, width)
    up_blocks = up_weight.reshape(depth, width // depth, 4, depth).transpose(2, 0, 1, 3)
    return jnp.concatenate(
        [
            parts,
            proj_weight[None],
            position_table[None],
            up_blocks.reshape(4, depth, width),
            down_weight.reshape(4, depth, width),
        ],
        axis=0,
    )


def split_blocks(total):
    depth, width = total.shape[1:]
    parts = total[:6].reshape(LAYERS, 3, depth, width).transpose(0, 2, 1, 3)
    qkv_grad = by_head(parts.reshape(LAYERS, depth, 3 * width), width // HD)
    up_grad = total[8:12].reshape(4, depth, width // depth, depth).transpose(1, 2, 0, 3)
    return (
        total[7],
        qkv_grad,
        total[6:7],
        up_grad.reshape(1, depth, 4 * width),
        total[12:16].reshape(1, 4 * depth, width),
    )


def arrange_gains(gains, n_dp):
    offset = 2 * D
    qkv_bias = by_part(gains[offset : offset + 3 * D], HEADS)
    up_bias = gains[offset + 4 * D : offset + 4 * D + FF].reshape(n_dp, 4, D // n_dp)
    return jnp.concatenate(
        [
            gains[:offset],
            qkv_bias,
            gains[offset + 3 * D : offset + 4 * D],
            up_bias.transpose(1, 0, 2).reshape(-1),
            gains[offset + 4 * D + FF : offset + 9 * D + FF],
            by_part(gains[offset + 9 * D + FF :], HEADS),
        ]
    ).reshape(GAIN_ROWS, D)


def restore_gains(rows, n_dp):
    up_bias = rows[6:10].reshape(4, n_dp, D // n_dp).transpose(1, 0, 2)
    return jnp.concatenate(
        [
            rows[0:2].reshape(-1),
            by_head(rows[2:5].reshape(-1), HEADS),
            rows[5],
            up_bias.reshape(-1),
            rows[10:15].reshape(-1),
            by_head(rows[15:18].reshape(-1), HEADS),
        ]
    )


def request_slots(token_ids, shard_rows, count, room, usable):
    here = token_ids.shape[0]
    index = jnp.arange(here, dtype=jnp.int32)
    owner = token_ids // shard_rows
    equal = token_ids[:, None] == token_ids[None, :]
    first = jnp.min(jnp.where(equal, index[:, None], here), axis=0)
    is_first = first == index
    earlier = (owner[:, None] == owner[None, :]) & is_first[:, None] & (index[:, None] < index[None, :])
    order = jnp.sum(earlier.astype(jnp.int32), axis=0)
    overflow = jnp.any(is_first & (order >= usable))
    slot_first = owner * room + order
    chosen = first[None, :] == index[:, None]
    slot = jnp.sum(jnp.where(chosen, slot_first[:, None], 0), axis=0)
    spots = jnp.arange(count * room, dtype=jnp.int32)
    asked = is_first[:, None] & (slot_first[:, None] == spots[None, :]) & (order < usable)[:, None]
    request = jnp.sum(jnp.where(asked, (token_ids % shard_rows)[:, None] + 1, 0), axis=0) - 1
    return slot, request, overflow


def one_hot(index, size):
    return (index[:, None] == jnp.arange(size, dtype=jnp.int32)[None, :]).astype(jnp.bfloat16)


def adam_update(master, first, second, grad_clip, rate):
    first_new = B_ONE * first + (1.0 - B_ONE) * grad_clip
    second_new = B_TWO * second + (1.0 - B_TWO) * grad_clip * grad_clip
    ascent = (
        first_new / (1.0 - B_ONE**STEP) / (jnp.sqrt(second_new / (1.0 - B_TWO**STEP)) + EPSILON)
    )
    return (master - rate * (ascent + DECAY * master), first_new, second_new)


def shards(
    token_ids,
    seq_lengths,
    teacher_hidden,
    teacher_weight,
    token_table,
    token_first,
    token_second,
    position_table,
    position_first,
    position_second,
    qkv_weight,
    qkv_first,
    qkv_second,
    proj_weight,
    proj_first,
    proj_second,
    up_weight,
    up_first,
    up_second,
    down_weight,
    down_first,
    down_second,
    gains_biases,
    gains_first,
    gains_second,
):
    n_dp, n_head = sizes = (lax.axis_size("dp"), lax.axis_size("head"))
    count = n_dp * n_head
    here, shard_rows = token_ids.shape[0], token_table.shape[0]
    room = 16 * -(-3 * here // (2 * count * 16))
    slot, request, overflow = request_slots(token_ids, shard_rows, count, room, room - 1)
    notes = jnp.stack([overflow.astype(jnp.float32), jnp.sum(seq_lengths).astype(jnp.float32)])
    small_size = gains_biases.shape[0]
    small_rows = -(-small_size // 128)
    small_mine = gains_biases.astype(jnp.bfloat16).astype(jnp.float32)
    small_mine = jnp.pad(small_mine, (0, small_rows * 128 - small_size)).reshape(1, small_rows, 128)
    message = jnp.concatenate(
        [
            jnp.pad(
                request.astype(jnp.float32).reshape(count, 1, room), ((0, 0), (0, 0), (0, 128 - room))
            ),
            jnp.broadcast_to(jnp.pad(notes, (0, 126)), (count, 1, 128)),
            jnp.broadcast_to(small_mine, (count, small_rows, 128)),
            jnp.zeros((count, 6 - small_rows, 128), jnp.float32),
        ],
        axis=1,
    )
    heard = small_exchange(sizes, message, 1)
    too_many = jnp.any(heard[:, 1, 0] > 0.0)
    valid_total = jnp.sum(heard[:, 1, 1])
    wanted = heard[:, 0, :room].reshape(-1).astype(jnp.int32)
    gains = arrange_gains(
        heard[:, 2 : 2 + small_rows].reshape(count, -1)[:, :small_size].reshape(-1), n_dp
    )
    table_low = token_table.astype(jnp.bfloat16)
    wanted_hot = one_hot(wanted, shard_rows)
    rows_out = dot(wanted_hot, table_low).astype(jnp.bfloat16).reshape(count, room, D)
    shard = stack_blocks(
        qkv_weight, proj_weight[0], up_weight[0], down_weight[0], position_table
    ).astype(jnp.bfloat16)
    teach = by_part(teacher_weight, teacher_weight.shape[1] // (3 * THD))
    teach = teach.reshape(TD, 3, -1).transpose(1, 0, 2)
    rows_in, big, teach_full = gather_weights(sizes, rows_out, shard, teach)
    if not is_direct(shard.shape):
        big = big.transpose(2, 0, 3, 1, 4).reshape(16, D, D)

    def owned_rows():
        group_ids = lax.all_gather(token_ids, "head", axis=0, tiled=True)
        block_ids = group_ids // shard_rows
        owned = block_ids % n_head == lax.axis_index("head")
        local = jnp.where(owned, block_ids // n_head * shard_rows + group_ids % shard_rows, 0)
        return owned, local

    def rows_by_owner():
        owned, local = owned_rows()
        rows_all = lax.all_gather(table_low, "dp", axis=0, tiled=True)
        picked = jnp.where(owned[:, None], rows_all[local], jnp.zeros((), jnp.bfloat16))
        rows_here = lax.psum_scatter(picked, "head", scatter_dimension=0, tiled=True)
        return (
            jnp.pad(rows_here, ((0, count * room - here), (0, 0))),
            jnp.arange(here, dtype=jnp.int32),
        )

    rows_used, slot_used = lax.cond(
        too_many, rows_by_owner, lambda: (rows_in.reshape(count * room, D), slot)
    )
    teacher_qkv = project_teacher(teacher_hidden, teach_full)
    final_qkv, *kept = forward_layer(seq_lengths, rows_used, slot_used, big, gains)
    final_grad, loss_local = relation(seq_lengths, final_qkv, teacher_qkv)
    pieces, gain_grads, slot_grads, row_low = backward_layer(
        seq_lengths, slot_used, big, gains, final_grad, kept, count * room
    )
    if not is_direct(shard.shape):
        pieces = pieces.reshape(16, n_dp, shard.shape[1], n_head, shard.shape[2])
        pieces = pieces.transpose(1, 3, 0, 2, 4)
    gain_rows = jnp.pad(
        restore_gains(gain_grads, n_dp).reshape(count, 1, small_size), ((0, 0), (0, 0), (0, D - small_size))
    )
    slot_grads = slot_grads.reshape(count, room, D).at[:, room - 1 :].set(gain_rows.astype(jnp.bfloat16))
    grads_in, total = reduce_grads(sizes, slot_grads, pieces, shard.shape)
    small_grad = jnp.sum(grads_in[:, room - 1, :small_size].astype(jnp.float32), axis=0)

    def table_by_owner():
        owned, local = owned_rows()
        spread = lax.all_gather(row_low, "head", axis=0, tiled=True)
        table_grad = jax.ops.segment_sum(
            spread.astype(jnp.float32),
            jnp.where(owned, local, n_dp * shard_rows),
            num_segments=n_dp * shard_rows + 1,
        )[:-1]
        return lax.psum_scatter(
            table_grad.astype(jnp.bfloat16), "dp", scatter_dimension=0, tiled=True
        ).astype(jnp.float32)

    def table_by_slot():
        return lax.dot_general(
            wanted_hot,
            grads_in.reshape(count * room, D),
            (((0,), (0,)), ((), ())),
            preferred_element_type=jnp.float32,
        )

    table_grad = lax.cond(too_many, table_by_owner, table_by_slot)
    shard_grads = (table_grad,) + split_blocks(total) + (small_grad,)
    squares = sum((jnp.sum(grad_item * grad_item) for grad_item in shard_grads))
    sums = jnp.pad(jnp.stack([squares, loss_local])[None], ((0, 7), (0, 126)))
    everyone = small_exchange(sizes, jnp.broadcast_to(sums, (count, 8, 128)), 4)
    square_total = jnp.sum(everyone[:, 0, 0])
    loss_total = jnp.sum(everyone[:, 0, 1])
    grad_norm = jnp.sqrt(square_total) / valid_total
    clip_factor = THRESHOLD / jnp.maximum(grad_norm, THRESHOLD)
    factor = clip_factor / valid_total
    token_new = adam_update(
        token_table, token_first, token_second, shard_grads[0] * factor, RATE_TABLE
    )
    position_new = adam_update(
        position_table, position_first, position_second, shard_grads[1] * factor, RATE_TABLE
    )
    qkv_new = adam_update(qkv_weight, qkv_first, qkv_second, shard_grads[2] * factor, RATE_MATRIX)
    proj_new = adam_update(
        proj_weight, proj_first, proj_second, shard_grads[3] * factor, RATE_MATRIX
    )
    up_new = adam_update(up_weight, up_first, up_second, shard_grads[4] * factor, RATE_MATRIX)
    down_new = adam_update(
        down_weight, down_first, down_second, shard_grads[5] * factor, RATE_MATRIX
    )
    gains_new = adam_update(
        gains_biases, gains_first, gains_second, shard_grads[6] * factor, RATE_SMALL
    )
    loss_parts = jnp.stack([loss_total, valid_total])
    return (
        token_new[0],
        token_new[1],
        token_new[2],
        position_new[0],
        position_new[1],
        position_new[2],
        qkv_new[0],
        qkv_new[1],
        qkv_new[2],
        proj_new[0],
        proj_new[1],
        proj_new[2],
        up_new[0],
        up_new[1],
        up_new[2],
        down_new[0],
        down_new[1],
        down_new[2],
        gains_new[0],
        gains_new[1],
        gains_new[2],
        grad_norm,
        loss_parts,
    )


def solution(mesh):
    placed = (
        P(("dp", "head")),
        P(("dp", "head")),
        P(("dp", "head"), None),
        P(None, "head"),
        P(("dp", "head"), None),
        P(("dp", "head"), None),
        P(("dp", "head"), None),
        P("dp", "head"),
        P("dp", "head"),
        P("dp", "head"),
        P(None, "dp", "head"),
        P(None, "dp", "head"),
        P(None, "dp", "head"),
        P(None, "dp", "head"),
        P(None, "dp", "head"),
        P(None, "dp", "head"),
        P(None, "dp", "head"),
        P(None, "dp", "head"),
        P(None, "dp", "head"),
        P(None, "dp", "head"),
        P(None, "dp", "head"),
        P(None, "dp", "head"),
        P(("dp", "head")),
        P(("dp", "head")),
        P(("dp", "head")),
    )
    return jax.shard_map(
        shards,
        mesh=mesh,
        in_specs=placed,
        out_specs=(
            P(("dp", "head"), None),
            P(("dp", "head"), None),
            P(("dp", "head"), None),
            P("dp", "head"),
            P("dp", "head"),
            P("dp", "head"),
            P(None, "dp", "head"),
            P(None, "dp", "head"),
            P(None, "dp", "head"),
            P(None, "dp", "head"),
            P(None, "dp", "head"),
            P(None, "dp", "head"),
            P(None, "dp", "head"),
            P(None, "dp", "head"),
            P(None, "dp", "head"),
            P(None, "dp", "head"),
            P(None, "dp", "head"),
            P(None, "dp", "head"),
            P(("dp", "head")),
            P(("dp", "head")),
            P(("dp", "head")),
            P(),
            P(),
        ),
        check_vma=False,
    )
```

```python
import functools
import math

import jax
import jax.numpy as jnp
from jax import lax
from jax.experimental import pallas as pl
from jax.experimental.pallas import tpu as pltpu
from jax.sharding import PartitionSpec as P

D = 512
HEADS = 8
HD = 64
FF = 2048
TD = 1024
THEADS = 16
THD = 64
REL = 64
LAYERS = 2
LA = 128
LB = 256
LC = 512
M = 1
STEP = 10


B_ONE = 0.9
B_TWO = 0.999
EPSILON = 1e-10
DECAY = 0.01
THRESHOLD = 0.0003
RATE_TABLE = 1.0
RATE_MATRIX = 0.1
RATE_SMALL = 2.0


def dot(left, right, dims=(((1,), (0,)), ((), ()))):
    return lax.dot_general(left, right, dims, preferred_element_type=jnp.float32)


NT = (((1,), (1,)), ((), ()))


LOG2E = 1.4426950408889634
LN2 = 0.6931471805599453
GROUPS = 4
S_WIDE = D // GROUPS
T_WIDE = TD // GROUPS
S_DIM = D // REL
T_DIM = TD // REL
FAST_LIMIT = 60.0
SEQS = ((0, LA), (LA, LA), (2 * LA, LB), (2 * LA + LB, LC))
TOKENS_HERE = 2 * LA + LB + LC
BLOCKS = ((2 * LA + LB, LC, (3,)), (2 * LA, LB, (2,)), (0, 2 * LA, (0, 1)))
AT_ONCE = 4
KEY_ROWS = 128


def relation_kernel(
    lens_ref,
    s_ref,
    t_ref,
    ds_ref,
    loss_ref,
    s_rows,
    t_rows,
    d_rows,
    exp_c,
    exp_b,
    exp_a,
    s_keep,
    t_keep,
):
    @pl.when((pl.program_id(0) == 0) & (pl.program_id(1) == 0))
    def _():
        loss_ref[...] = jnp.zeros_like(loss_ref)
        exp_a[...] = jnp.zeros_like(exp_a)

    s_scale = LOG2E / math.sqrt(S_DIM)
    t_scale = LOG2E / math.sqrt(T_DIM)
    zero = jnp.zeros((), jnp.bfloat16)
    half_heads = 128 // T_DIM
    exps = (exp_c, exp_b, exp_a)

    def valid_rows(block):
        off, length, seqs = BLOCKS[block]
        each = length // len(seqs)
        row = lax.broadcasted_iota(jnp.int32, (length, 128), 0)
        valid = row < 0
        for place, seq in enumerate(seqs):
            start = place * each
            valid = valid | (row >= start) & (row < start + lens_ref[seq])
        return valid

    def prepare(block):
        off, length, seqs = BLOCKS[block]
        each = length // len(seqs)
        lane = lax.broadcasted_iota(jnp.int32, (8, length), 1)
        lane_valid, padded = lane < 0, jnp.zeros((8, length), jnp.float32)
        for place, seq in enumerate(seqs):
            start = place * each
            lane_valid = lane_valid | (lane >= start) & (lane < start + lens_ref[seq])
            padded = jnp.where(lane >= start, (each - lens_ref[seq]).astype(jnp.float32), padded)
        row_valid = valid_rows(block)
        rows = slice(off, off + length)
        s_block = jnp.where(row_valid, s_ref[rows, :], zero).astype(jnp.float32)
        s_keep[rows, :] = (s_block * math.sqrt(s_scale)).astype(jnp.bfloat16)
        s_rows[:, rows] = s_block.T
        for half in range(2):
            cols = slice(half * 128, half * 128 + 128)
            t_block = jnp.where(row_valid, t_ref[rows, cols], zero).astype(jnp.float32)
            t_keep[half, rows, :] = (t_block * math.sqrt(t_scale)).astype(jnp.bfloat16)
            t_rows[cols, rows] = t_block.T
        s_here = s_rows[:, rows]
        t_here = t_rows[:, rows]
        s_square = jnp.sum((s_here * s_here).reshape(16, S_DIM, length), axis=1)
        t_square = jnp.sum((t_here * t_here).reshape(16, T_DIM, length), axis=1)
        bound = jnp.maximum(jnp.max(s_square) * s_scale, jnp.max(t_square) * t_scale)
        return bound, lane_valid.astype(jnp.float32), padded[0:1]

    info = [prepare(block) for block in range(len(BLOCKS))]

    def fold_rows(value):
        total = value[0:8]
        for start in range(8, value.shape[0], 8):
            total = total + value[start : start + 8]
        return total

    def one_head(rows, length, head):
        lane = lax.broadcasted_iota(jnp.int32, (length, 128), 1)
        half = head // half_heads
        s_one = jnp.where(lane // S_DIM == head, s_keep[rows, :], zero)
        t_one = jnp.where(lane // T_DIM == head - half * half_heads, t_keep[half, rows, :], zero)
        return half, s_one, t_one

    def row_slices(head):
        s_slice = pl.ds(pl.multiple_of(head * S_DIM, S_DIM), S_DIM)
        t_slice = pl.ds(pl.multiple_of(head * T_DIM, T_DIM), T_DIM)
        return s_slice, t_slice

    def fill(block, keys, one, target):
        off, length, seqs = BLOCKS[block]
        each = length // len(seqs)
        if len(seqs) > 1:
            scores = dot(keys[...], one, NT)
            sums = []
            for place in range(len(seqs)):
                here = slice(place * each, place * each + each)
                value = jnp.exp2(scores[here, here])
                sums.append(fold_rows(value))
                target[here, here] = value.astype(jnp.bfloat16)
            return jnp.concatenate(sums, axis=1)
        total = jnp.zeros((8, length), jnp.float32)
        for start in range(0, length, KEY_ROWS):
            here = slice(start, start + KEY_ROWS)
            value = jnp.exp2(dot(keys[here, :], one, NT))
            total = total + fold_rows(value)
            target[here, :] = value.astype(jnp.bfloat16)
        return total

    def fill_both(block, head, slot):
        off, length, seqs = BLOCKS[block]
        rows = slice(off, off + length)
        half, s_one, t_one = one_head(rows, length, head)
        return (
            fill(block, s_keep.at[rows, :], s_one, exps[block].at[slot, 0]),
            fill(block, t_keep.at[half, rows, :], t_one, exps[block].at[slot, 1]),
        )

    def use_both(block, head, slot, sums):
        off, length, seqs = BLOCKS[block]
        rows = slice(off, off + length)
        bound, valid_row, padded = info[block]
        s_total = jnp.sum(sums[0], axis=0, keepdims=True) - padded
        t_total = jnp.sum(sums[1], axis=0, keepdims=True) - padded
        s_recip = valid_row / s_total
        t_recip = valid_row / t_total
        s_slice, t_slice = row_slices(head)
        s_vec = s_rows[s_slice, rows]
        t_vec = t_rows[t_slice, rows]
        t_left = jnp.concatenate([s_vec, s_vec * t_recip, t_vec], axis=0).astype(jnp.bfloat16)
        s_left = jnp.concatenate([s_vec, s_vec * s_recip], axis=0).astype(jnp.bfloat16)
        t_out = dot(t_left, exps[block][slot, 1])
        s_out = dot(s_left, exps[block][slot, 0])
        d_rows[s_slice, rows] = (
            s_out[0:8] * s_recip - t_out[0:8] * t_recip + (s_out[8:16] - t_out[8:16]) * valid_row
        )
        inner = t_vec * t_out[16:32]
        inner = (inner[0:8] + inner[8:16]) * t_scale - s_vec * t_out[0:8] * s_scale
        parts = inner * t_recip + (jnp.log2(s_total) - jnp.log2(t_total)) * (valid_row * 0.125)
        return fold_lanes(parts, length)

    def fold_lanes(parts, length):
        total = parts[:, 0:128]
        for start in range(128, length, 128):
            total = total + parts[:, start : start + 128]
        return total

    def fast_heads(step, carry):
        work = [
            (block, step * AT_ONCE + slot, slot)
            for slot in range(AT_ONCE)
            for block in range(len(BLOCKS))
        ]
        sums = [fill_both(*item) for item in work]
        total = jnp.zeros((8, 128), jnp.float32)
        for item, item_sums in zip(work, sums):
            total = total + use_both(*item, item_sums)
        loss_ref[...] += total
        return carry

    def exact_head(seq, head):
        off, length = SEQS[seq]
        rows = slice(off, off + length)
        valid = lens_ref[seq]
        half, s_one, t_one = one_head(rows, length, head)
        s_slice, t_slice = row_slices(head)
        key_valid = lax.broadcasted_iota(jnp.int32, (length, 128), 0) < valid
        exp_c[0, 0, 0:length, 0:128] = s_one
        exp_c[0, 1, 0:length, 0:128] = t_one

        def log_soft(scores, scale):
            scaled = jnp.where(key_valid, scores * scale, -1e30)
            top = jnp.max(scaled, axis=0, keepdims=True)
            shifted = scaled - top
            total = jnp.sum(jnp.exp2(shifted), axis=0, keepdims=True)
            return shifted - jnp.log2(total)

        def queries(block, carry):
            start = pl.multiple_of(block * 128, 128)
            here = pl.ds(start, 128)
            query_valid = lax.broadcasted_iota(jnp.int32, (length, 128), 1) + start < valid
            both = key_valid & query_valid
            s_log = log_soft(dot(s_keep[rows, :], exp_c[0, 0, here, 0:128], NT), s_scale)
            t_log = log_soft(dot(t_keep[half, rows, :], exp_c[0, 1, here, 0:128], NT), t_scale)
            t_soft = jnp.exp2(t_log)
            change = jnp.where(both, jnp.exp2(s_log) - t_soft, 0.0)
            exp_c[1, 0, 0:length, here] = change.astype(jnp.bfloat16)
            loss_ref[...] += fold_rows(jnp.where(both, t_soft * (t_log - s_log), 0.0))
            return carry

        lax.fori_loop(0, length // 128, queries, 0)
        s_vec = s_rows[s_slice, rows]
        left = jnp.concatenate([s_vec, jnp.zeros_like(s_vec)], axis=0).astype(jnp.bfloat16)
        change = exp_c[1, 0, 0:length, 0:length]
        d_rows[s_slice, rows] = (dot(left, change) + dot(left, change, NT))[0:8]

    top_bound = info[0][0]
    for entry in info:
        top_bound = jnp.maximum(top_bound, entry[0])
    fast = top_bound < FAST_LIMIT

    @pl.when(fast)
    def _():
        lax.fori_loop(0, 2 * half_heads // AT_ONCE, fast_heads, 0)

    @pl.when(jnp.logical_not(fast))
    def _():
        for block, (off, length, seqs) in enumerate(BLOCKS):
            rows = slice(off, off + length)
            row_valid = valid_rows(block)
            s_keep[rows, :] = jnp.where(row_valid, s_ref[rows, :], zero)
            for half in range(2):
                t_block = t_ref[rows, half * 128 : half * 128 + 128]
                t_keep[half, rows, :] = jnp.where(row_valid, t_block, zero)
        for seq in range(len(SEQS)):

            def body(head, carry, seq=seq):
                exact_head(seq, head)
                return carry

            lax.fori_loop(0, 2 * half_heads, body, 0)

    for off, length in SEQS:
        ds_ref[off : off + length, :] = (
            d_rows[:, off : off + length].T * (1.0 / math.sqrt(S_DIM) / (3 * REL))
        ).astype(ds_ref.dtype)


def relation(seq_lengths, student, teacher):
    block_s = pl.BlockSpec((None, TOKENS_HERE, S_WIDE), lambda part, group: (part, 0, group))
    block_t = pl.BlockSpec((None, TOKENS_HERE, T_WIDE), lambda part, group: (part, 0, group))
    grads, loss = pl.pallas_call(
        relation_kernel,
        grid=(3, GROUPS),
        in_specs=[pl.BlockSpec(memory_space=pltpu.SMEM), block_s, block_t],
        out_specs=[block_s, pl.BlockSpec((8, 128), lambda part, group: (0, 0))],
        out_shape=[
            jax.ShapeDtypeStruct((3, TOKENS_HERE, D), jnp.bfloat16),
            jax.ShapeDtypeStruct((8, 128), jnp.float32),
        ],
        scratch_shapes=[
            pltpu.VMEM((S_WIDE, TOKENS_HERE), jnp.float32),
            pltpu.VMEM((T_WIDE, TOKENS_HERE), jnp.float32),
            pltpu.VMEM((S_WIDE, TOKENS_HERE), jnp.float32),
            pltpu.VMEM((AT_ONCE, 2, LC, LC), jnp.bfloat16),
            pltpu.VMEM((AT_ONCE, 2, LB, LB), jnp.bfloat16),
            pltpu.VMEM((AT_ONCE, 2, 2 * LA, 2 * LA), jnp.bfloat16),
            pltpu.VMEM((TOKENS_HERE, 128), jnp.bfloat16),
            pltpu.VMEM((2, TOKENS_HERE, 128), jnp.bfloat16),
        ],
        compiler_params=pltpu.CompilerParams(vmem_limit_bytes=48 * 2**20),
    )(seq_lengths, student, teacher)
    return grads, jnp.sum(loss) * (LN2 / (3 * REL))


def by_part(columns, heads):
    lead = columns.shape[:-1]
    size = columns.shape[-1] // heads // 3
    shaped = columns.reshape(lead + (heads, 3, size))
    return jnp.moveaxis(shaped, -2, -3).reshape(columns.shape)


def by_head(columns, heads):
    lead = columns.shape[:-1]
    size = columns.shape[-1] // heads // 3
    shaped = columns.reshape(lead + (3, heads, size))
    return jnp.moveaxis(shaped, -2, -3).reshape(columns.shape)


POS_AT = 7
GAIN_ROWS = 18
ERF_TOP = (
    -2.72614225801306e-10,
    2.77068142495902e-08,
    -2.10102402082508e-06,
    -5.69250639462346e-05,
    -7.34990630326855e-04,
    -2.95459980854025e-03,
    -1.60960333262415e-02,
)
ERF_LOW = (
    -1.45660718464996e-05,
    -2.13374055278905e-04,
    -1.68282697438203e-03,
    -7.37332916720468e-03,
    -1.42647390514189e-02,
)
STEP_ROWS = 256


def erf(value):
    value = jnp.clip(value, -4.0, 4.0)
    square = value * value
    top = jnp.full_like(value, ERF_TOP[0])
    for factor in ERF_TOP[1:]:
        top = top * square + factor
    low_part = jnp.full_like(value, ERF_LOW[0])
    for factor in ERF_LOW[1:]:
        low_part = low_part * square + factor
    return value * top / low_part


def normal_cdf(value):
    return 0.5 + 0.5 * erf(value * math.sqrt(0.5))


def normalize(values):
    average = jnp.mean(values, axis=-1, keepdims=True)
    centered = values - average
    variance = jnp.mean(centered * centered, axis=-1, keepdims=True)
    scale = lax.rsqrt(variance + 1e-05)
    return centered * scale, scale


def low16(value):
    return value.astype(jnp.bfloat16)


def step_slice(step):
    return pl.ds(pl.multiple_of(step * STEP_ROWS, STEP_ROWS), STEP_ROWS)


def head_soft(q_pair, k_one, valid, length):
    scores = dot(q_pair, k_one, NT) * (1.0 / math.sqrt(HD))
    lane = lax.broadcasted_iota(jnp.int32, scores.shape, 1)
    scores = jnp.where(lane < valid, scores, -1e30)
    top = jnp.max(scores, axis=-1, keepdims=True)
    value = jnp.exp(scores - top)
    return value / jnp.sum(value, axis=-1, keepdims=True)


def forward_kernel(
    lens_ref,
    rows_ref,
    slot_ref,
    big,
    gains,
    s_out,
    hat0,
    hat1,
    hat2,
    scale0,
    scale1,
    scale2,
    hid_low,
    qkv_low,
    ctx_low,
    mid_low,
    pre_low,
    act_low,
    x_low,
    hidden_kept,
):
    steps = TOKENS_HERE // STEP_ROWS

    def embed(step, carry):
        here = step_slice(step)
        spots = lax.broadcasted_iota(jnp.int32, (STEP_ROWS, rows_ref.shape[0]), 1)
        chosen = low16(jnp.where(slot_ref[here, :] == spots, 1.0, 0.0))
        first = big[POS_AT, 0:STEP_ROWS, :].astype(jnp.float32)
        twice = jnp.concatenate([first[0:LA], first[0:LA]], axis=0)
        late = big[POS_AT, STEP_ROWS : 2 * STEP_ROWS, :].astype(jnp.float32)
        place = jnp.where(step == 0, twice, jnp.where(step == 3, late, first))
        hat, scale = normalize(dot(chosen, rows_ref[...]) + place)
        hat0[here, :] = low16(hat)
        scale0[here, :] = scale
        wide = hat * gains[0:1, :] + gains[1:2, :]
        hidden_kept[here, :] = wide
        hidden = low16(wide)
        hid_low[here, :] = hidden
        for part in range(3):
            qkv_low[part, here, :] = low16(dot(hidden, big[part]) + gains[2 + part : 3 + part, :])
        return carry

    lax.fori_loop(0, steps, embed, 0)
    zero = jnp.zeros((), jnp.bfloat16)
    for seq, (off, length) in enumerate(SEQS):

        def attend_pair(pair, carry, seq=seq, off=off, length=length):
            rows = slice(off, off + length)
            cols = pl.ds(pl.multiple_of(pair * 128, 128), 128)
            query, key, value = (qkv_low[part, rows, cols] for part in range(3))
            lane = lax.broadcasted_iota(jnp.int32, (length, 128), 1)
            total = jnp.zeros((length, 128), jnp.float32)
            for side in range(2):
                mine = lane // HD == side
                soft = head_soft(query, jnp.where(mine, key, zero), lens_ref[seq], length)
                total = total + dot(low16(soft), jnp.where(mine, value, zero))
            ctx_low[rows, cols] = low16(total)
            return carry

        lax.fori_loop(0, D // 128, attend_pair, 0)

    def rest(step, carry):
        here = step_slice(step)
        hat, scale = normalize(hidden_kept[here, :] + dot(ctx_low[here, :], big[6]) + gains[5:6, :])
        hat1[here, :] = low16(hat)
        scale1[here, :] = scale
        middle = hat * gains[11:12, :] + gains[12:13, :]
        middle_low = low16(middle)
        mid_low[here, :] = middle_low
        output = middle + gains[10:11, :]
        for block in range(4):
            cols = slice(block * D, block * D + D)
            pre = dot(middle_low, big[8 + block]) + gains[6 + block : 7 + block, :]
            act = low16(pre * normal_cdf(pre))
            pre_low[here, cols] = low16(pre)
            act_low[here, cols] = act
            output = output + dot(act, big[12 + block])
        hat, scale = normalize(output)
        hat2[here, :] = low16(hat)
        scale2[here, :] = scale
        final = low16(hat * gains[13:14, :] + gains[14:15, :])
        x_low[here, :] = final
        for part in range(3):
            s_out[part, here, :] = low16(dot(final, big[3 + part]) + gains[15 + part : 16 + part, :])
        return carry

    lax.fori_loop(0, steps, rest, 0)


def forward_layer(seq_lengths, rows, slot, big, gains):
    vmem = pl.BlockSpec(memory_space=pltpu.VMEM)
    shape = lambda *dims: jax.ShapeDtypeStruct(dims, jnp.float32)
    half = lambda *dims: jax.ShapeDtypeStruct(dims, jnp.bfloat16)
    tokens = TOKENS_HERE
    outs = [half(3, tokens, D)]
    outs += [half(tokens, D)] * 3 + [shape(tokens, 1)] * 3
    outs += [half(tokens, D), half(3, tokens, D), half(tokens, D), half(tokens, D)]
    outs += [half(tokens, FF), half(tokens, FF), half(tokens, D)]
    return pl.pallas_call(
        forward_kernel,
        in_specs=[pl.BlockSpec(memory_space=pltpu.SMEM)] + [vmem] * 4,
        out_specs=[vmem] * len(outs),
        out_shape=outs,
        scratch_shapes=[pltpu.VMEM((tokens, D), jnp.float32)],
        compiler_params=pltpu.CompilerParams(vmem_limit_bytes=56 * 2**20),
    )(seq_lengths, rows, slot[:, None], big, gains)


def backward_kernel(
    lens_ref,
    slot_ref,
    big,
    gains,
    ds_ref,
    hat0,
    hat1,
    hat2,
    scale0,
    scale1,
    scale2,
    hid_low,
    qkv_low,
    ctx_low,
    mid_low,
    pre_low,
    act_low,
    x_low,
    grads,
    small,
    slot_grads,
    row_low,
    flow,
    flow_low,
    wide_low,
    turned,
    dqkv_low,
):
    steps = TOKENS_HERE // STEP_ROWS
    small[...] = jnp.zeros_like(small)

    def add_small(row, value):
        small[row : row + 1, :] += jnp.sum(value, axis=0, keepdims=True)

    def norm_back(here, grad, hat_ref, scale_ref, row):
        hat = hat_ref[here, :].astype(jnp.float32)
        add_small(row, grad * hat)
        add_small(row + 1, grad)
        inner = grad * gains[row : row + 1, :]
        mean_inner = jnp.mean(inner, axis=-1, keepdims=True)
        mean_hat = jnp.mean(inner * hat, axis=-1, keepdims=True)
        return scale_ref[here, :] * (inner - mean_inner - hat * mean_hat)

    def turn(source, width):
        for start in range(0, TOKENS_HERE, STEP_ROWS):
            turned[0:width, start : start + STEP_ROWS] = source[start : start + STEP_ROWS, 0:width].T

    def weight_grads(pairs):
        for index, right in pairs:
            grads[index] = low16(dot(turned[0:D, :], right))

    def last(step, carry):
        here = step_slice(step)
        grad = jnp.zeros((STEP_ROWS, D), jnp.float32)
        for part in range(3):
            piece = ds_ref[part, here, :]
            add_small(15 + part, piece.astype(jnp.float32))
            grad = grad + dot(piece, big[3 + part], NT)
        grad = norm_back(here, grad, hat2, scale2, 13)
        add_small(10, grad)
        grad_low = low16(grad)
        flow_low[here, :] = grad_low
        total = grad
        for block in range(4):
            cols = slice(block * D, block * D + D)
            pre = pre_low[here, cols].astype(jnp.float32)
            slope = normal_cdf(pre) + pre * jnp.exp(pre * pre * -0.5) * (1.0 / math.sqrt(2.0 * math.pi))
            inner = dot(grad_low, big[12 + block], NT) * slope
            add_small(6 + block, inner)
            inner_low = low16(inner)
            wide_low[here, cols] = inner_low
            total = total + dot(inner_low, big[8 + block], NT)
        flow[here, :] = total
        return carry

    lax.fori_loop(0, steps, last, 0)
    turn(x_low, D)
    weight_grads([(3 + part, ds_ref[part]) for part in range(3)])
    for block in range(4):
        cols = slice(block * D, block * D + D)
        for start in range(0, TOKENS_HERE, STEP_ROWS):
            turned[:, start : start + STEP_ROWS] = act_low[start : start + STEP_ROWS, cols].T
        weight_grads([(12 + block, flow_low[...])])
    turn(mid_low, D)
    weight_grads([(8 + block, wide_low[:, block * D : block * D + D]) for block in range(4)])

    def middle(step, carry):
        here = step_slice(step)
        grad = norm_back(here, flow[here, :], hat1, scale1, 11)
        add_small(5, grad)
        flow[here, :] = grad
        grad_low = low16(grad)
        flow_low[here, :] = grad_low
        wide_low[here, 0:D] = low16(dot(grad_low, big[6], NT))
        return carry

    lax.fori_loop(0, steps, middle, 0)
    turn(ctx_low, D)
    weight_grads([(6, flow_low[...])])
    zero = jnp.zeros((), jnp.bfloat16)
    for seq, (off, length) in enumerate(SEQS):

        def attend_pair(pair, carry, seq=seq, off=off, length=length):
            rows = slice(off, off + length)
            cols = pl.ds(pl.multiple_of(pair * 128, 128), 128)
            query, key, value = (qkv_low[part, rows, cols] for part in range(3))
            out_grad = wide_low[rows, cols]
            lane = lax.broadcasted_iota(jnp.int32, (length, 128), 1)
            sums = [jnp.zeros((length, 128), jnp.float32)] * 3
            for side in range(2):
                mine = lane // HD == side
                key_one = jnp.where(mine, key, zero)
                soft = head_soft(query, key_one, lens_ref[seq], length)
                grad_one = jnp.where(mine, out_grad, zero)
                soft_grad = dot(grad_one, value, NT)
                inner = jnp.sum(soft_grad * soft, axis=-1, keepdims=True)
                score_grad = low16((soft_grad - inner) * soft * (1.0 / math.sqrt(HD)))
                query_one = jnp.where(mine, query, zero)
                sums[0] = sums[0] + dot(score_grad, key_one)
                sums[1] = sums[1] + dot(score_grad.T, query_one)
                sums[2] = sums[2] + dot(low16(soft).T, grad_one)
            for part in range(3):
                dqkv_low[part, rows, cols] = low16(sums[part])
            return carry

        lax.fori_loop(0, D // 128, attend_pair, 0)

    def first(step, carry):
        here = step_slice(step)
        grad = flow[here, :]
        for part in range(3):
            piece = dqkv_low[part, here, :]
            add_small(2 + part, piece.astype(jnp.float32))
            grad = grad + dot(piece, big[part], NT)
        grad = norm_back(here, grad, hat0, scale0, 0)
        flow[here, :] = grad
        row_low[here, :] = low16(grad)
        return carry

    lax.fori_loop(0, steps, first, 0)
    turn(hid_low, D)
    weight_grads([(part, dqkv_low[part]) for part in range(3)])
    near = flow[0:LA, :] + flow[LA : 2 * LA, :] + flow[2 * LA : 3 * LA, :] + flow[4 * LA : 5 * LA, :]
    grads[POS_AT, 0:LA, :] = low16(near)
    grads[POS_AT, LA:LB, :] = low16(flow[3 * LA : 4 * LA, :] + flow[5 * LA : 6 * LA, :])
    grads[POS_AT, LB:LC, :] = low16(flow[2 * LA + LB + LB :, :])
    places = slot_grads.shape[0]
    size = 512 if places % 512 == 0 else places

    def spread(block, carry):
        start = pl.multiple_of(block * size, size)
        spots = lax.broadcasted_iota(jnp.int32, (size, TOKENS_HERE), 0) + start
        chosen = low16(jnp.where(slot_ref[...] == spots, 1.0, 0.0))
        slot_grads[pl.ds(start, size), :] = low16(dot(chosen, row_low[...]))
        return carry

    lax.fori_loop(0, places // size, spread, 0)


def backward_layer(seq_lengths, slot, big, gains, final_grad, kept, places):
    vmem = pl.BlockSpec(memory_space=pltpu.VMEM)
    half = lambda *dims: jax.ShapeDtypeStruct(dims, jnp.bfloat16)
    tokens = TOKENS_HERE
    return pl.pallas_call(
        backward_kernel,
        in_specs=[pl.BlockSpec(memory_space=pltpu.SMEM)] + [vmem] * (4 + len(kept)),
        out_specs=[vmem] * 4,
        out_shape=[
            half(16, D, D),
            jax.ShapeDtypeStruct((GAIN_ROWS, D), jnp.float32),
            half(places, D),
            half(tokens, D),
        ],
        scratch_shapes=[
            pltpu.VMEM((tokens, D), jnp.float32),
            pltpu.VMEM((tokens, D), jnp.bfloat16),
            pltpu.VMEM((tokens, FF), jnp.bfloat16),
            pltpu.VMEM((D, tokens), jnp.bfloat16),
            pltpu.VMEM((3, tokens, D), jnp.bfloat16),
        ],
        compiler_params=pltpu.CompilerParams(vmem_limit_bytes=60 * 2**20),
    )(seq_lengths, slot[None, :], big, gains, final_grad, *kept)


def teacher_kernel(hidden, weight, out):
    out[...] = low16(dot(hidden[...], weight[...]))


def project_teacher(hidden, weight):
    tokens = hidden.shape[0]
    owners, parts, depth, width = weight.shape
    return pl.pallas_call(
        teacher_kernel,
        grid=(parts, owners),
        in_specs=[
            pl.BlockSpec((tokens, depth), lambda part, owner: (0, 0)),
            pl.BlockSpec((None, None, depth, width), lambda part, owner: (owner, part, 0, 0)),
        ],
        out_specs=pl.BlockSpec((None, tokens, width), lambda part, owner: (part, 0, owner)),
        out_shape=jax.ShapeDtypeStruct((parts, tokens, owners * width), jnp.bfloat16),
        compiler_params=pltpu.CompilerParams(vmem_limit_bytes=32 * 2**20),
    )(hidden, weight)


MESH_IDS = pl.DeviceIdType.MESH


def barrier_all(rank, count, place):
    barrier = pltpu.get_barrier_semaphore()

    def greet(step, carry):
        pl.semaphore_signal(
            barrier, inc=1, device_id=place(lax.rem(rank + step, count)), device_id_type=MESH_IDS
        )
        return carry

    lax.fori_loop(1, count, greet, 0)
    pl.semaphore_wait(barrier, count - 1)


class Spot:
    def __init__(self, n_dp, n_head):
        self.n_dp, self.n_head = n_dp, n_head
        self.count = n_dp * n_head
        self.nz, self.nx = n_dp // 2, n_head // 2
        dp, head = lax.axis_index("dp"), lax.axis_index("head")
        self.rank = dp * n_head + head
        self.z, self.y = dp // 2, lax.rem(dp, 2)
        self.x, self.c = head // 2, lax.rem(head, 2)

    def place(self, rank):
        return (rank // self.n_head, lax.rem(rank, self.n_head))

    def device(self, z, y, x, c):
        return (z * 2 + y, x * 2 + c)


def remote(source, target, send_sem, recv_sem, device):
    return pltpu.make_async_remote_copy(
        src_ref=source,
        dst_ref=target,
        send_sem=send_sem,
        recv_sem=recv_sem,
        device_id=device,
        device_id_type=MESH_IDS,
    )


def start_all_to_all(spot, source, target, send_sems, recv_sems, local_sem):
    pltpu.make_async_copy(source.at[spot.rank], target.at[spot.rank], local_sem).start()

    def send(step, carry):
        peer = lax.rem(spot.rank + step, spot.count)
        remote(
            source.at[peer], target.at[spot.rank], send_sems.at[step], recv_sems.at[step], spot.place(peer)
        ).start()
        return carry

    lax.fori_loop(1, spot.count, send, 0)


def finish_all_to_all(spot, source, target, send_sems, recv_sems, local_sem):
    def take(step, carry):
        origin = lax.rem(spot.rank + spot.count - step, spot.count)
        copy = remote(
            source.at[origin], target.at[origin], send_sems.at[step], recv_sems.at[step], spot.place(origin)
        )
        copy.wait_recv()
        copy.wait_send()
        return carry

    lax.fori_loop(1, spot.count, take, 0)
    pltpu.make_async_copy(source.at[spot.rank], target.at[spot.rank], local_sem).wait()


def small_exchange_kernel(sizes, source, target, send_sems, recv_sems, local_sem):
    spot = Spot(*sizes)
    barrier_all(spot.rank, spot.count, spot.place)
    start_all_to_all(spot, source, target, send_sems, recv_sems, local_sem)
    finish_all_to_all(spot, source, target, send_sems, recv_sems, local_sem)


def small_exchange(sizes, messages, collective_id):
    count = sizes[0] * sizes[1]
    return pl.pallas_call(
        functools.partial(small_exchange_kernel, sizes),
        in_specs=[pl.BlockSpec(memory_space=pltpu.VMEM)],
        out_specs=pl.BlockSpec(memory_space=pltpu.VMEM),
        out_shape=jax.ShapeDtypeStruct(messages.shape, messages.dtype),
        scratch_shapes=[
            pltpu.SemaphoreType.DMA((count,)),
            pltpu.SemaphoreType.DMA((count,)),
            pltpu.SemaphoreType.DMA,
        ],
        compiler_params=pltpu.CompilerParams(collective_id=collective_id, has_side_effects=True),
    )(messages)


def is_direct(shape):
    return shape[1] % 16 == 0 and shape[2] % 128 == 0


def piece_of(whole, shape, dp, head):
    if not is_direct(shape):
        return whole.at[dp, head]
    rows = pl.ds(pl.multiple_of(dp * shape[1], shape[1]), shape[1])
    return whole.at[:, rows, pl.ds(pl.multiple_of(head * shape[2], shape[2]), shape[2])]


def whole_shape(sizes, shape):
    if not is_direct(shape):
        return sizes + shape
    return (shape[0], sizes[0] * shape[1], sizes[1] * shape[2])


def gather_kernel(
    sizes,
    rows,
    shard,
    rows_out,
    full,
    row_send,
    row_recv,
    piece_send,
    piece_recv,
    local_sems,
):
    spot = Spot(*sizes)
    z, y, x, c, nz, nx = spot.z, spot.y, spot.x, spot.c, spot.nz, spot.nx
    barrier_all(spot.rank, spot.count, spot.place)
    own_copy = pltpu.make_async_copy(
        shard, piece_of(full, shard.shape, z * 2 + y, x * 2 + c), local_sems.at[1]
    )
    own_copy.start()

    sends = []

    def send_piece(source, piece, device):
        copy = remote(
            source,
            piece_of(full, shard.shape, piece[0] * 2 + piece[1], piece[2] * 2 + piece[3]),
            piece_send.at[len(sends)],
            piece_recv.at[piece[0] * 2 + piece[1], piece[2] * 2 + piece[3]],
            device,
        )
        copy.start()
        sends.append(copy)

    def wait_piece(piece):
        here = piece_of(full, shard.shape, piece[0] * 2 + piece[1], piece[2] * 2 + piece[3])
        remote(
            here,
            here,
            piece_send.at[0],
            piece_recv.at[piece[0] * 2 + piece[1], piece[2] * 2 + piece[3]],
            spot.device(z, y, x, 1 - c),
        ).wait_recv()
        return here

    own = (z, y, x, c)
    others_x = [lax.rem(x + step, nx) for step in range(1, nx)]
    for step in range(1, nz):
        send_piece(shard, own, spot.device(lax.rem(z + step, nz), y, x, c))
    for other in others_x:
        send_piece(shard, own, spot.device(z, y, other, c))
    send_piece(shard, own, spot.device(z, 1 - y, x, c))
    send_piece(shard, own, spot.device(z, y, x, 1 - c))
    start_all_to_all(spot, rows, rows_out, row_send, row_recv, local_sems.at[0])
    for step in range(1, nz):
        piece = (lax.rem(z + nz - step, nz), y, x, c)
        here = wait_piece(piece)
        for other in others_x:
            send_piece(here, piece, spot.device(z, y, other, c))
        send_piece(here, piece, spot.device(z, 1 - y, x, c))
        send_piece(here, piece, spot.device(z, y, x, 1 - c))
    for step in range(nz):
        for other in others_x:
            piece = (lax.rem(z + nz - step, nz), y, other, c)
            here = wait_piece(piece)
            send_piece(here, piece, spot.device(z, 1 - y, x, c))
            send_piece(here, piece, spot.device(z, y, x, 1 - c))

    for step in range(nz):
        for column in [x] + others_x:
            piece = (lax.rem(z + nz - step, nz), 1 - y, column, c)
            here = wait_piece(piece)
            send_piece(here, piece, spot.device(z, y, x, 1 - c))
    for step in range(nz):
        for side in (y, 1 - y):
            for column in [x] + others_x:
                wait_piece((lax.rem(z + nz - step, nz), side, column, 1 - c))
    for copy in sends:
        copy.wait_send()
    finish_all_to_all(spot, rows, rows_out, row_send, row_recv, local_sems.at[0])
    own_copy.wait()


def gather_weights(sizes, rows, shard):
    n_dp, n_head = sizes
    count = n_dp * n_head
    nz, nx = n_dp // 2, n_head // 2
    sends = (nz - 1) + (nx - 1) + 2 + (nz - 1) * (nx + 1) + nz * (nx - 1) * 2 + nz * nx
    anywhere = pl.BlockSpec(memory_space=pl.ANY)
    return pl.pallas_call(
        functools.partial(gather_kernel, sizes),
        in_specs=[anywhere] * 2,
        out_specs=[anywhere] * 2,
        out_shape=[
            jax.ShapeDtypeStruct(rows.shape, rows.dtype),
            jax.ShapeDtypeStruct(whole_shape(sizes, shard.shape), shard.dtype),
        ],
        scratch_shapes=[
            pltpu.SemaphoreType.DMA((count,)),
            pltpu.SemaphoreType.DMA((count,)),
            pltpu.SemaphoreType.DMA((sends,)),
            pltpu.SemaphoreType.DMA((n_dp, n_head)),
            pltpu.SemaphoreType.DMA((2,)),
        ],
        compiler_params=pltpu.CompilerParams(collective_id=2, has_side_effects=True),
    )(rows, shard)


def reduce_kernel(
    sizes,
    rows,
    pieces,
    rows_out,
    total,
    core_in,
    y_in,
    x_in,
    z_in,
    row_send,
    row_recv,
    core_send,
    core_recv,
    y_send,
    y_recv,
    x_send,
    x_recv,
    z_send,
    z_recv,
    local_sem,
):
    spot = Spot(*sizes)
    z, y, x, c, nz, nx = spot.z, spot.y, spot.x, spot.c, spot.nz, spot.nx
    shape = total.shape
    barrier_all(spot.rank, spot.count, spot.place)
    sibling = spot.device(z, y, x, 1 - c)
    opposite = spot.device(z, 1 - y, x, c)

    def core_copy(deep, side, column):
        return remote(
            piece_of(pieces, shape, deep * 2 + side, column * 2 + 1 - c),
            core_in.at[deep, side, column],
            core_send.at[deep, side, column],
            core_recv.at[deep, side, column],
            sibling,
        )

    def y_copy(deep, column):
        return remote(
            core_in.at[deep, 1 - y, column],
            y_in.at[deep, column],
            y_send.at[deep, column],
            y_recv.at[deep, column],
            opposite,
        )

    def x_copy(step, deep):
        column = lax.rem(x + step, nx)
        return remote(
            y_in.at[deep, column],
            x_in.at[step - 1, deep],
            x_send.at[step - 1, deep],
            x_recv.at[step - 1, deep],
            spot.device(z, y, column, c),
        )

    def z_copy(step):
        deep = lax.rem(z + step, nz)
        return remote(
            y_in.at[deep, x],
            z_in.at[step - 1],
            z_send.at[step - 1],
            z_recv.at[step - 1],
            spot.device(deep, y, x, c),
        )

    def add_into(target, sources):
        def some(block, carry):
            value = target[block].astype(jnp.float32)
            for source in sources:
                value = value + source[block].astype(jnp.float32)
            target[block] = value.astype(target.dtype)
            return carry

        lax.fori_loop(0, shape[0], some, 0)

    depth_order = lambda step: lax.rem(z + 1 + step, nz)
    columns = [lax.rem(x + step, nx) for step in range(1, nx)] + [x]
    for side in (1 - y, y):
        for column in columns:

            def send_core(step, carry, side=side, column=column):
                core_copy(depth_order(step), side, column).start()
                return carry

            lax.fori_loop(0, nz, send_core, 0)
    start_all_to_all(spot, rows, rows_out, row_send, row_recv, local_sem)
    for side in (1 - y, y):
        for column in columns:

            def take_core(step, carry, side=side, column=column):
                deep = depth_order(step)
                core_copy(deep, side, column).wait_recv()
                own = piece_of(pieces, shape, deep * 2 + side, column * 2 + c)
                add_into(core_in.at[deep, side, column], [own])
                return carry

            def send_y(step, carry, column=column):
                take_core(step, carry, 1 - y, column)
                y_copy(depth_order(step), column).start()
                return carry

            lax.fori_loop(0, nz, send_y if side is not y else take_core, 0)
    for step_x, column in enumerate(columns):

        def take_y(step, carry, step_x=step_x, column=column):
            deep = depth_order(step)
            y_copy(deep, column).wait_recv()
            add_into(y_in.at[deep, column], [core_in.at[deep, y, column]])
            if step_x + 1 < nx:
                x_copy(step_x + 1, deep).start()
            return carry

        lax.fori_loop(0, nz, take_y, 0)
    for step in range(nz):
        deep = depth_order(step)
        for step_x in range(1, nx):
            x_copy(step_x, deep).wait_recv()
        add_into(y_in.at[deep, x], [x_in.at[step_x, deep] for step_x in range(nx - 1)])
        if step + 1 < nz:
            z_copy(step + 1).start()
    for step in range(1, nz):
        z_copy(step).wait_recv()

    def finish(block, carry):
        value = y_in[z, x, block].astype(jnp.float32)
        for step in range(nz - 1):
            value = value + z_in[step, block].astype(jnp.float32)
        total[block] = value
        return carry

    lax.fori_loop(0, shape[0], finish, 0)
    for side in (1 - y, y):
        for column in columns:

            def end_core(step, carry, side=side, column=column):
                core_copy(depth_order(step), side, column).wait_send()
                return carry

            lax.fori_loop(0, nz, end_core, 0)
    for column in columns:

        def end_y(step, carry, column=column):
            y_copy(depth_order(step), column).wait_send()
            return carry

        lax.fori_loop(0, nz, end_y, 0)
    for step_x in range(1, nx):

        def end_x(step, carry, step_x=step_x):
            x_copy(step_x, depth_order(step)).wait_send()
            return carry

        lax.fori_loop(0, nz, end_x, 0)
    for step in range(1, nz):
        z_copy(step).wait_send()
    finish_all_to_all(spot, rows, rows_out, row_send, row_recv, local_sem)


def reduce_grads(sizes, rows, pieces, one):
    n_dp, n_head = sizes
    count = n_dp * n_head
    nz, nx = n_dp // 2, n_head // 2
    dma = pltpu.SemaphoreType.DMA
    return pl.pallas_call(
        functools.partial(reduce_kernel, sizes),
        in_specs=[pl.BlockSpec(memory_space=pl.ANY), pl.BlockSpec(memory_space=pltpu.VMEM)],
        out_specs=[pl.BlockSpec(memory_space=pl.ANY), pl.BlockSpec(memory_space=pltpu.VMEM)],
        out_shape=[
            jax.ShapeDtypeStruct(rows.shape, rows.dtype),
            jax.ShapeDtypeStruct(one, jnp.float32),
        ],
        scratch_shapes=[
            pltpu.VMEM((nz, 2, nx) + one, pieces.dtype),
            pltpu.VMEM((nz, nx) + one, pieces.dtype),
            pltpu.VMEM((nx - 1, nz) + one, pieces.dtype),
            pltpu.VMEM((nz - 1,) + one, pieces.dtype),
            dma((count,)),
            dma((count,)),
            dma((nz, 2, nx)),
            dma((nz, 2, nx)),
            dma((nz, nx)),
            dma((nz, nx)),
            dma((nx - 1, nz)),
            dma((nx - 1, nz)),
            dma((nz - 1,)),
            dma((nz - 1,)),
            dma,
        ],
        compiler_params=pltpu.CompilerParams(
            collective_id=3, has_side_effects=True, vmem_limit_bytes=40 * 2**20
        ),
    )(rows, pieces)


def stack_blocks(qkv_weight, proj_weight, up_weight, down_weight, position_table):
    depth, width = position_table.shape
    parts = by_part(qkv_weight, qkv_weight.shape[2] // (3 * HD))
    parts = parts.reshape(LAYERS, depth, 3, width).transpose(0, 2, 1, 3).reshape(6, depth, width)
    up_blocks = up_weight.reshape(depth, width // depth, 4, depth).transpose(2, 0, 1, 3)
    return jnp.concatenate(
        [
            parts,
            proj_weight[None],
            position_table[None],
            up_blocks.reshape(4, depth, width),
            down_weight.reshape(4, depth, width),
        ],
        axis=0,
    )


def split_blocks(total):
    depth, width = total.shape[1:]
    parts = total[:6].reshape(LAYERS, 3, depth, width).transpose(0, 2, 1, 3)
    qkv_grad = by_head(parts.reshape(LAYERS, depth, 3 * width), width // HD)
    up_grad = total[8:12].reshape(4, depth, width // depth, depth).transpose(1, 2, 0, 3)
    return (
        total[7],
        qkv_grad,
        total[6:7],
        up_grad.reshape(1, depth, 4 * width),
        total[12:16].reshape(1, 4 * depth, width),
    )


def arrange_gains(gains, n_dp):
    offset = 2 * D
    qkv_bias = by_part(gains[offset : offset + 3 * D], HEADS)
    up_bias = gains[offset + 4 * D : offset + 4 * D + FF].reshape(n_dp, 4, D // n_dp)
    return jnp.concatenate(
        [
            gains[:offset],
            qkv_bias,
            gains[offset + 3 * D : offset + 4 * D],
            up_bias.transpose(1, 0, 2).reshape(-1),
            gains[offset + 4 * D + FF : offset + 9 * D + FF],
            by_part(gains[offset + 9 * D + FF :], HEADS),
        ]
    ).reshape(GAIN_ROWS, D)


def restore_gains(rows, n_dp):
    up_bias = rows[6:10].reshape(4, n_dp, D // n_dp).transpose(1, 0, 2)
    return jnp.concatenate(
        [
            rows[0:2].reshape(-1),
            by_head(rows[2:5].reshape(-1), HEADS),
            rows[5],
            up_bias.reshape(-1),
            rows[10:15].reshape(-1),
            by_head(rows[15:18].reshape(-1), HEADS),
        ]
    )


def gather_teacher(weight):
    width = weight.shape[1]
    order = by_part(jnp.arange(width, dtype=jnp.int32), width // (3 * THD))
    turned = dot(weight, one_hot(order, width).T).astype(jnp.bfloat16)
    return lax.all_gather(turned.reshape(TD, 3, -1).transpose(1, 0, 2), "head", axis=0)


def request_slots(token_ids, shard_rows, count, room, usable):
    here = token_ids.shape[0]
    index = jnp.arange(here, dtype=jnp.int32)
    owner = token_ids // shard_rows
    equal = token_ids[:, None] == token_ids[None, :]
    first = jnp.min(jnp.where(equal, index[:, None], here), axis=0)
    is_first = first == index
    earlier = (owner[:, None] == owner[None, :]) & is_first[:, None] & (index[:, None] < index[None, :])
    order = jnp.sum(earlier.astype(jnp.int32), axis=0)
    overflow = jnp.any(is_first & (order >= usable))
    slot_first = owner * room + order
    chosen = first[None, :] == index[:, None]
    slot = jnp.sum(jnp.where(chosen, slot_first[:, None], 0), axis=0)
    spots = jnp.arange(count * room, dtype=jnp.int32)
    asked = is_first[:, None] & (slot_first[:, None] == spots[None, :]) & (order < usable)[:, None]
    request = jnp.sum(jnp.where(asked, (token_ids % shard_rows)[:, None] + 1, 0), axis=0) - 1
    return slot, request, overflow


def one_hot(index, size):
    return (index[:, None] == jnp.arange(size, dtype=jnp.int32)[None, :]).astype(jnp.bfloat16)


def adam_update(master, first, second, grad_clip, rate):
    first_new = B_ONE * first + (1.0 - B_ONE) * grad_clip
    second_new = B_TWO * second + (1.0 - B_TWO) * grad_clip * grad_clip
    ascent = (
        first_new / (1.0 - B_ONE**STEP) / (jnp.sqrt(second_new / (1.0 - B_TWO**STEP)) + EPSILON)
    )
    return (master - rate * (ascent + DECAY * master), first_new, second_new)


def shards(
    token_ids,
    seq_lengths,
    teacher_hidden,
    teacher_weight,
    token_table,
    token_first,
    token_second,
    position_table,
    position_first,
    position_second,
    qkv_weight,
    qkv_first,
    qkv_second,
    proj_weight,
    proj_first,
    proj_second,
    up_weight,
    up_first,
    up_second,
    down_weight,
    down_first,
    down_second,
    gains_biases,
    gains_first,
    gains_second,
):
    n_dp, n_head = sizes = (lax.axis_size("dp"), lax.axis_size("head"))
    count = n_dp * n_head
    here, shard_rows = token_ids.shape[0], token_table.shape[0]
    room = 16 * -(-3 * here // (2 * count * 16))
    slot, request, overflow = request_slots(token_ids, shard_rows, count, room, room - 1)
    notes = jnp.stack([overflow.astype(jnp.float32), jnp.sum(seq_lengths).astype(jnp.float32)])
    small_size = gains_biases.shape[0]
    small_rows = -(-small_size // 128)
    small_mine = gains_biases.astype(jnp.bfloat16).astype(jnp.float32)
    small_mine = jnp.pad(small_mine, (0, small_rows * 128 - small_size)).reshape(1, small_rows, 128)
    message = jnp.concatenate(
        [
            jnp.pad(
                request.astype(jnp.float32).reshape(count, 1, room), ((0, 0), (0, 0), (0, 128 - room))
            ),
            jnp.broadcast_to(jnp.pad(notes, (0, 126)), (count, 1, 128)),
            jnp.broadcast_to(small_mine, (count, small_rows, 128)),
            jnp.zeros((count, 6 - small_rows, 128), jnp.float32),
        ],
        axis=1,
    )
    heard = small_exchange(sizes, message, 1)
    too_many = jnp.any(heard[:, 1, 0] > 0.0)
    valid_total = jnp.sum(heard[:, 1, 1])
    wanted = heard[:, 0, :room].reshape(-1).astype(jnp.int32)
    gains = arrange_gains(
        heard[:, 2 : 2 + small_rows].reshape(count, -1)[:, :small_size].reshape(-1), n_dp
    )
    table_low = token_table.astype(jnp.bfloat16)
    wanted_hot = one_hot(wanted, shard_rows)
    rows_out = dot(wanted_hot, table_low).astype(jnp.bfloat16).reshape(count, room, D)
    shard = stack_blocks(
        qkv_weight, proj_weight[0], up_weight[0], down_weight[0], position_table
    ).astype(jnp.bfloat16)
    teach_full = gather_teacher(teacher_weight)
    rows_in, big = gather_weights(sizes, rows_out, shard)
    if not is_direct(shard.shape):
        big = big.transpose(2, 0, 3, 1, 4).reshape(16, D, D)

    def owned_rows():
        group_ids = lax.all_gather(token_ids, "head", axis=0, tiled=True)
        block_ids = group_ids // shard_rows
        owned = block_ids % n_head == lax.axis_index("head")
        local = jnp.where(owned, block_ids // n_head * shard_rows + group_ids % shard_rows, 0)
        return owned, local

    def rows_by_owner():
        owned, local = owned_rows()
        rows_all = lax.all_gather(table_low, "dp", axis=0, tiled=True)
        picked = jnp.where(owned[:, None], rows_all[local], jnp.zeros((), jnp.bfloat16))
        rows_here = lax.psum_scatter(picked, "head", scatter_dimension=0, tiled=True)
        return (
            jnp.pad(rows_here, ((0, count * room - here), (0, 0))),
            jnp.arange(here, dtype=jnp.int32),
        )

    rows_used, slot_used = lax.cond(
        too_many, rows_by_owner, lambda: (rows_in.reshape(count * room, D), slot)
    )
    teacher_qkv = project_teacher(teacher_hidden, teach_full)
    final_qkv, *kept = forward_layer(seq_lengths, rows_used, slot_used, big, gains)
    final_grad, loss_local = relation(seq_lengths, final_qkv, teacher_qkv)
    pieces, gain_grads, slot_grads, row_low = backward_layer(
        seq_lengths, slot_used, big, gains, final_grad, kept, count * room
    )
    if not is_direct(shard.shape):
        pieces = pieces.reshape(16, n_dp, shard.shape[1], n_head, shard.shape[2])
        pieces = pieces.transpose(1, 3, 0, 2, 4)
    gain_rows = jnp.pad(
        restore_gains(gain_grads, n_dp).reshape(count, 1, small_size), ((0, 0), (0, 0), (0, D - small_size))
    )
    slot_grads = slot_grads.reshape(count, room, D).at[:, room - 1 :].set(gain_rows.astype(jnp.bfloat16))
    grads_in, total = reduce_grads(sizes, slot_grads, pieces, shard.shape)
    small_grad = jnp.sum(grads_in[:, room - 1, :small_size].astype(jnp.float32), axis=0)

    def table_by_owner():
        owned, local = owned_rows()
        spread = lax.all_gather(row_low, "head", axis=0, tiled=True)
        table_grad = jax.ops.segment_sum(
            spread.astype(jnp.float32),
            jnp.where(owned, local, n_dp * shard_rows),
            num_segments=n_dp * shard_rows + 1,
        )[:-1]
        return lax.psum_scatter(
            table_grad.astype(jnp.bfloat16), "dp", scatter_dimension=0, tiled=True
        ).astype(jnp.float32)

    def table_by_slot():
        return lax.dot_general(
            wanted_hot,
            grads_in.reshape(count * room, D),
            (((0,), (0,)), ((), ())),
            preferred_element_type=jnp.float32,
        )

    table_grad = lax.cond(too_many, table_by_owner, table_by_slot)
    shard_grads = (table_grad,) + split_blocks(total) + (small_grad,)
    squares = sum((jnp.sum(grad_item * grad_item) for grad_item in shard_grads))
    sums = jnp.pad(jnp.stack([squares, loss_local])[None], ((0, 7), (0, 126)))
    everyone = small_exchange(sizes, jnp.broadcast_to(sums, (count, 8, 128)), 4)
    square_total = jnp.sum(everyone[:, 0, 0])
    loss_total = jnp.sum(everyone[:, 0, 1])
    grad_norm = jnp.sqrt(square_total) / valid_total
    clip_factor = THRESHOLD / jnp.maximum(grad_norm, THRESHOLD)
    factor = clip_factor / valid_total
    token_new = adam_update(
        token_table, token_first, token_second, shard_grads[0] * factor, RATE_TABLE
    )
    position_new = adam_update(
        position_table, position_first, position_second, shard_grads[1] * factor, RATE_TABLE
    )
    qkv_new = adam_update(qkv_weight, qkv_first, qkv_second, shard_grads[2] * factor, RATE_MATRIX)
    proj_new = adam_update(
        proj_weight, proj_first, proj_second, shard_grads[3] * factor, RATE_MATRIX
    )
    up_new = adam_update(up_weight, up_first, up_second, shard_grads[4] * factor, RATE_MATRIX)
    down_new = adam_update(
        down_weight, down_first, down_second, shard_grads[5] * factor, RATE_MATRIX
    )
    gains_new = adam_update(
        gains_biases, gains_first, gains_second, shard_grads[6] * factor, RATE_SMALL
    )
    loss_parts = jnp.stack([loss_total, valid_total])
    return (
        token_new[0],
        token_new[1],
        token_new[2],
        position_new[0],
        position_new[1],
        position_new[2],
        qkv_new[0],
        qkv_new[1],
        qkv_new[2],
        proj_new[0],
        proj_new[1],
        proj_new[2],
        up_new[0],
        up_new[1],
        up_new[2],
        down_new[0],
        down_new[1],
        down_new[2],
        gains_new[0],
        gains_new[1],
        gains_new[2],
        grad_norm,
        loss_parts,
    )


def solution(mesh):
    placed = (
        P(("dp", "head")),
        P(("dp", "head")),
        P(("dp", "head"), None),
        P(None, "head"),
        P(("dp", "head"), None),
        P(("dp", "head"), None),
        P(("dp", "head"), None),
        P("dp", "head"),
        P("dp", "head"),
        P("dp", "head"),
        P(None, "dp", "head"),
        P(None, "dp", "head"),
        P(None, "dp", "head"),
        P(None, "dp", "head"),
        P(None, "dp", "head"),
        P(None, "dp", "head"),
        P(None, "dp", "head"),
        P(None, "dp", "head"),
        P(None, "dp", "head"),
        P(None, "dp", "head"),
        P(None, "dp", "head"),
        P(None, "dp", "head"),
        P(("dp", "head")),
        P(("dp", "head")),
        P(("dp", "head")),
    )
    return jax.shard_map(
        shards,
        mesh=mesh,
        in_specs=placed,
        out_specs=(
            P(("dp", "head"), None),
            P(("dp", "head"), None),
            P(("dp", "head"), None),
            P("dp", "head"),
            P("dp", "head"),
            P("dp", "head"),
            P(None, "dp", "head"),
            P(None, "dp", "head"),
            P(None, "dp", "head"),
            P(None, "dp", "head"),
            P(None, "dp", "head"),
            P(None, "dp", "head"),
            P(None, "dp", "head"),
            P(None, "dp", "head"),
            P(None, "dp", "head"),
            P(None, "dp", "head"),
            P(None, "dp", "head"),
            P(None, "dp", "head"),
            P(("dp", "head")),
            P(("dp", "head")),
            P(("dp", "head")),
            P(),
            P(),
        ),
        check_vma=False,
    )
```

```python
import functools
import math

import jax
import jax.numpy as jnp
from jax import lax
from jax.experimental import pallas as pl
from jax.experimental.pallas import tpu as pltpu
from jax.sharding import PartitionSpec as P

D = 512
HEADS = 8
HD = 64
FF = 2048
TD = 1024
THEADS = 16
THD = 64
REL = 64
LAYERS = 2
LA = 128
LB = 256
LC = 512
M = 1
STEP = 10


B_ONE = 0.9
B_TWO = 0.999
EPSILON = 1e-10
DECAY = 0.01
THRESHOLD = 0.0003
RATE_TABLE = 1.0
RATE_MATRIX = 0.1
RATE_SMALL = 2.0


def dot(left, right, dims=(((1,), (0,)), ((), ()))):
    return lax.dot_general(left, right, dims, preferred_element_type=jnp.float32)


NT = (((1,), (1,)), ((), ()))


LOG2E = 1.4426950408889634
LN2 = 0.6931471805599453
GROUPS = 4
S_WIDE = D // GROUPS
T_WIDE = TD // GROUPS
S_DIM = D // REL
T_DIM = TD // REL
FAST_LIMIT = 60.0
SEQS = ((0, LA), (LA, LA), (2 * LA, LB), (2 * LA + LB, LC))
TOKENS_HERE = 2 * LA + LB + LC
BLOCKS = ((2 * LA + LB, LC, (3,)), (2 * LA, LB, (2,)), (0, 2 * LA, (0, 1)))
AT_ONCE = 4
KEY_ROWS = 128


def relation_kernel(
    lens_ref,
    s_ref,
    t_ref,
    ds_ref,
    loss_ref,
    s_rows,
    t_rows,
    d_rows,
    exp_c,
    exp_b,
    exp_a,
    s_keep,
    t_keep,
):
    @pl.when((pl.program_id(0) == 0) & (pl.program_id(1) == 0))
    def _():
        loss_ref[...] = jnp.zeros_like(loss_ref)
        exp_a[...] = jnp.zeros_like(exp_a)

    s_scale = LOG2E / math.sqrt(S_DIM)
    t_scale = LOG2E / math.sqrt(T_DIM)
    zero = jnp.zeros((), jnp.bfloat16)
    half_heads = 128 // T_DIM
    exps = (exp_c, exp_b, exp_a)

    def valid_rows(block):
        off, length, seqs = BLOCKS[block]
        each = length // len(seqs)
        row = lax.broadcasted_iota(jnp.int32, (length, 128), 0)
        valid = row < 0
        for place, seq in enumerate(seqs):
            start = place * each
            valid = valid | (row >= start) & (row < start + lens_ref[seq])
        return valid

    def prepare(block):
        off, length, seqs = BLOCKS[block]
        each = length // len(seqs)
        lane = lax.broadcasted_iota(jnp.int32, (8, length), 1)
        lane_valid, padded = lane < 0, jnp.zeros((8, length), jnp.float32)
        for place, seq in enumerate(seqs):
            start = place * each
            lane_valid = lane_valid | (lane >= start) & (lane < start + lens_ref[seq])
            padded = jnp.where(lane >= start, (each - lens_ref[seq]).astype(jnp.float32), padded)
        row_valid = valid_rows(block)
        rows = slice(off, off + length)
        s_block = jnp.where(row_valid, s_ref[rows, :], zero).astype(jnp.float32)
        s_keep[rows, :] = (s_block * math.sqrt(s_scale)).astype(jnp.bfloat16)
        s_rows[:, rows] = s_block.T
        for half in range(2):
            cols = slice(half * 128, half * 128 + 128)
            t_block = jnp.where(row_valid, t_ref[rows, cols], zero).astype(jnp.float32)
            t_keep[half, rows, :] = (t_block * math.sqrt(t_scale)).astype(jnp.bfloat16)
            t_rows[cols, rows] = t_block.T
        s_here = s_rows[:, rows]
        t_here = t_rows[:, rows]
        s_square = jnp.sum((s_here * s_here).reshape(16, S_DIM, length), axis=1)
        t_square = jnp.sum((t_here * t_here).reshape(16, T_DIM, length), axis=1)
        bound = jnp.maximum(jnp.max(s_square) * s_scale, jnp.max(t_square) * t_scale)
        return bound, lane_valid.astype(jnp.float32), padded[0:1]

    info = [prepare(block) for block in range(len(BLOCKS))]

    def fold_rows(value):
        total = value[0:8]
        for start in range(8, value.shape[0], 8):
            total = total + value[start : start + 8]
        return total

    def one_head(rows, length, head):
        lane = lax.broadcasted_iota(jnp.int32, (length, 128), 1)
        half = head // half_heads
        s_one = jnp.where(lane // S_DIM == head, s_keep[rows, :], zero)
        t_one = jnp.where(lane // T_DIM == head - half * half_heads, t_keep[half, rows, :], zero)
        return half, s_one, t_one

    def row_slices(head):
        s_slice = pl.ds(pl.multiple_of(head * S_DIM, S_DIM), S_DIM)
        t_slice = pl.ds(pl.multiple_of(head * T_DIM, T_DIM), T_DIM)
        return s_slice, t_slice

    def fill(block, keys, one, target):
        off, length, seqs = BLOCKS[block]
        each = length // len(seqs)
        if len(seqs) > 1:
            scores = dot(keys[...], one, NT)
            sums = []
            for place in range(len(seqs)):
                here = slice(place * each, place * each + each)
                value = jnp.exp2(scores[here, here])
                sums.append(fold_rows(value))
                target[here, here] = value.astype(jnp.bfloat16)
            return jnp.concatenate(sums, axis=1)
        total = jnp.zeros((8, length), jnp.float32)
        for start in range(0, length, KEY_ROWS):
            here = slice(start, start + KEY_ROWS)
            value = jnp.exp2(dot(keys[here, :], one, NT))
            total = total + fold_rows(value)
            target[here, :] = value.astype(jnp.bfloat16)
        return total

    def fill_both(block, head, slot):
        off, length, seqs = BLOCKS[block]
        rows = slice(off, off + length)
        half, s_one, t_one = one_head(rows, length, head)
        return (
            fill(block, s_keep.at[rows, :], s_one, exps[block].at[slot, 0]),
            fill(block, t_keep.at[half, rows, :], t_one, exps[block].at[slot, 1]),
        )

    def use_both(block, head, slot, sums):
        off, length, seqs = BLOCKS[block]
        rows = slice(off, off + length)
        bound, valid_row, padded = info[block]
        s_total = jnp.sum(sums[0], axis=0, keepdims=True) - padded
        t_total = jnp.sum(sums[1], axis=0, keepdims=True) - padded
        s_recip = valid_row / s_total
        t_recip = valid_row / t_total
        s_slice, t_slice = row_slices(head)
        s_vec = s_rows[s_slice, rows]
        t_vec = t_rows[t_slice, rows]
        t_left = jnp.concatenate([s_vec, s_vec * t_recip, t_vec], axis=0).astype(jnp.bfloat16)
        s_left = jnp.concatenate([s_vec, s_vec * s_recip], axis=0).astype(jnp.bfloat16)
        t_out = dot(t_left, exps[block][slot, 1])
        s_out = dot(s_left, exps[block][slot, 0])
        d_rows[s_slice, rows] = (
            s_out[0:8] * s_recip - t_out[0:8] * t_recip + (s_out[8:16] - t_out[8:16]) * valid_row
        )
        inner = t_vec * t_out[16:32]
        inner = (inner[0:8] + inner[8:16]) * t_scale - s_vec * t_out[0:8] * s_scale
        parts = inner * t_recip + (jnp.log2(s_total) - jnp.log2(t_total)) * (valid_row * 0.125)
        return fold_lanes(parts, length)

    def fold_lanes(parts, length):
        total = parts[:, 0:128]
        for start in range(128, length, 128):
            total = total + parts[:, start : start + 128]
        return total

    def fast_heads(step, carry):
        work = [
            (block, step * AT_ONCE + slot, slot)
            for slot in range(AT_ONCE)
            for block in range(len(BLOCKS))
        ]
        sums = [fill_both(*item) for item in work]
        total = jnp.zeros((8, 128), jnp.float32)
        for item, item_sums in zip(work, sums):
            total = total + use_both(*item, item_sums)
        loss_ref[...] += total
        return carry

    def exact_head(seq, head):
        off, length = SEQS[seq]
        rows = slice(off, off + length)
        valid = lens_ref[seq]
        half, s_one, t_one = one_head(rows, length, head)
        s_slice, t_slice = row_slices(head)
        key_valid = lax.broadcasted_iota(jnp.int32, (length, 128), 0) < valid
        exp_c[0, 0, 0:length, 0:128] = s_one
        exp_c[0, 1, 0:length, 0:128] = t_one

        def log_soft(scores, scale):
            scaled = jnp.where(key_valid, scores * scale, -1e30)
            top = jnp.max(scaled, axis=0, keepdims=True)
            shifted = scaled - top
            total = jnp.sum(jnp.exp2(shifted), axis=0, keepdims=True)
            return shifted - jnp.log2(total)

        def queries(block, carry):
            start = pl.multiple_of(block * 128, 128)
            here = pl.ds(start, 128)
            query_valid = lax.broadcasted_iota(jnp.int32, (length, 128), 1) + start < valid
            both = key_valid & query_valid
            s_log = log_soft(dot(s_keep[rows, :], exp_c[0, 0, here, 0:128], NT), s_scale)
            t_log = log_soft(dot(t_keep[half, rows, :], exp_c[0, 1, here, 0:128], NT), t_scale)
            t_soft = jnp.exp2(t_log)
            change = jnp.where(both, jnp.exp2(s_log) - t_soft, 0.0)
            exp_c[1, 0, 0:length, here] = change.astype(jnp.bfloat16)
            loss_ref[...] += fold_rows(jnp.where(both, t_soft * (t_log - s_log), 0.0))
            return carry

        lax.fori_loop(0, length // 128, queries, 0)
        s_vec = s_rows[s_slice, rows]
        left = jnp.concatenate([s_vec, jnp.zeros_like(s_vec)], axis=0).astype(jnp.bfloat16)
        change = exp_c[1, 0, 0:length, 0:length]
        d_rows[s_slice, rows] = (dot(left, change) + dot(left, change, NT))[0:8]

    top_bound = info[0][0]
    for entry in info:
        top_bound = jnp.maximum(top_bound, entry[0])
    fast = top_bound < FAST_LIMIT

    @pl.when(fast)
    def _():
        lax.fori_loop(0, 2 * half_heads // AT_ONCE, fast_heads, 0)

    @pl.when(jnp.logical_not(fast))
    def _():
        for block, (off, length, seqs) in enumerate(BLOCKS):
            rows = slice(off, off + length)
            row_valid = valid_rows(block)
            s_keep[rows, :] = jnp.where(row_valid, s_ref[rows, :], zero)
            for half in range(2):
                t_block = t_ref[rows, half * 128 : half * 128 + 128]
                t_keep[half, rows, :] = jnp.where(row_valid, t_block, zero)
        for seq in range(len(SEQS)):

            def body(head, carry, seq=seq):
                exact_head(seq, head)
                return carry

            lax.fori_loop(0, 2 * half_heads, body, 0)

    for off, length in SEQS:
        ds_ref[off : off + length, :] = (
            d_rows[:, off : off + length].T * (1.0 / math.sqrt(S_DIM) / (3 * REL))
        ).astype(ds_ref.dtype)


def relation(seq_lengths, student, teacher):
    block_s = pl.BlockSpec((None, TOKENS_HERE, S_WIDE), lambda part, group: (part, 0, group))
    block_t = pl.BlockSpec((None, TOKENS_HERE, T_WIDE), lambda part, group: (part, 0, group))
    grads, loss = pl.pallas_call(
        relation_kernel,
        grid=(3, GROUPS),
        in_specs=[pl.BlockSpec(memory_space=pltpu.SMEM), block_s, block_t],
        out_specs=[block_s, pl.BlockSpec((8, 128), lambda part, group: (0, 0))],
        out_shape=[
            jax.ShapeDtypeStruct((3, TOKENS_HERE, D), jnp.bfloat16),
            jax.ShapeDtypeStruct((8, 128), jnp.float32),
        ],
        scratch_shapes=[
            pltpu.VMEM((S_WIDE, TOKENS_HERE), jnp.float32),
            pltpu.VMEM((T_WIDE, TOKENS_HERE), jnp.float32),
            pltpu.VMEM((S_WIDE, TOKENS_HERE), jnp.float32),
            pltpu.VMEM((AT_ONCE, 2, LC, LC), jnp.bfloat16),
            pltpu.VMEM((AT_ONCE, 2, LB, LB), jnp.bfloat16),
            pltpu.VMEM((AT_ONCE, 2, 2 * LA, 2 * LA), jnp.bfloat16),
            pltpu.VMEM((TOKENS_HERE, 128), jnp.bfloat16),
            pltpu.VMEM((2, TOKENS_HERE, 128), jnp.bfloat16),
        ],
        compiler_params=pltpu.CompilerParams(vmem_limit_bytes=48 * 2**20),
    )(seq_lengths, student, teacher)
    return grads, loss


def by_part(columns, heads):
    lead = columns.shape[:-1]
    size = columns.shape[-1] // heads // 3
    shaped = columns.reshape(lead + (heads, 3, size))
    return jnp.moveaxis(shaped, -2, -3).reshape(columns.shape)


def by_head(columns, heads):
    lead = columns.shape[:-1]
    size = columns.shape[-1] // heads // 3
    shaped = columns.reshape(lead + (3, heads, size))
    return jnp.moveaxis(shaped, -2, -3).reshape(columns.shape)


POS_AT = 7
GAIN_ROWS = 18
ERF_TOP = (
    -2.72614225801306e-10,
    2.77068142495902e-08,
    -2.10102402082508e-06,
    -5.69250639462346e-05,
    -7.34990630326855e-04,
    -2.95459980854025e-03,
    -1.60960333262415e-02,
)
ERF_LOW = (
    -1.45660718464996e-05,
    -2.13374055278905e-04,
    -1.68282697438203e-03,
    -7.37332916720468e-03,
    -1.42647390514189e-02,
)
STEP_ROWS = 256


def erf(value):
    value = jnp.clip(value, -4.0, 4.0)
    square = value * value
    top = jnp.full_like(value, ERF_TOP[0])
    for factor in ERF_TOP[1:]:
        top = top * square + factor
    low_part = jnp.full_like(value, ERF_LOW[0])
    for factor in ERF_LOW[1:]:
        low_part = low_part * square + factor
    return value * top / low_part


def normal_cdf(value):
    return 0.5 + 0.5 * erf(value * math.sqrt(0.5))


def normalize(values):
    average = jnp.mean(values, axis=-1, keepdims=True)
    centered = values - average
    variance = jnp.mean(centered * centered, axis=-1, keepdims=True)
    scale = lax.rsqrt(variance + 1e-05)
    return centered * scale, scale


def low16(value):
    return value.astype(jnp.bfloat16)


def step_slice(step):
    return pl.ds(pl.multiple_of(step * STEP_ROWS, STEP_ROWS), STEP_ROWS)


def head_soft(q_pair, k_one, valid, length):
    scores = dot(q_pair, k_one, NT) * (1.0 / math.sqrt(HD))
    lane = lax.broadcasted_iota(jnp.int32, scores.shape, 1)
    scores = jnp.where(lane < valid, scores, -1e30)
    top = jnp.max(scores, axis=-1, keepdims=True)
    value = jnp.exp(scores - top)
    return value / jnp.sum(value, axis=-1, keepdims=True)


def forward_kernel(
    lens_ref,
    rows_ref,
    slot_ref,
    big,
    gains,
    s_out,
    hat0,
    hat1,
    hat2,
    scale0,
    scale1,
    scale2,
    hid_low,
    qkv_low,
    ctx_low,
    mid_low,
    pre_low,
    x_low,
    hidden_kept,
):
    steps = TOKENS_HERE // STEP_ROWS

    def embed(step, carry):
        here = step_slice(step)
        spots = lax.broadcasted_iota(jnp.int32, (STEP_ROWS, rows_ref.shape[0]), 1)
        chosen = low16(jnp.where(slot_ref[here, :] == spots, 1.0, 0.0))
        first = big[POS_AT, 0:STEP_ROWS, :].astype(jnp.float32)
        twice = jnp.concatenate([first[0:LA], first[0:LA]], axis=0)
        late = big[POS_AT, STEP_ROWS : 2 * STEP_ROWS, :].astype(jnp.float32)
        place = jnp.where(step == 0, twice, jnp.where(step == 3, late, first))
        hat, scale = normalize(dot(chosen, rows_ref[...]) + place)
        hat0[here, :] = low16(hat)
        scale0[here, :] = scale
        wide = hat * gains[0:1, :] + gains[1:2, :]
        hidden_kept[here, :] = wide
        hidden = low16(wide)
        hid_low[here, :] = hidden
        for part in range(3):
            qkv_low[part, here, :] = low16(dot(hidden, big[part]) + gains[2 + part : 3 + part, :])
        return carry

    lax.fori_loop(0, steps, embed, 0)
    zero = jnp.zeros((), jnp.bfloat16)
    for seq, (off, length) in enumerate(SEQS):

        def attend_pair(pair, carry, seq=seq, off=off, length=length):
            rows = slice(off, off + length)
            cols = pl.ds(pl.multiple_of(pair * 128, 128), 128)
            query, key, value = (qkv_low[part, rows, cols] for part in range(3))
            lane = lax.broadcasted_iota(jnp.int32, (length, 128), 1)
            total = jnp.zeros((length, 128), jnp.float32)
            for side in range(2):
                mine = lane // HD == side
                soft = head_soft(query, jnp.where(mine, key, zero), lens_ref[seq], length)
                total = total + dot(low16(soft), jnp.where(mine, value, zero))
            ctx_low[rows, cols] = low16(total)
            return carry

        lax.fori_loop(0, D // 128, attend_pair, 0)

    def rest(step, carry):
        here = step_slice(step)
        hat, scale = normalize(hidden_kept[here, :] + dot(ctx_low[here, :], big[6]) + gains[5:6, :])
        hat1[here, :] = low16(hat)
        scale1[here, :] = scale
        middle = hat * gains[11:12, :] + gains[12:13, :]
        middle_low = low16(middle)
        mid_low[here, :] = middle_low
        output = middle + gains[10:11, :]
        for block in range(4):
            cols = slice(block * D, block * D + D)
            pre = dot(middle_low, big[8 + block]) + gains[6 + block : 7 + block, :]
            act = low16(pre * normal_cdf(pre))
            pre_low[here, cols] = low16(pre)
            output = output + dot(act, big[12 + block])
        hat, scale = normalize(output)
        hat2[here, :] = low16(hat)
        scale2[here, :] = scale
        final = low16(hat * gains[13:14, :] + gains[14:15, :])
        x_low[here, :] = final
        for part in range(3):
            s_out[part, here, :] = low16(dot(final, big[3 + part]) + gains[15 + part : 16 + part, :])
        return carry

    lax.fori_loop(0, steps, rest, 0)


def forward_layer(seq_lengths, rows, slot, big, gains):
    vmem = pl.BlockSpec(memory_space=pltpu.VMEM)
    shape = lambda *dims: jax.ShapeDtypeStruct(dims, jnp.float32)
    half = lambda *dims: jax.ShapeDtypeStruct(dims, jnp.bfloat16)
    tokens = TOKENS_HERE
    outs = [half(3, tokens, D)]
    outs += [half(tokens, D)] * 3 + [shape(tokens, 1)] * 3
    outs += [half(tokens, D), half(3, tokens, D), half(tokens, D), half(tokens, D)]
    outs += [half(tokens, FF), half(tokens, D)]
    return pl.pallas_call(
        forward_kernel,
        in_specs=[pl.BlockSpec(memory_space=pltpu.SMEM)] + [vmem] * 4,
        out_specs=[vmem] * len(outs),
        out_shape=outs,
        scratch_shapes=[pltpu.VMEM((tokens, D), jnp.float32)],
        compiler_params=pltpu.CompilerParams(vmem_limit_bytes=56 * 2**20),
    )(seq_lengths, rows, slot[:, None], big, gains)


def backward_kernel(
    lens_ref,
    slot_ref,
    big,
    gains,
    ds_ref,
    hat0,
    hat1,
    hat2,
    scale0,
    scale1,
    scale2,
    hid_low,
    qkv_low,
    ctx_low,
    mid_low,
    pre_low,
    x_low,
    grads,
    small,
    slot_grads,
    row_low,
    flow,
    flow_low,
    wide_low,
    turned,
    dqkv_low,
    act_low,
):
    steps = TOKENS_HERE // STEP_ROWS
    small[...] = jnp.zeros_like(small)

    def add_small(row, value):
        small[row : row + 1, :] += jnp.sum(value, axis=0, keepdims=True)

    def norm_back(here, grad, hat_ref, scale_ref, row):
        hat = hat_ref[here, :].astype(jnp.float32)
        add_small(row, grad * hat)
        add_small(row + 1, grad)
        inner = grad * gains[row : row + 1, :]
        mean_inner = jnp.mean(inner, axis=-1, keepdims=True)
        mean_hat = jnp.mean(inner * hat, axis=-1, keepdims=True)
        return scale_ref[here, :] * (inner - mean_inner - hat * mean_hat)

    def turn(source, width):
        for start in range(0, TOKENS_HERE, STEP_ROWS):
            turned[0:width, start : start + STEP_ROWS] = source[start : start + STEP_ROWS, 0:width].T

    def weight_grads(pairs):
        for index, right in pairs:
            grads[index] = low16(dot(turned[0:D, :], right))

    def last(step, carry):
        here = step_slice(step)
        grad = jnp.zeros((STEP_ROWS, D), jnp.float32)
        for part in range(3):
            piece = ds_ref[part, here, :]
            add_small(15 + part, piece.astype(jnp.float32))
            grad = grad + dot(piece, big[3 + part], NT)
        grad = norm_back(here, grad, hat2, scale2, 13)
        add_small(10, grad)
        grad_low = low16(grad)
        flow_low[here, :] = grad_low
        total = grad
        for block in range(4):
            cols = slice(block * D, block * D + D)
            pre = pre_low[here, cols].astype(jnp.float32)
            below = normal_cdf(pre)
            act_low[here, cols] = low16(pre * below)
            slope = below + pre * jnp.exp(pre * pre * -0.5) * (1.0 / math.sqrt(2.0 * math.pi))
            inner = dot(grad_low, big[12 + block], NT) * slope
            add_small(6 + block, inner)
            inner_low = low16(inner)
            wide_low[here, cols] = inner_low
            total = total + dot(inner_low, big[8 + block], NT)
        flow[here, :] = total
        return carry

    lax.fori_loop(0, steps, last, 0)
    turn(x_low, D)
    weight_grads([(3 + part, ds_ref[part]) for part in range(3)])
    for block in range(4):
        cols = slice(block * D, block * D + D)
        for start in range(0, TOKENS_HERE, STEP_ROWS):
            turned[:, start : start + STEP_ROWS] = act_low[start : start + STEP_ROWS, cols].T
        weight_grads([(12 + block, flow_low[...])])
    turn(mid_low, D)
    weight_grads([(8 + block, wide_low[:, block * D : block * D + D]) for block in range(4)])

    def middle(step, carry):
        here = step_slice(step)
        grad = norm_back(here, flow[here, :], hat1, scale1, 11)
        add_small(5, grad)
        flow[here, :] = grad
        grad_low = low16(grad)
        flow_low[here, :] = grad_low
        wide_low[here, 0:D] = low16(dot(grad_low, big[6], NT))
        return carry

    lax.fori_loop(0, steps, middle, 0)
    turn(ctx_low, D)
    weight_grads([(6, flow_low[...])])
    zero = jnp.zeros((), jnp.bfloat16)
    for seq, (off, length) in enumerate(SEQS):

        def attend_pair(pair, carry, seq=seq, off=off, length=length):
            rows = slice(off, off + length)
            cols = pl.ds(pl.multiple_of(pair * 128, 128), 128)
            query, key, value = (qkv_low[part, rows, cols] for part in range(3))
            out_grad = wide_low[rows, cols]
            lane = lax.broadcasted_iota(jnp.int32, (length, 128), 1)
            sums = [jnp.zeros((length, 128), jnp.float32)] * 3
            for side in range(2):
                mine = lane // HD == side
                key_one = jnp.where(mine, key, zero)
                soft = head_soft(query, key_one, lens_ref[seq], length)
                grad_one = jnp.where(mine, out_grad, zero)
                soft_grad = dot(grad_one, value, NT)
                inner = jnp.sum(soft_grad * soft, axis=-1, keepdims=True)
                score_grad = low16((soft_grad - inner) * soft * (1.0 / math.sqrt(HD)))
                query_one = jnp.where(mine, query, zero)
                sums[0] = sums[0] + dot(score_grad, key_one)
                sums[1] = sums[1] + dot(score_grad.T, query_one)
                sums[2] = sums[2] + dot(low16(soft).T, grad_one)
            for part in range(3):
                dqkv_low[part, rows, cols] = low16(sums[part])
            return carry

        lax.fori_loop(0, D // 128, attend_pair, 0)

    def first(step, carry):
        here = step_slice(step)
        grad = flow[here, :]
        for part in range(3):
            piece = dqkv_low[part, here, :]
            add_small(2 + part, piece.astype(jnp.float32))
            grad = grad + dot(piece, big[part], NT)
        grad = norm_back(here, grad, hat0, scale0, 0)
        flow[here, :] = grad
        row_low[here, :] = low16(grad)
        return carry

    lax.fori_loop(0, steps, first, 0)
    turn(hid_low, D)
    weight_grads([(part, dqkv_low[part]) for part in range(3)])
    near = flow[0:LA, :] + flow[LA : 2 * LA, :] + flow[2 * LA : 3 * LA, :] + flow[4 * LA : 5 * LA, :]
    grads[POS_AT, 0:LA, :] = low16(near)
    grads[POS_AT, LA:LB, :] = low16(flow[3 * LA : 4 * LA, :] + flow[5 * LA : 6 * LA, :])
    grads[POS_AT, LB:LC, :] = low16(flow[2 * LA + LB + LB :, :])
    places = slot_grads.shape[0]
    size = 512 if places % 512 == 0 else places

    def spread(block, carry):
        start = pl.multiple_of(block * size, size)
        spots = lax.broadcasted_iota(jnp.int32, (size, TOKENS_HERE), 0) + start
        chosen = low16(jnp.where(slot_ref[...] == spots, 1.0, 0.0))
        slot_grads[pl.ds(start, size), :] = low16(dot(chosen, row_low[...]))
        return carry

    lax.fori_loop(0, places // size, spread, 0)


def backward_layer(seq_lengths, slot, big, gains, final_grad, kept, places):
    vmem = pl.BlockSpec(memory_space=pltpu.VMEM)
    half = lambda *dims: jax.ShapeDtypeStruct(dims, jnp.bfloat16)
    tokens = TOKENS_HERE
    return pl.pallas_call(
        backward_kernel,
        in_specs=[pl.BlockSpec(memory_space=pltpu.SMEM)] + [vmem] * (4 + len(kept)),
        out_specs=[vmem] * 4,
        out_shape=[
            half(16, D, D),
            jax.ShapeDtypeStruct((GAIN_ROWS, D), jnp.float32),
            half(places, D),
            half(tokens, D),
        ],
        scratch_shapes=[
            pltpu.VMEM((tokens, D), jnp.float32),
            pltpu.VMEM((tokens, D), jnp.bfloat16),
            pltpu.VMEM((tokens, FF), jnp.bfloat16),
            pltpu.VMEM((D, tokens), jnp.bfloat16),
            pltpu.VMEM((3, tokens, D), jnp.bfloat16),
            pltpu.VMEM((tokens, FF), jnp.bfloat16),
        ],
        compiler_params=pltpu.CompilerParams(vmem_limit_bytes=60 * 2**20),
    )(seq_lengths, slot[None, :], big, gains, final_grad, *kept)


def teacher_kernel(hidden, weight, out):
    out[...] = low16(dot(hidden[...], weight[...]))


def project_teacher(hidden, weight):
    tokens = hidden.shape[0]
    owners, parts, depth, width = weight.shape
    return pl.pallas_call(
        teacher_kernel,
        grid=(parts, owners),
        in_specs=[
            pl.BlockSpec((tokens, depth), lambda part, owner: (0, 0)),
            pl.BlockSpec((None, None, depth, width), lambda part, owner: (owner, part, 0, 0)),
        ],
        out_specs=pl.BlockSpec((None, tokens, width), lambda part, owner: (part, 0, owner)),
        out_shape=jax.ShapeDtypeStruct((parts, tokens, owners * width), jnp.bfloat16),
        compiler_params=pltpu.CompilerParams(vmem_limit_bytes=32 * 2**20),
    )(hidden, weight)


MESH_IDS = pl.DeviceIdType.MESH


def barrier_all(rank, count, place):
    barrier = pltpu.get_barrier_semaphore()

    def greet(step, carry):
        pl.semaphore_signal(
            barrier, inc=1, device_id=place(lax.rem(rank + step, count)), device_id_type=MESH_IDS
        )
        return carry

    lax.fori_loop(1, count, greet, 0)
    pl.semaphore_wait(barrier, count - 1)


class Spot:
    def __init__(self, n_dp, n_head):
        self.n_dp, self.n_head = n_dp, n_head
        self.count = n_dp * n_head
        self.nz, self.nx = n_dp // 2, n_head // 2
        dp, head = lax.axis_index("dp"), lax.axis_index("head")
        self.rank = dp * n_head + head
        self.z, self.y = dp // 2, lax.rem(dp, 2)
        self.x, self.c = head // 2, lax.rem(head, 2)

    def place(self, rank):
        return (rank // self.n_head, lax.rem(rank, self.n_head))

    def device(self, z, y, x, c):
        return (z * 2 + y, x * 2 + c)


def remote(source, target, send_sem, recv_sem, device):
    return pltpu.make_async_remote_copy(
        src_ref=source,
        dst_ref=target,
        send_sem=send_sem,
        recv_sem=recv_sem,
        device_id=device,
        device_id_type=MESH_IDS,
    )


def start_all_to_all(spot, source, target, send_sems, recv_sems, local_sem):
    pltpu.make_async_copy(source.at[spot.rank], target.at[spot.rank], local_sem).start()

    def send(step, carry):
        peer = lax.rem(spot.rank + step, spot.count)
        remote(
            source.at[peer], target.at[spot.rank], send_sems.at[step], recv_sems.at[step], spot.place(peer)
        ).start()
        return carry

    lax.fori_loop(1, spot.count, send, 0)


def finish_all_to_all(spot, source, target, send_sems, recv_sems, local_sem):
    def take(step, carry):
        origin = lax.rem(spot.rank + spot.count - step, spot.count)
        copy = remote(
            source.at[origin], target.at[origin], send_sems.at[step], recv_sems.at[step], spot.place(origin)
        )
        copy.wait_recv()
        copy.wait_send()
        return carry

    lax.fori_loop(1, spot.count, take, 0)
    pltpu.make_async_copy(source.at[spot.rank], target.at[spot.rank], local_sem).wait()


def is_direct(shape):
    return shape[1] % 16 == 0 and shape[2] % 128 == 0


def piece_of(whole, shape, dp, head):
    if not is_direct(shape):
        return whole.at[dp, head]
    rows = pl.ds(pl.multiple_of(dp * shape[1], shape[1]), shape[1])
    return whole.at[:, rows, pl.ds(pl.multiple_of(head * shape[2], shape[2]), shape[2])]


def whole_shape(sizes, shape):
    if not is_direct(shape):
        return sizes + shape
    return (shape[0], sizes[0] * shape[1], sizes[1] * shape[2])


def answer(heard, table, rows, at_once):
    count, room = rows.shape[:2]
    spare = -count % 128
    asked = heard[:, 0, :]
    if spare:
        asked = jnp.concatenate([asked, jnp.full((spare, 128), -1.0, jnp.float32)], axis=0)
    turned = asked.T
    lane = lax.broadcasted_iota(jnp.int32, (room, count + spare), 1)
    spots = lax.broadcasted_iota(jnp.int32, (at_once * room, table.shape[0]), 1)

    def some(step, carry):
        columns = []
        for place in range(at_once):
            mine = lane == step * at_once + place
            columns.append(jnp.sum(jnp.where(mine, turned[0:room, :], 0.0), axis=1, keepdims=True))
        wanted = jnp.concatenate(columns, axis=0).astype(jnp.int32)
        chosen = low16(jnp.where(wanted == spots, 1.0, 0.0))
        found = low16(dot(chosen, table[...]))
        for place in range(at_once):
            rows[step * at_once + place] = found[place * room : place * room + room]
        return carry

    lax.fori_loop(0, count // at_once, some, 0)


def gather_kernel(
    sizes,
    messages,
    table,
    shard,
    heard,
    rows_out,
    full,
    rows,
    message_send,
    message_recv,
    row_send,
    row_recv,
    piece_send,
    piece_recv,
    local_sems,
):
    spot = Spot(*sizes)
    z, y, x, c, nz, nx = spot.z, spot.y, spot.x, spot.c, spot.nz, spot.nx
    barrier_all(spot.rank, spot.count, spot.place)
    own_copy = pltpu.make_async_copy(
        shard, piece_of(full, shard.shape, z * 2 + y, x * 2 + c), local_sems.at[1]
    )
    own_copy.start()

    sends = []

    def send_piece(source, piece, device):
        copy = remote(
            source,
            piece_of(full, shard.shape, piece[0] * 2 + piece[1], piece[2] * 2 + piece[3]),
            piece_send.at[len(sends)],
            piece_recv.at[piece[0] * 2 + piece[1], piece[2] * 2 + piece[3]],
            device,
        )
        copy.start()
        sends.append(copy)

    def wait_piece(piece):
        here = piece_of(full, shard.shape, piece[0] * 2 + piece[1], piece[2] * 2 + piece[3])
        remote(
            here,
            here,
            piece_send.at[0],
            piece_recv.at[piece[0] * 2 + piece[1], piece[2] * 2 + piece[3]],
            spot.device(z, y, x, 1 - c),
        ).wait_recv()
        return here

    start_all_to_all(spot, messages, heard, message_send, message_recv, local_sems.at[2])
    own = (z, y, x, c)
    others_x = [lax.rem(x + step, nx) for step in range(1, nx)]
    for step in range(1, nz):
        send_piece(shard, own, spot.device(lax.rem(z + step, nz), y, x, c))
    for other in others_x:
        send_piece(shard, own, spot.device(z, y, other, c))
    send_piece(shard, own, spot.device(z, 1 - y, x, c))
    send_piece(shard, own, spot.device(z, y, x, 1 - c))
    finish_all_to_all(spot, messages, heard, message_send, message_recv, local_sems.at[2])
    answer(heard, table, rows, 8)
    start_all_to_all(spot, rows, rows_out, row_send, row_recv, local_sems.at[0])
    for step in range(1, nz):
        piece = (lax.rem(z + nz - step, nz), y, x, c)
        here = wait_piece(piece)
        for other in others_x:
            send_piece(here, piece, spot.device(z, y, other, c))
        send_piece(here, piece, spot.device(z, 1 - y, x, c))
        send_piece(here, piece, spot.device(z, y, x, 1 - c))
    for step in range(nz):
        for other in others_x:
            piece = (lax.rem(z + nz - step, nz), y, other, c)
            here = wait_piece(piece)
            send_piece(here, piece, spot.device(z, 1 - y, x, c))
            send_piece(here, piece, spot.device(z, y, x, 1 - c))

    for step in range(nz):
        for column in [x] + others_x:
            piece = (lax.rem(z + nz - step, nz), 1 - y, column, c)
            here = wait_piece(piece)
            send_piece(here, piece, spot.device(z, y, x, 1 - c))
    for step in range(nz):
        for side in (y, 1 - y):
            for column in [x] + others_x:
                wait_piece((lax.rem(z + nz - step, nz), side, column, 1 - c))
    for copy in sends:
        copy.wait_send()
    finish_all_to_all(spot, rows, rows_out, row_send, row_recv, local_sems.at[0])
    own_copy.wait()


def gather_weights(sizes, messages, table, shard, room):
    n_dp, n_head = sizes
    count = n_dp * n_head
    nz, nx = n_dp // 2, n_head // 2
    sends = (nz - 1) + (nx - 1) + 2 + (nz - 1) * (nx + 1) + nz * (nx - 1) * 2 + nz * nx
    anywhere = pl.BlockSpec(memory_space=pl.ANY)
    vmem = pl.BlockSpec(memory_space=pltpu.VMEM)
    dma = pltpu.SemaphoreType.DMA
    rows_shape = (count, room, table.shape[1])
    return pl.pallas_call(
        functools.partial(gather_kernel, sizes),
        in_specs=[vmem, vmem, anywhere],
        out_specs=[vmem, anywhere, anywhere],
        out_shape=[
            jax.ShapeDtypeStruct(messages.shape, messages.dtype),
            jax.ShapeDtypeStruct(rows_shape, table.dtype),
            jax.ShapeDtypeStruct(whole_shape(sizes, shard.shape), shard.dtype),
        ],
        scratch_shapes=[
            pltpu.VMEM(rows_shape, table.dtype),
            dma((count,)),
            dma((count,)),
            dma((count,)),
            dma((count,)),
            dma((sends,)),
            dma((n_dp, n_head)),
            dma((3,)),
        ],
        compiler_params=pltpu.CompilerParams(
            collective_id=2, has_side_effects=True, vmem_limit_bytes=40 * 2**20
        ),
    )(messages, table, shard)


def table_rows_at_once(rows):
    sizes = [size for size in range(8, 265, 8) if rows % size == 0]
    return max(sizes) if sizes and rows > 264 else rows


def place_rows(rows, wanted, table_grad):
    count, room, width = rows.shape
    at_once = table_rows_at_once(table_grad.shape[0])
    arrived = rows[...].reshape(count * room, width)

    def some(step, squares):
        start = step * at_once
        if at_once % 8 == 0:
            start = pl.multiple_of(start, 8)
        spots = lax.broadcasted_iota(jnp.int32, (at_once, count * room), 0) + start
        chosen = low16(jnp.where(wanted[...] == spots, 1.0, 0.0))
        value = dot(chosen, arrived)
        table_grad[pl.ds(start, at_once), :] = value
        return squares + jnp.sum(value * value, axis=0, keepdims=True)

    zero = jnp.zeros((1, width), jnp.float32)
    return lax.fori_loop(0, table_grad.shape[0] // at_once, some, zero)


def reduce_kernel(
    sizes,
    rows,
    pieces,
    wanted,
    loss,
    rows_out,
    total,
    table_grad,
    small,
    everyone,
    mine,
    sum_send,
    sum_recv,
    core_in,
    y_in,
    x_in,
    z_in,
    row_send,
    row_recv,
    core_send,
    core_recv,
    y_send,
    y_recv,
    x_send,
    x_recv,
    z_send,
    z_recv,
    local_sem,
):
    spot = Spot(*sizes)
    z, y, x, c, nz, nx = spot.z, spot.y, spot.x, spot.c, spot.nz, spot.nx
    shape = total.shape
    barrier_all(spot.rank, spot.count, spot.place)
    sibling = spot.device(z, y, x, 1 - c)
    opposite = spot.device(z, 1 - y, x, c)

    def core_copy(deep, side, column):
        return remote(
            piece_of(pieces, shape, deep * 2 + side, column * 2 + 1 - c),
            core_in.at[deep, side, column],
            core_send.at[deep, side, column],
            core_recv.at[deep, side, column],
            sibling,
        )

    def y_copy(deep, column):
        return remote(
            core_in.at[deep, 1 - y, column],
            y_in.at[deep, column],
            y_send.at[deep, column],
            y_recv.at[deep, column],
            opposite,
        )

    def x_copy(step, deep):
        column = lax.rem(x + step, nx)
        return remote(
            y_in.at[deep, column],
            x_in.at[step - 1, deep],
            x_send.at[step - 1, deep],
            x_recv.at[step - 1, deep],
            spot.device(z, y, column, c),
        )

    def z_copy(step):
        deep = lax.rem(z + step, nz)
        return remote(
            y_in.at[deep, x],
            z_in.at[step - 1],
            z_send.at[step - 1],
            z_recv.at[step - 1],
            spot.device(deep, y, x, c),
        )

    def add_into(target, sources):
        def some(block, carry):
            value = target[block].astype(jnp.float32)
            for source in sources:
                value = value + source[block].astype(jnp.float32)
            target[block] = value.astype(target.dtype)
            return carry

        lax.fori_loop(0, shape[0], some, 0)

    depth_order = lambda step: lax.rem(z + 1 + step, nz)
    columns = [lax.rem(x + step, nx) for step in range(1, nx)] + [x]
    for side in (1 - y, y):
        for column in columns:

            def send_core(step, carry, side=side, column=column):
                core_copy(depth_order(step), side, column).start()
                return carry

            lax.fori_loop(0, nz, send_core, 0)
    start_all_to_all(spot, rows, rows_out, row_send, row_recv, local_sem)
    for side in (1 - y, y):
        for column in columns:

            def take_core(step, carry, side=side, column=column):
                deep = depth_order(step)
                core_copy(deep, side, column).wait_recv()
                own = piece_of(pieces, shape, deep * 2 + side, column * 2 + c)
                add_into(core_in.at[deep, side, column], [own])
                return carry

            def send_y(step, carry, column=column):
                take_core(step, carry, 1 - y, column)
                y_copy(depth_order(step), column).start()
                return carry

            lax.fori_loop(0, nz, send_y if side is not y else take_core, 0)
    for step_x, column in enumerate(columns):

        def take_y(step, carry, step_x=step_x, column=column):
            deep = depth_order(step)
            y_copy(deep, column).wait_recv()
            add_into(y_in.at[deep, column], [core_in.at[deep, y, column]])
            if step_x + 1 < nx:
                x_copy(step_x + 1, deep).start()
            return carry

        lax.fori_loop(0, nz, take_y, 0)
    for step in range(nz):
        deep = depth_order(step)
        for step_x in range(1, nx):
            x_copy(step_x, deep).wait_recv()
        add_into(y_in.at[deep, x], [x_in.at[step_x, deep] for step_x in range(nx - 1)])
        if step + 1 < nz:
            z_copy(step + 1).start()
    finish_all_to_all(spot, rows, rows_out, row_send, row_recv, local_sem)
    squares = place_rows(rows_out, wanted, table_grad)
    room = rows_out.shape[1]
    small[...] = jnp.sum(rows_out[:, room - 16 : room, :].astype(jnp.float32), axis=0)
    last_small = small[15:16, :]
    for step in range(1, nz):
        z_copy(step).wait_recv()

    def finish(block, carry):
        value = y_in[z, x, block].astype(jnp.float32)
        for step in range(nz - 1):
            value = value + z_in[step, block].astype(jnp.float32)
        total[block] = value
        return carry + jnp.sum(value * value, axis=0, keepdims=True)

    others = lax.fori_loop(0, shape[0], finish, jnp.zeros((1, shape[2]), jnp.float32))
    lane = lax.broadcasted_iota(jnp.int32, (8, 128), 1)
    sums = jnp.where(lane == 0, jnp.sum(squares), 0.0)
    sums = jnp.where(lane == 1, jnp.sum(others) + jnp.sum(last_small * last_small), sums)
    mine[...] = jnp.where(lane == 2, jnp.sum(loss[...]), sums)
    everyone[spot.rank] = mine[...]

    def tell(step, carry):
        peer = lax.rem(spot.rank + step, spot.count)
        remote(
            mine, everyone.at[spot.rank], sum_send.at[step], sum_recv.at[step], spot.place(peer)
        ).start()
        return carry

    lax.fori_loop(1, spot.count, tell, 0)
    for side in (1 - y, y):
        for column in columns:

            def end_core(step, carry, side=side, column=column):
                core_copy(depth_order(step), side, column).wait_send()
                return carry

            lax.fori_loop(0, nz, end_core, 0)
    for column in columns:

        def end_y(step, carry, column=column):
            y_copy(depth_order(step), column).wait_send()
            return carry

        lax.fori_loop(0, nz, end_y, 0)
    for step_x in range(1, nx):

        def end_x(step, carry, step_x=step_x):
            x_copy(step_x, depth_order(step)).wait_send()
            return carry

        lax.fori_loop(0, nz, end_x, 0)
    for step in range(1, nz):
        z_copy(step).wait_send()

    def hear(step, carry):
        origin = lax.rem(spot.rank + spot.count - step, spot.count)
        copy = remote(
            mine, everyone.at[origin], sum_send.at[step], sum_recv.at[step], spot.place(origin)
        )
        copy.wait_recv()
        copy.wait_send()
        return carry

    lax.fori_loop(1, spot.count, hear, 0)


def reduce_grads(sizes, rows, pieces, one, wanted, loss, table_shape):
    n_dp, n_head = sizes
    count = n_dp * n_head
    nz, nx = n_dp // 2, n_head // 2
    dma = pltpu.SemaphoreType.DMA
    return pl.pallas_call(
        functools.partial(reduce_kernel, sizes),
        in_specs=[pl.BlockSpec(memory_space=pl.ANY)] + [pl.BlockSpec(memory_space=pltpu.VMEM)] * 3,
        out_specs=[pl.BlockSpec(memory_space=pltpu.VMEM)] * 5,
        out_shape=[
            jax.ShapeDtypeStruct(rows.shape, rows.dtype),
            jax.ShapeDtypeStruct(one, jnp.float32),
            jax.ShapeDtypeStruct(table_shape, jnp.float32),
            jax.ShapeDtypeStruct((16, rows.shape[2]), jnp.float32),
            jax.ShapeDtypeStruct((count, 8, 128), jnp.float32),
        ],
        scratch_shapes=[
            pltpu.VMEM((8, 128), jnp.float32),
            dma((count,)),
            dma((count,)),
            pltpu.VMEM((nz, 2, nx) + one, pieces.dtype),
            pltpu.VMEM((nz, nx) + one, pieces.dtype),
            pltpu.VMEM((nx - 1, nz) + one, pieces.dtype),
            pltpu.VMEM((nz - 1,) + one, pieces.dtype),
            dma((count,)),
            dma((count,)),
            dma((nz, 2, nx)),
            dma((nz, 2, nx)),
            dma((nz, nx)),
            dma((nz, nx)),
            dma((nx - 1, nz)),
            dma((nx - 1, nz)),
            dma((nz - 1,)),
            dma((nz - 1,)),
            dma,
        ],
        compiler_params=pltpu.CompilerParams(
            collective_id=3, has_side_effects=True, vmem_limit_bytes=40 * 2**20
        ),
    )(rows, pieces, wanted, loss)


def stack_blocks(qkv_weight, proj_weight, up_weight, down_weight, position_table):
    depth, width = position_table.shape
    parts = by_part(qkv_weight, qkv_weight.shape[2] // (3 * HD))
    parts = parts.reshape(LAYERS, depth, 3, width).transpose(0, 2, 1, 3).reshape(6, depth, width)
    up_blocks = up_weight.reshape(depth, width // depth, 4, depth).transpose(2, 0, 1, 3)
    return jnp.concatenate(
        [
            parts,
            proj_weight[None],
            position_table[None],
            up_blocks.reshape(4, depth, width),
            down_weight.reshape(4, depth, width),
        ],
        axis=0,
    )


def stack_kernel(qkv_weight, proj_weight, up_weight, down_weight, position_table, shard):
    depth, width = position_table.shape
    heads = width // HD
    for layer in range(LAYERS):
        value = low16(qkv_weight[layer])
        for part in range(3):
            pieces = [
                value[:, (head * 3 + part) * HD : (head * 3 + part) * HD + HD] for head in range(heads)
            ]
            shard[layer * 3 + part] = jnp.concatenate(pieces, axis=1)
    shard[6] = low16(proj_weight[...])
    shard[7] = low16(position_table[...])
    value = low16(up_weight[...])
    for block in range(4):
        starts = [(turn * 4 + block) * depth for turn in range(width // depth)]
        pieces = [value[:, start : start + depth] for start in starts]
        shard[8 + block] = jnp.concatenate(pieces, axis=1)
        shard[12 + block] = low16(down_weight[block * depth : block * depth + depth, :])


def stack_shard(qkv_weight, proj_weight, up_weight, down_weight, position_table):
    depth, width = position_table.shape
    if not is_direct((16, depth, width)):
        blocks = stack_blocks(qkv_weight, proj_weight, up_weight, down_weight, position_table)
        return blocks.astype(jnp.bfloat16)
    vmem = pl.BlockSpec(memory_space=pltpu.VMEM)
    return pl.pallas_call(
        stack_kernel,
        in_specs=[vmem] * 5,
        out_specs=vmem,
        out_shape=jax.ShapeDtypeStruct((16, depth, width), jnp.bfloat16),
    )(qkv_weight, proj_weight, up_weight, down_weight, position_table)


def split_blocks(total):
    depth, width = total.shape[1:]
    parts = total[:6].reshape(LAYERS, 3, depth, width).transpose(0, 2, 1, 3)
    qkv_grad = by_head(parts.reshape(LAYERS, depth, 3 * width), width // HD)
    up_grad = total[8:12].reshape(4, depth, width // depth, depth).transpose(1, 2, 0, 3)
    return (
        total[7],
        qkv_grad,
        total[6:7],
        up_grad.reshape(1, depth, 4 * width),
        total[12:16].reshape(1, 4 * depth, width),
    )


def arrange_gains(gains, n_dp):
    offset = 2 * D
    qkv_bias = by_part(gains[offset : offset + 3 * D], HEADS)
    up_bias = gains[offset + 4 * D : offset + 4 * D + FF].reshape(n_dp, 4, D // n_dp)
    return jnp.concatenate(
        [
            gains[:offset],
            qkv_bias,
            gains[offset + 3 * D : offset + 4 * D],
            up_bias.transpose(1, 0, 2).reshape(-1),
            gains[offset + 4 * D + FF : offset + 9 * D + FF],
            by_part(gains[offset + 9 * D + FF :], HEADS),
        ]
    ).reshape(GAIN_ROWS, D)


def restore_gains(rows, n_dp):
    up_bias = rows[6:10].reshape(4, n_dp, D // n_dp).transpose(1, 0, 2)
    return jnp.concatenate(
        [
            rows[0:2].reshape(-1),
            by_head(rows[2:5].reshape(-1), HEADS),
            rows[5],
            up_bias.reshape(-1),
            rows[10:15].reshape(-1),
            by_head(rows[15:18].reshape(-1), HEADS),
        ]
    )


def gather_teacher(weight):
    width = weight.shape[1]
    order = by_part(jnp.arange(width, dtype=jnp.int32), width // (3 * THD))
    turned = dot(weight, one_hot(order, width).T).astype(jnp.bfloat16)
    return lax.all_gather(turned.reshape(TD, 3, -1).transpose(1, 0, 2), "head", axis=0)


def request_slots(token_ids, shard_rows, count, room, usable):
    here = token_ids.shape[0]
    index = jnp.arange(here, dtype=jnp.int32)
    owner = token_ids // shard_rows
    equal = token_ids[:, None] == token_ids[None, :]
    first = jnp.min(jnp.where(equal, index[:, None], here), axis=0)
    is_first = first == index
    earlier = (owner[:, None] == owner[None, :]) & is_first[:, None] & (index[:, None] < index[None, :])
    order = jnp.sum(earlier.astype(jnp.int32), axis=0)
    overflow = jnp.any(is_first & (order >= usable))
    slot_first = owner * room + order
    chosen = first[None, :] == index[:, None]
    slot = jnp.sum(jnp.where(chosen, slot_first[:, None], 0), axis=0)
    spots = jnp.arange(count * room, dtype=jnp.int32)
    asked = is_first[:, None] & (slot_first[:, None] == spots[None, :]) & (order < usable)[:, None]
    request = jnp.sum(jnp.where(asked, (token_ids % shard_rows)[:, None] + 1, 0), axis=0) - 1
    return slot, request, overflow


def one_hot(index, size):
    return (index[:, None] == jnp.arange(size, dtype=jnp.int32)[None, :]).astype(jnp.bfloat16)


def adam_update(master, first, second, grad_clip, rate):
    first_new = B_ONE * first + (1.0 - B_ONE) * grad_clip
    second_new = B_TWO * second + (1.0 - B_TWO) * grad_clip * grad_clip
    ascent = (
        first_new / (1.0 - B_ONE**STEP) / (jnp.sqrt(second_new / (1.0 - B_TWO**STEP)) + EPSILON)
    )
    return (master - rate * (ascent + DECAY * master), first_new, second_new)


def shards(
    token_ids,
    seq_lengths,
    teacher_hidden,
    teacher_weight,
    token_table,
    token_first,
    token_second,
    position_table,
    position_first,
    position_second,
    qkv_weight,
    qkv_first,
    qkv_second,
    proj_weight,
    proj_first,
    proj_second,
    up_weight,
    up_first,
    up_second,
    down_weight,
    down_first,
    down_second,
    gains_biases,
    gains_first,
    gains_second,
):
    n_dp, n_head = sizes = (lax.axis_size("dp"), lax.axis_size("head"))
    count = n_dp * n_head
    here, shard_rows = token_ids.shape[0], token_table.shape[0]
    room = 16 * -(-3 * here // (2 * count * 16))
    slot, request, overflow = request_slots(token_ids, shard_rows, count, room, room - 1)
    notes = jnp.stack([overflow.astype(jnp.float32), jnp.sum(seq_lengths).astype(jnp.float32)])
    small_size = gains_biases.shape[0]
    small_rows = -(-small_size // 128)
    small_mine = gains_biases.astype(jnp.bfloat16).astype(jnp.float32)
    small_mine = jnp.pad(small_mine, (0, small_rows * 128 - small_size)).reshape(1, small_rows, 128)
    message = jnp.concatenate(
        [
            jnp.pad(
                request.astype(jnp.float32).reshape(count, 1, room), ((0, 0), (0, 0), (0, 128 - room))
            ),
            jnp.broadcast_to(jnp.pad(notes, (0, 126)), (count, 1, 128)),
            jnp.broadcast_to(small_mine, (count, small_rows, 128)),
            jnp.zeros((count, 6 - small_rows, 128), jnp.float32),
        ],
        axis=1,
    )
    shard = stack_shard(qkv_weight, proj_weight[0], up_weight[0], down_weight[0], position_table)
    table_low = token_table.astype(jnp.bfloat16)
    heard, rows_in, big = gather_weights(sizes, message, table_low, shard, room)
    too_many = jnp.any(heard[:, 1, 0] > 0.0)
    valid_total = jnp.sum(heard[:, 1, 1])
    wanted = heard[:, 0, :room].reshape(1, -1).astype(jnp.int32)
    gains = arrange_gains(
        heard[:, 2 : 2 + small_rows].reshape(count, -1)[:, :small_size].reshape(-1), n_dp
    )
    teach_full = gather_teacher(teacher_weight)
    if not is_direct(shard.shape):
        big = big.transpose(2, 0, 3, 1, 4).reshape(16, D, D)

    def owned_rows():
        group_ids = lax.all_gather(token_ids, "head", axis=0, tiled=True)
        block_ids = group_ids // shard_rows
        owned = block_ids % n_head == lax.axis_index("head")
        local = jnp.where(owned, block_ids // n_head * shard_rows + group_ids % shard_rows, 0)
        return owned, local

    def rows_by_owner():
        owned, local = owned_rows()
        rows_all = lax.all_gather(table_low, "dp", axis=0, tiled=True)
        picked = jnp.where(owned[:, None], rows_all[local], jnp.zeros((), jnp.bfloat16))
        rows_here = lax.psum_scatter(picked, "head", scatter_dimension=0, tiled=True)
        return (
            jnp.pad(rows_here, ((0, count * room - here), (0, 0))),
            jnp.arange(here, dtype=jnp.int32),
        )

    rows_used, slot_used = lax.cond(
        too_many, rows_by_owner, lambda: (rows_in.reshape(count * room, D), slot)
    )
    teacher_qkv = project_teacher(teacher_hidden, teach_full)
    final_qkv, *kept = forward_layer(seq_lengths, rows_used, slot_used, big, gains)
    final_grad, loss_part = relation(seq_lengths, final_qkv, teacher_qkv)
    pieces, gain_grads, slot_grads, row_low = backward_layer(
        seq_lengths, slot_used, big, gains, final_grad, kept, count * room
    )
    if not is_direct(shard.shape):
        pieces = pieces.reshape(16, n_dp, shard.shape[1], n_head, shard.shape[2])
        pieces = pieces.transpose(1, 3, 0, 2, 4)
    gain_rows = jnp.pad(
        restore_gains(gain_grads, n_dp).reshape(count, 1, small_size), ((0, 0), (0, 0), (0, D - small_size))
    )
    slot_grads = slot_grads.reshape(count, room, D).at[:, room - 1 :].set(gain_rows.astype(jnp.bfloat16))
    rows_arrived, total, fast_grad, small_sum, everyone = reduce_grads(
        sizes, slot_grads, pieces, shard.shape, wanted, loss_part, token_table.shape
    )
    small_grad = small_sum[15, :small_size]

    def table_by_owner():
        owned, local = owned_rows()
        spread = lax.all_gather(row_low, "head", axis=0, tiled=True)
        table_grad = jax.ops.segment_sum(
            spread.astype(jnp.float32),
            jnp.where(owned, local, n_dp * shard_rows),
            num_segments=n_dp * shard_rows + 1,
        )[:-1]
        table_grad = lax.psum_scatter(
            table_grad.astype(jnp.bfloat16), "dp", scatter_dimension=0, tiled=True
        ).astype(jnp.float32)
        return table_grad, lax.psum(jnp.sum(table_grad * table_grad), ("dp", "head"))

    table_grad, table_squares = lax.cond(
        too_many, table_by_owner, lambda: (fast_grad, jnp.sum(everyone[:, 0, 0]))
    )
    shard_grads = (table_grad,) + split_blocks(total) + (small_grad,)
    square_total = table_squares + jnp.sum(everyone[:, 0, 1])
    loss_total = jnp.sum(everyone[:, 0, 2]) * (LN2 / (3 * REL))
    grad_norm = jnp.sqrt(square_total) / valid_total
    clip_factor = THRESHOLD / jnp.maximum(grad_norm, THRESHOLD)
    factor = clip_factor / valid_total
    token_new = adam_update(
        token_table, token_first, token_second, shard_grads[0] * factor, RATE_TABLE
    )
    position_new = adam_update(
        position_table, position_first, position_second, shard_grads[1] * factor, RATE_TABLE
    )
    qkv_new = adam_update(qkv_weight, qkv_first, qkv_second, shard_grads[2] * factor, RATE_MATRIX)
    proj_new = adam_update(
        proj_weight, proj_first, proj_second, shard_grads[3] * factor, RATE_MATRIX
    )
    up_new = adam_update(up_weight, up_first, up_second, shard_grads[4] * factor, RATE_MATRIX)
    down_new = adam_update(
        down_weight, down_first, down_second, shard_grads[5] * factor, RATE_MATRIX
    )
    gains_new = adam_update(
        gains_biases, gains_first, gains_second, shard_grads[6] * factor, RATE_SMALL
    )
    loss_parts = jnp.stack([loss_total, valid_total])
    return (
        token_new[0],
        token_new[1],
        token_new[2],
        position_new[0],
        position_new[1],
        position_new[2],
        qkv_new[0],
        qkv_new[1],
        qkv_new[2],
        proj_new[0],
        proj_new[1],
        proj_new[2],
        up_new[0],
        up_new[1],
        up_new[2],
        down_new[0],
        down_new[1],
        down_new[2],
        gains_new[0],
        gains_new[1],
        gains_new[2],
        grad_norm,
        loss_parts,
    )


def solution(mesh):
    placed = (
        P(("dp", "head")),
        P(("dp", "head")),
        P(("dp", "head"), None),
        P(None, "head"),
        P(("dp", "head"), None),
        P(("dp", "head"), None),
        P(("dp", "head"), None),
        P("dp", "head"),
        P("dp", "head"),
        P("dp", "head"),
        P(None, "dp", "head"),
        P(None, "dp", "head"),
        P(None, "dp", "head"),
        P(None, "dp", "head"),
        P(None, "dp", "head"),
        P(None, "dp", "head"),
        P(None, "dp", "head"),
        P(None, "dp", "head"),
        P(None, "dp", "head"),
        P(None, "dp", "head"),
        P(None, "dp", "head"),
        P(None, "dp", "head"),
        P(("dp", "head")),
        P(("dp", "head")),
        P(("dp", "head")),
    )
    return jax.shard_map(
        shards,
        mesh=mesh,
        in_specs=placed,
        out_specs=(
            P(("dp", "head"), None),
            P(("dp", "head"), None),
            P(("dp", "head"), None),
            P("dp", "head"),
            P("dp", "head"),
            P("dp", "head"),
            P(None, "dp", "head"),
            P(None, "dp", "head"),
            P(None, "dp", "head"),
            P(None, "dp", "head"),
            P(None, "dp", "head"),
            P(None, "dp", "head"),
            P(None, "dp", "head"),
            P(None, "dp", "head"),
            P(None, "dp", "head"),
            P(None, "dp", "head"),
            P(None, "dp", "head"),
            P(None, "dp", "head"),
            P(("dp", "head")),
            P(("dp", "head")),
            P(("dp", "head")),
            P(),
            P(),
        ),
        check_vma=False,
    )
```

```python
import functools
import math

import jax
import jax.numpy as jnp
from jax import lax
from jax.experimental import pallas as pl
from jax.experimental.pallas import tpu as pltpu
from jax.sharding import PartitionSpec as P

D = 512
HEADS = 8
HD = 64
FF = 2048
TD = 1024
THEADS = 16
THD = 64
REL = 64
LAYERS = 2
LA = 128
LB = 256
LC = 512
M = 1
STEP = 10


B_ONE = 0.9
B_TWO = 0.999
EPSILON = 1e-10
DECAY = 0.01
THRESHOLD = 0.0003
RATE_TABLE = 1.0
RATE_MATRIX = 0.1
RATE_SMALL = 2.0


def dot(left, right, dims=(((1,), (0,)), ((), ()))):
    return lax.dot_general(left, right, dims, preferred_element_type=jnp.float32)


NT = (((1,), (1,)), ((), ()))


LOG2E = 1.4426950408889634
LN2 = 0.6931471805599453
GROUPS = 4
S_WIDE = D // GROUPS
T_WIDE = TD // GROUPS
S_DIM = D // REL
T_DIM = TD // REL
FAST_LIMIT = 60.0
SEQS = ((0, LA), (LA, LA), (2 * LA, LB), (2 * LA + LB, LC))
TOKENS_HERE = 2 * LA + LB + LC
BLOCKS = ((2 * LA + LB, LC, (3,)), (2 * LA, LB, (2,)), (0, 2 * LA, (0, 1)))
AT_ONCE = 4
KEY_ROWS = 128


def relation_kernel(
    lens_ref,
    s_ref,
    t_ref,
    ds_ref,
    loss_ref,
    s_rows,
    t_rows,
    d_rows,
    exp_c,
    exp_b,
    exp_a,
    s_keep,
    t_keep,
):
    @pl.when((pl.program_id(0) == 0) & (pl.program_id(1) == 0))
    def _():
        loss_ref[...] = jnp.zeros_like(loss_ref)
        exp_a[...] = jnp.zeros_like(exp_a)

    s_scale = LOG2E / math.sqrt(S_DIM)
    t_scale = LOG2E / math.sqrt(T_DIM)
    zero = jnp.zeros((), jnp.bfloat16)
    half_heads = 128 // T_DIM
    exps = (exp_c, exp_b, exp_a)

    def valid_rows(block):
        off, length, seqs = BLOCKS[block]
        each = length // len(seqs)
        row = lax.broadcasted_iota(jnp.int32, (length, 128), 0)
        valid = row < 0
        for place, seq in enumerate(seqs):
            start = place * each
            valid = valid | (row >= start) & (row < start + lens_ref[seq])
        return valid

    def prepare(block):
        off, length, seqs = BLOCKS[block]
        each = length // len(seqs)
        lane = lax.broadcasted_iota(jnp.int32, (8, length), 1)
        lane_valid, padded = lane < 0, jnp.zeros((8, length), jnp.float32)
        for place, seq in enumerate(seqs):
            start = place * each
            lane_valid = lane_valid | (lane >= start) & (lane < start + lens_ref[seq])
            padded = jnp.where(lane >= start, (each - lens_ref[seq]).astype(jnp.float32), padded)
        row_valid = valid_rows(block)
        rows = slice(off, off + length)
        s_block = jnp.where(row_valid, s_ref[rows, :], zero).astype(jnp.float32)
        s_keep[rows, :] = (s_block * math.sqrt(s_scale)).astype(jnp.bfloat16)
        s_rows[:, rows] = s_block.T
        for half in range(2):
            cols = slice(half * 128, half * 128 + 128)
            t_block = jnp.where(row_valid, t_ref[rows, cols], zero).astype(jnp.float32)
            t_keep[half, rows, :] = (t_block * math.sqrt(t_scale)).astype(jnp.bfloat16)
            t_rows[cols, rows] = t_block.T
        s_here = s_rows[:, rows]
        t_here = t_rows[:, rows]
        s_square = jnp.sum((s_here * s_here).reshape(16, S_DIM, length), axis=1)
        t_square = jnp.sum((t_here * t_here).reshape(16, T_DIM, length), axis=1)
        bound = jnp.maximum(jnp.max(s_square) * s_scale, jnp.max(t_square) * t_scale)
        return bound, lane_valid.astype(jnp.float32), padded[0:1]

    info = [prepare(block) for block in range(len(BLOCKS))]

    def fold_rows(value):
        total = value[0:8]
        for start in range(8, value.shape[0], 8):
            total = total + value[start : start + 8]
        return total

    def one_head(rows, length, head):
        lane = lax.broadcasted_iota(jnp.int32, (length, 128), 1)
        half = head // half_heads
        s_one = jnp.where(lane // S_DIM == head, s_keep[rows, :], zero)
        t_one = jnp.where(lane // T_DIM == head - half * half_heads, t_keep[half, rows, :], zero)
        return half, s_one, t_one

    def row_slices(head):
        s_slice = pl.ds(pl.multiple_of(head * S_DIM, S_DIM), S_DIM)
        t_slice = pl.ds(pl.multiple_of(head * T_DIM, T_DIM), T_DIM)
        return s_slice, t_slice

    def fill(block, keys, one, target):
        off, length, seqs = BLOCKS[block]
        each = length // len(seqs)
        if len(seqs) > 1:
            scores = dot(keys[...], one, NT)
            sums = []
            for place in range(len(seqs)):
                here = slice(place * each, place * each + each)
                value = jnp.exp2(scores[here, here])
                sums.append(fold_rows(value))
                target[here, here] = value.astype(jnp.bfloat16)
            return jnp.concatenate(sums, axis=1)
        total = jnp.zeros((8, length), jnp.float32)
        for start in range(0, length, KEY_ROWS):
            here = slice(start, start + KEY_ROWS)
            value = jnp.exp2(dot(keys[here, :], one, NT))
            total = total + fold_rows(value)
            target[here, :] = value.astype(jnp.bfloat16)
        return total

    def fill_both(block, head, slot):
        off, length, seqs = BLOCKS[block]
        rows = slice(off, off + length)
        half, s_one, t_one = one_head(rows, length, head)
        return (
            fill(block, s_keep.at[rows, :], s_one, exps[block].at[slot, 0]),
            fill(block, t_keep.at[half, rows, :], t_one, exps[block].at[slot, 1]),
        )

    def use_both(block, head, slot, sums):
        off, length, seqs = BLOCKS[block]
        rows = slice(off, off + length)
        bound, valid_row, padded = info[block]
        s_total = jnp.sum(sums[0], axis=0, keepdims=True) - padded
        t_total = jnp.sum(sums[1], axis=0, keepdims=True) - padded
        s_recip = valid_row / s_total
        t_recip = valid_row / t_total
        s_slice, t_slice = row_slices(head)
        s_vec = s_rows[s_slice, rows]
        t_vec = t_rows[t_slice, rows]
        t_left = jnp.concatenate([s_vec, s_vec * t_recip, t_vec], axis=0).astype(jnp.bfloat16)
        s_left = jnp.concatenate([s_vec, s_vec * s_recip], axis=0).astype(jnp.bfloat16)
        t_out = dot(t_left, exps[block][slot, 1])
        s_out = dot(s_left, exps[block][slot, 0])
        d_rows[s_slice, rows] = (
            s_out[0:8] * s_recip - t_out[0:8] * t_recip + (s_out[8:16] - t_out[8:16]) * valid_row
        )
        inner = t_vec * t_out[16:32]
        inner = (inner[0:8] + inner[8:16]) * t_scale - s_vec * t_out[0:8] * s_scale
        parts = inner * t_recip + (jnp.log2(s_total) - jnp.log2(t_total)) * (valid_row * 0.125)
        return fold_lanes(parts, length)

    def fold_lanes(parts, length):
        total = parts[:, 0:128]
        for start in range(128, length, 128):
            total = total + parts[:, start : start + 128]
        return total

    def fast_heads(step, carry):
        work = [
            (block, step * AT_ONCE + slot, slot)
            for slot in range(AT_ONCE)
            for block in range(len(BLOCKS))
        ]
        sums = [fill_both(*item) for item in work]
        total = jnp.zeros((8, 128), jnp.float32)
        for item, item_sums in zip(work, sums):
            total = total + use_both(*item, item_sums)
        loss_ref[...] += total
        return carry

    def exact_head(seq, head):
        off, length = SEQS[seq]
        rows = slice(off, off + length)
        valid = lens_ref[seq]
        half, s_one, t_one = one_head(rows, length, head)
        s_slice, t_slice = row_slices(head)
        key_valid = lax.broadcasted_iota(jnp.int32, (length, 128), 0) < valid
        exp_c[0, 0, 0:length, 0:128] = s_one
        exp_c[0, 1, 0:length, 0:128] = t_one

        def log_soft(scores, scale):
            scaled = jnp.where(key_valid, scores * scale, -1e30)
            top = jnp.max(scaled, axis=0, keepdims=True)
            shifted = scaled - top
            total = jnp.sum(jnp.exp2(shifted), axis=0, keepdims=True)
            return shifted - jnp.log2(total)

        def queries(block, carry):
            start = pl.multiple_of(block * 128, 128)
            here = pl.ds(start, 128)
            query_valid = lax.broadcasted_iota(jnp.int32, (length, 128), 1) + start < valid
            both = key_valid & query_valid
            s_log = log_soft(dot(s_keep[rows, :], exp_c[0, 0, here, 0:128], NT), s_scale)
            t_log = log_soft(dot(t_keep[half, rows, :], exp_c[0, 1, here, 0:128], NT), t_scale)
            t_soft = jnp.exp2(t_log)
            change = jnp.where(both, jnp.exp2(s_log) - t_soft, 0.0)
            exp_c[1, 0, 0:length, here] = change.astype(jnp.bfloat16)
            loss_ref[...] += fold_rows(jnp.where(both, t_soft * (t_log - s_log), 0.0))
            return carry

        lax.fori_loop(0, length // 128, queries, 0)
        s_vec = s_rows[s_slice, rows]
        left = jnp.concatenate([s_vec, jnp.zeros_like(s_vec)], axis=0).astype(jnp.bfloat16)
        change = exp_c[1, 0, 0:length, 0:length]
        d_rows[s_slice, rows] = (dot(left, change) + dot(left, change, NT))[0:8]

    top_bound = info[0][0]
    for entry in info:
        top_bound = jnp.maximum(top_bound, entry[0])
    fast = top_bound < FAST_LIMIT

    @pl.when(fast)
    def _():
        lax.fori_loop(0, 2 * half_heads // AT_ONCE, fast_heads, 0)

    @pl.when(jnp.logical_not(fast))
    def _():
        for block, (off, length, seqs) in enumerate(BLOCKS):
            rows = slice(off, off + length)
            row_valid = valid_rows(block)
            s_keep[rows, :] = jnp.where(row_valid, s_ref[rows, :], zero)
            for half in range(2):
                t_block = t_ref[rows, half * 128 : half * 128 + 128]
                t_keep[half, rows, :] = jnp.where(row_valid, t_block, zero)
        for seq in range(len(SEQS)):

            def body(head, carry, seq=seq):
                exact_head(seq, head)
                return carry

            lax.fori_loop(0, 2 * half_heads, body, 0)

    for off, length in SEQS:
        ds_ref[off : off + length, :] = (
            d_rows[:, off : off + length].T * (1.0 / math.sqrt(S_DIM) / (3 * REL))
        ).astype(ds_ref.dtype)


def relation(seq_lengths, student, teacher):
    block_s = pl.BlockSpec((None, TOKENS_HERE, S_WIDE), lambda part, group: (part, 0, group))
    block_t = pl.BlockSpec((None, TOKENS_HERE, T_WIDE), lambda part, group: (part, 0, group))
    grads, loss = pl.pallas_call(
        relation_kernel,
        grid=(3, GROUPS),
        in_specs=[pl.BlockSpec(memory_space=pltpu.SMEM), block_s, block_t],
        out_specs=[block_s, pl.BlockSpec((8, 128), lambda part, group: (0, 0))],
        out_shape=[
            jax.ShapeDtypeStruct((3, TOKENS_HERE, D), jnp.bfloat16),
            jax.ShapeDtypeStruct((8, 128), jnp.float32),
        ],
        scratch_shapes=[
            pltpu.VMEM((S_WIDE, TOKENS_HERE), jnp.float32),
            pltpu.VMEM((T_WIDE, TOKENS_HERE), jnp.float32),
            pltpu.VMEM((S_WIDE, TOKENS_HERE), jnp.float32),
            pltpu.VMEM((AT_ONCE, 2, LC, LC), jnp.bfloat16),
            pltpu.VMEM((AT_ONCE, 2, LB, LB), jnp.bfloat16),
            pltpu.VMEM((AT_ONCE, 2, 2 * LA, 2 * LA), jnp.bfloat16),
            pltpu.VMEM((TOKENS_HERE, 128), jnp.bfloat16),
            pltpu.VMEM((2, TOKENS_HERE, 128), jnp.bfloat16),
        ],
        compiler_params=pltpu.CompilerParams(vmem_limit_bytes=48 * 2**20),
    )(seq_lengths, student, teacher)
    return grads, loss


def by_part(columns, heads):
    lead = columns.shape[:-1]
    size = columns.shape[-1] // heads // 3
    shaped = columns.reshape(lead + (heads, 3, size))
    return jnp.moveaxis(shaped, -2, -3).reshape(columns.shape)


def by_head(columns, heads):
    lead = columns.shape[:-1]
    size = columns.shape[-1] // heads // 3
    shaped = columns.reshape(lead + (3, heads, size))
    return jnp.moveaxis(shaped, -2, -3).reshape(columns.shape)


POS_AT = 7
GAIN_ROWS = 18
ERF_TOP = (
    -2.72614225801306e-10,
    2.77068142495902e-08,
    -2.10102402082508e-06,
    -5.69250639462346e-05,
    -7.34990630326855e-04,
    -2.95459980854025e-03,
    -1.60960333262415e-02,
)
ERF_LOW = (
    -1.45660718464996e-05,
    -2.13374055278905e-04,
    -1.68282697438203e-03,
    -7.37332916720468e-03,
    -1.42647390514189e-02,
)
STEP_ROWS = 256


def erf(value):
    value = jnp.clip(value, -4.0, 4.0)
    square = value * value
    top = jnp.full_like(value, ERF_TOP[0])
    for factor in ERF_TOP[1:]:
        top = top * square + factor
    low_part = jnp.full_like(value, ERF_LOW[0])
    for factor in ERF_LOW[1:]:
        low_part = low_part * square + factor
    return value * top / low_part


def normal_cdf(value):
    return 0.5 + 0.5 * erf(value * math.sqrt(0.5))


def normalize(values):
    average = jnp.mean(values, axis=-1, keepdims=True)
    centered = values - average
    variance = jnp.mean(centered * centered, axis=-1, keepdims=True)
    scale = lax.rsqrt(variance + 1e-05)
    return centered * scale, scale


def low16(value):
    return value.astype(jnp.bfloat16)


def step_slice(step):
    return pl.ds(pl.multiple_of(step * STEP_ROWS, STEP_ROWS), STEP_ROWS)


def head_soft(q_pair, k_one, valid, length):
    scores = dot(q_pair, k_one, NT) * (1.0 / math.sqrt(HD))
    lane = lax.broadcasted_iota(jnp.int32, scores.shape, 1)
    scores = jnp.where(lane < valid, scores, -1e30)
    top = jnp.max(scores, axis=-1, keepdims=True)
    value = jnp.exp(scores - top)
    return value / jnp.sum(value, axis=-1, keepdims=True)


def forward_kernel(
    lens_ref,
    rows_ref,
    slot_ref,
    big,
    gains,
    s_out,
    hat0,
    hat1,
    hat2,
    scale0,
    scale1,
    scale2,
    hid_low,
    qkv_low,
    ctx_low,
    mid_low,
    pre_low,
    x_low,
    hidden_kept,
):
    steps = TOKENS_HERE // STEP_ROWS

    def embed(step, carry):
        here = step_slice(step)
        spots = lax.broadcasted_iota(jnp.int32, (STEP_ROWS, rows_ref.shape[0]), 1)
        chosen = low16(jnp.where(slot_ref[here, :] == spots, 1.0, 0.0))
        first = big[POS_AT, 0:STEP_ROWS, :].astype(jnp.float32)
        twice = jnp.concatenate([first[0:LA], first[0:LA]], axis=0)
        late = big[POS_AT, STEP_ROWS : 2 * STEP_ROWS, :].astype(jnp.float32)
        place = jnp.where(step == 0, twice, jnp.where(step == 3, late, first))
        hat, scale = normalize(dot(chosen, rows_ref[...]) + place)
        hat0[here, :] = low16(hat)
        scale0[here, :] = scale
        wide = hat * gains[0:1, :] + gains[1:2, :]
        hidden_kept[here, :] = wide
        hidden = low16(wide)
        hid_low[here, :] = hidden
        for part in range(3):
            qkv_low[part, here, :] = low16(dot(hidden, big[part]) + gains[2 + part : 3 + part, :])
        return carry

    lax.fori_loop(0, steps, embed, 0)
    zero = jnp.zeros((), jnp.bfloat16)
    for seq, (off, length) in enumerate(SEQS):

        def attend_pair(pair, carry, seq=seq, off=off, length=length):
            rows = slice(off, off + length)
            cols = pl.ds(pl.multiple_of(pair * 128, 128), 128)
            query, key, value = (qkv_low[part, rows, cols] for part in range(3))
            lane = lax.broadcasted_iota(jnp.int32, (length, 128), 1)
            total = jnp.zeros((length, 128), jnp.float32)
            for side in range(2):
                mine = lane // HD == side
                soft = head_soft(query, jnp.where(mine, key, zero), lens_ref[seq], length)
                total = total + dot(low16(soft), jnp.where(mine, value, zero))
            ctx_low[rows, cols] = low16(total)
            return carry

        lax.fori_loop(0, D // 128, attend_pair, 0)

    def rest(step, carry):
        here = step_slice(step)
        hat, scale = normalize(hidden_kept[here, :] + dot(ctx_low[here, :], big[6]) + gains[5:6, :])
        hat1[here, :] = low16(hat)
        scale1[here, :] = scale
        middle = hat * gains[11:12, :] + gains[12:13, :]
        middle_low = low16(middle)
        mid_low[here, :] = middle_low
        output = middle + gains[10:11, :]
        for block in range(4):
            cols = slice(block * D, block * D + D)
            pre = dot(middle_low, big[8 + block]) + gains[6 + block : 7 + block, :]
            act = low16(pre * normal_cdf(pre))
            pre_low[here, cols] = low16(pre)
            output = output + dot(act, big[12 + block])
        hat, scale = normalize(output)
        hat2[here, :] = low16(hat)
        scale2[here, :] = scale
        final = low16(hat * gains[13:14, :] + gains[14:15, :])
        x_low[here, :] = final
        for part in range(3):
            s_out[part, here, :] = low16(dot(final, big[3 + part]) + gains[15 + part : 16 + part, :])
        return carry

    lax.fori_loop(0, steps, rest, 0)


def forward_layer(seq_lengths, rows, slot, big, gains):
    vmem = pl.BlockSpec(memory_space=pltpu.VMEM)
    shape = lambda *dims: jax.ShapeDtypeStruct(dims, jnp.float32)
    half = lambda *dims: jax.ShapeDtypeStruct(dims, jnp.bfloat16)
    tokens = TOKENS_HERE
    outs = [half(3, tokens, D)]
    outs += [half(tokens, D)] * 3 + [shape(tokens, 1)] * 3
    outs += [half(tokens, D), half(3, tokens, D), half(tokens, D), half(tokens, D)]
    outs += [half(tokens, FF), half(tokens, D)]
    return pl.pallas_call(
        forward_kernel,
        in_specs=[pl.BlockSpec(memory_space=pltpu.SMEM)] + [vmem] * 4,
        out_specs=[vmem] * len(outs),
        out_shape=outs,
        scratch_shapes=[pltpu.VMEM((tokens, D), jnp.float32)],
        compiler_params=pltpu.CompilerParams(vmem_limit_bytes=56 * 2**20),
    )(seq_lengths, rows, slot[:, None], big, gains)


def backward_kernel(
    lens_ref,
    slot_ref,
    big,
    gains,
    ds_ref,
    hat0,
    hat1,
    hat2,
    scale0,
    scale1,
    scale2,
    hid_low,
    qkv_low,
    ctx_low,
    mid_low,
    pre_low,
    x_low,
    grads,
    small,
    slot_grads,
    row_low,
    flow,
    flow_low,
    wide_low,
    turned,
    dqkv_low,
    act_low,
):
    steps = TOKENS_HERE // STEP_ROWS
    small[...] = jnp.zeros_like(small)

    def add_small(row, value):
        small[row : row + 1, :] += jnp.sum(value, axis=0, keepdims=True)

    def norm_back(here, grad, hat_ref, scale_ref, row):
        hat = hat_ref[here, :].astype(jnp.float32)
        add_small(row, grad * hat)
        add_small(row + 1, grad)
        inner = grad * gains[row : row + 1, :]
        mean_inner = jnp.mean(inner, axis=-1, keepdims=True)
        mean_hat = jnp.mean(inner * hat, axis=-1, keepdims=True)
        return scale_ref[here, :] * (inner - mean_inner - hat * mean_hat)

    def turn(source, width):
        for start in range(0, TOKENS_HERE, STEP_ROWS):
            turned[0:width, start : start + STEP_ROWS] = source[start : start + STEP_ROWS, 0:width].T

    def weight_grads(pairs):
        for index, right in pairs:
            grads[index] = low16(dot(turned[0:D, :], right))

    def last(step, carry):
        here = step_slice(step)
        grad = jnp.zeros((STEP_ROWS, D), jnp.float32)
        for part in range(3):
            piece = ds_ref[part, here, :]
            add_small(15 + part, piece.astype(jnp.float32))
            grad = grad + dot(piece, big[3 + part], NT)
        grad = norm_back(here, grad, hat2, scale2, 13)
        add_small(10, grad)
        grad_low = low16(grad)
        flow_low[here, :] = grad_low
        total = grad
        for block in range(4):
            cols = slice(block * D, block * D + D)
            pre = pre_low[here, cols].astype(jnp.float32)
            below = normal_cdf(pre)
            act_low[here, cols] = low16(pre * below)
            slope = below + pre * jnp.exp(pre * pre * -0.5) * (1.0 / math.sqrt(2.0 * math.pi))
            inner = dot(grad_low, big[12 + block], NT) * slope
            add_small(6 + block, inner)
            inner_low = low16(inner)
            wide_low[here, cols] = inner_low
            total = total + dot(inner_low, big[8 + block], NT)
        flow[here, :] = total
        return carry

    lax.fori_loop(0, steps, last, 0)
    turn(x_low, D)
    weight_grads([(3 + part, ds_ref[part]) for part in range(3)])
    for block in range(4):
        cols = slice(block * D, block * D + D)
        for start in range(0, TOKENS_HERE, STEP_ROWS):
            turned[:, start : start + STEP_ROWS] = act_low[start : start + STEP_ROWS, cols].T
        weight_grads([(12 + block, flow_low[...])])
    turn(mid_low, D)
    weight_grads([(8 + block, wide_low[:, block * D : block * D + D]) for block in range(4)])

    def middle(step, carry):
        here = step_slice(step)
        grad = norm_back(here, flow[here, :], hat1, scale1, 11)
        add_small(5, grad)
        flow[here, :] = grad
        grad_low = low16(grad)
        flow_low[here, :] = grad_low
        wide_low[here, 0:D] = low16(dot(grad_low, big[6], NT))
        return carry

    lax.fori_loop(0, steps, middle, 0)
    turn(ctx_low, D)
    weight_grads([(6, flow_low[...])])
    zero = jnp.zeros((), jnp.bfloat16)
    for seq, (off, length) in enumerate(SEQS):

        def attend_pair(pair, carry, seq=seq, off=off, length=length):
            rows = slice(off, off + length)
            cols = pl.ds(pl.multiple_of(pair * 128, 128), 128)
            query, key, value = (qkv_low[part, rows, cols] for part in range(3))
            out_grad = wide_low[rows, cols]
            lane = lax.broadcasted_iota(jnp.int32, (length, 128), 1)
            sums = [jnp.zeros((length, 128), jnp.float32)] * 3
            for side in range(2):
                mine = lane // HD == side
                key_one = jnp.where(mine, key, zero)
                soft = head_soft(query, key_one, lens_ref[seq], length)
                grad_one = jnp.where(mine, out_grad, zero)
                soft_grad = dot(grad_one, value, NT)
                inner = jnp.sum(soft_grad * soft, axis=-1, keepdims=True)
                score_grad = low16((soft_grad - inner) * soft * (1.0 / math.sqrt(HD)))
                query_one = jnp.where(mine, query, zero)
                sums[0] = sums[0] + dot(score_grad, key_one)
                sums[1] = sums[1] + dot(score_grad.T, query_one)
                sums[2] = sums[2] + dot(low16(soft).T, grad_one)
            for part in range(3):
                dqkv_low[part, rows, cols] = low16(sums[part])
            return carry

        lax.fori_loop(0, D // 128, attend_pair, 0)

    def first(step, carry):
        here = step_slice(step)
        grad = flow[here, :]
        for part in range(3):
            piece = dqkv_low[part, here, :]
            add_small(2 + part, piece.astype(jnp.float32))
            grad = grad + dot(piece, big[part], NT)
        grad = norm_back(here, grad, hat0, scale0, 0)
        flow[here, :] = grad
        row_low[here, :] = low16(grad)
        return carry

    lax.fori_loop(0, steps, first, 0)
    turn(hid_low, D)
    weight_grads([(part, dqkv_low[part]) for part in range(3)])
    near = flow[0:LA, :] + flow[LA : 2 * LA, :] + flow[2 * LA : 3 * LA, :] + flow[4 * LA : 5 * LA, :]
    grads[POS_AT, 0:LA, :] = low16(near)
    grads[POS_AT, LA:LB, :] = low16(flow[3 * LA : 4 * LA, :] + flow[5 * LA : 6 * LA, :])
    grads[POS_AT, LB:LC, :] = low16(flow[2 * LA + LB + LB :, :])
    places = slot_grads.shape[0]
    size = 512 if places % 512 == 0 else places

    def spread(block, carry):
        start = pl.multiple_of(block * size, size)
        spots = lax.broadcasted_iota(jnp.int32, (size, TOKENS_HERE), 0) + start
        chosen = low16(jnp.where(slot_ref[...] == spots, 1.0, 0.0))
        slot_grads[pl.ds(start, size), :] = low16(dot(chosen, row_low[...]))
        return carry

    lax.fori_loop(0, places // size, spread, 0)


def backward_layer(seq_lengths, slot, big, gains, final_grad, kept, places):
    vmem = pl.BlockSpec(memory_space=pltpu.VMEM)
    half = lambda *dims: jax.ShapeDtypeStruct(dims, jnp.bfloat16)
    tokens = TOKENS_HERE
    return pl.pallas_call(
        backward_kernel,
        in_specs=[pl.BlockSpec(memory_space=pltpu.SMEM)] + [vmem] * (4 + len(kept)),
        out_specs=[vmem] * 4,
        out_shape=[
            half(16, D, D),
            jax.ShapeDtypeStruct((GAIN_ROWS, D), jnp.float32),
            half(places, D),
            half(tokens, D),
        ],
        scratch_shapes=[
            pltpu.VMEM((tokens, D), jnp.float32),
            pltpu.VMEM((tokens, D), jnp.bfloat16),
            pltpu.VMEM((tokens, FF), jnp.bfloat16),
            pltpu.VMEM((D, tokens), jnp.bfloat16),
            pltpu.VMEM((3, tokens, D), jnp.bfloat16),
            pltpu.VMEM((tokens, FF), jnp.bfloat16),
        ],
        compiler_params=pltpu.CompilerParams(vmem_limit_bytes=60 * 2**20),
    )(seq_lengths, slot[None, :], big, gains, final_grad, *kept)


def teacher_kernel(hidden, weight, out):
    out[...] = low16(dot(hidden[...], weight[...]))


def project_teacher(hidden, weight):
    tokens = hidden.shape[0]
    owners, parts, depth, width = weight.shape
    return pl.pallas_call(
        teacher_kernel,
        grid=(parts, owners),
        in_specs=[
            pl.BlockSpec((tokens, depth), lambda part, owner: (0, 0)),
            pl.BlockSpec((None, None, depth, width), lambda part, owner: (owner, part, 0, 0)),
        ],
        out_specs=pl.BlockSpec((None, tokens, width), lambda part, owner: (part, 0, owner)),
        out_shape=jax.ShapeDtypeStruct((parts, tokens, owners * width), jnp.bfloat16),
        compiler_params=pltpu.CompilerParams(vmem_limit_bytes=32 * 2**20),
    )(hidden, weight)


MESH_IDS = pl.DeviceIdType.MESH


def barrier_all(rank, count, place):
    barrier = pltpu.get_barrier_semaphore()

    def greet(step, carry):
        pl.semaphore_signal(
            barrier, inc=1, device_id=place(lax.rem(rank + step, count)), device_id_type=MESH_IDS
        )
        return carry

    lax.fori_loop(1, count, greet, 0)
    pl.semaphore_wait(barrier, count - 1)


class Spot:
    def __init__(self, n_dp, n_head):
        self.n_dp, self.n_head = n_dp, n_head
        self.count = n_dp * n_head
        self.nz, self.nx = n_dp // 2, n_head // 2
        dp, head = lax.axis_index("dp"), lax.axis_index("head")
        self.rank = dp * n_head + head
        self.z, self.y = dp // 2, lax.rem(dp, 2)
        self.x, self.c = head // 2, lax.rem(head, 2)

    def place(self, rank):
        return (rank // self.n_head, lax.rem(rank, self.n_head))

    def device(self, z, y, x, c):
        return (z * 2 + y, x * 2 + c)


def remote(source, target, send_sem, recv_sem, device):
    return pltpu.make_async_remote_copy(
        src_ref=source,
        dst_ref=target,
        send_sem=send_sem,
        recv_sem=recv_sem,
        device_id=device,
        device_id_type=MESH_IDS,
    )


def start_all_to_all(spot, source, target, send_sems, recv_sems, local_sem):
    pltpu.make_async_copy(source.at[spot.rank], target.at[spot.rank], local_sem).start()

    def send(step, carry):
        peer = lax.rem(spot.rank + step, spot.count)
        remote(
            source.at[peer], target.at[spot.rank], send_sems.at[step], recv_sems.at[step], spot.place(peer)
        ).start()
        return carry

    lax.fori_loop(1, spot.count, send, 0)


def finish_all_to_all(spot, source, target, send_sems, recv_sems, local_sem):
    def take(step, carry):
        origin = lax.rem(spot.rank + spot.count - step, spot.count)
        copy = remote(
            source.at[origin], target.at[origin], send_sems.at[step], recv_sems.at[step], spot.place(origin)
        )
        copy.wait_recv()
        copy.wait_send()
        return carry

    lax.fori_loop(1, spot.count, take, 0)
    pltpu.make_async_copy(source.at[spot.rank], target.at[spot.rank], local_sem).wait()


def is_direct(shape):
    return shape[1] % 16 == 0 and shape[2] % 128 == 0


def piece_of(whole, shape, dp, head, half):
    blocks = pl.ds(half * (shape[0] // 2), shape[0] // 2)
    if not is_direct(shape):
        return whole.at[dp, head, blocks]
    rows = pl.ds(pl.multiple_of(dp * shape[1], shape[1]), shape[1])
    return whole.at[blocks, rows, pl.ds(pl.multiple_of(head * shape[2], shape[2]), shape[2])]


def whole_shape(sizes, shape):
    if not is_direct(shape):
        return sizes + shape
    return (shape[0], sizes[0] * shape[1], sizes[1] * shape[2])


def answer(heard, table, rows, at_once):
    count, room = rows.shape[:2]
    spare = -count % 128
    asked = heard[:, 0, :]
    if spare:
        asked = jnp.concatenate([asked, jnp.full((spare, 128), -1.0, jnp.float32)], axis=0)
    turned = asked.T
    lane = lax.broadcasted_iota(jnp.int32, (room, count + spare), 1)
    spots = lax.broadcasted_iota(jnp.int32, (at_once * room, table.shape[0]), 1)

    def some(step, carry):
        columns = []
        for place in range(at_once):
            mine = lane == step * at_once + place
            columns.append(jnp.sum(jnp.where(mine, turned[0:room, :], 0.0), axis=1, keepdims=True))
        wanted = jnp.concatenate(columns, axis=0).astype(jnp.int32)
        chosen = low16(jnp.where(wanted == spots, 1.0, 0.0))
        found = low16(dot(chosen, table[...]))
        for place in range(at_once):
            rows[step * at_once + place] = found[place * room : place * room + room]
        return carry

    lax.fori_loop(0, count // at_once, some, 0)


def gather_kernel(
    sizes,
    messages,
    table,
    shard,
    heard,
    rows_out,
    full,
    rows,
    message_send,
    message_recv,
    row_send,
    row_recv,
    piece_send,
    piece_recv,
    local_sems,
):
    spot = Spot(*sizes)
    z, y, x, c, nz, nx = spot.z, spot.y, spot.x, spot.c, spot.nz, spot.nx
    barrier_all(spot.rank, spot.count, spot.place)
    sends = []

    def spot_of(piece, half):
        return piece_of(full, shard.shape, piece[0] * 2 + piece[1], piece[2] * 2 + piece[3], half)

    def arrival(piece, half):
        return piece_recv.at[half, piece[0] * 2 + piece[1], piece[2] * 2 + piece[3]]

    def send_piece(source, piece, half, device):
        copy = remote(
            source, spot_of(piece, half), piece_send.at[len(sends)], arrival(piece, half), device
        )
        copy.start()
        sends.append(copy)

    def wait_piece(piece, half):
        here = spot_of(piece, half)
        remote(
            here, here, piece_send.at[0], arrival(piece, half), spot.device(z, y, x, 1 - c)
        ).wait_recv()
        return here

    own = (z, y, x, c)
    own_halves = [shard.at[pl.ds(half * (shard.shape[0] // 2), shard.shape[0] // 2)] for half in range(2)]
    own_copies = [
        pltpu.make_async_copy(own_halves[half], spot_of(own, half), local_sems.at[half]) for half in range(2)
    ]
    for copy in own_copies:
        copy.start()
    start_all_to_all(spot, messages, heard, message_send, message_recv, local_sems.at[2])
    others_x = [lax.rem(x + step, nx) for step in range(1, nx)]
    sibling, opposite = spot.device(z, y, x, 1 - c), spot.device(z, 1 - y, x, c)
    across = [spot.device(z, y, other, c) for other in others_x]
    for half in range(2):
        for step in range(1, nz):
            send_piece(own_halves[half], own, half, spot.device(lax.rem(z + step, nz), y, x, c))
    for half in range(2):
        for device in across + [opposite, sibling]:
            send_piece(own_halves[half], own, half, device)
    finish_all_to_all(spot, messages, heard, message_send, message_recv, local_sems.at[2])
    answer(heard, table, rows, 8)
    start_all_to_all(spot, rows, rows_out, row_send, row_recv, local_sems.at[3])
    depths = [lax.rem(z + nz - step, nz) for step in range(nz)]

    def pass_on(piece, half, devices):
        here = wait_piece(piece, half)
        for device in devices:
            send_piece(here, piece, half, device)

    for deep in depths[1:]:
        for half in range(2):
            pass_on((deep, y, x, c), half, across + [opposite, sibling])
    for deep in depths:
        for other in others_x:
            pass_on((deep, y, other, c), 0, [opposite, sibling])
        pass_on((deep, 1 - y, x, c), 1, across + [sibling])
    for deep in depths:
        for column in [x] + others_x:
            pass_on((deep, 1 - y, column, c), 0, [sibling])
        for other in others_x:
            for side in (y, 1 - y):
                pass_on((deep, side, other, c), 1, [sibling])
    for deep in depths:
        for side in (y, 1 - y):
            for column in [x] + others_x:
                for half in range(2):
                    wait_piece((deep, side, column, 1 - c), half)
    for copy in sends:
        copy.wait_send()
    finish_all_to_all(spot, rows, rows_out, row_send, row_recv, local_sems.at[3])
    for copy in own_copies:
        copy.wait()


def gather_weights(sizes, messages, table, shard, room):
    n_dp, n_head = sizes
    count = n_dp * n_head
    nz, nx = n_dp // 2, n_head // 2
    sends = 2 * (nz - 1) + 2 * nz * (nx + 1) + nz * (nx - 1) * 2 + nz * nx + nz * nx + 2 * nz * (nx - 1)
    anywhere = pl.BlockSpec(memory_space=pl.ANY)
    vmem = pl.BlockSpec(memory_space=pltpu.VMEM)
    dma = pltpu.SemaphoreType.DMA
    rows_shape = (count, room, table.shape[1])
    return pl.pallas_call(
        functools.partial(gather_kernel, sizes),
        in_specs=[vmem, vmem, anywhere],
        out_specs=[vmem, anywhere, anywhere],
        out_shape=[
            jax.ShapeDtypeStruct(messages.shape, messages.dtype),
            jax.ShapeDtypeStruct(rows_shape, table.dtype),
            jax.ShapeDtypeStruct(whole_shape(sizes, shard.shape), shard.dtype),
        ],
        scratch_shapes=[
            pltpu.VMEM(rows_shape, table.dtype),
            dma((count,)),
            dma((count,)),
            dma((count,)),
            dma((count,)),
            dma((sends,)),
            dma((2, n_dp, n_head)),
            dma((4,)),
        ],
        compiler_params=pltpu.CompilerParams(
            collective_id=2, has_side_effects=True, vmem_limit_bytes=40 * 2**20
        ),
    )(messages, table, shard)


def table_rows_at_once(rows):
    sizes = [size for size in range(8, 265, 8) if rows % size == 0]
    return max(sizes) if sizes and rows > 264 else rows


def place_rows(rows, wanted, table_grad):
    count, room, width = rows.shape
    at_once = table_rows_at_once(table_grad.shape[0])
    arrived = rows[...].reshape(count * room, width)

    def some(step, squares):
        start = step * at_once
        if at_once % 8 == 0:
            start = pl.multiple_of(start, 8)
        spots = lax.broadcasted_iota(jnp.int32, (at_once, count * room), 0) + start
        chosen = low16(jnp.where(wanted[...] == spots, 1.0, 0.0))
        value = dot(chosen, arrived)
        table_grad[pl.ds(start, at_once), :] = value
        return squares + jnp.sum(value * value, axis=0, keepdims=True)

    zero = jnp.zeros((1, width), jnp.float32)
    return lax.fori_loop(0, table_grad.shape[0] // at_once, some, zero)


def reduce_kernel(
    sizes,
    rows,
    pieces,
    wanted,
    loss,
    rows_out,
    total,
    table_grad,
    small,
    everyone,
    mine,
    sum_send,
    sum_recv,
    core_in,
    y_in,
    x_in,
    z_in,
    row_send,
    row_recv,
    core_send,
    core_recv,
    y_send,
    y_recv,
    x_send,
    x_recv,
    z_send,
    z_recv,
    local_sem,
):
    spot = Spot(*sizes)
    z, y, x, c, nz, nx = spot.z, spot.y, spot.x, spot.c, spot.nz, spot.nx
    shape = total.shape
    blocks = shape[0] // 2
    barrier_all(spot.rank, spot.count, spot.place)
    sibling = spot.device(z, y, x, 1 - c)
    opposite = spot.device(z, 1 - y, x, c)

    def core_sum(deep, side, column, half):
        return core_in.at[deep, side, column, pl.ds(half * blocks, blocks)]

    def core_copy(deep, side, column, half):
        return remote(
            piece_of(pieces, shape, deep * 2 + side, column * 2 + 1 - c, half),
            core_sum(deep, side, column, half),
            core_send.at[half, deep, side, column],
            core_recv.at[half, deep, side, column],
            sibling,
        )

    def y_copy(half, deep, column):
        return remote(
            core_sum(deep, 1 - y, column, half),
            y_in.at[half, deep, column],
            y_send.at[half, deep, column],
            y_recv.at[half, deep, column],
            opposite,
        )

    def x_copy(half, step, deep, side):
        column = lax.rem(x + step, nx)
        source = y_in.at[0, deep, column] if half == 0 else core_sum(deep, side, column, 1)
        return remote(
            source,
            x_in.at[half, step - 1, deep, side],
            x_send.at[half, step - 1, deep, side],
            x_recv.at[half, step - 1, deep, side],
            spot.device(z, y, column, c),
        )

    def summed(half, deep):
        return y_in.at[0, deep, x] if half == 0 else core_sum(deep, y, x, 1)

    def z_copy(half, step):
        deep = lax.rem(z + step, nz)
        return remote(
            summed(half, deep),
            z_in.at[half, step - 1],
            z_send.at[half, step - 1],
            z_recv.at[half, step - 1],
            spot.device(deep, y, x, c),
        )

    def add_into(target, sources):
        def some(block, carry):
            value = target[block].astype(jnp.float32)
            for source in sources:
                value = value + source[block].astype(jnp.float32)
            target[block] = value.astype(target.dtype)
            return carry

        lax.fori_loop(0, blocks, some, 0)

    def over_depths(action):
        def one(step, carry):
            action(lax.rem(z + 1 + step, nz))
            return carry

        lax.fori_loop(0, nz, one, 0)

    steps_x = list(range(1, nx))
    columns = [lax.rem(x + step, nx) for step in steps_x]
    core_order = [(0, 1 - y, column) for column in columns + [x]]
    core_order += [(1, side, column) for column in columns for side in (1 - y, y)]
    core_order += [(0, y, column) for column in columns + [x]]
    core_order += [(1, side, x) for side in (1 - y, y)]
    for half, side, column in core_order:
        over_depths(lambda deep: core_copy(deep, side, column, half).start())
    start_all_to_all(spot, rows, rows_out, row_send, row_recv, local_sem)

    def take_core(deep, side, column, half):
        core_copy(deep, side, column, half).wait_recv()
        own = piece_of(pieces, shape, deep * 2 + side, column * 2 + c, half)
        add_into(core_sum(deep, side, column, half), [own])

    def core_then_y(deep, column):
        take_core(deep, 1 - y, column, 0)
        y_copy(0, deep, column).start()

    def core_then_x(deep, step, side):
        take_core(deep, side, lax.rem(x + step, nx), 1)
        x_copy(1, step, deep, side).start()

    def take_y(deep, column):
        y_copy(0, deep, column).wait_recv()
        add_into(y_in.at[0, deep, column], [core_sum(deep, y, column, 0)])

    def take_x(deep, side):
        for step in steps_x:
            x_copy(1, step, deep, side).wait_recv()
        add_into(core_sum(deep, side, x, 1), [x_in.at[1, step - 1, deep, side] for step in steps_x])

    def y_then_x(deep, step):
        take_y(deep, lax.rem(x + step, nx))
        x_copy(0, step, deep, 0).start()

    def x_then_y(deep):
        take_x(deep, 1 - y)
        y_copy(1, deep, x).start()

    for column in columns + [x]:
        over_depths(lambda deep: core_then_y(deep, column))
    for step in steps_x:
        for side in (1 - y, y):
            over_depths(lambda deep: core_then_x(deep, step, side))
    for column in columns + [x]:
        over_depths(lambda deep: take_core(deep, y, column, 0))
    for side in (1 - y, y):
        over_depths(lambda deep: take_core(deep, side, x, 1))
    for step in steps_x:
        over_depths(lambda deep: y_then_x(deep, step))
    over_depths(x_then_y)
    over_depths(lambda deep: take_y(deep, x))
    over_depths(lambda deep: take_x(deep, y))
    for step in range(nz):
        deep = lax.rem(z + 1 + step, nz)
        for step_x in steps_x:
            x_copy(0, step_x, deep, 0).wait_recv()
        add_into(y_in.at[0, deep, x], [x_in.at[0, step_x - 1, deep, 0] for step_x in steps_x])
        if step + 1 < nz:
            z_copy(0, step + 1).start()
        y_copy(1, deep, x).wait_recv()
        add_into(core_sum(deep, y, x, 1), [y_in.at[1, deep, x]])
        if step + 1 < nz:
            z_copy(1, step + 1).start()
    finish_all_to_all(spot, rows, rows_out, row_send, row_recv, local_sem)
    squares = place_rows(rows_out, wanted, table_grad)
    room = rows_out.shape[1]
    small[...] = jnp.sum(rows_out[:, room - 16 : room, :].astype(jnp.float32), axis=0)
    last_small = small[15:16, :]
    for half in range(2):
        for step in range(1, nz):
            z_copy(half, step).wait_recv()

    def finish(block, carry):
        for half in range(2):
            value = summed(half, z)[block].astype(jnp.float32)
            for step in range(nz - 1):
                value = value + z_in[half, step, block].astype(jnp.float32)
            total[half * blocks + block] = value
            carry = carry + jnp.sum(value * value, axis=0, keepdims=True)
        return carry

    others = lax.fori_loop(0, blocks, finish, jnp.zeros((1, shape[2]), jnp.float32))
    lane = lax.broadcasted_iota(jnp.int32, (8, 128), 1)
    sums = jnp.where(lane == 0, jnp.sum(squares), 0.0)
    sums = jnp.where(lane == 1, jnp.sum(others) + jnp.sum(last_small * last_small), sums)
    mine[...] = jnp.where(lane == 2, jnp.sum(loss[...]), sums)
    everyone[spot.rank] = mine[...]

    def tell(step, carry):
        peer = lax.rem(spot.rank + step, spot.count)
        remote(
            mine, everyone.at[spot.rank], sum_send.at[step], sum_recv.at[step], spot.place(peer)
        ).start()
        return carry

    lax.fori_loop(1, spot.count, tell, 0)
    for half, side, column in core_order:
        over_depths(lambda deep: core_copy(deep, side, column, half).wait_send())
    for column in columns + [x]:
        over_depths(lambda deep: y_copy(0, deep, column).wait_send())
    over_depths(lambda deep: y_copy(1, deep, x).wait_send())
    for step in steps_x:
        over_depths(lambda deep: x_copy(0, step, deep, 0).wait_send())
        for side in (1 - y, y):
            over_depths(lambda deep: x_copy(1, step, deep, side).wait_send())
    for half in range(2):
        for step in range(1, nz):
            z_copy(half, step).wait_send()

    def hear(step, carry):
        origin = lax.rem(spot.rank + spot.count - step, spot.count)
        copy = remote(
            mine, everyone.at[origin], sum_send.at[step], sum_recv.at[step], spot.place(origin)
        )
        copy.wait_recv()
        copy.wait_send()
        return carry

    lax.fori_loop(1, spot.count, hear, 0)


def reduce_grads(sizes, rows, pieces, one, wanted, loss, table_shape):
    n_dp, n_head = sizes
    count = n_dp * n_head
    nz, nx = n_dp // 2, n_head // 2
    dma = pltpu.SemaphoreType.DMA
    half = (one[0] // 2,) + one[1:]
    return pl.pallas_call(
        functools.partial(reduce_kernel, sizes),
        in_specs=[pl.BlockSpec(memory_space=pl.ANY)] + [pl.BlockSpec(memory_space=pltpu.VMEM)] * 3,
        out_specs=[pl.BlockSpec(memory_space=pltpu.VMEM)] * 5,
        out_shape=[
            jax.ShapeDtypeStruct(rows.shape, rows.dtype),
            jax.ShapeDtypeStruct(one, jnp.float32),
            jax.ShapeDtypeStruct(table_shape, jnp.float32),
            jax.ShapeDtypeStruct((16, rows.shape[2]), jnp.float32),
            jax.ShapeDtypeStruct((count, 8, 128), jnp.float32),
        ],
        scratch_shapes=[
            pltpu.VMEM((8, 128), jnp.float32),
            dma((count,)),
            dma((count,)),
            pltpu.VMEM((nz, 2, nx) + one, pieces.dtype),
            pltpu.VMEM((2, nz, nx) + half, pieces.dtype),
            pltpu.VMEM((2, nx - 1, nz, 2) + half, pieces.dtype),
            pltpu.VMEM((2, nz - 1) + half, pieces.dtype),
            dma((count,)),
            dma((count,)),
            dma((2, nz, 2, nx)),
            dma((2, nz, 2, nx)),
            dma((2, nz, nx)),
            dma((2, nz, nx)),
            dma((2, nx - 1, nz, 2)),
            dma((2, nx - 1, nz, 2)),
            dma((2, nz - 1)),
            dma((2, nz - 1)),
            dma,
        ],
        compiler_params=pltpu.CompilerParams(
            collective_id=3, has_side_effects=True, vmem_limit_bytes=52 * 2**20
        ),
    )(rows, pieces, wanted, loss)


def stack_blocks(qkv_weight, proj_weight, up_weight, down_weight, position_table):
    depth, width = position_table.shape
    parts = by_part(qkv_weight, qkv_weight.shape[2] // (3 * HD))
    parts = parts.reshape(LAYERS, depth, 3, width).transpose(0, 2, 1, 3).reshape(6, depth, width)
    up_blocks = up_weight.reshape(depth, width // depth, 4, depth).transpose(2, 0, 1, 3)
    return jnp.concatenate(
        [
            parts,
            proj_weight[None],
            position_table[None],
            up_blocks.reshape(4, depth, width),
            down_weight.reshape(4, depth, width),
        ],
        axis=0,
    )


def stack_kernel(qkv_weight, proj_weight, up_weight, down_weight, position_table, shard):
    depth, width = position_table.shape
    heads = width // HD
    for layer in range(LAYERS):
        value = low16(qkv_weight[layer])
        for part in range(3):
            pieces = [
                value[:, (head * 3 + part) * HD : (head * 3 + part) * HD + HD] for head in range(heads)
            ]
            shard[layer * 3 + part] = jnp.concatenate(pieces, axis=1)
    shard[6] = low16(proj_weight[...])
    shard[7] = low16(position_table[...])
    value = low16(up_weight[...])
    for block in range(4):
        starts = [(turn * 4 + block) * depth for turn in range(width // depth)]
        pieces = [value[:, start : start + depth] for start in starts]
        shard[8 + block] = jnp.concatenate(pieces, axis=1)
        shard[12 + block] = low16(down_weight[block * depth : block * depth + depth, :])


def stack_shard(qkv_weight, proj_weight, up_weight, down_weight, position_table):
    depth, width = position_table.shape
    if not is_direct((16, depth, width)):
        blocks = stack_blocks(qkv_weight, proj_weight, up_weight, down_weight, position_table)
        return blocks.astype(jnp.bfloat16)
    vmem = pl.BlockSpec(memory_space=pltpu.VMEM)
    return pl.pallas_call(
        stack_kernel,
        in_specs=[vmem] * 5,
        out_specs=vmem,
        out_shape=jax.ShapeDtypeStruct((16, depth, width), jnp.bfloat16),
    )(qkv_weight, proj_weight, up_weight, down_weight, position_table)


def split_blocks(total):
    depth, width = total.shape[1:]
    parts = total[:6].reshape(LAYERS, 3, depth, width).transpose(0, 2, 1, 3)
    qkv_grad = by_head(parts.reshape(LAYERS, depth, 3 * width), width // HD)
    up_grad = total[8:12].reshape(4, depth, width // depth, depth).transpose(1, 2, 0, 3)
    return (
        total[7],
        qkv_grad,
        total[6:7],
        up_grad.reshape(1, depth, 4 * width),
        total[12:16].reshape(1, 4 * depth, width),
    )


def arrange_gains(gains, n_dp):
    offset = 2 * D
    qkv_bias = by_part(gains[offset : offset + 3 * D], HEADS)
    up_bias = gains[offset + 4 * D : offset + 4 * D + FF].reshape(n_dp, 4, D // n_dp)
    return jnp.concatenate(
        [
            gains[:offset],
            qkv_bias,
            gains[offset + 3 * D : offset + 4 * D],
            up_bias.transpose(1, 0, 2).reshape(-1),
            gains[offset + 4 * D + FF : offset + 9 * D + FF],
            by_part(gains[offset + 9 * D + FF :], HEADS),
        ]
    ).reshape(GAIN_ROWS, D)


def restore_gains(rows, n_dp):
    up_bias = rows[6:10].reshape(4, n_dp, D // n_dp).transpose(1, 0, 2)
    return jnp.concatenate(
        [
            rows[0:2].reshape(-1),
            by_head(rows[2:5].reshape(-1), HEADS),
            rows[5],
            up_bias.reshape(-1),
            rows[10:15].reshape(-1),
            by_head(rows[15:18].reshape(-1), HEADS),
        ]
    )


def gather_teacher(weight):
    width = weight.shape[1]
    order = by_part(jnp.arange(width, dtype=jnp.int32), width // (3 * THD))
    turned = dot(weight, one_hot(order, width).T).astype(jnp.bfloat16)
    return lax.all_gather(turned.reshape(TD, 3, -1).transpose(1, 0, 2), "head", axis=0)


def request_slots(token_ids, shard_rows, count, room, usable):
    here = token_ids.shape[0]
    index = jnp.arange(here, dtype=jnp.int32)
    owner = token_ids // shard_rows
    equal = token_ids[:, None] == token_ids[None, :]
    first = jnp.min(jnp.where(equal, index[:, None], here), axis=0)
    is_first = first == index
    earlier = (owner[:, None] == owner[None, :]) & is_first[:, None] & (index[:, None] < index[None, :])
    order = jnp.sum(earlier.astype(jnp.int32), axis=0)
    overflow = jnp.any(is_first & (order >= usable))
    slot_first = owner * room + order
    chosen = first[None, :] == index[:, None]
    slot = jnp.sum(jnp.where(chosen, slot_first[:, None], 0), axis=0)
    spots = jnp.arange(count * room, dtype=jnp.int32)
    asked = is_first[:, None] & (slot_first[:, None] == spots[None, :]) & (order < usable)[:, None]
    request = jnp.sum(jnp.where(asked, (token_ids % shard_rows)[:, None] + 1, 0), axis=0) - 1
    return slot, request, overflow


def one_hot(index, size):
    return (index[:, None] == jnp.arange(size, dtype=jnp.int32)[None, :]).astype(jnp.bfloat16)


def adam_update(master, first, second, grad_clip, rate):
    first_new = B_ONE * first + (1.0 - B_ONE) * grad_clip
    second_new = B_TWO * second + (1.0 - B_TWO) * grad_clip * grad_clip
    ascent = (
        first_new / (1.0 - B_ONE**STEP) / (jnp.sqrt(second_new / (1.0 - B_TWO**STEP)) + EPSILON)
    )
    return (master - rate * (ascent + DECAY * master), first_new, second_new)


def shards(
    token_ids,
    seq_lengths,
    teacher_hidden,
    teacher_weight,
    token_table,
    token_first,
    token_second,
    position_table,
    position_first,
    position_second,
    qkv_weight,
    qkv_first,
    qkv_second,
    proj_weight,
    proj_first,
    proj_second,
    up_weight,
    up_first,
    up_second,
    down_weight,
    down_first,
    down_second,
    gains_biases,
    gains_first,
    gains_second,
):
    n_dp, n_head = sizes = (lax.axis_size("dp"), lax.axis_size("head"))
    count = n_dp * n_head
    here, shard_rows = token_ids.shape[0], token_table.shape[0]
    room = 16 * -(-3 * here // (2 * count * 16))
    slot, request, overflow = request_slots(token_ids, shard_rows, count, room, room - 1)
    notes = jnp.stack([overflow.astype(jnp.float32), jnp.sum(seq_lengths).astype(jnp.float32)])
    small_size = gains_biases.shape[0]
    small_rows = -(-small_size // 128)
    small_mine = gains_biases.astype(jnp.bfloat16).astype(jnp.float32)
    small_mine = jnp.pad(small_mine, (0, small_rows * 128 - small_size)).reshape(1, small_rows, 128)
    message = jnp.concatenate(
        [
            jnp.pad(
                request.astype(jnp.float32).reshape(count, 1, room), ((0, 0), (0, 0), (0, 128 - room))
            ),
            jnp.broadcast_to(jnp.pad(notes, (0, 126)), (count, 1, 128)),
            jnp.broadcast_to(small_mine, (count, small_rows, 128)),
            jnp.zeros((count, 6 - small_rows, 128), jnp.float32),
        ],
        axis=1,
    )
    shard = stack_shard(qkv_weight, proj_weight[0], up_weight[0], down_weight[0], position_table)
    table_low = token_table.astype(jnp.bfloat16)
    heard, rows_in, big = gather_weights(sizes, message, table_low, shard, room)
    too_many = jnp.any(heard[:, 1, 0] > 0.0)
    valid_total = jnp.sum(heard[:, 1, 1])
    wanted = heard[:, 0, :room].reshape(1, -1).astype(jnp.int32)
    gains = arrange_gains(
        heard[:, 2 : 2 + small_rows].reshape(count, -1)[:, :small_size].reshape(-1), n_dp
    )
    teach_full = gather_teacher(teacher_weight)
    if not is_direct(shard.shape):
        big = big.transpose(2, 0, 3, 1, 4).reshape(16, D, D)

    def owned_rows():
        group_ids = lax.all_gather(token_ids, "head", axis=0, tiled=True)
        block_ids = group_ids // shard_rows
        owned = block_ids % n_head == lax.axis_index("head")
        local = jnp.where(owned, block_ids // n_head * shard_rows + group_ids % shard_rows, 0)
        return owned, local

    def rows_by_owner():
        owned, local = owned_rows()
        rows_all = lax.all_gather(table_low, "dp", axis=0, tiled=True)
        picked = jnp.where(owned[:, None], rows_all[local], jnp.zeros((), jnp.bfloat16))
        rows_here = lax.psum_scatter(picked, "head", scatter_dimension=0, tiled=True)
        return (
            jnp.pad(rows_here, ((0, count * room - here), (0, 0))),
            jnp.arange(here, dtype=jnp.int32),
        )

    rows_used, slot_used = lax.cond(
        too_many, rows_by_owner, lambda: (rows_in.reshape(count * room, D), slot)
    )
    teacher_qkv = project_teacher(teacher_hidden, teach_full)
    final_qkv, *kept = forward_layer(seq_lengths, rows_used, slot_used, big, gains)
    final_grad, loss_part = relation(seq_lengths, final_qkv, teacher_qkv)
    pieces, gain_grads, slot_grads, row_low = backward_layer(
        seq_lengths, slot_used, big, gains, final_grad, kept, count * room
    )
    if not is_direct(shard.shape):
        pieces = pieces.reshape(16, n_dp, shard.shape[1], n_head, shard.shape[2])
        pieces = pieces.transpose(1, 3, 0, 2, 4)
    gain_rows = jnp.pad(
        restore_gains(gain_grads, n_dp).reshape(count, 1, small_size), ((0, 0), (0, 0), (0, D - small_size))
    )
    slot_grads = slot_grads.reshape(count, room, D).at[:, room - 1 :].set(gain_rows.astype(jnp.bfloat16))
    rows_arrived, total, fast_grad, small_sum, everyone = reduce_grads(
        sizes, slot_grads, pieces, shard.shape, wanted, loss_part, token_table.shape
    )
    small_grad = small_sum[15, :small_size]

    def table_by_owner():
        owned, local = owned_rows()
        spread = lax.all_gather(row_low, "head", axis=0, tiled=True)
        table_grad = jax.ops.segment_sum(
            spread.astype(jnp.float32),
            jnp.where(owned, local, n_dp * shard_rows),
            num_segments=n_dp * shard_rows + 1,
        )[:-1]
        table_grad = lax.psum_scatter(
            table_grad.astype(jnp.bfloat16), "dp", scatter_dimension=0, tiled=True
        ).astype(jnp.float32)
        return table_grad, lax.psum(jnp.sum(table_grad * table_grad), ("dp", "head"))

    table_grad, table_squares = lax.cond(
        too_many, table_by_owner, lambda: (fast_grad, jnp.sum(everyone[:, 0, 0]))
    )
    shard_grads = (table_grad,) + split_blocks(total) + (small_grad,)
    square_total = table_squares + jnp.sum(everyone[:, 0, 1])
    loss_total = jnp.sum(everyone[:, 0, 2]) * (LN2 / (3 * REL))
    grad_norm = jnp.sqrt(square_total) / valid_total
    clip_factor = THRESHOLD / jnp.maximum(grad_norm, THRESHOLD)
    factor = clip_factor / valid_total
    token_new = adam_update(
        token_table, token_first, token_second, shard_grads[0] * factor, RATE_TABLE
    )
    position_new = adam_update(
        position_table, position_first, position_second, shard_grads[1] * factor, RATE_TABLE
    )
    qkv_new = adam_update(qkv_weight, qkv_first, qkv_second, shard_grads[2] * factor, RATE_MATRIX)
    proj_new = adam_update(
        proj_weight, proj_first, proj_second, shard_grads[3] * factor, RATE_MATRIX
    )
    up_new = adam_update(up_weight, up_first, up_second, shard_grads[4] * factor, RATE_MATRIX)
    down_new = adam_update(
        down_weight, down_first, down_second, shard_grads[5] * factor, RATE_MATRIX
    )
    gains_new = adam_update(
        gains_biases, gains_first, gains_second, shard_grads[6] * factor, RATE_SMALL
    )
    loss_parts = jnp.stack([loss_total, valid_total])
    return (
        token_new[0],
        token_new[1],
        token_new[2],
        position_new[0],
        position_new[1],
        position_new[2],
        qkv_new[0],
        qkv_new[1],
        qkv_new[2],
        proj_new[0],
        proj_new[1],
        proj_new[2],
        up_new[0],
        up_new[1],
        up_new[2],
        down_new[0],
        down_new[1],
        down_new[2],
        gains_new[0],
        gains_new[1],
        gains_new[2],
        grad_norm,
        loss_parts,
    )


def solution(mesh):
    placed = (
        P(("dp", "head")),
        P(("dp", "head")),
        P(("dp", "head"), None),
        P(None, "head"),
        P(("dp", "head"), None),
        P(("dp", "head"), None),
        P(("dp", "head"), None),
        P("dp", "head"),
        P("dp", "head"),
        P("dp", "head"),
        P(None, "dp", "head"),
        P(None, "dp", "head"),
        P(None, "dp", "head"),
        P(None, "dp", "head"),
        P(None, "dp", "head"),
        P(None, "dp", "head"),
        P(None, "dp", "head"),
        P(None, "dp", "head"),
        P(None, "dp", "head"),
        P(None, "dp", "head"),
        P(None, "dp", "head"),
        P(None, "dp", "head"),
        P(("dp", "head")),
        P(("dp", "head")),
        P(("dp", "head")),
    )
    return jax.shard_map(
        shards,
        mesh=mesh,
        in_specs=placed,
        out_specs=(
            P(("dp", "head"), None),
            P(("dp", "head"), None),
            P(("dp", "head"), None),
            P("dp", "head"),
            P("dp", "head"),
            P("dp", "head"),
            P(None, "dp", "head"),
            P(None, "dp", "head"),
            P(None, "dp", "head"),
            P(None, "dp", "head"),
            P(None, "dp", "head"),
            P(None, "dp", "head"),
            P(None, "dp", "head"),
            P(None, "dp", "head"),
            P(None, "dp", "head"),
            P(None, "dp", "head"),
            P(None, "dp", "head"),
            P(None, "dp", "head"),
            P(("dp", "head")),
            P(("dp", "head")),
            P(("dp", "head")),
            P(),
            P(),
        ),
        check_vma=False,
    )
```

```python
import functools
import math

import jax
import jax.numpy as jnp
from jax import lax
from jax.experimental import pallas as pl
from jax.experimental.pallas import tpu as pltpu
from jax.sharding import PartitionSpec as P

D = 512
HEADS = 8
HD = 64
FF = 2048
TD = 1024
THEADS = 16
THD = 64
REL = 64
LAYERS = 2
LA = 128
LB = 256
LC = 512
M = 1
STEP = 10


B_ONE = 0.9
B_TWO = 0.999
EPSILON = 1e-10
DECAY = 0.01
THRESHOLD = 0.0003
RATE_TABLE = 1.0
RATE_MATRIX = 0.1
RATE_SMALL = 2.0


def dot(left, right, dims=(((1,), (0,)), ((), ()))):
    return lax.dot_general(left, right, dims, preferred_element_type=jnp.float32)


NT = (((1,), (1,)), ((), ()))


LOG2E = 1.4426950408889634
LN2 = 0.6931471805599453
GROUPS = 4
S_WIDE = D // GROUPS
T_WIDE = TD // GROUPS
S_DIM = D // REL
T_DIM = TD // REL
FAST_LIMIT = 60.0
SEQS = ((0, LA), (LA, LA), (2 * LA, LB), (2 * LA + LB, LC))
TOKENS_HERE = 2 * LA + LB + LC
BLOCKS = ((2 * LA + LB, LC, (3,)), (2 * LA, LB, (2,)), (0, 2 * LA, (0, 1)))
AT_ONCE = 4
KEY_ROWS = 128


def relation_kernel(
    lens_ref,
    s_ref,
    t_ref,
    ds_ref,
    loss_ref,
    s_rows,
    t_rows,
    d_rows,
    exp_c,
    exp_b,
    exp_a,
    s_keep,
    t_keep,
):
    @pl.when((pl.program_id(0) == 0) & (pl.program_id(1) == 0))
    def _():
        loss_ref[...] = jnp.zeros_like(loss_ref)
        exp_a[...] = jnp.zeros_like(exp_a)

    s_scale = LOG2E / math.sqrt(S_DIM)
    t_scale = LOG2E / math.sqrt(T_DIM)
    zero = jnp.zeros((), jnp.bfloat16)
    half_heads = 128 // T_DIM
    exps = (exp_c, exp_b, exp_a)

    def valid_rows(block):
        off, length, seqs = BLOCKS[block]
        each = length // len(seqs)
        row = lax.broadcasted_iota(jnp.int32, (length, 128), 0)
        valid = row < 0
        for place, seq in enumerate(seqs):
            start = place * each
            valid = valid | (row >= start) & (row < start + lens_ref[seq])
        return valid

    def prepare(block):
        off, length, seqs = BLOCKS[block]
        each = length // len(seqs)
        lane = lax.broadcasted_iota(jnp.int32, (8, length), 1)
        lane_valid, padded = lane < 0, jnp.zeros((8, length), jnp.float32)
        for place, seq in enumerate(seqs):
            start = place * each
            lane_valid = lane_valid | (lane >= start) & (lane < start + lens_ref[seq])
            padded = jnp.where(lane >= start, (each - lens_ref[seq]).astype(jnp.float32), padded)
        row_valid = valid_rows(block)
        rows = slice(off, off + length)
        s_block = jnp.where(row_valid, s_ref[rows, :], zero).astype(jnp.float32)
        s_keep[rows, :] = (s_block * math.sqrt(s_scale)).astype(jnp.bfloat16)
        s_rows[:, rows] = s_block.T
        for half in range(2):
            cols = slice(half * 128, half * 128 + 128)
            t_block = jnp.where(row_valid, t_ref[rows, cols], zero).astype(jnp.float32)
            t_keep[half, rows, :] = (t_block * math.sqrt(t_scale)).astype(jnp.bfloat16)
            t_rows[cols, rows] = t_block.T
        s_here = s_rows[:, rows]
        t_here = t_rows[:, rows]
        s_square = jnp.sum((s_here * s_here).reshape(16, S_DIM, length), axis=1)
        t_square = jnp.sum((t_here * t_here).reshape(16, T_DIM, length), axis=1)
        bound = jnp.maximum(jnp.max(s_square) * s_scale, jnp.max(t_square) * t_scale)
        return bound, lane_valid.astype(jnp.float32), padded[0:1]

    info = [prepare(block) for block in range(len(BLOCKS))]

    def fold_rows(value):
        total = value[0:8]
        for start in range(8, value.shape[0], 8):
            total = total + value[start : start + 8]
        return total

    def one_head(rows, length, head):
        lane = lax.broadcasted_iota(jnp.int32, (length, 128), 1)
        half = head // half_heads
        s_one = jnp.where(lane // S_DIM == head, s_keep[rows, :], zero)
        t_one = jnp.where(lane // T_DIM == head - half * half_heads, t_keep[half, rows, :], zero)
        return half, s_one, t_one

    def row_slices(head):
        s_slice = pl.ds(pl.multiple_of(head * S_DIM, S_DIM), S_DIM)
        t_slice = pl.ds(pl.multiple_of(head * T_DIM, T_DIM), T_DIM)
        return s_slice, t_slice

    def fill(block, keys, one, target):
        off, length, seqs = BLOCKS[block]
        each = length // len(seqs)
        if len(seqs) > 1:
            scores = dot(keys[...], one, NT)
            sums = []
            for place in range(len(seqs)):
                here = slice(place * each, place * each + each)
                value = jnp.exp2(scores[here, here])
                sums.append(fold_rows(value))
                target[here, here] = value.astype(jnp.bfloat16)
            return jnp.concatenate(sums, axis=1)
        total = jnp.zeros((8, length), jnp.float32)
        for start in range(0, length, KEY_ROWS):
            here = slice(start, start + KEY_ROWS)
            value = jnp.exp2(dot(keys[here, :], one, NT))
            total = total + fold_rows(value)
            target[here, :] = value.astype(jnp.bfloat16)
        return total

    def fill_both(block, head, slot):
        off, length, seqs = BLOCKS[block]
        rows = slice(off, off + length)
        half, s_one, t_one = one_head(rows, length, head)
        return (
            fill(block, s_keep.at[rows, :], s_one, exps[block].at[slot, 0]),
            fill(block, t_keep.at[half, rows, :], t_one, exps[block].at[slot, 1]),
        )

    def use_both(block, head, slot, sums):
        off, length, seqs = BLOCKS[block]
        rows = slice(off, off + length)
        bound, valid_row, padded = info[block]
        s_total = jnp.sum(sums[0], axis=0, keepdims=True) - padded
        t_total = jnp.sum(sums[1], axis=0, keepdims=True) - padded
        s_recip = valid_row / s_total
        t_recip = valid_row / t_total
        s_slice, t_slice = row_slices(head)
        s_vec = s_rows[s_slice, rows]
        t_vec = t_rows[t_slice, rows]
        t_left = jnp.concatenate([s_vec, s_vec * t_recip, t_vec], axis=0).astype(jnp.bfloat16)
        s_left = jnp.concatenate([s_vec, s_vec * s_recip], axis=0).astype(jnp.bfloat16)
        t_out = dot(t_left, exps[block][slot, 1])
        s_out = dot(s_left, exps[block][slot, 0])
        d_rows[s_slice, rows] = (
            s_out[0:8] * s_recip - t_out[0:8] * t_recip + (s_out[8:16] - t_out[8:16]) * valid_row
        )
        inner = t_vec * t_out[16:32]
        inner = (inner[0:8] + inner[8:16]) * t_scale - s_vec * t_out[0:8] * s_scale
        parts = inner * t_recip + (jnp.log2(s_total) - jnp.log2(t_total)) * (valid_row * 0.125)
        return fold_lanes(parts, length)

    def fold_lanes(parts, length):
        total = parts[:, 0:128]
        for start in range(128, length, 128):
            total = total + parts[:, start : start + 128]
        return total

    def fast_heads(step, carry):
        work = [
            (block, step * AT_ONCE + slot, slot)
            for slot in range(AT_ONCE)
            for block in range(len(BLOCKS))
        ]
        sums = [fill_both(*item) for item in work]
        total = jnp.zeros((8, 128), jnp.float32)
        for item, item_sums in zip(work, sums):
            total = total + use_both(*item, item_sums)
        loss_ref[...] += total
        return carry

    def exact_head(seq, head):
        off, length = SEQS[seq]
        rows = slice(off, off + length)
        valid = lens_ref[seq]
        half, s_one, t_one = one_head(rows, length, head)
        s_slice, t_slice = row_slices(head)
        key_valid = lax.broadcasted_iota(jnp.int32, (length, 128), 0) < valid
        exp_c[0, 0, 0:length, 0:128] = s_one
        exp_c[0, 1, 0:length, 0:128] = t_one

        def log_soft(scores, scale):
            scaled = jnp.where(key_valid, scores * scale, -1e30)
            top = jnp.max(scaled, axis=0, keepdims=True)
            shifted = scaled - top
            total = jnp.sum(jnp.exp2(shifted), axis=0, keepdims=True)
            return shifted - jnp.log2(total)

        def queries(block, carry):
            start = pl.multiple_of(block * 128, 128)
            here = pl.ds(start, 128)
            query_valid = lax.broadcasted_iota(jnp.int32, (length, 128), 1) + start < valid
            both = key_valid & query_valid
            s_log = log_soft(dot(s_keep[rows, :], exp_c[0, 0, here, 0:128], NT), s_scale)
            t_log = log_soft(dot(t_keep[half, rows, :], exp_c[0, 1, here, 0:128], NT), t_scale)
            t_soft = jnp.exp2(t_log)
            change = jnp.where(both, jnp.exp2(s_log) - t_soft, 0.0)
            exp_c[1, 0, 0:length, here] = change.astype(jnp.bfloat16)
            loss_ref[...] += fold_rows(jnp.where(both, t_soft * (t_log - s_log), 0.0))
            return carry

        lax.fori_loop(0, length // 128, queries, 0)
        s_vec = s_rows[s_slice, rows]
        left = jnp.concatenate([s_vec, jnp.zeros_like(s_vec)], axis=0).astype(jnp.bfloat16)
        change = exp_c[1, 0, 0:length, 0:length]
        d_rows[s_slice, rows] = (dot(left, change) + dot(left, change, NT))[0:8]

    top_bound = info[0][0]
    for entry in info:
        top_bound = jnp.maximum(top_bound, entry[0])
    fast = top_bound < FAST_LIMIT

    @pl.when(fast)
    def _():
        lax.fori_loop(0, 2 * half_heads // AT_ONCE, fast_heads, 0)

    @pl.when(jnp.logical_not(fast))
    def _():
        for block, (off, length, seqs) in enumerate(BLOCKS):
            rows = slice(off, off + length)
            row_valid = valid_rows(block)
            s_keep[rows, :] = jnp.where(row_valid, s_ref[rows, :], zero)
            for half in range(2):
                t_block = t_ref[rows, half * 128 : half * 128 + 128]
                t_keep[half, rows, :] = jnp.where(row_valid, t_block, zero)
        for seq in range(len(SEQS)):

            def body(head, carry, seq=seq):
                exact_head(seq, head)
                return carry

            lax.fori_loop(0, 2 * half_heads, body, 0)

    for off, length in SEQS:
        ds_ref[off : off + length, :] = (
            d_rows[:, off : off + length].T * (1.0 / math.sqrt(S_DIM) / (3 * REL))
        ).astype(ds_ref.dtype)


def relation(seq_lengths, student, teacher):
    block_s = pl.BlockSpec((None, TOKENS_HERE, S_WIDE), lambda part, group: (part, 0, group))
    block_t = pl.BlockSpec((None, TOKENS_HERE, T_WIDE), lambda part, group: (part, 0, group))
    grads, loss = pl.pallas_call(
        relation_kernel,
        grid=(3, GROUPS),
        in_specs=[pl.BlockSpec(memory_space=pltpu.SMEM), block_s, block_t],
        out_specs=[block_s, pl.BlockSpec((8, 128), lambda part, group: (0, 0))],
        out_shape=[
            jax.ShapeDtypeStruct((3, TOKENS_HERE, D), jnp.bfloat16),
            jax.ShapeDtypeStruct((8, 128), jnp.float32),
        ],
        scratch_shapes=[
            pltpu.VMEM((S_WIDE, TOKENS_HERE), jnp.float32),
            pltpu.VMEM((T_WIDE, TOKENS_HERE), jnp.float32),
            pltpu.VMEM((S_WIDE, TOKENS_HERE), jnp.float32),
            pltpu.VMEM((AT_ONCE, 2, LC, LC), jnp.bfloat16),
            pltpu.VMEM((AT_ONCE, 2, LB, LB), jnp.bfloat16),
            pltpu.VMEM((AT_ONCE, 2, 2 * LA, 2 * LA), jnp.bfloat16),
            pltpu.VMEM((TOKENS_HERE, 128), jnp.bfloat16),
            pltpu.VMEM((2, TOKENS_HERE, 128), jnp.bfloat16),
        ],
        compiler_params=pltpu.CompilerParams(vmem_limit_bytes=48 * 2**20),
    )(seq_lengths, student, teacher)
    return grads, loss


def by_part(columns, heads):
    lead = columns.shape[:-1]
    size = columns.shape[-1] // heads // 3
    shaped = columns.reshape(lead + (heads, 3, size))
    return jnp.moveaxis(shaped, -2, -3).reshape(columns.shape)


def by_head(columns, heads):
    lead = columns.shape[:-1]
    size = columns.shape[-1] // heads // 3
    shaped = columns.reshape(lead + (3, heads, size))
    return jnp.moveaxis(shaped, -2, -3).reshape(columns.shape)


POS_AT = 7
GAIN_ROWS = 18
ERF_TOP = (
    -2.72614225801306e-10,
    2.77068142495902e-08,
    -2.10102402082508e-06,
    -5.69250639462346e-05,
    -7.34990630326855e-04,
    -2.95459980854025e-03,
    -1.60960333262415e-02,
)
ERF_LOW = (
    -1.45660718464996e-05,
    -2.13374055278905e-04,
    -1.68282697438203e-03,
    -7.37332916720468e-03,
    -1.42647390514189e-02,
)
STEP_ROWS = 256


def erf(value):
    value = jnp.clip(value, -4.0, 4.0)
    square = value * value
    top = jnp.full_like(value, ERF_TOP[0])
    for factor in ERF_TOP[1:]:
        top = top * square + factor
    low_part = jnp.full_like(value, ERF_LOW[0])
    for factor in ERF_LOW[1:]:
        low_part = low_part * square + factor
    return value * top / low_part


def normal_cdf(value):
    return 0.5 + 0.5 * erf(value * math.sqrt(0.5))


def normalize(values):
    average = jnp.mean(values, axis=-1, keepdims=True)
    centered = values - average
    variance = jnp.mean(centered * centered, axis=-1, keepdims=True)
    scale = lax.rsqrt(variance + 1e-05)
    return centered * scale, scale


def low16(value):
    return value.astype(jnp.bfloat16)


def step_slice(step):
    return pl.ds(pl.multiple_of(step * STEP_ROWS, STEP_ROWS), STEP_ROWS)


def head_soft(q_pair, k_one, valid, length):
    scores = dot(q_pair, k_one, NT) * (1.0 / math.sqrt(HD))
    lane = lax.broadcasted_iota(jnp.int32, scores.shape, 1)
    scores = jnp.where(lane < valid, scores, -1e30)
    top = jnp.max(scores, axis=-1, keepdims=True)
    value = jnp.exp(scores - top)
    return value / jnp.sum(value, axis=-1, keepdims=True)


def forward_kernel(
    lens_ref,
    rows_ref,
    slot_ref,
    big,
    gains,
    s_out,
    hat0,
    hat1,
    hat2,
    scale0,
    scale1,
    scale2,
    hid_low,
    qkv_low,
    ctx_low,
    mid_low,
    pre_low,
    x_low,
    hidden_kept,
):
    steps = TOKENS_HERE // STEP_ROWS

    def embed(step, carry):
        here = step_slice(step)
        spots = lax.broadcasted_iota(jnp.int32, (STEP_ROWS, rows_ref.shape[0]), 1)
        chosen = low16(jnp.where(slot_ref[here, :] == spots, 1.0, 0.0))
        first = big[POS_AT, 0:STEP_ROWS, :].astype(jnp.float32)
        twice = jnp.concatenate([first[0:LA], first[0:LA]], axis=0)
        late = big[POS_AT, STEP_ROWS : 2 * STEP_ROWS, :].astype(jnp.float32)
        place = jnp.where(step == 0, twice, jnp.where(step == 3, late, first))
        hat, scale = normalize(dot(chosen, rows_ref[...]) + place)
        hat0[here, :] = low16(hat)
        scale0[here, :] = scale
        wide = hat * gains[0:1, :] + gains[1:2, :]
        hidden_kept[here, :] = wide
        hidden = low16(wide)
        hid_low[here, :] = hidden
        for part in range(3):
            qkv_low[part, here, :] = low16(dot(hidden, big[part]) + gains[2 + part : 3 + part, :])
        return carry

    lax.fori_loop(0, steps, embed, 0, unroll=2)
    zero = jnp.zeros((), jnp.bfloat16)

    def attend_pair(pair, carry):
        cols = pl.ds(pl.multiple_of(pair * 128, 128), 128)
        for seq, (off, length) in enumerate(SEQS):
            rows = slice(off, off + length)
            query, key, value = (qkv_low[part, rows, cols] for part in range(3))
            lane = lax.broadcasted_iota(jnp.int32, (length, 128), 1)
            total = jnp.zeros((length, 128), jnp.float32)
            for side in range(2):
                mine = lane // HD == side
                soft = head_soft(query, jnp.where(mine, key, zero), lens_ref[seq], length)
                total = total + dot(low16(soft), jnp.where(mine, value, zero))
            ctx_low[rows, cols] = low16(total)
        return carry

    lax.fori_loop(0, D // 128, attend_pair, 0, unroll=2)

    def rest(step, carry):
        here = step_slice(step)
        hat, scale = normalize(hidden_kept[here, :] + dot(ctx_low[here, :], big[6]) + gains[5:6, :])
        hat1[here, :] = low16(hat)
        scale1[here, :] = scale
        middle = hat * gains[11:12, :] + gains[12:13, :]
        middle_low = low16(middle)
        mid_low[here, :] = middle_low
        output = middle + gains[10:11, :]
        for block in range(4):
            cols = slice(block * D, block * D + D)
            pre = dot(middle_low, big[8 + block]) + gains[6 + block : 7 + block, :]
            act = low16(pre * normal_cdf(pre))
            pre_low[here, cols] = low16(pre)
            output = output + dot(act, big[12 + block])
        hat, scale = normalize(output)
        hat2[here, :] = low16(hat)
        scale2[here, :] = scale
        final = low16(hat * gains[13:14, :] + gains[14:15, :])
        x_low[here, :] = final
        for part in range(3):
            s_out[part, here, :] = low16(dot(final, big[3 + part]) + gains[15 + part : 16 + part, :])
        return carry

    lax.fori_loop(0, steps, rest, 0, unroll=2)


def forward_layer(seq_lengths, rows, slot, big, gains):
    vmem = pl.BlockSpec(memory_space=pltpu.VMEM)
    shape = lambda *dims: jax.ShapeDtypeStruct(dims, jnp.float32)
    half = lambda *dims: jax.ShapeDtypeStruct(dims, jnp.bfloat16)
    tokens = TOKENS_HERE
    outs = [half(3, tokens, D)]
    outs += [half(tokens, D)] * 3 + [shape(tokens, 1)] * 3
    outs += [half(tokens, D), half(3, tokens, D), half(tokens, D), half(tokens, D)]
    outs += [half(tokens, FF), half(tokens, D)]
    return pl.pallas_call(
        forward_kernel,
        in_specs=[pl.BlockSpec(memory_space=pltpu.SMEM)] + [vmem] * 4,
        out_specs=[vmem] * len(outs),
        out_shape=outs,
        scratch_shapes=[pltpu.VMEM((tokens, D), jnp.float32)],
        compiler_params=pltpu.CompilerParams(vmem_limit_bytes=56 * 2**20),
    )(seq_lengths, rows, slot[:, None], big, gains)


def backward_kernel(
    lens_ref,
    slot_ref,
    big,
    gains,
    ds_ref,
    hat0,
    hat1,
    hat2,
    scale0,
    scale1,
    scale2,
    hid_low,
    qkv_low,
    ctx_low,
    mid_low,
    pre_low,
    x_low,
    grads,
    small,
    slot_grads,
    row_low,
    flow,
    flow_low,
    wide_low,
    turned,
    dqkv_low,
    act_low,
):
    steps = TOKENS_HERE // STEP_ROWS
    small[...] = jnp.zeros_like(small)

    def add_small(row, value):
        small[row : row + 1, :] += jnp.sum(value, axis=0, keepdims=True)

    def norm_back(here, grad, hat_ref, scale_ref, row):
        hat = hat_ref[here, :].astype(jnp.float32)
        add_small(row, grad * hat)
        add_small(row + 1, grad)
        inner = grad * gains[row : row + 1, :]
        mean_inner = jnp.mean(inner, axis=-1, keepdims=True)
        mean_hat = jnp.mean(inner * hat, axis=-1, keepdims=True)
        return scale_ref[here, :] * (inner - mean_inner - hat * mean_hat)

    def turn(source, width):
        for start in range(0, TOKENS_HERE, STEP_ROWS):
            turned[0:width, start : start + STEP_ROWS] = source[start : start + STEP_ROWS, 0:width].T

    def weight_grads(pairs):
        for index, right in pairs:
            grads[index] = low16(dot(turned[0:D, :], right))

    def last(step, carry):
        here = step_slice(step)
        grad = jnp.zeros((STEP_ROWS, D), jnp.float32)
        for part in range(3):
            piece = ds_ref[part, here, :]
            add_small(15 + part, piece.astype(jnp.float32))
            grad = grad + dot(piece, big[3 + part], NT)
        grad = norm_back(here, grad, hat2, scale2, 13)
        add_small(10, grad)
        grad_low = low16(grad)
        flow_low[here, :] = grad_low
        total = grad
        for block in range(4):
            cols = slice(block * D, block * D + D)
            pre = pre_low[here, cols].astype(jnp.float32)
            below = normal_cdf(pre)
            act_low[here, cols] = low16(pre * below)
            slope = below + pre * jnp.exp(pre * pre * -0.5) * (1.0 / math.sqrt(2.0 * math.pi))
            inner = dot(grad_low, big[12 + block], NT) * slope
            add_small(6 + block, inner)
            inner_low = low16(inner)
            wide_low[here, cols] = inner_low
            total = total + dot(inner_low, big[8 + block], NT)
        flow[here, :] = total
        return carry

    lax.fori_loop(0, steps, last, 0, unroll=2)
    turn(x_low, D)
    weight_grads([(3 + part, ds_ref[part]) for part in range(3)])
    for block in range(4):
        cols = slice(block * D, block * D + D)
        for start in range(0, TOKENS_HERE, STEP_ROWS):
            turned[:, start : start + STEP_ROWS] = act_low[start : start + STEP_ROWS, cols].T
        weight_grads([(12 + block, flow_low[...])])
    turn(mid_low, D)
    weight_grads([(8 + block, wide_low[:, block * D : block * D + D]) for block in range(4)])

    def middle(step, carry):
        here = step_slice(step)
        grad = norm_back(here, flow[here, :], hat1, scale1, 11)
        add_small(5, grad)
        flow[here, :] = grad
        grad_low = low16(grad)
        flow_low[here, :] = grad_low
        wide_low[here, 0:D] = low16(dot(grad_low, big[6], NT))
        return carry

    lax.fori_loop(0, steps, middle, 0, unroll=2)
    turn(ctx_low, D)
    weight_grads([(6, flow_low[...])])
    zero = jnp.zeros((), jnp.bfloat16)

    def attend_pair(pair, carry):
        cols = pl.ds(pl.multiple_of(pair * 128, 128), 128)
        for seq, (off, length) in enumerate(SEQS):
            rows = slice(off, off + length)
            query, key, value = (qkv_low[part, rows, cols] for part in range(3))
            out_grad = wide_low[rows, cols]
            lane = lax.broadcasted_iota(jnp.int32, (length, 128), 1)
            sums = [jnp.zeros((length, 128), jnp.float32)] * 3
            for side in range(2):
                mine = lane // HD == side
                key_one = jnp.where(mine, key, zero)
                soft = head_soft(query, key_one, lens_ref[seq], length)
                grad_one = jnp.where(mine, out_grad, zero)
                soft_grad = dot(grad_one, value, NT)
                inner = jnp.sum(soft_grad * soft, axis=-1, keepdims=True)
                score_grad = low16((soft_grad - inner) * soft * (1.0 / math.sqrt(HD)))
                query_one = jnp.where(mine, query, zero)
                sums[0] = sums[0] + dot(score_grad, key_one)
                sums[1] = sums[1] + dot(score_grad.T, query_one)
                sums[2] = sums[2] + dot(low16(soft).T, grad_one)
            for part in range(3):
                dqkv_low[part, rows, cols] = low16(sums[part])
        return carry

    lax.fori_loop(0, D // 128, attend_pair, 0, unroll=2)

    def first(step, carry):
        here = step_slice(step)
        grad = flow[here, :]
        for part in range(3):
            piece = dqkv_low[part, here, :]
            add_small(2 + part, piece.astype(jnp.float32))
            grad = grad + dot(piece, big[part], NT)
        grad = norm_back(here, grad, hat0, scale0, 0)
        flow[here, :] = grad
        row_low[here, :] = low16(grad)
        return carry

    lax.fori_loop(0, steps, first, 0, unroll=2)
    turn(hid_low, D)
    weight_grads([(part, dqkv_low[part]) for part in range(3)])
    near = flow[0:LA, :] + flow[LA : 2 * LA, :] + flow[2 * LA : 3 * LA, :] + flow[4 * LA : 5 * LA, :]
    grads[POS_AT, 0:LA, :] = low16(near)
    grads[POS_AT, LA:LB, :] = low16(flow[3 * LA : 4 * LA, :] + flow[5 * LA : 6 * LA, :])
    grads[POS_AT, LB:LC, :] = low16(flow[2 * LA + LB + LB :, :])
    places = slot_grads.shape[0]
    size = 512 if places % 512 == 0 else places

    def spread(block, carry):
        start = pl.multiple_of(block * size, size)
        spots = lax.broadcasted_iota(jnp.int32, (size, TOKENS_HERE), 0) + start
        chosen = low16(jnp.where(slot_ref[...] == spots, 1.0, 0.0))
        slot_grads[pl.ds(start, size), :] = low16(dot(chosen, row_low[...]))
        return carry

    lax.fori_loop(0, places // size, spread, 0)


def backward_layer(seq_lengths, slot, big, gains, final_grad, kept, places):
    vmem = pl.BlockSpec(memory_space=pltpu.VMEM)
    half = lambda *dims: jax.ShapeDtypeStruct(dims, jnp.bfloat16)
    tokens = TOKENS_HERE
    return pl.pallas_call(
        backward_kernel,
        in_specs=[pl.BlockSpec(memory_space=pltpu.SMEM)] + [vmem] * (4 + len(kept)),
        out_specs=[vmem] * 4,
        out_shape=[
            half(16, D, D),
            jax.ShapeDtypeStruct((GAIN_ROWS, D), jnp.float32),
            half(places, D),
            half(tokens, D),
        ],
        scratch_shapes=[
            pltpu.VMEM((tokens, D), jnp.float32),
            pltpu.VMEM((tokens, D), jnp.bfloat16),
            pltpu.VMEM((tokens, FF), jnp.bfloat16),
            pltpu.VMEM((D, tokens), jnp.bfloat16),
            pltpu.VMEM((3, tokens, D), jnp.bfloat16),
            pltpu.VMEM((tokens, FF), jnp.bfloat16),
        ],
        compiler_params=pltpu.CompilerParams(vmem_limit_bytes=60 * 2**20),
    )(seq_lengths, slot[None, :], big, gains, final_grad, *kept)


def teacher_kernel(hidden, weight, out):
    out[...] = low16(dot(hidden[...], weight[...]))


def project_teacher(hidden, weight):
    tokens = hidden.shape[0]
    owners, parts, depth, width = weight.shape
    return pl.pallas_call(
        teacher_kernel,
        grid=(parts, owners),
        in_specs=[
            pl.BlockSpec((tokens, depth), lambda part, owner: (0, 0)),
            pl.BlockSpec((None, None, depth, width), lambda part, owner: (owner, part, 0, 0)),
        ],
        out_specs=pl.BlockSpec((None, tokens, width), lambda part, owner: (part, 0, owner)),
        out_shape=jax.ShapeDtypeStruct((parts, tokens, owners * width), jnp.bfloat16),
        compiler_params=pltpu.CompilerParams(vmem_limit_bytes=32 * 2**20),
    )(hidden, weight)


MESH_IDS = pl.DeviceIdType.MESH


def barrier_all(rank, count, place):
    barrier = pltpu.get_barrier_semaphore()

    def greet(step, carry):
        pl.semaphore_signal(
            barrier, inc=1, device_id=place(lax.rem(rank + step, count)), device_id_type=MESH_IDS
        )
        return carry

    lax.fori_loop(1, count, greet, 0)
    pl.semaphore_wait(barrier, count - 1)


class Spot:
    def __init__(self, n_dp, n_head):
        self.n_dp, self.n_head = n_dp, n_head
        self.count = n_dp * n_head
        self.nz, self.nx = n_dp // 2, n_head // 2
        dp, head = lax.axis_index("dp"), lax.axis_index("head")
        self.rank = dp * n_head + head
        self.z, self.y = dp // 2, lax.rem(dp, 2)
        self.x, self.c = head // 2, lax.rem(head, 2)

    def place(self, rank):
        return (rank // self.n_head, lax.rem(rank, self.n_head))

    def device(self, z, y, x, c):
        return (z * 2 + y, x * 2 + c)


def remote(source, target, send_sem, recv_sem, device):
    return pltpu.make_async_remote_copy(
        src_ref=source,
        dst_ref=target,
        send_sem=send_sem,
        recv_sem=recv_sem,
        device_id=device,
        device_id_type=MESH_IDS,
    )


def start_all_to_all(spot, source, target, send_sems, recv_sems, local_sem):
    pltpu.make_async_copy(source.at[spot.rank], target.at[spot.rank], local_sem).start()

    def send(step, carry):
        peer = lax.rem(spot.rank + step, spot.count)
        remote(
            source.at[peer], target.at[spot.rank], send_sems.at[step], recv_sems.at[step], spot.place(peer)
        ).start()
        return carry

    lax.fori_loop(1, spot.count, send, 0)


def finish_all_to_all(spot, source, target, send_sems, recv_sems, local_sem):
    def take(step, carry):
        origin = lax.rem(spot.rank + spot.count - step, spot.count)
        copy = remote(
            source.at[origin], target.at[origin], send_sems.at[step], recv_sems.at[step], spot.place(origin)
        )
        copy.wait_recv()
        copy.wait_send()
        return carry

    lax.fori_loop(1, spot.count, take, 0)
    pltpu.make_async_copy(source.at[spot.rank], target.at[spot.rank], local_sem).wait()


def is_direct(shape):
    return shape[1] % 16 == 0 and shape[2] % 128 == 0


def piece_of(whole, shape, dp, head, half):
    blocks = pl.ds(half * (shape[0] // 2), shape[0] // 2)
    if not is_direct(shape):
        return whole.at[dp, head, blocks]
    rows = pl.ds(pl.multiple_of(dp * shape[1], shape[1]), shape[1])
    return whole.at[blocks, rows, pl.ds(pl.multiple_of(head * shape[2], shape[2]), shape[2])]


def whole_shape(sizes, shape):
    if not is_direct(shape):
        return sizes + shape
    return (shape[0], sizes[0] * shape[1], sizes[1] * shape[2])


def answer(heard, table, rows, at_once):
    count, room = rows.shape[:2]
    spare = -count % 128
    asked = heard[:, 0, :]
    if spare:
        asked = jnp.concatenate([asked, jnp.full((spare, 128), -1.0, jnp.float32)], axis=0)
    turned = asked.T
    lane = lax.broadcasted_iota(jnp.int32, (room, count + spare), 1)
    spots = lax.broadcasted_iota(jnp.int32, (at_once * room, table.shape[0]), 1)

    def some(step, carry):
        columns = []
        for place in range(at_once):
            mine = lane == step * at_once + place
            columns.append(jnp.sum(jnp.where(mine, turned[0:room, :], 0.0), axis=1, keepdims=True))
        wanted = jnp.concatenate(columns, axis=0).astype(jnp.int32)
        chosen = low16(jnp.where(wanted == spots, 1.0, 0.0))
        found = low16(dot(chosen, table[...]))
        for place in range(at_once):
            rows[step * at_once + place] = found[place * room : place * room + room]
        return carry

    lax.fori_loop(0, count // at_once, some, 0)


def gather_kernel(
    sizes,
    messages,
    table,
    shard,
    heard,
    rows_out,
    full,
    rows,
    message_send,
    message_recv,
    row_send,
    row_recv,
    piece_send,
    piece_recv,
    local_sems,
):
    spot = Spot(*sizes)
    z, y, x, c, nz, nx = spot.z, spot.y, spot.x, spot.c, spot.nz, spot.nx
    barrier_all(spot.rank, spot.count, spot.place)
    sends = []

    def spot_of(piece, half):
        return piece_of(full, shard.shape, piece[0] * 2 + piece[1], piece[2] * 2 + piece[3], half)

    def arrival(piece, half):
        return piece_recv.at[half, piece[0] * 2 + piece[1], piece[2] * 2 + piece[3]]

    def send_piece(source, piece, half, device):
        copy = remote(
            source, spot_of(piece, half), piece_send.at[len(sends)], arrival(piece, half), device
        )
        copy.start()
        sends.append(copy)

    def wait_piece(piece, half):
        here = spot_of(piece, half)
        remote(
            here, here, piece_send.at[0], arrival(piece, half), spot.device(z, y, x, 1 - c)
        ).wait_recv()
        return here

    own = (z, y, x, c)
    own_halves = [shard.at[pl.ds(half * (shard.shape[0] // 2), shard.shape[0] // 2)] for half in range(2)]
    own_copies = [
        pltpu.make_async_copy(own_halves[half], spot_of(own, half), local_sems.at[half]) for half in range(2)
    ]
    for copy in own_copies:
        copy.start()
    start_all_to_all(spot, messages, heard, message_send, message_recv, local_sems.at[2])
    others_x = [lax.rem(x + step, nx) for step in range(1, nx)]
    sibling, opposite = spot.device(z, y, x, 1 - c), spot.device(z, 1 - y, x, c)
    across = [spot.device(z, y, other, c) for other in others_x]
    for half in range(2):
        for step in range(1, nz):
            send_piece(own_halves[half], own, half, spot.device(lax.rem(z + step, nz), y, x, c))
    for half in range(2):
        for device in across + [opposite, sibling]:
            send_piece(own_halves[half], own, half, device)
    finish_all_to_all(spot, messages, heard, message_send, message_recv, local_sems.at[2])
    answer(heard, table, rows, 8)
    start_all_to_all(spot, rows, rows_out, row_send, row_recv, local_sems.at[3])
    depths = [lax.rem(z + nz - step, nz) for step in range(nz)]

    def pass_on(piece, half, devices):
        here = wait_piece(piece, half)
        for device in devices:
            send_piece(here, piece, half, device)

    for deep in depths[1:]:
        for half in range(2):
            pass_on((deep, y, x, c), half, across + [opposite, sibling])
    for deep in depths:
        for other in others_x:
            pass_on((deep, y, other, c), 0, [opposite, sibling])
        pass_on((deep, 1 - y, x, c), 1, across + [sibling])
    for deep in depths:
        for column in [x] + others_x:
            pass_on((deep, 1 - y, column, c), 0, [sibling])
        for other in others_x:
            for side in (y, 1 - y):
                pass_on((deep, side, other, c), 1, [sibling])
    for deep in depths:
        for side in (y, 1 - y):
            for column in [x] + others_x:
                for half in range(2):
                    wait_piece((deep, side, column, 1 - c), half)
    for copy in sends:
        copy.wait_send()
    finish_all_to_all(spot, rows, rows_out, row_send, row_recv, local_sems.at[3])
    for copy in own_copies:
        copy.wait()


def gather_weights(sizes, messages, table, shard, room):
    n_dp, n_head = sizes
    count = n_dp * n_head
    nz, nx = n_dp // 2, n_head // 2
    sends = 2 * (nz - 1) + 2 * nz * (nx + 1) + nz * (nx - 1) * 2 + nz * nx + nz * nx + 2 * nz * (nx - 1)
    anywhere = pl.BlockSpec(memory_space=pl.ANY)
    vmem = pl.BlockSpec(memory_space=pltpu.VMEM)
    dma = pltpu.SemaphoreType.DMA
    rows_shape = (count, room, table.shape[1])
    return pl.pallas_call(
        functools.partial(gather_kernel, sizes),
        in_specs=[vmem, vmem, anywhere],
        out_specs=[vmem, anywhere, anywhere],
        out_shape=[
            jax.ShapeDtypeStruct(messages.shape, messages.dtype),
            jax.ShapeDtypeStruct(rows_shape, table.dtype),
            jax.ShapeDtypeStruct(whole_shape(sizes, shard.shape), shard.dtype),
        ],
        scratch_shapes=[
            pltpu.VMEM(rows_shape, table.dtype),
            dma((count,)),
            dma((count,)),
            dma((count,)),
            dma((count,)),
            dma((sends,)),
            dma((2, n_dp, n_head)),
            dma((4,)),
        ],
        compiler_params=pltpu.CompilerParams(
            collective_id=2, has_side_effects=True, vmem_limit_bytes=40 * 2**20
        ),
    )(messages, table, shard)


def table_rows_at_once(rows):
    sizes = [size for size in range(8, 265, 8) if rows % size == 0]
    return max(sizes) if sizes and rows > 264 else rows


def place_rows(rows, wanted, table_grad):
    count, room, width = rows.shape
    at_once = table_rows_at_once(table_grad.shape[0])
    arrived = rows[...].reshape(count * room, width)

    def some(step, squares):
        start = step * at_once
        if at_once % 8 == 0:
            start = pl.multiple_of(start, 8)
        spots = lax.broadcasted_iota(jnp.int32, (at_once, count * room), 0) + start
        chosen = low16(jnp.where(wanted[...] == spots, 1.0, 0.0))
        value = dot(chosen, arrived)
        table_grad[pl.ds(start, at_once), :] = value
        return squares + jnp.sum(value * value, axis=0, keepdims=True)

    zero = jnp.zeros((1, width), jnp.float32)
    return lax.fori_loop(0, table_grad.shape[0] // at_once, some, zero)


def reduce_kernel(
    sizes,
    rows,
    pieces,
    wanted,
    loss,
    rows_out,
    total,
    table_grad,
    small,
    everyone,
    mine,
    sum_send,
    sum_recv,
    core_in,
    y_in,
    x_in,
    z_in,
    row_send,
    row_recv,
    core_send,
    core_recv,
    y_send,
    y_recv,
    x_send,
    x_recv,
    z_send,
    z_recv,
    local_sem,
):
    spot = Spot(*sizes)
    z, y, x, c, nz, nx = spot.z, spot.y, spot.x, spot.c, spot.nz, spot.nx
    shape = total.shape
    blocks = shape[0] // 2
    barrier_all(spot.rank, spot.count, spot.place)
    sibling = spot.device(z, y, x, 1 - c)
    opposite = spot.device(z, 1 - y, x, c)

    def core_sum(deep, side, column, half):
        return core_in.at[deep, side, column, pl.ds(half * blocks, blocks)]

    def core_copy(deep, side, column, half):
        return remote(
            piece_of(pieces, shape, deep * 2 + side, column * 2 + 1 - c, half),
            core_sum(deep, side, column, half),
            core_send.at[half, deep, side, column],
            core_recv.at[half, deep, side, column],
            sibling,
        )

    def y_copy(half, deep, column):
        return remote(
            core_sum(deep, 1 - y, column, half),
            y_in.at[half, deep, column],
            y_send.at[half, deep, column],
            y_recv.at[half, deep, column],
            opposite,
        )

    def x_copy(half, step, deep, side):
        column = lax.rem(x + step, nx)
        source = y_in.at[0, deep, column] if half == 0 else core_sum(deep, side, column, 1)
        return remote(
            source,
            x_in.at[half, step - 1, deep, side],
            x_send.at[half, step - 1, deep, side],
            x_recv.at[half, step - 1, deep, side],
            spot.device(z, y, column, c),
        )

    def summed(half, deep):
        return y_in.at[0, deep, x] if half == 0 else core_sum(deep, y, x, 1)

    def z_copy(half, step):
        deep = lax.rem(z + step, nz)
        return remote(
            summed(half, deep),
            z_in.at[half, step - 1],
            z_send.at[half, step - 1],
            z_recv.at[half, step - 1],
            spot.device(deep, y, x, c),
        )

    def add_into(target, sources):
        def some(block, carry):
            value = target[block].astype(jnp.float32)
            for source in sources:
                value = value + source[block].astype(jnp.float32)
            target[block] = value.astype(target.dtype)
            return carry

        lax.fori_loop(0, blocks, some, 0)

    def over_depths(action):
        def one(step, carry):
            action(lax.rem(z + 1 + step, nz))
            return carry

        lax.fori_loop(0, nz, one, 0)

    steps_x = list(range(1, nx))
    columns = [lax.rem(x + step, nx) for step in steps_x]
    core_order = [(0, 1 - y, column) for column in columns + [x]]
    core_order += [(1, side, column) for column in columns for side in (1 - y, y)]
    core_order += [(0, y, column) for column in columns + [x]]
    core_order += [(1, side, x) for side in (1 - y, y)]
    for half, side, column in core_order:
        over_depths(lambda deep: core_copy(deep, side, column, half).start())
    start_all_to_all(spot, rows, rows_out, row_send, row_recv, local_sem)

    def take_core(deep, side, column, half):
        core_copy(deep, side, column, half).wait_recv()
        own = piece_of(pieces, shape, deep * 2 + side, column * 2 + c, half)
        add_into(core_sum(deep, side, column, half), [own])

    def core_then_y(deep, column):
        take_core(deep, 1 - y, column, 0)
        y_copy(0, deep, column).start()

    def core_then_x(deep, step, side):
        take_core(deep, side, lax.rem(x + step, nx), 1)
        x_copy(1, step, deep, side).start()

    def take_y(deep, column):
        y_copy(0, deep, column).wait_recv()
        add_into(y_in.at[0, deep, column], [core_sum(deep, y, column, 0)])

    def take_x(deep, side):
        for step in steps_x:
            x_copy(1, step, deep, side).wait_recv()
        add_into(core_sum(deep, side, x, 1), [x_in.at[1, step - 1, deep, side] for step in steps_x])

    def y_then_x(deep, step):
        take_y(deep, lax.rem(x + step, nx))
        x_copy(0, step, deep, 0).start()

    def x_then_y(deep):
        take_x(deep, 1 - y)
        y_copy(1, deep, x).start()

    for column in columns + [x]:
        over_depths(lambda deep: core_then_y(deep, column))
    for step in steps_x:
        for side in (1 - y, y):
            over_depths(lambda deep: core_then_x(deep, step, side))
    for column in columns + [x]:
        over_depths(lambda deep: take_core(deep, y, column, 0))
    for side in (1 - y, y):
        over_depths(lambda deep: take_core(deep, side, x, 1))
    for step in steps_x:
        over_depths(lambda deep: y_then_x(deep, step))
    over_depths(x_then_y)
    over_depths(lambda deep: take_y(deep, x))
    over_depths(lambda deep: take_x(deep, y))
    for step in range(nz):
        deep = lax.rem(z + 1 + step, nz)
        for step_x in steps_x:
            x_copy(0, step_x, deep, 0).wait_recv()
        add_into(y_in.at[0, deep, x], [x_in.at[0, step_x - 1, deep, 0] for step_x in steps_x])
        if step + 1 < nz:
            z_copy(0, step + 1).start()
        y_copy(1, deep, x).wait_recv()
        add_into(core_sum(deep, y, x, 1), [y_in.at[1, deep, x]])
        if step + 1 < nz:
            z_copy(1, step + 1).start()
    finish_all_to_all(spot, rows, rows_out, row_send, row_recv, local_sem)
    squares = place_rows(rows_out, wanted, table_grad)
    room = rows_out.shape[1]
    small[...] = jnp.sum(rows_out[:, room - 16 : room, :].astype(jnp.float32), axis=0)
    last_small = small[15:16, :]
    for half in range(2):
        for step in range(1, nz):
            z_copy(half, step).wait_recv()

    def finish(block, carry):
        for half in range(2):
            value = summed(half, z)[block].astype(jnp.float32)
            for step in range(nz - 1):
                value = value + z_in[half, step, block].astype(jnp.float32)
            total[half * blocks + block] = value
            carry = carry + jnp.sum(value * value, axis=0, keepdims=True)
        return carry

    others = lax.fori_loop(0, blocks, finish, jnp.zeros((1, shape[2]), jnp.float32))
    lane = lax.broadcasted_iota(jnp.int32, (8, 128), 1)
    sums = jnp.where(lane == 0, jnp.sum(squares), 0.0)
    sums = jnp.where(lane == 1, jnp.sum(others) + jnp.sum(last_small * last_small), sums)
    mine[...] = jnp.where(lane == 2, jnp.sum(loss[...]), sums)
    everyone[spot.rank] = mine[...]

    def tell(step, carry):
        peer = lax.rem(spot.rank + step, spot.count)
        remote(
            mine, everyone.at[spot.rank], sum_send.at[step], sum_recv.at[step], spot.place(peer)
        ).start()
        return carry

    lax.fori_loop(1, spot.count, tell, 0)
    for half, side, column in core_order:
        over_depths(lambda deep: core_copy(deep, side, column, half).wait_send())
    for column in columns + [x]:
        over_depths(lambda deep: y_copy(0, deep, column).wait_send())
    over_depths(lambda deep: y_copy(1, deep, x).wait_send())
    for step in steps_x:
        over_depths(lambda deep: x_copy(0, step, deep, 0).wait_send())
        for side in (1 - y, y):
            over_depths(lambda deep: x_copy(1, step, deep, side).wait_send())
    for half in range(2):
        for step in range(1, nz):
            z_copy(half, step).wait_send()

    def hear(step, carry):
        origin = lax.rem(spot.rank + spot.count - step, spot.count)
        copy = remote(
            mine, everyone.at[origin], sum_send.at[step], sum_recv.at[step], spot.place(origin)
        )
        copy.wait_recv()
        copy.wait_send()
        return carry

    lax.fori_loop(1, spot.count, hear, 0)


def reduce_grads(sizes, rows, pieces, one, wanted, loss, table_shape):
    n_dp, n_head = sizes
    count = n_dp * n_head
    nz, nx = n_dp // 2, n_head // 2
    dma = pltpu.SemaphoreType.DMA
    half = (one[0] // 2,) + one[1:]
    return pl.pallas_call(
        functools.partial(reduce_kernel, sizes),
        in_specs=[pl.BlockSpec(memory_space=pl.ANY)] + [pl.BlockSpec(memory_space=pltpu.VMEM)] * 3,
        out_specs=[pl.BlockSpec(memory_space=pltpu.VMEM)] * 5,
        out_shape=[
            jax.ShapeDtypeStruct(rows.shape, rows.dtype),
            jax.ShapeDtypeStruct(one, jnp.float32),
            jax.ShapeDtypeStruct(table_shape, jnp.float32),
            jax.ShapeDtypeStruct((16, rows.shape[2]), jnp.float32),
            jax.ShapeDtypeStruct((count, 8, 128), jnp.float32),
        ],
        scratch_shapes=[
            pltpu.VMEM((8, 128), jnp.float32),
            dma((count,)),
            dma((count,)),
            pltpu.VMEM((nz, 2, nx) + one, pieces.dtype),
            pltpu.VMEM((2, nz, nx) + half, pieces.dtype),
            pltpu.VMEM((2, nx - 1, nz, 2) + half, pieces.dtype),
            pltpu.VMEM((2, nz - 1) + half, pieces.dtype),
            dma((count,)),
            dma((count,)),
            dma((2, nz, 2, nx)),
            dma((2, nz, 2, nx)),
            dma((2, nz, nx)),
            dma((2, nz, nx)),
            dma((2, nx - 1, nz, 2)),
            dma((2, nx - 1, nz, 2)),
            dma((2, nz - 1)),
            dma((2, nz - 1)),
            dma,
        ],
        compiler_params=pltpu.CompilerParams(
            collective_id=3, has_side_effects=True, vmem_limit_bytes=52 * 2**20
        ),
    )(rows, pieces, wanted, loss)


def stack_blocks(qkv_weight, proj_weight, up_weight, down_weight, position_table):
    depth, width = position_table.shape
    parts = by_part(qkv_weight, qkv_weight.shape[2] // (3 * HD))
    parts = parts.reshape(LAYERS, depth, 3, width).transpose(0, 2, 1, 3).reshape(6, depth, width)
    up_blocks = up_weight.reshape(depth, width // depth, 4, depth).transpose(2, 0, 1, 3)
    return jnp.concatenate(
        [
            parts,
            proj_weight[None],
            position_table[None],
            up_blocks.reshape(4, depth, width),
            down_weight.reshape(4, depth, width),
        ],
        axis=0,
    )


def stack_kernel(qkv_weight, proj_weight, up_weight, down_weight, position_table, shard):
    depth, width = position_table.shape
    heads = width // HD
    for layer in range(LAYERS):
        value = low16(qkv_weight[layer])
        for part in range(3):
            pieces = [
                value[:, (head * 3 + part) * HD : (head * 3 + part) * HD + HD] for head in range(heads)
            ]
            shard[layer * 3 + part] = jnp.concatenate(pieces, axis=1)
    shard[6] = low16(proj_weight[...])
    shard[7] = low16(position_table[...])
    value = low16(up_weight[...])
    for block in range(4):
        starts = [(turn * 4 + block) * depth for turn in range(width // depth)]
        pieces = [value[:, start : start + depth] for start in starts]
        shard[8 + block] = jnp.concatenate(pieces, axis=1)
        shard[12 + block] = low16(down_weight[block * depth : block * depth + depth, :])


def stack_shard(qkv_weight, proj_weight, up_weight, down_weight, position_table):
    depth, width = position_table.shape
    if not is_direct((16, depth, width)):
        blocks = stack_blocks(qkv_weight, proj_weight, up_weight, down_weight, position_table)
        return blocks.astype(jnp.bfloat16)
    vmem = pl.BlockSpec(memory_space=pltpu.VMEM)
    return pl.pallas_call(
        stack_kernel,
        in_specs=[vmem] * 5,
        out_specs=vmem,
        out_shape=jax.ShapeDtypeStruct((16, depth, width), jnp.bfloat16),
    )(qkv_weight, proj_weight, up_weight, down_weight, position_table)


def split_blocks(total):
    depth, width = total.shape[1:]
    parts = total[:6].reshape(LAYERS, 3, depth, width).transpose(0, 2, 1, 3)
    qkv_grad = by_head(parts.reshape(LAYERS, depth, 3 * width), width // HD)
    up_grad = total[8:12].reshape(4, depth, width // depth, depth).transpose(1, 2, 0, 3)
    return (
        total[7],
        qkv_grad,
        total[6:7],
        up_grad.reshape(1, depth, 4 * width),
        total[12:16].reshape(1, 4 * depth, width),
    )


def arrange_gains(gains, n_dp):
    offset = 2 * D
    qkv_bias = by_part(gains[offset : offset + 3 * D], HEADS)
    up_bias = gains[offset + 4 * D : offset + 4 * D + FF].reshape(n_dp, 4, D // n_dp)
    return jnp.concatenate(
        [
            gains[:offset],
            qkv_bias,
            gains[offset + 3 * D : offset + 4 * D],
            up_bias.transpose(1, 0, 2).reshape(-1),
            gains[offset + 4 * D + FF : offset + 9 * D + FF],
            by_part(gains[offset + 9 * D + FF :], HEADS),
        ]
    ).reshape(GAIN_ROWS, D)


def restore_gains(rows, n_dp):
    up_bias = rows[6:10].reshape(4, n_dp, D // n_dp).transpose(1, 0, 2)
    return jnp.concatenate(
        [
            rows[0:2].reshape(-1),
            by_head(rows[2:5].reshape(-1), HEADS),
            rows[5],
            up_bias.reshape(-1),
            rows[10:15].reshape(-1),
            by_head(rows[15:18].reshape(-1), HEADS),
        ]
    )


def gather_teacher(weight):
    width = weight.shape[1]
    order = by_part(jnp.arange(width, dtype=jnp.int32), width // (3 * THD))
    turned = dot(weight, one_hot(order, width).T).astype(jnp.bfloat16)
    return lax.all_gather(turned.reshape(TD, 3, -1).transpose(1, 0, 2), "head", axis=0)


def request_slots(token_ids, shard_rows, count, room, usable):
    here = token_ids.shape[0]
    index = jnp.arange(here, dtype=jnp.int32)
    owner = token_ids // shard_rows
    equal = token_ids[:, None] == token_ids[None, :]
    first = jnp.min(jnp.where(equal, index[:, None], here), axis=0)
    is_first = first == index
    earlier = (owner[:, None] == owner[None, :]) & is_first[:, None] & (index[:, None] < index[None, :])
    order = jnp.sum(earlier.astype(jnp.int32), axis=0)
    overflow = jnp.any(is_first & (order >= usable))
    slot_first = owner * room + order
    chosen = first[None, :] == index[:, None]
    slot = jnp.sum(jnp.where(chosen, slot_first[:, None], 0), axis=0)
    spots = jnp.arange(count * room, dtype=jnp.int32)
    asked = is_first[:, None] & (slot_first[:, None] == spots[None, :]) & (order < usable)[:, None]
    request = jnp.sum(jnp.where(asked, (token_ids % shard_rows)[:, None] + 1, 0), axis=0) - 1
    return slot, request, overflow


def one_hot(index, size):
    return (index[:, None] == jnp.arange(size, dtype=jnp.int32)[None, :]).astype(jnp.bfloat16)


def adam_update(master, first, second, grad_clip, rate):
    first_new = B_ONE * first + (1.0 - B_ONE) * grad_clip
    second_new = B_TWO * second + (1.0 - B_TWO) * grad_clip * grad_clip
    ascent = (
        first_new / (1.0 - B_ONE**STEP) / (jnp.sqrt(second_new / (1.0 - B_TWO**STEP)) + EPSILON)
    )
    return (master - rate * (ascent + DECAY * master), first_new, second_new)


def update_kernel(factor_ref, total, *refs):
    sources, targets = refs[:15], refs[15:]
    factor = factor_ref[0, 0]
    depth, width = total.shape[1:]
    heads = width // HD

    def apply(index, rate, grad, at):
        values = [ref[at] for ref in sources[index * 3 : index * 3 + 3]]
        for target, value in zip(
            targets[index * 3 : index * 3 + 3], adam_update(*values, grad * factor, rate)
        ):
            target[at] = value

    apply(0, RATE_TABLE, total[7], ...)
    for layer in range(LAYERS):
        parts = [total[layer * 3 + part] for part in range(3)]
        columns = [
            parts[part][:, head * HD : head * HD + HD] for head in range(heads) for part in range(3)
        ]
        apply(1, RATE_MATRIX, jnp.concatenate(columns, axis=1), layer)
    apply(2, RATE_MATRIX, total[6], 0)
    blocks = [total[8 + block] for block in range(4)]
    columns = [
        blocks[block][:, turn * depth : turn * depth + depth]
        for turn in range(width // depth)
        for block in range(4)
    ]
    apply(3, RATE_MATRIX, jnp.concatenate(columns, axis=1), 0)
    for block in range(4):
        rows = slice(block * depth, block * depth + depth)
        apply(4, RATE_MATRIX, total[12 + block], (0, rows))


def update_blocks(factor, total, groups):
    arrays = [array for group in groups for array in group]
    if not is_direct(total.shape):
        rates = [RATE_TABLE] + [RATE_MATRIX] * 4
        grads = split_blocks(total)
        return [
            adam_update(*group, grad * factor, rate) for group, grad, rate in zip(groups, grads, rates)
        ]
    vmem = pl.BlockSpec(memory_space=pltpu.VMEM)
    outs = pl.pallas_call(
        update_kernel,
        in_specs=[pl.BlockSpec(memory_space=pltpu.SMEM)] + [vmem] * 16,
        out_specs=[vmem] * 15,
        out_shape=[jax.ShapeDtypeStruct(array.shape, array.dtype) for array in arrays],
    )(factor.reshape(1, 1), total, *arrays)
    return [tuple(outs[start : start + 3]) for start in range(0, 15, 3)]


def shards(
    token_ids,
    seq_lengths,
    teacher_hidden,
    teacher_weight,
    token_table,
    token_first,
    token_second,
    position_table,
    position_first,
    position_second,
    qkv_weight,
    qkv_first,
    qkv_second,
    proj_weight,
    proj_first,
    proj_second,
    up_weight,
    up_first,
    up_second,
    down_weight,
    down_first,
    down_second,
    gains_biases,
    gains_first,
    gains_second,
):
    n_dp, n_head = sizes = (lax.axis_size("dp"), lax.axis_size("head"))
    count = n_dp * n_head
    here, shard_rows = token_ids.shape[0], token_table.shape[0]
    room = 16 * -(-3 * here // (2 * count * 16))
    slot, request, overflow = request_slots(token_ids, shard_rows, count, room, room - 1)
    notes = jnp.stack([overflow.astype(jnp.float32), jnp.sum(seq_lengths).astype(jnp.float32)])
    small_size = gains_biases.shape[0]
    small_rows = -(-small_size // 128)
    small_mine = gains_biases.astype(jnp.bfloat16).astype(jnp.float32)
    small_mine = jnp.pad(small_mine, (0, small_rows * 128 - small_size)).reshape(1, small_rows, 128)
    message = jnp.concatenate(
        [
            jnp.pad(
                request.astype(jnp.float32).reshape(count, 1, room), ((0, 0), (0, 0), (0, 128 - room))
            ),
            jnp.broadcast_to(jnp.pad(notes, (0, 126)), (count, 1, 128)),
            jnp.broadcast_to(small_mine, (count, small_rows, 128)),
            jnp.zeros((count, 6 - small_rows, 128), jnp.float32),
        ],
        axis=1,
    )
    shard = stack_shard(qkv_weight, proj_weight[0], up_weight[0], down_weight[0], position_table)
    table_low = token_table.astype(jnp.bfloat16)
    heard, rows_in, big = gather_weights(sizes, message, table_low, shard, room)
    too_many = jnp.any(heard[:, 1, 0] > 0.0)
    valid_total = jnp.sum(heard[:, 1, 1])
    wanted = heard[:, 0, :room].reshape(1, -1).astype(jnp.int32)
    gains = arrange_gains(
        heard[:, 2 : 2 + small_rows].reshape(count, -1)[:, :small_size].reshape(-1), n_dp
    )
    teach_full = gather_teacher(teacher_weight)
    if not is_direct(shard.shape):
        big = big.transpose(2, 0, 3, 1, 4).reshape(16, D, D)

    def owned_rows():
        group_ids = lax.all_gather(token_ids, "head", axis=0, tiled=True)
        block_ids = group_ids // shard_rows
        owned = block_ids % n_head == lax.axis_index("head")
        local = jnp.where(owned, block_ids // n_head * shard_rows + group_ids % shard_rows, 0)
        return owned, local

    def rows_by_owner():
        owned, local = owned_rows()
        rows_all = lax.all_gather(table_low, "dp", axis=0, tiled=True)
        picked = jnp.where(owned[:, None], rows_all[local], jnp.zeros((), jnp.bfloat16))
        rows_here = lax.psum_scatter(picked, "head", scatter_dimension=0, tiled=True)
        return (
            jnp.pad(rows_here, ((0, count * room - here), (0, 0))),
            jnp.arange(here, dtype=jnp.int32),
        )

    rows_used, slot_used = lax.cond(
        too_many, rows_by_owner, lambda: (rows_in.reshape(count * room, D), slot)
    )
    teacher_qkv = project_teacher(teacher_hidden, teach_full)
    final_qkv, *kept = forward_layer(seq_lengths, rows_used, slot_used, big, gains)
    final_grad, loss_part = relation(seq_lengths, final_qkv, teacher_qkv)
    pieces, gain_grads, slot_grads, row_low = backward_layer(
        seq_lengths, slot_used, big, gains, final_grad, kept, count * room
    )
    if not is_direct(shard.shape):
        pieces = pieces.reshape(16, n_dp, shard.shape[1], n_head, shard.shape[2])
        pieces = pieces.transpose(1, 3, 0, 2, 4)
    gain_rows = jnp.pad(
        restore_gains(gain_grads, n_dp).reshape(count, 1, small_size), ((0, 0), (0, 0), (0, D - small_size))
    )
    slot_grads = slot_grads.reshape(count, room, D).at[:, room - 1 :].set(gain_rows.astype(jnp.bfloat16))
    rows_arrived, total, fast_grad, small_sum, everyone = reduce_grads(
        sizes, slot_grads, pieces, shard.shape, wanted, loss_part, token_table.shape
    )
    small_grad = small_sum[15, :small_size]

    def table_by_owner():
        owned, local = owned_rows()
        spread = lax.all_gather(row_low, "head", axis=0, tiled=True)
        table_grad = jax.ops.segment_sum(
            spread.astype(jnp.float32),
            jnp.where(owned, local, n_dp * shard_rows),
            num_segments=n_dp * shard_rows + 1,
        )[:-1]
        table_grad = lax.psum_scatter(
            table_grad.astype(jnp.bfloat16), "dp", scatter_dimension=0, tiled=True
        ).astype(jnp.float32)
        return table_grad, lax.psum(jnp.sum(table_grad * table_grad), ("dp", "head"))

    table_grad, table_squares = lax.cond(
        too_many, table_by_owner, lambda: (fast_grad, jnp.sum(everyone[:, 0, 0]))
    )
    square_total = table_squares + jnp.sum(everyone[:, 0, 1])
    loss_total = jnp.sum(everyone[:, 0, 2]) * (LN2 / (3 * REL))
    grad_norm = jnp.sqrt(square_total) / valid_total
    clip_factor = THRESHOLD / jnp.maximum(grad_norm, THRESHOLD)
    factor = clip_factor / valid_total
    token_new = adam_update(token_table, token_first, token_second, table_grad * factor, RATE_TABLE)
    position_new, qkv_new, proj_new, up_new, down_new = update_blocks(
        factor,
        total,
        (
            (position_table, position_first, position_second),
            (qkv_weight, qkv_first, qkv_second),
            (proj_weight, proj_first, proj_second),
            (up_weight, up_first, up_second),
            (down_weight, down_first, down_second),
        ),
    )
    gains_new = adam_update(gains_biases, gains_first, gains_second, small_grad * factor, RATE_SMALL)
    loss_parts = jnp.stack([loss_total, valid_total])
    return (
        token_new[0],
        token_new[1],
        token_new[2],
        position_new[0],
        position_new[1],
        position_new[2],
        qkv_new[0],
        qkv_new[1],
        qkv_new[2],
        proj_new[0],
        proj_new[1],
        proj_new[2],
        up_new[0],
        up_new[1],
        up_new[2],
        down_new[0],
        down_new[1],
        down_new[2],
        gains_new[0],
        gains_new[1],
        gains_new[2],
        grad_norm,
        loss_parts,
    )


def solution(mesh):
    placed = (
        P(("dp", "head")),
        P(("dp", "head")),
        P(("dp", "head"), None),
        P(None, "head"),
        P(("dp", "head"), None),
        P(("dp", "head"), None),
        P(("dp", "head"), None),
        P("dp", "head"),
        P("dp", "head"),
        P("dp", "head"),
        P(None, "dp", "head"),
        P(None, "dp", "head"),
        P(None, "dp", "head"),
        P(None, "dp", "head"),
        P(None, "dp", "head"),
        P(None, "dp", "head"),
        P(None, "dp", "head"),
        P(None, "dp", "head"),
        P(None, "dp", "head"),
        P(None, "dp", "head"),
        P(None, "dp", "head"),
        P(None, "dp", "head"),
        P(("dp", "head")),
        P(("dp", "head")),
        P(("dp", "head")),
    )
    return jax.shard_map(
        shards,
        mesh=mesh,
        in_specs=placed,
        out_specs=(
            P(("dp", "head"), None),
            P(("dp", "head"), None),
            P(("dp", "head"), None),
            P("dp", "head"),
            P("dp", "head"),
            P("dp", "head"),
            P(None, "dp", "head"),
            P(None, "dp", "head"),
            P(None, "dp", "head"),
            P(None, "dp", "head"),
            P(None, "dp", "head"),
            P(None, "dp", "head"),
            P(None, "dp", "head"),
            P(None, "dp", "head"),
            P(None, "dp", "head"),
            P(None, "dp", "head"),
            P(None, "dp", "head"),
            P(None, "dp", "head"),
            P(("dp", "head")),
            P(("dp", "head")),
            P(("dp", "head")),
            P(),
            P(),
        ),
        check_vma=False,
    )
```

```python
import functools
import math

import jax
import jax.numpy as jnp
from jax import lax
from jax.experimental import pallas as pl
from jax.experimental.pallas import tpu as pltpu
from jax.sharding import PartitionSpec as P

D = 512
HEADS = 8
HD = 64
FF = 2048
TD = 1024
THEADS = 16
THD = 64
REL = 64
LAYERS = 2
LA = 128
LB = 256
LC = 512
M = 1
STEP = 10


B_ONE = 0.9
B_TWO = 0.999
EPSILON = 1e-10
DECAY = 0.01
THRESHOLD = 0.0003
RATE_TABLE = 1.0
RATE_MATRIX = 0.1
RATE_SMALL = 2.0


def dot(left, right, dims=(((1,), (0,)), ((), ()))):
    return lax.dot_general(left, right, dims, preferred_element_type=jnp.float32)


NT = (((1,), (1,)), ((), ()))


LOG2E = 1.4426950408889634
LN2 = 0.6931471805599453
GROUPS = 4
S_WIDE = D // GROUPS
T_WIDE = TD // GROUPS
S_DIM = D // REL
T_DIM = TD // REL
FAST_LIMIT = 60.0
SEQS = ((0, LA), (LA, LA), (2 * LA, LB), (2 * LA + LB, LC))
TOKENS_HERE = 2 * LA + LB + LC
BLOCKS = ((2 * LA + LB, LC, (3,)), (2 * LA, LB, (2,)), (0, 2 * LA, (0, 1)))
AT_ONCE = 16
KEY_ROWS = 128


def relation_kernel(
    lens_ref,
    s_ref,
    t_ref,
    ds_ref,
    loss_ref,
    s_rows,
    t_rows,
    d_rows,
    exp_c,
    exp_b,
    exp_a,
    s_keep,
    t_keep,
):
    @pl.when((pl.program_id(0) == 0) & (pl.program_id(1) == 0))
    def _():
        loss_ref[...] = jnp.zeros_like(loss_ref)
        exp_a[...] = jnp.zeros_like(exp_a)

    s_scale = LOG2E / math.sqrt(S_DIM)
    t_scale = LOG2E / math.sqrt(T_DIM)
    zero = jnp.zeros((), jnp.bfloat16)
    half_heads = 128 // T_DIM
    exps = (exp_c, exp_b, exp_a)

    def valid_rows(block):
        off, length, seqs = BLOCKS[block]
        each = length // len(seqs)
        row = lax.broadcasted_iota(jnp.int32, (length, 128), 0)
        valid = row < 0
        for place, seq in enumerate(seqs):
            start = place * each
            valid = valid | (row >= start) & (row < start + lens_ref[seq])
        return valid

    def prepare(block):
        off, length, seqs = BLOCKS[block]
        each = length // len(seqs)
        lane = lax.broadcasted_iota(jnp.int32, (8, length), 1)
        lane_valid, padded = lane < 0, jnp.zeros((8, length), jnp.float32)
        for place, seq in enumerate(seqs):
            start = place * each
            lane_valid = lane_valid | (lane >= start) & (lane < start + lens_ref[seq])
            padded = jnp.where(lane >= start, (each - lens_ref[seq]).astype(jnp.float32), padded)
        row_valid = valid_rows(block)
        rows = slice(off, off + length)
        s_block = jnp.where(row_valid, s_ref[rows, :], zero).astype(jnp.float32)
        s_keep[rows, :] = (s_block * math.sqrt(s_scale)).astype(jnp.bfloat16)
        s_rows[:, rows] = s_block.T
        for half in range(2):
            cols = slice(half * 128, half * 128 + 128)
            t_block = jnp.where(row_valid, t_ref[rows, cols], zero).astype(jnp.float32)
            t_keep[half, rows, :] = (t_block * math.sqrt(t_scale)).astype(jnp.bfloat16)
            t_rows[cols, rows] = t_block.T
        s_here = s_rows[:, rows]
        t_here = t_rows[:, rows]
        s_square = jnp.sum((s_here * s_here).reshape(16, S_DIM, length), axis=1)
        t_square = jnp.sum((t_here * t_here).reshape(16, T_DIM, length), axis=1)
        bound = jnp.maximum(jnp.max(s_square) * s_scale, jnp.max(t_square) * t_scale)
        return bound, lane_valid.astype(jnp.float32), padded[0:1]

    info = [prepare(block) for block in range(len(BLOCKS))]

    def fold_rows(value):
        total = value[0:8]
        for start in range(8, value.shape[0], 8):
            total = total + value[start : start + 8]
        return total

    def one_head(rows, length, head):
        lane = lax.broadcasted_iota(jnp.int32, (length, 128), 1)
        half = head // half_heads
        s_one = jnp.where(lane // S_DIM == head, s_keep[rows, :], zero)
        t_one = jnp.where(lane // T_DIM == head - half * half_heads, t_keep[half, rows, :], zero)
        return half, s_one, t_one

    def row_slices(head):
        s_slice = pl.ds(pl.multiple_of(head * S_DIM, S_DIM), S_DIM)
        t_slice = pl.ds(pl.multiple_of(head * T_DIM, T_DIM), T_DIM)
        return s_slice, t_slice

    def fill(block, keys, one, target):
        off, length, seqs = BLOCKS[block]
        each = length // len(seqs)
        if len(seqs) > 1:
            scores = dot(keys[...], one, NT)
            sums = []
            for place in range(len(seqs)):
                here = slice(place * each, place * each + each)
                value = jnp.exp2(scores[here, here])
                sums.append(fold_rows(value))
                target[here, here] = value.astype(jnp.bfloat16)
            return jnp.concatenate(sums, axis=1)
        total = jnp.zeros((8, length), jnp.float32)
        for start in range(0, length, KEY_ROWS):
            here = slice(start, start + KEY_ROWS)
            value = jnp.exp2(dot(keys[here, :], one, NT))
            total = total + fold_rows(value)
            target[here, :] = value.astype(jnp.bfloat16)
        return total

    def fill_both(block, head, slot):
        off, length, seqs = BLOCKS[block]
        rows = slice(off, off + length)
        half, s_one, t_one = one_head(rows, length, head)
        return (
            fill(block, s_keep.at[rows, :], s_one, exps[block].at[slot, 0]),
            fill(block, t_keep.at[half, rows, :], t_one, exps[block].at[slot, 1]),
        )

    def use_both(block, head, slot, sums):
        off, length, seqs = BLOCKS[block]
        rows = slice(off, off + length)
        bound, valid_row, padded = info[block]
        s_total = jnp.sum(sums[0], axis=0, keepdims=True) - padded
        t_total = jnp.sum(sums[1], axis=0, keepdims=True) - padded
        s_recip = valid_row / s_total
        t_recip = valid_row / t_total
        s_slice, t_slice = row_slices(head)
        s_vec = s_rows[s_slice, rows]
        t_vec = t_rows[t_slice, rows]
        t_left = jnp.concatenate([s_vec, s_vec * t_recip, t_vec], axis=0).astype(jnp.bfloat16)
        s_left = jnp.concatenate([s_vec, s_vec * s_recip], axis=0).astype(jnp.bfloat16)
        t_out = dot(t_left, exps[block][slot, 1])
        s_out = dot(s_left, exps[block][slot, 0])
        d_rows[s_slice, rows] = (
            s_out[0:8] * s_recip - t_out[0:8] * t_recip + (s_out[8:16] - t_out[8:16]) * valid_row
        )
        inner = t_vec * t_out[16:32]
        inner = (inner[0:8] + inner[8:16]) * t_scale - s_vec * t_out[0:8] * s_scale
        parts = inner * t_recip + (jnp.log2(s_total) - jnp.log2(t_total)) * (valid_row * 0.125)
        return fold_lanes(parts, length)

    def fold_lanes(parts, length):
        total = parts[:, 0:128]
        for start in range(128, length, 128):
            total = total + parts[:, start : start + 128]
        return total

    def fast_heads(step, carry):
        work = [
            (block, step * AT_ONCE + slot, slot)
            for slot in range(AT_ONCE)
            for block in range(len(BLOCKS))
        ]
        sums = [fill_both(*item) for item in work]
        total = jnp.zeros((8, 128), jnp.float32)
        for item, item_sums in zip(work, sums):
            total = total + use_both(*item, item_sums)
        loss_ref[...] += total
        return carry

    def exact_head(seq, head):
        off, length = SEQS[seq]
        rows = slice(off, off + length)
        valid = lens_ref[seq]
        half, s_one, t_one = one_head(rows, length, head)
        s_slice, t_slice = row_slices(head)
        key_valid = lax.broadcasted_iota(jnp.int32, (length, 128), 0) < valid
        exp_c[0, 0, 0:length, 0:128] = s_one
        exp_c[0, 1, 0:length, 0:128] = t_one

        def log_soft(scores, scale):
            scaled = jnp.where(key_valid, scores * scale, -1e30)
            top = jnp.max(scaled, axis=0, keepdims=True)
            shifted = scaled - top
            total = jnp.sum(jnp.exp2(shifted), axis=0, keepdims=True)
            return shifted - jnp.log2(total)

        def queries(block, carry):
            start = pl.multiple_of(block * 128, 128)
            here = pl.ds(start, 128)
            query_valid = lax.broadcasted_iota(jnp.int32, (length, 128), 1) + start < valid
            both = key_valid & query_valid
            s_log = log_soft(dot(s_keep[rows, :], exp_c[0, 0, here, 0:128], NT), s_scale)
            t_log = log_soft(dot(t_keep[half, rows, :], exp_c[0, 1, here, 0:128], NT), t_scale)
            t_soft = jnp.exp2(t_log)
            change = jnp.where(both, jnp.exp2(s_log) - t_soft, 0.0)
            exp_c[1, 0, 0:length, here] = change.astype(jnp.bfloat16)
            loss_ref[...] += fold_rows(jnp.where(both, t_soft * (t_log - s_log), 0.0))
            return carry

        lax.fori_loop(0, length // 128, queries, 0)
        s_vec = s_rows[s_slice, rows]
        left = jnp.concatenate([s_vec, jnp.zeros_like(s_vec)], axis=0).astype(jnp.bfloat16)
        change = exp_c[1, 0, 0:length, 0:length]
        d_rows[s_slice, rows] = (dot(left, change) + dot(left, change, NT))[0:8]

    top_bound = info[0][0]
    for entry in info:
        top_bound = jnp.maximum(top_bound, entry[0])
    fast = top_bound < FAST_LIMIT

    @pl.when(fast)
    def _():
        lax.fori_loop(0, 2 * half_heads // AT_ONCE, fast_heads, 0)

    @pl.when(jnp.logical_not(fast))
    def _():
        for block, (off, length, seqs) in enumerate(BLOCKS):
            rows = slice(off, off + length)
            row_valid = valid_rows(block)
            s_keep[rows, :] = jnp.where(row_valid, s_ref[rows, :], zero)
            for half in range(2):
                t_block = t_ref[rows, half * 128 : half * 128 + 128]
                t_keep[half, rows, :] = jnp.where(row_valid, t_block, zero)
        for seq in range(len(SEQS)):

            def body(head, carry, seq=seq):
                exact_head(seq, head)
                return carry

            lax.fori_loop(0, 2 * half_heads, body, 0)

    for off, length in SEQS:
        ds_ref[off : off + length, :] = (
            d_rows[:, off : off + length].T * (1.0 / math.sqrt(S_DIM) / (3 * REL))
        ).astype(ds_ref.dtype)


def relation(seq_lengths, student, teacher):
    block_s = pl.BlockSpec((None, TOKENS_HERE, S_WIDE), lambda part, group: (part, 0, group))
    block_t = pl.BlockSpec((None, TOKENS_HERE, T_WIDE), lambda part, group: (part, 0, group))
    grads, loss = pl.pallas_call(
        relation_kernel,
        grid=(3, GROUPS),
        in_specs=[pl.BlockSpec(memory_space=pltpu.SMEM), block_s, block_t],
        out_specs=[block_s, pl.BlockSpec((8, 128), lambda part, group: (0, 0))],
        out_shape=[
            jax.ShapeDtypeStruct((3, TOKENS_HERE, D), jnp.bfloat16),
            jax.ShapeDtypeStruct((8, 128), jnp.float32),
        ],
        scratch_shapes=[
            pltpu.VMEM((S_WIDE, TOKENS_HERE), jnp.float32),
            pltpu.VMEM((T_WIDE, TOKENS_HERE), jnp.float32),
            pltpu.VMEM((S_WIDE, TOKENS_HERE), jnp.float32),
            pltpu.VMEM((AT_ONCE, 2, LC, LC), jnp.bfloat16),
            pltpu.VMEM((AT_ONCE, 2, LB, LB), jnp.bfloat16),
            pltpu.VMEM((AT_ONCE, 2, 2 * LA, 2 * LA), jnp.bfloat16),
            pltpu.VMEM((TOKENS_HERE, 128), jnp.bfloat16),
            pltpu.VMEM((2, TOKENS_HERE, 128), jnp.bfloat16),
        ],
        compiler_params=pltpu.CompilerParams(vmem_limit_bytes=48 * 2**20),
    )(seq_lengths, student, teacher)
    return grads, loss


def by_part(columns, heads):
    lead = columns.shape[:-1]
    size = columns.shape[-1] // heads // 3
    shaped = columns.reshape(lead + (heads, 3, size))
    return jnp.moveaxis(shaped, -2, -3).reshape(columns.shape)


def by_head(columns, heads):
    lead = columns.shape[:-1]
    size = columns.shape[-1] // heads // 3
    shaped = columns.reshape(lead + (3, heads, size))
    return jnp.moveaxis(shaped, -2, -3).reshape(columns.shape)


POS_AT = 7
GAIN_ROWS = 18
ERF_TOP = (
    -2.72614225801306e-10,
    2.77068142495902e-08,
    -2.10102402082508e-06,
    -5.69250639462346e-05,
    -7.34990630326855e-04,
    -2.95459980854025e-03,
    -1.60960333262415e-02,
)
ERF_LOW = (
    -1.45660718464996e-05,
    -2.13374055278905e-04,
    -1.68282697438203e-03,
    -7.37332916720468e-03,
    -1.42647390514189e-02,
)
STEP_ROWS = 256


def erf(value):
    value = jnp.clip(value, -4.0, 4.0)
    square = value * value
    top = jnp.full_like(value, ERF_TOP[0])
    for factor in ERF_TOP[1:]:
        top = top * square + factor
    low_part = jnp.full_like(value, ERF_LOW[0])
    for factor in ERF_LOW[1:]:
        low_part = low_part * square + factor
    return value * top / low_part


def normal_cdf(value):
    return 0.5 + 0.5 * erf(value * math.sqrt(0.5))


def normalize(values):
    average = jnp.mean(values, axis=-1, keepdims=True)
    centered = values - average
    variance = jnp.mean(centered * centered, axis=-1, keepdims=True)
    scale = lax.rsqrt(variance + 1e-05)
    return centered * scale, scale


def low16(value):
    return value.astype(jnp.bfloat16)


def step_slice(step):
    return pl.ds(pl.multiple_of(step * STEP_ROWS, STEP_ROWS), STEP_ROWS)


def head_soft(q_pair, k_one, valid, length):
    scores = dot(q_pair, k_one, NT) * (1.0 / math.sqrt(HD))
    lane = lax.broadcasted_iota(jnp.int32, scores.shape, 1)
    scores = jnp.where(lane < valid, scores, -1e30)
    top = jnp.max(scores, axis=-1, keepdims=True)
    value = jnp.exp(scores - top)
    return value / jnp.sum(value, axis=-1, keepdims=True)


def forward_kernel(
    lens_ref,
    rows_ref,
    slot_ref,
    big,
    gains,
    s_out,
    hat0,
    hat1,
    hat2,
    scale0,
    scale1,
    scale2,
    hid_low,
    qkv_low,
    ctx_low,
    mid_low,
    pre_low,
    x_low,
    hidden_kept,
):
    steps = TOKENS_HERE // STEP_ROWS

    def embed(step, carry):
        here = step_slice(step)
        spots = lax.broadcasted_iota(jnp.int32, (STEP_ROWS, rows_ref.shape[0]), 1)
        chosen = low16(jnp.where(slot_ref[here, :] == spots, 1.0, 0.0))
        first = big[POS_AT, 0:STEP_ROWS, :].astype(jnp.float32)
        twice = jnp.concatenate([first[0:LA], first[0:LA]], axis=0)
        late = big[POS_AT, STEP_ROWS : 2 * STEP_ROWS, :].astype(jnp.float32)
        place = jnp.where(step == 0, twice, jnp.where(step == 3, late, first))
        hat, scale = normalize(dot(chosen, rows_ref[...]) + place)
        hat0[here, :] = low16(hat)
        scale0[here, :] = scale
        wide = hat * gains[0:1, :] + gains[1:2, :]
        hidden_kept[here, :] = wide
        hidden = low16(wide)
        hid_low[here, :] = hidden
        for part in range(3):
            qkv_low[part, here, :] = low16(dot(hidden, big[part]) + gains[2 + part : 3 + part, :])
        return carry

    lax.fori_loop(0, steps, embed, 0, unroll=2)
    zero = jnp.zeros((), jnp.bfloat16)

    def attend_pair(pair, carry):
        cols = pl.ds(pl.multiple_of(pair * 128, 128), 128)
        for seq, (off, length) in enumerate(SEQS):
            rows = slice(off, off + length)
            query, key, value = (qkv_low[part, rows, cols] for part in range(3))
            lane = lax.broadcasted_iota(jnp.int32, (length, 128), 1)
            total = jnp.zeros((length, 128), jnp.float32)
            for side in range(2):
                mine = lane // HD == side
                soft = head_soft(query, jnp.where(mine, key, zero), lens_ref[seq], length)
                total = total + dot(low16(soft), jnp.where(mine, value, zero))
            ctx_low[rows, cols] = low16(total)
        return carry

    lax.fori_loop(0, D // 128, attend_pair, 0, unroll=2)

    def rest(step, carry):
        here = step_slice(step)
        hat, scale = normalize(hidden_kept[here, :] + dot(ctx_low[here, :], big[6]) + gains[5:6, :])
        hat1[here, :] = low16(hat)
        scale1[here, :] = scale
        middle = hat * gains[11:12, :] + gains[12:13, :]
        middle_low = low16(middle)
        mid_low[here, :] = middle_low
        output = middle + gains[10:11, :]
        for block in range(4):
            cols = slice(block * D, block * D + D)
            pre = dot(middle_low, big[8 + block]) + gains[6 + block : 7 + block, :]
            act = low16(pre * normal_cdf(pre))
            pre_low[here, cols] = low16(pre)
            output = output + dot(act, big[12 + block])
        hat, scale = normalize(output)
        hat2[here, :] = low16(hat)
        scale2[here, :] = scale
        final = low16(hat * gains[13:14, :] + gains[14:15, :])
        x_low[here, :] = final
        for part in range(3):
            s_out[part, here, :] = low16(dot(final, big[3 + part]) + gains[15 + part : 16 + part, :])
        return carry

    lax.fori_loop(0, steps, rest, 0, unroll=2)


def forward_layer(seq_lengths, rows, slot, big, gains):
    vmem = pl.BlockSpec(memory_space=pltpu.VMEM)
    shape = lambda *dims: jax.ShapeDtypeStruct(dims, jnp.float32)
    half = lambda *dims: jax.ShapeDtypeStruct(dims, jnp.bfloat16)
    tokens = TOKENS_HERE
    outs = [half(3, tokens, D)]
    outs += [half(tokens, D)] * 3 + [shape(tokens, 1)] * 3
    outs += [half(tokens, D), half(3, tokens, D), half(tokens, D), half(tokens, D)]
    outs += [half(tokens, FF), half(tokens, D)]
    return pl.pallas_call(
        forward_kernel,
        in_specs=[pl.BlockSpec(memory_space=pltpu.SMEM)] + [vmem] * 4,
        out_specs=[vmem] * len(outs),
        out_shape=outs,
        scratch_shapes=[pltpu.VMEM((tokens, D), jnp.float32)],
        compiler_params=pltpu.CompilerParams(vmem_limit_bytes=56 * 2**20),
    )(seq_lengths, rows, slot[:, None], big, gains)


def backward_kernel(
    lens_ref,
    slot_ref,
    big,
    gains,
    ds_ref,
    hat0,
    hat1,
    hat2,
    scale0,
    scale1,
    scale2,
    hid_low,
    qkv_low,
    ctx_low,
    mid_low,
    pre_low,
    x_low,
    grads,
    small,
    slot_grads,
    row_low,
    flow,
    flow_low,
    wide_low,
    turned,
    dqkv_low,
    act_low,
):
    steps = TOKENS_HERE // STEP_ROWS
    small[...] = jnp.zeros_like(small)

    def add_small(row, value):
        small[row : row + 1, :] += jnp.sum(value, axis=0, keepdims=True)

    def norm_back(here, grad, hat_ref, scale_ref, row):
        hat = hat_ref[here, :].astype(jnp.float32)
        add_small(row, grad * hat)
        add_small(row + 1, grad)
        inner = grad * gains[row : row + 1, :]
        mean_inner = jnp.mean(inner, axis=-1, keepdims=True)
        mean_hat = jnp.mean(inner * hat, axis=-1, keepdims=True)
        return scale_ref[here, :] * (inner - mean_inner - hat * mean_hat)

    def turn(source, width):
        for start in range(0, TOKENS_HERE, STEP_ROWS):
            turned[0:width, start : start + STEP_ROWS] = source[start : start + STEP_ROWS, 0:width].T

    def weight_grads(pairs):
        for index, right in pairs:
            grads[index] = low16(dot(turned[0:D, :], right))

    def last(step, carry):
        here = step_slice(step)
        grad = jnp.zeros((STEP_ROWS, D), jnp.float32)
        for part in range(3):
            piece = ds_ref[part, here, :]
            add_small(15 + part, piece.astype(jnp.float32))
            grad = grad + dot(piece, big[3 + part], NT)
        grad = norm_back(here, grad, hat2, scale2, 13)
        add_small(10, grad)
        grad_low = low16(grad)
        flow_low[here, :] = grad_low
        total = grad
        for block in range(4):
            cols = slice(block * D, block * D + D)
            pre = pre_low[here, cols].astype(jnp.float32)
            below = normal_cdf(pre)
            act_low[here, cols] = low16(pre * below)
            slope = below + pre * jnp.exp(pre * pre * -0.5) * (1.0 / math.sqrt(2.0 * math.pi))
            inner = dot(grad_low, big[12 + block], NT) * slope
            add_small(6 + block, inner)
            inner_low = low16(inner)
            wide_low[here, cols] = inner_low
            total = total + dot(inner_low, big[8 + block], NT)
        flow[here, :] = total
        return carry

    lax.fori_loop(0, steps, last, 0, unroll=2)
    turn(x_low, D)
    weight_grads([(3 + part, ds_ref[part]) for part in range(3)])
    for block in range(4):
        cols = slice(block * D, block * D + D)
        for start in range(0, TOKENS_HERE, STEP_ROWS):
            turned[:, start : start + STEP_ROWS] = act_low[start : start + STEP_ROWS, cols].T
        weight_grads([(12 + block, flow_low[...])])
    turn(mid_low, D)
    weight_grads([(8 + block, wide_low[:, block * D : block * D + D]) for block in range(4)])

    def middle(step, carry):
        here = step_slice(step)
        grad = norm_back(here, flow[here, :], hat1, scale1, 11)
        add_small(5, grad)
        flow[here, :] = grad
        grad_low = low16(grad)
        flow_low[here, :] = grad_low
        wide_low[here, 0:D] = low16(dot(grad_low, big[6], NT))
        return carry

    lax.fori_loop(0, steps, middle, 0, unroll=2)
    turn(ctx_low, D)
    weight_grads([(6, flow_low[...])])
    zero = jnp.zeros((), jnp.bfloat16)

    def attend_pair(pair, carry):
        cols = pl.ds(pl.multiple_of(pair * 128, 128), 128)
        for seq, (off, length) in enumerate(SEQS):
            rows = slice(off, off + length)
            query, key, value = (qkv_low[part, rows, cols] for part in range(3))
            out_grad = wide_low[rows, cols]
            lane = lax.broadcasted_iota(jnp.int32, (length, 128), 1)
            sums = [jnp.zeros((length, 128), jnp.float32)] * 3
            for side in range(2):
                mine = lane // HD == side
                key_one = jnp.where(mine, key, zero)
                soft = head_soft(query, key_one, lens_ref[seq], length)
                grad_one = jnp.where(mine, out_grad, zero)
                soft_grad = dot(grad_one, value, NT)
                inner = jnp.sum(soft_grad * soft, axis=-1, keepdims=True)
                score_grad = low16((soft_grad - inner) * soft * (1.0 / math.sqrt(HD)))
                query_one = jnp.where(mine, query, zero)
                sums[0] = sums[0] + dot(score_grad, key_one)
                sums[1] = sums[1] + dot(score_grad.T, query_one)
                sums[2] = sums[2] + dot(low16(soft).T, grad_one)
            for part in range(3):
                dqkv_low[part, rows, cols] = low16(sums[part])
        return carry

    lax.fori_loop(0, D // 128, attend_pair, 0, unroll=2)

    def first(step, carry):
        here = step_slice(step)
        grad = flow[here, :]
        for part in range(3):
            piece = dqkv_low[part, here, :]
            add_small(2 + part, piece.astype(jnp.float32))
            grad = grad + dot(piece, big[part], NT)
        grad = norm_back(here, grad, hat0, scale0, 0)
        flow[here, :] = grad
        row_low[here, :] = low16(grad)
        return carry

    lax.fori_loop(0, steps, first, 0, unroll=2)
    turn(hid_low, D)
    weight_grads([(part, dqkv_low[part]) for part in range(3)])
    near = flow[0:LA, :] + flow[LA : 2 * LA, :] + flow[2 * LA : 3 * LA, :] + flow[4 * LA : 5 * LA, :]
    grads[POS_AT, 0:LA, :] = low16(near)
    grads[POS_AT, LA:LB, :] = low16(flow[3 * LA : 4 * LA, :] + flow[5 * LA : 6 * LA, :])
    grads[POS_AT, LB:LC, :] = low16(flow[2 * LA + LB + LB :, :])
    places = slot_grads.shape[0]
    size = 512 if places % 512 == 0 else places

    def spread(block, carry):
        start = pl.multiple_of(block * size, size)
        spots = lax.broadcasted_iota(jnp.int32, (size, TOKENS_HERE), 0) + start
        chosen = low16(jnp.where(slot_ref[...] == spots, 1.0, 0.0))
        slot_grads[pl.ds(start, size), :] = low16(dot(chosen, row_low[...]))
        return carry

    lax.fori_loop(0, places // size, spread, 0)


def backward_layer(seq_lengths, slot, big, gains, final_grad, kept, places):
    vmem = pl.BlockSpec(memory_space=pltpu.VMEM)
    half = lambda *dims: jax.ShapeDtypeStruct(dims, jnp.bfloat16)
    tokens = TOKENS_HERE
    return pl.pallas_call(
        backward_kernel,
        in_specs=[pl.BlockSpec(memory_space=pltpu.SMEM)] + [vmem] * (4 + len(kept)),
        out_specs=[vmem] * 4,
        out_shape=[
            half(16, D, D),
            jax.ShapeDtypeStruct((GAIN_ROWS, D), jnp.float32),
            half(places, D),
            half(tokens, D),
        ],
        scratch_shapes=[
            pltpu.VMEM((tokens, D), jnp.float32),
            pltpu.VMEM((tokens, D), jnp.bfloat16),
            pltpu.VMEM((tokens, FF), jnp.bfloat16),
            pltpu.VMEM((D, tokens), jnp.bfloat16),
            pltpu.VMEM((3, tokens, D), jnp.bfloat16),
            pltpu.VMEM((tokens, FF), jnp.bfloat16),
        ],
        compiler_params=pltpu.CompilerParams(vmem_limit_bytes=60 * 2**20),
    )(seq_lengths, slot[None, :], big, gains, final_grad, *kept)


def teacher_kernel(hidden, weight, out):
    out[...] = low16(dot(hidden[...], weight[...]))


def project_teacher(hidden, weight):
    tokens = hidden.shape[0]
    owners, parts, depth, width = weight.shape
    return pl.pallas_call(
        teacher_kernel,
        grid=(parts, owners),
        in_specs=[
            pl.BlockSpec((tokens, depth), lambda part, owner: (0, 0)),
            pl.BlockSpec((None, None, depth, width), lambda part, owner: (owner, part, 0, 0)),
        ],
        out_specs=pl.BlockSpec((None, tokens, width), lambda part, owner: (part, 0, owner)),
        out_shape=jax.ShapeDtypeStruct((parts, tokens, owners * width), jnp.bfloat16),
        compiler_params=pltpu.CompilerParams(vmem_limit_bytes=32 * 2**20),
    )(hidden, weight)


MESH_IDS = pl.DeviceIdType.MESH


def barrier_all(rank, count, place):
    barrier = pltpu.get_barrier_semaphore()

    def greet(step, carry):
        pl.semaphore_signal(
            barrier, inc=1, device_id=place(lax.rem(rank + step, count)), device_id_type=MESH_IDS
        )
        return carry

    lax.fori_loop(1, count, greet, 0)
    pl.semaphore_wait(barrier, count - 1)


class Spot:
    def __init__(self, n_dp, n_head):
        self.n_dp, self.n_head = n_dp, n_head
        self.count = n_dp * n_head
        self.nz, self.nx = n_dp // 2, n_head // 2
        dp, head = lax.axis_index("dp"), lax.axis_index("head")
        self.rank = dp * n_head + head
        self.z, self.y = dp // 2, lax.rem(dp, 2)
        self.x, self.c = head // 2, lax.rem(head, 2)

    def place(self, rank):
        return (rank // self.n_head, lax.rem(rank, self.n_head))

    def device(self, z, y, x, c):
        return (z * 2 + y, x * 2 + c)


def remote(source, target, send_sem, recv_sem, device):
    return pltpu.make_async_remote_copy(
        src_ref=source,
        dst_ref=target,
        send_sem=send_sem,
        recv_sem=recv_sem,
        device_id=device,
        device_id_type=MESH_IDS,
    )


def start_all_to_all(spot, source, target, send_sems, recv_sems, local_sem):
    pltpu.make_async_copy(source.at[spot.rank], target.at[spot.rank], local_sem).start()

    def send(step, carry):
        peer = lax.rem(spot.rank + step, spot.count)
        remote(
            source.at[peer], target.at[spot.rank], send_sems.at[step], recv_sems.at[step], spot.place(peer)
        ).start()
        return carry

    lax.fori_loop(1, spot.count, send, 0)


def finish_all_to_all(spot, source, target, send_sems, recv_sems, local_sem):
    def take(step, carry):
        origin = lax.rem(spot.rank + spot.count - step, spot.count)
        copy = remote(
            source.at[origin], target.at[origin], send_sems.at[step], recv_sems.at[step], spot.place(origin)
        )
        copy.wait_recv()
        copy.wait_send()
        return carry

    lax.fori_loop(1, spot.count, take, 0)
    pltpu.make_async_copy(source.at[spot.rank], target.at[spot.rank], local_sem).wait()


def is_direct(shape):
    return shape[1] % 16 == 0 and shape[2] % 128 == 0


def piece_of(whole, shape, dp, head, half):
    blocks = pl.ds(half * (shape[0] // 2), shape[0] // 2)
    if not is_direct(shape):
        return whole.at[dp, head, blocks]
    rows = pl.ds(pl.multiple_of(dp * shape[1], shape[1]), shape[1])
    return whole.at[blocks, rows, pl.ds(pl.multiple_of(head * shape[2], shape[2]), shape[2])]


def whole_shape(sizes, shape):
    if not is_direct(shape):
        return sizes + shape
    return (shape[0], sizes[0] * shape[1], sizes[1] * shape[2])


def answer(heard, table, rows, at_once):
    count, room = rows.shape[:2]
    spare = -count % 128
    asked = heard[:, 0, :]
    if spare:
        asked = jnp.concatenate([asked, jnp.full((spare, 128), -1.0, jnp.float32)], axis=0)
    turned = asked.T
    lane = lax.broadcasted_iota(jnp.int32, (room, count + spare), 1)
    spots = lax.broadcasted_iota(jnp.int32, (at_once * room, table.shape[0]), 1)

    def some(step, carry):
        columns = []
        for place in range(at_once):
            mine = lane == step * at_once + place
            columns.append(jnp.sum(jnp.where(mine, turned[0:room, :], 0.0), axis=1, keepdims=True))
        wanted = jnp.concatenate(columns, axis=0).astype(jnp.int32)
        chosen = low16(jnp.where(wanted == spots, 1.0, 0.0))
        found = low16(dot(chosen, table[...]))
        for place in range(at_once):
            rows[step * at_once + place] = found[place * room : place * room + room]
        return carry

    lax.fori_loop(0, count // at_once, some, 0)


def gather_kernel(
    sizes,
    messages,
    table,
    shard,
    heard,
    rows_out,
    full,
    rows,
    message_send,
    message_recv,
    row_send,
    row_recv,
    piece_send,
    piece_recv,
    local_sems,
):
    spot = Spot(*sizes)
    z, y, x, c, nz, nx = spot.z, spot.y, spot.x, spot.c, spot.nz, spot.nx
    barrier_all(spot.rank, spot.count, spot.place)
    sends = []

    def spot_of(piece, half):
        return piece_of(full, shard.shape, piece[0] * 2 + piece[1], piece[2] * 2 + piece[3], half)

    def arrival(piece, half):
        return piece_recv.at[half, piece[0] * 2 + piece[1], piece[2] * 2 + piece[3]]

    def send_piece(source, piece, half, device):
        copy = remote(
            source, spot_of(piece, half), piece_send.at[len(sends)], arrival(piece, half), device
        )
        copy.start()
        sends.append(copy)

    def wait_piece(piece, half):
        here = spot_of(piece, half)
        remote(
            here, here, piece_send.at[0], arrival(piece, half), spot.device(z, y, x, 1 - c)
        ).wait_recv()
        return here

    own = (z, y, x, c)
    own_halves = [shard.at[pl.ds(half * (shard.shape[0] // 2), shard.shape[0] // 2)] for half in range(2)]
    own_copies = [
        pltpu.make_async_copy(own_halves[half], spot_of(own, half), local_sems.at[half]) for half in range(2)
    ]
    for copy in own_copies:
        copy.start()
    start_all_to_all(spot, messages, heard, message_send, message_recv, local_sems.at[2])
    others_x = [lax.rem(x + step, nx) for step in range(1, nx)]
    sibling, opposite = spot.device(z, y, x, 1 - c), spot.device(z, 1 - y, x, c)
    across = [spot.device(z, y, other, c) for other in others_x]
    for half in range(2):
        for step in range(1, nz):
            send_piece(own_halves[half], own, half, spot.device(lax.rem(z + step, nz), y, x, c))
    for half in range(2):
        for device in across + [opposite, sibling]:
            send_piece(own_halves[half], own, half, device)
    finish_all_to_all(spot, messages, heard, message_send, message_recv, local_sems.at[2])
    answer(heard, table, rows, 8)
    start_all_to_all(spot, rows, rows_out, row_send, row_recv, local_sems.at[3])
    depths = [lax.rem(z + nz - step, nz) for step in range(nz)]

    def pass_on(piece, half, devices):
        here = wait_piece(piece, half)
        for device in devices:
            send_piece(here, piece, half, device)

    for deep in depths[1:]:
        for half in range(2):
            pass_on((deep, y, x, c), half, across + [opposite, sibling])
    for deep in depths:
        for other in others_x:
            pass_on((deep, y, other, c), 0, [opposite, sibling])
        pass_on((deep, 1 - y, x, c), 1, across + [sibling])
    for deep in depths:
        for column in [x] + others_x:
            pass_on((deep, 1 - y, column, c), 0, [sibling])
        for other in others_x:
            for side in (y, 1 - y):
                pass_on((deep, side, other, c), 1, [sibling])
    for deep in depths:
        for side in (y, 1 - y):
            for column in [x] + others_x:
                for half in range(2):
                    wait_piece((deep, side, column, 1 - c), half)
    for copy in sends:
        copy.wait_send()
    finish_all_to_all(spot, rows, rows_out, row_send, row_recv, local_sems.at[3])
    for copy in own_copies:
        copy.wait()


def gather_weights(sizes, messages, table, shard, room):
    n_dp, n_head = sizes
    count = n_dp * n_head
    nz, nx = n_dp // 2, n_head // 2
    sends = 2 * (nz - 1) + 2 * nz * (nx + 1) + nz * (nx - 1) * 2 + nz * nx + nz * nx + 2 * nz * (nx - 1)
    anywhere = pl.BlockSpec(memory_space=pl.ANY)
    vmem = pl.BlockSpec(memory_space=pltpu.VMEM)
    dma = pltpu.SemaphoreType.DMA
    rows_shape = (count, room, table.shape[1])
    return pl.pallas_call(
        functools.partial(gather_kernel, sizes),
        in_specs=[vmem, vmem, anywhere],
        out_specs=[vmem, anywhere, anywhere],
        out_shape=[
            jax.ShapeDtypeStruct(messages.shape, messages.dtype),
            jax.ShapeDtypeStruct(rows_shape, table.dtype),
            jax.ShapeDtypeStruct(whole_shape(sizes, shard.shape), shard.dtype),
        ],
        scratch_shapes=[
            pltpu.VMEM(rows_shape, table.dtype),
            dma((count,)),
            dma((count,)),
            dma((count,)),
            dma((count,)),
            dma((sends,)),
            dma((2, n_dp, n_head)),
            dma((4,)),
        ],
        compiler_params=pltpu.CompilerParams(
            collective_id=2, has_side_effects=True, vmem_limit_bytes=40 * 2**20
        ),
    )(messages, table, shard)


def table_rows_at_once(rows):
    sizes = [size for size in range(8, 265, 8) if rows % size == 0]
    return max(sizes) if sizes and rows > 264 else rows


def place_rows(rows, wanted, table_grad):
    count, room, width = rows.shape
    at_once = table_rows_at_once(table_grad.shape[0])
    arrived = rows[...].reshape(count * room, width)

    def some(step, squares):
        start = step * at_once
        if at_once % 8 == 0:
            start = pl.multiple_of(start, 8)
        spots = lax.broadcasted_iota(jnp.int32, (at_once, count * room), 0) + start
        chosen = low16(jnp.where(wanted[...] == spots, 1.0, 0.0))
        value = dot(chosen, arrived)
        table_grad[pl.ds(start, at_once), :] = value
        return squares + jnp.sum(value * value, axis=0, keepdims=True)

    zero = jnp.zeros((1, width), jnp.float32)
    return lax.fori_loop(0, table_grad.shape[0] // at_once, some, zero)


def reduce_kernel(
    sizes,
    rows,
    pieces,
    wanted,
    loss,
    rows_out,
    total,
    table_grad,
    small,
    everyone,
    mine,
    sum_send,
    sum_recv,
    core_in,
    y_in,
    x_in,
    z_in,
    row_send,
    row_recv,
    core_send,
    core_recv,
    y_send,
    y_recv,
    x_send,
    x_recv,
    z_send,
    z_recv,
    local_sem,
):
    spot = Spot(*sizes)
    z, y, x, c, nz, nx = spot.z, spot.y, spot.x, spot.c, spot.nz, spot.nx
    shape = total.shape
    blocks = shape[0] // 2
    barrier_all(spot.rank, spot.count, spot.place)
    sibling = spot.device(z, y, x, 1 - c)
    opposite = spot.device(z, 1 - y, x, c)

    def core_sum(deep, side, column, half):
        return core_in.at[deep, side, column, pl.ds(half * blocks, blocks)]

    def core_copy(deep, side, column, half):
        return remote(
            piece_of(pieces, shape, deep * 2 + side, column * 2 + 1 - c, half),
            core_sum(deep, side, column, half),
            core_send.at[half, deep, side, column],
            core_recv.at[half, deep, side, column],
            sibling,
        )

    def y_copy(half, deep, column):
        return remote(
            core_sum(deep, 1 - y, column, half),
            y_in.at[half, deep, column],
            y_send.at[half, deep, column],
            y_recv.at[half, deep, column],
            opposite,
        )

    def x_copy(half, step, deep, side):
        column = lax.rem(x + step, nx)
        source = y_in.at[0, deep, column] if half == 0 else core_sum(deep, side, column, 1)
        return remote(
            source,
            x_in.at[half, step - 1, deep, side],
            x_send.at[half, step - 1, deep, side],
            x_recv.at[half, step - 1, deep, side],
            spot.device(z, y, column, c),
        )

    def summed(half, deep):
        return y_in.at[0, deep, x] if half == 0 else core_sum(deep, y, x, 1)

    def z_copy(half, step):
        deep = lax.rem(z + step, nz)
        return remote(
            summed(half, deep),
            z_in.at[half, step - 1],
            z_send.at[half, step - 1],
            z_recv.at[half, step - 1],
            spot.device(deep, y, x, c),
        )

    def add_into(target, sources):
        def some(block, carry):
            value = target[block].astype(jnp.float32)
            for source in sources:
                value = value + source[block].astype(jnp.float32)
            target[block] = value.astype(target.dtype)
            return carry

        lax.fori_loop(0, blocks, some, 0)

    def over_depths(action):
        def one(step, carry):
            action(lax.rem(z + 1 + step, nz))
            return carry

        lax.fori_loop(0, nz, one, 0)

    steps_x = list(range(1, nx))
    columns = [lax.rem(x + step, nx) for step in steps_x]
    core_order = [(0, 1 - y, column) for column in columns + [x]]
    core_order += [(1, side, column) for column in columns for side in (1 - y, y)]
    core_order += [(0, y, column) for column in columns + [x]]
    core_order += [(1, side, x) for side in (1 - y, y)]
    for half, side, column in core_order:
        over_depths(lambda deep: core_copy(deep, side, column, half).start())
    start_all_to_all(spot, rows, rows_out, row_send, row_recv, local_sem)

    def take_core(deep, side, column, half):
        core_copy(deep, side, column, half).wait_recv()
        own = piece_of(pieces, shape, deep * 2 + side, column * 2 + c, half)
        add_into(core_sum(deep, side, column, half), [own])

    def core_then_y(deep, column):
        take_core(deep, 1 - y, column, 0)
        y_copy(0, deep, column).start()

    def core_then_x(deep, step, side):
        take_core(deep, side, lax.rem(x + step, nx), 1)
        x_copy(1, step, deep, side).start()

    def take_y(deep, column):
        y_copy(0, deep, column).wait_recv()
        add_into(y_in.at[0, deep, column], [core_sum(deep, y, column, 0)])

    def take_x(deep, side):
        for step in steps_x:
            x_copy(1, step, deep, side).wait_recv()
        add_into(core_sum(deep, side, x, 1), [x_in.at[1, step - 1, deep, side] for step in steps_x])

    def y_then_x(deep, step):
        take_y(deep, lax.rem(x + step, nx))
        x_copy(0, step, deep, 0).start()

    def x_then_y(deep):
        take_x(deep, 1 - y)
        y_copy(1, deep, x).start()

    for column in columns + [x]:
        over_depths(lambda deep: core_then_y(deep, column))
    for step in steps_x:
        for side in (1 - y, y):
            over_depths(lambda deep: core_then_x(deep, step, side))
    for column in columns + [x]:
        over_depths(lambda deep: take_core(deep, y, column, 0))
    for side in (1 - y, y):
        over_depths(lambda deep: take_core(deep, side, x, 1))
    for step in steps_x:
        over_depths(lambda deep: y_then_x(deep, step))
    over_depths(x_then_y)
    over_depths(lambda deep: take_y(deep, x))
    over_depths(lambda deep: take_x(deep, y))
    for step in range(nz):
        deep = lax.rem(z + 1 + step, nz)
        for step_x in steps_x:
            x_copy(0, step_x, deep, 0).wait_recv()
        add_into(y_in.at[0, deep, x], [x_in.at[0, step_x - 1, deep, 0] for step_x in steps_x])
        if step + 1 < nz:
            z_copy(0, step + 1).start()
        y_copy(1, deep, x).wait_recv()
        add_into(core_sum(deep, y, x, 1), [y_in.at[1, deep, x]])
        if step + 1 < nz:
            z_copy(1, step + 1).start()
    finish_all_to_all(spot, rows, rows_out, row_send, row_recv, local_sem)
    squares = place_rows(rows_out, wanted, table_grad)
    room = rows_out.shape[1]
    small[...] = jnp.sum(rows_out[:, room - 16 : room, :].astype(jnp.float32), axis=0)
    last_small = small[15:16, :]
    for half in range(2):
        for step in range(1, nz):
            z_copy(half, step).wait_recv()

    def finish(block, carry):
        for half in range(2):
            value = summed(half, z)[block].astype(jnp.float32)
            for step in range(nz - 1):
                value = value + z_in[half, step, block].astype(jnp.float32)
            total[half * blocks + block] = value
            carry = carry + jnp.sum(value * value, axis=0, keepdims=True)
        return carry

    others = lax.fori_loop(0, blocks, finish, jnp.zeros((1, shape[2]), jnp.float32))
    lane = lax.broadcasted_iota(jnp.int32, (8, 128), 1)
    sums = jnp.where(lane == 0, jnp.sum(squares), 0.0)
    sums = jnp.where(lane == 1, jnp.sum(others) + jnp.sum(last_small * last_small), sums)
    mine[...] = jnp.where(lane == 2, jnp.sum(loss[...]), sums)
    everyone[spot.rank] = mine[...]

    def tell(step, carry):
        peer = lax.rem(spot.rank + step, spot.count)
        remote(
            mine, everyone.at[spot.rank], sum_send.at[step], sum_recv.at[step], spot.place(peer)
        ).start()
        return carry

    lax.fori_loop(1, spot.count, tell, 0)
    for half, side, column in core_order:
        over_depths(lambda deep: core_copy(deep, side, column, half).wait_send())
    for column in columns + [x]:
        over_depths(lambda deep: y_copy(0, deep, column).wait_send())
    over_depths(lambda deep: y_copy(1, deep, x).wait_send())
    for step in steps_x:
        over_depths(lambda deep: x_copy(0, step, deep, 0).wait_send())
        for side in (1 - y, y):
            over_depths(lambda deep: x_copy(1, step, deep, side).wait_send())
    for half in range(2):
        for step in range(1, nz):
            z_copy(half, step).wait_send()

    def hear(step, carry):
        origin = lax.rem(spot.rank + spot.count - step, spot.count)
        copy = remote(
            mine, everyone.at[origin], sum_send.at[step], sum_recv.at[step], spot.place(origin)
        )
        copy.wait_recv()
        copy.wait_send()
        return carry

    lax.fori_loop(1, spot.count, hear, 0)


def reduce_grads(sizes, rows, pieces, one, wanted, loss, table_shape):
    n_dp, n_head = sizes
    count = n_dp * n_head
    nz, nx = n_dp // 2, n_head // 2
    dma = pltpu.SemaphoreType.DMA
    half = (one[0] // 2,) + one[1:]
    return pl.pallas_call(
        functools.partial(reduce_kernel, sizes),
        in_specs=[pl.BlockSpec(memory_space=pl.ANY)] + [pl.BlockSpec(memory_space=pltpu.VMEM)] * 3,
        out_specs=[pl.BlockSpec(memory_space=pltpu.VMEM)] * 5,
        out_shape=[
            jax.ShapeDtypeStruct(rows.shape, rows.dtype),
            jax.ShapeDtypeStruct(one, jnp.float32),
            jax.ShapeDtypeStruct(table_shape, jnp.float32),
            jax.ShapeDtypeStruct((16, rows.shape[2]), jnp.float32),
            jax.ShapeDtypeStruct((count, 8, 128), jnp.float32),
        ],
        scratch_shapes=[
            pltpu.VMEM((8, 128), jnp.float32),
            dma((count,)),
            dma((count,)),
            pltpu.VMEM((nz, 2, nx) + one, pieces.dtype),
            pltpu.VMEM((2, nz, nx) + half, pieces.dtype),
            pltpu.VMEM((2, nx - 1, nz, 2) + half, pieces.dtype),
            pltpu.VMEM((2, nz - 1) + half, pieces.dtype),
            dma((count,)),
            dma((count,)),
            dma((2, nz, 2, nx)),
            dma((2, nz, 2, nx)),
            dma((2, nz, nx)),
            dma((2, nz, nx)),
            dma((2, nx - 1, nz, 2)),
            dma((2, nx - 1, nz, 2)),
            dma((2, nz - 1)),
            dma((2, nz - 1)),
            dma,
        ],
        compiler_params=pltpu.CompilerParams(
            collective_id=3, has_side_effects=True, vmem_limit_bytes=52 * 2**20
        ),
    )(rows, pieces, wanted, loss)


def stack_blocks(qkv_weight, proj_weight, up_weight, down_weight, position_table):
    depth, width = position_table.shape
    parts = by_part(qkv_weight, qkv_weight.shape[2] // (3 * HD))
    parts = parts.reshape(LAYERS, depth, 3, width).transpose(0, 2, 1, 3).reshape(6, depth, width)
    up_blocks = up_weight.reshape(depth, width // depth, 4, depth).transpose(2, 0, 1, 3)
    return jnp.concatenate(
        [
            parts,
            proj_weight[None],
            position_table[None],
            up_blocks.reshape(4, depth, width),
            down_weight.reshape(4, depth, width),
        ],
        axis=0,
    )


def stack_kernel(qkv_weight, proj_weight, up_weight, down_weight, position_table, shard):
    depth, width = position_table.shape
    heads = width // HD
    for layer in range(LAYERS):
        value = low16(qkv_weight[layer])
        for part in range(3):
            pieces = [
                value[:, (head * 3 + part) * HD : (head * 3 + part) * HD + HD] for head in range(heads)
            ]
            shard[layer * 3 + part] = jnp.concatenate(pieces, axis=1)
    shard[6] = low16(proj_weight[...])
    shard[7] = low16(position_table[...])
    value = low16(up_weight[...])
    for block in range(4):
        starts = [(turn * 4 + block) * depth for turn in range(width // depth)]
        pieces = [value[:, start : start + depth] for start in starts]
        shard[8 + block] = jnp.concatenate(pieces, axis=1)
        shard[12 + block] = low16(down_weight[block * depth : block * depth + depth, :])


def stack_shard(qkv_weight, proj_weight, up_weight, down_weight, position_table):
    depth, width = position_table.shape
    if not is_direct((16, depth, width)):
        blocks = stack_blocks(qkv_weight, proj_weight, up_weight, down_weight, position_table)
        return blocks.astype(jnp.bfloat16)
    vmem = pl.BlockSpec(memory_space=pltpu.VMEM)
    return pl.pallas_call(
        stack_kernel,
        in_specs=[vmem] * 5,
        out_specs=vmem,
        out_shape=jax.ShapeDtypeStruct((16, depth, width), jnp.bfloat16),
    )(qkv_weight, proj_weight, up_weight, down_weight, position_table)


def split_blocks(total):
    depth, width = total.shape[1:]
    parts = total[:6].reshape(LAYERS, 3, depth, width).transpose(0, 2, 1, 3)
    qkv_grad = by_head(parts.reshape(LAYERS, depth, 3 * width), width // HD)
    up_grad = total[8:12].reshape(4, depth, width // depth, depth).transpose(1, 2, 0, 3)
    return (
        total[7],
        qkv_grad,
        total[6:7],
        up_grad.reshape(1, depth, 4 * width),
        total[12:16].reshape(1, 4 * depth, width),
    )


def arrange_gains(gains, n_dp):
    offset = 2 * D
    qkv_bias = by_part(gains[offset : offset + 3 * D], HEADS)
    up_bias = gains[offset + 4 * D : offset + 4 * D + FF].reshape(n_dp, 4, D // n_dp)
    return jnp.concatenate(
        [
            gains[:offset],
            qkv_bias,
            gains[offset + 3 * D : offset + 4 * D],
            up_bias.transpose(1, 0, 2).reshape(-1),
            gains[offset + 4 * D + FF : offset + 9 * D + FF],
            by_part(gains[offset + 9 * D + FF :], HEADS),
        ]
    ).reshape(GAIN_ROWS, D)


def restore_gains(rows, n_dp):
    up_bias = rows[6:10].reshape(4, n_dp, D // n_dp).transpose(1, 0, 2)
    return jnp.concatenate(
        [
            rows[0:2].reshape(-1),
            by_head(rows[2:5].reshape(-1), HEADS),
            rows[5],
            up_bias.reshape(-1),
            rows[10:15].reshape(-1),
            by_head(rows[15:18].reshape(-1), HEADS),
        ]
    )


def gather_teacher(weight):
    width = weight.shape[1]
    order = by_part(jnp.arange(width, dtype=jnp.int32), width // (3 * THD))
    turned = dot(weight, one_hot(order, width).T).astype(jnp.bfloat16)
    return lax.all_gather(turned.reshape(TD, 3, -1).transpose(1, 0, 2), "head", axis=0)


def request_slots(token_ids, shard_rows, count, room, usable):
    here = token_ids.shape[0]
    index = jnp.arange(here, dtype=jnp.int32)
    owner = token_ids // shard_rows
    equal = token_ids[:, None] == token_ids[None, :]
    first = jnp.min(jnp.where(equal, index[:, None], here), axis=0)
    is_first = first == index
    earlier = (owner[:, None] == owner[None, :]) & is_first[:, None] & (index[:, None] < index[None, :])
    order = jnp.sum(earlier.astype(jnp.int32), axis=0)
    overflow = jnp.any(is_first & (order >= usable))
    slot_first = owner * room + order
    chosen = first[None, :] == index[:, None]
    slot = jnp.sum(jnp.where(chosen, slot_first[:, None], 0), axis=0)
    spots = jnp.arange(count * room, dtype=jnp.int32)
    asked = is_first[:, None] & (slot_first[:, None] == spots[None, :]) & (order < usable)[:, None]
    request = jnp.sum(jnp.where(asked, (token_ids % shard_rows)[:, None] + 1, 0), axis=0) - 1
    return slot, request, overflow


def one_hot(index, size):
    return (index[:, None] == jnp.arange(size, dtype=jnp.int32)[None, :]).astype(jnp.bfloat16)


def adam_update(master, first, second, grad_clip, rate):
    first_new = B_ONE * first + (1.0 - B_ONE) * grad_clip
    second_new = B_TWO * second + (1.0 - B_TWO) * grad_clip * grad_clip
    ascent = (
        first_new / (1.0 - B_ONE**STEP) / (jnp.sqrt(second_new / (1.0 - B_TWO**STEP)) + EPSILON)
    )
    return (master - rate * (ascent + DECAY * master), first_new, second_new)


def update_kernel(factor_ref, total, *refs):
    sources, targets = refs[:15], refs[15:]
    factor = factor_ref[0, 0]
    depth, width = total.shape[1:]
    heads = width // HD

    def apply(index, rate, grad, at):
        values = [ref[at] for ref in sources[index * 3 : index * 3 + 3]]
        for target, value in zip(
            targets[index * 3 : index * 3 + 3], adam_update(*values, grad * factor, rate)
        ):
            target[at] = value

    apply(0, RATE_TABLE, total[7], ...)
    for layer in range(LAYERS):
        parts = [total[layer * 3 + part] for part in range(3)]
        columns = [
            parts[part][:, head * HD : head * HD + HD] for head in range(heads) for part in range(3)
        ]
        apply(1, RATE_MATRIX, jnp.concatenate(columns, axis=1), layer)
    apply(2, RATE_MATRIX, total[6], 0)
    blocks = [total[8 + block] for block in range(4)]
    columns = [
        blocks[block][:, turn * depth : turn * depth + depth]
        for turn in range(width // depth)
        for block in range(4)
    ]
    apply(3, RATE_MATRIX, jnp.concatenate(columns, axis=1), 0)
    for block in range(4):
        rows = slice(block * depth, block * depth + depth)
        apply(4, RATE_MATRIX, total[12 + block], (0, rows))


def update_blocks(factor, total, groups):
    arrays = [array for group in groups for array in group]
    if not is_direct(total.shape):
        rates = [RATE_TABLE] + [RATE_MATRIX] * 4
        grads = split_blocks(total)
        return [
            adam_update(*group, grad * factor, rate) for group, grad, rate in zip(groups, grads, rates)
        ]
    vmem = pl.BlockSpec(memory_space=pltpu.VMEM)
    outs = pl.pallas_call(
        update_kernel,
        in_specs=[pl.BlockSpec(memory_space=pltpu.SMEM)] + [vmem] * 16,
        out_specs=[vmem] * 15,
        out_shape=[jax.ShapeDtypeStruct(array.shape, array.dtype) for array in arrays],
    )(factor.reshape(1, 1), total, *arrays)
    return [tuple(outs[start : start + 3]) for start in range(0, 15, 3)]


def shards(
    token_ids,
    seq_lengths,
    teacher_hidden,
    teacher_weight,
    token_table,
    token_first,
    token_second,
    position_table,
    position_first,
    position_second,
    qkv_weight,
    qkv_first,
    qkv_second,
    proj_weight,
    proj_first,
    proj_second,
    up_weight,
    up_first,
    up_second,
    down_weight,
    down_first,
    down_second,
    gains_biases,
    gains_first,
    gains_second,
):
    n_dp, n_head = sizes = (lax.axis_size("dp"), lax.axis_size("head"))
    count = n_dp * n_head
    here, shard_rows = token_ids.shape[0], token_table.shape[0]
    room = 16 * -(-3 * here // (2 * count * 16))
    slot, request, overflow = request_slots(token_ids, shard_rows, count, room, room - 1)
    notes = jnp.stack([overflow.astype(jnp.float32), jnp.sum(seq_lengths).astype(jnp.float32)])
    small_size = gains_biases.shape[0]
    small_rows = -(-small_size // 128)
    small_mine = gains_biases.astype(jnp.bfloat16).astype(jnp.float32)
    small_mine = jnp.pad(small_mine, (0, small_rows * 128 - small_size)).reshape(1, small_rows, 128)
    message = jnp.concatenate(
        [
            jnp.pad(
                request.astype(jnp.float32).reshape(count, 1, room), ((0, 0), (0, 0), (0, 128 - room))
            ),
            jnp.broadcast_to(jnp.pad(notes, (0, 126)), (count, 1, 128)),
            jnp.broadcast_to(small_mine, (count, small_rows, 128)),
            jnp.zeros((count, 6 - small_rows, 128), jnp.float32),
        ],
        axis=1,
    )
    shard = stack_shard(qkv_weight, proj_weight[0], up_weight[0], down_weight[0], position_table)
    table_low = token_table.astype(jnp.bfloat16)
    heard, rows_in, big = gather_weights(sizes, message, table_low, shard, room)
    too_many = jnp.any(heard[:, 1, 0] > 0.0)
    valid_total = jnp.sum(heard[:, 1, 1])
    wanted = heard[:, 0, :room].reshape(1, -1).astype(jnp.int32)
    gains = arrange_gains(
        heard[:, 2 : 2 + small_rows].reshape(count, -1)[:, :small_size].reshape(-1), n_dp
    )
    teach_full = gather_teacher(teacher_weight)
    if not is_direct(shard.shape):
        big = big.transpose(2, 0, 3, 1, 4).reshape(16, D, D)

    def owned_rows():
        group_ids = lax.all_gather(token_ids, "head", axis=0, tiled=True)
        block_ids = group_ids // shard_rows
        owned = block_ids % n_head == lax.axis_index("head")
        local = jnp.where(owned, block_ids // n_head * shard_rows + group_ids % shard_rows, 0)
        return owned, local

    def rows_by_owner():
        owned, local = owned_rows()
        rows_all = lax.all_gather(table_low, "dp", axis=0, tiled=True)
        picked = jnp.where(owned[:, None], rows_all[local], jnp.zeros((), jnp.bfloat16))
        rows_here = lax.psum_scatter(picked, "head", scatter_dimension=0, tiled=True)
        return (
            jnp.pad(rows_here, ((0, count * room - here), (0, 0))),
            jnp.arange(here, dtype=jnp.int32),
        )

    rows_used, slot_used = lax.cond(
        too_many, rows_by_owner, lambda: (rows_in.reshape(count * room, D), slot)
    )
    teacher_qkv = project_teacher(teacher_hidden, teach_full)
    final_qkv, *kept = forward_layer(seq_lengths, rows_used, slot_used, big, gains)
    final_grad, loss_part = relation(seq_lengths, final_qkv, teacher_qkv)
    pieces, gain_grads, slot_grads, row_low = backward_layer(
        seq_lengths, slot_used, big, gains, final_grad, kept, count * room
    )
    if not is_direct(shard.shape):
        pieces = pieces.reshape(16, n_dp, shard.shape[1], n_head, shard.shape[2])
        pieces = pieces.transpose(1, 3, 0, 2, 4)
    gain_rows = jnp.pad(
        restore_gains(gain_grads, n_dp).reshape(count, 1, small_size), ((0, 0), (0, 0), (0, D - small_size))
    )
    slot_grads = slot_grads.reshape(count, room, D).at[:, room - 1 :].set(gain_rows.astype(jnp.bfloat16))
    rows_arrived, total, fast_grad, small_sum, everyone = reduce_grads(
        sizes, slot_grads, pieces, shard.shape, wanted, loss_part, token_table.shape
    )
    small_grad = small_sum[15, :small_size]

    def table_by_owner():
        owned, local = owned_rows()
        spread = lax.all_gather(row_low, "head", axis=0, tiled=True)
        table_grad = jax.ops.segment_sum(
            spread.astype(jnp.float32),
            jnp.where(owned, local, n_dp * shard_rows),
            num_segments=n_dp * shard_rows + 1,
        )[:-1]
        table_grad = lax.psum_scatter(
            table_grad.astype(jnp.bfloat16), "dp", scatter_dimension=0, tiled=True
        ).astype(jnp.float32)
        return table_grad, lax.psum(jnp.sum(table_grad * table_grad), ("dp", "head"))

    table_grad, table_squares = lax.cond(
        too_many, table_by_owner, lambda: (fast_grad, jnp.sum(everyone[:, 0, 0]))
    )
    square_total = table_squares + jnp.sum(everyone[:, 0, 1])
    loss_total = jnp.sum(everyone[:, 0, 2]) * (LN2 / (3 * REL))
    grad_norm = jnp.sqrt(square_total) / valid_total
    clip_factor = THRESHOLD / jnp.maximum(grad_norm, THRESHOLD)
    factor = clip_factor / valid_total
    token_new = adam_update(token_table, token_first, token_second, table_grad * factor, RATE_TABLE)
    position_new, qkv_new, proj_new, up_new, down_new = update_blocks(
        factor,
        total,
        (
            (position_table, position_first, position_second),
            (qkv_weight, qkv_first, qkv_second),
            (proj_weight, proj_first, proj_second),
            (up_weight, up_first, up_second),
            (down_weight, down_first, down_second),
        ),
    )
    gains_new = adam_update(gains_biases, gains_first, gains_second, small_grad * factor, RATE_SMALL)
    loss_parts = jnp.stack([loss_total, valid_total])
    return (
        token_new[0],
        token_new[1],
        token_new[2],
        position_new[0],
        position_new[1],
        position_new[2],
        qkv_new[0],
        qkv_new[1],
        qkv_new[2],
        proj_new[0],
        proj_new[1],
        proj_new[2],
        up_new[0],
        up_new[1],
        up_new[2],
        down_new[0],
        down_new[1],
        down_new[2],
        gains_new[0],
        gains_new[1],
        gains_new[2],
        grad_norm,
        loss_parts,
    )


def solution(mesh):
    placed = (
        P(("dp", "head")),
        P(("dp", "head")),
        P(("dp", "head"), None),
        P(None, "head"),
        P(("dp", "head"), None),
        P(("dp", "head"), None),
        P(("dp", "head"), None),
        P("dp", "head"),
        P("dp", "head"),
        P("dp", "head"),
        P(None, "dp", "head"),
        P(None, "dp", "head"),
        P(None, "dp", "head"),
        P(None, "dp", "head"),
        P(None, "dp", "head"),
        P(None, "dp", "head"),
        P(None, "dp", "head"),
        P(None, "dp", "head"),
        P(None, "dp", "head"),
        P(None, "dp", "head"),
        P(None, "dp", "head"),
        P(None, "dp", "head"),
        P(("dp", "head")),
        P(("dp", "head")),
        P(("dp", "head")),
    )
    return jax.shard_map(
        shards,
        mesh=mesh,
        in_specs=placed,
        out_specs=(
            P(("dp", "head"), None),
            P(("dp", "head"), None),
            P(("dp", "head"), None),
            P("dp", "head"),
            P("dp", "head"),
            P("dp", "head"),
            P(None, "dp", "head"),
            P(None, "dp", "head"),
            P(None, "dp", "head"),
            P(None, "dp", "head"),
            P(None, "dp", "head"),
            P(None, "dp", "head"),
            P(None, "dp", "head"),
            P(None, "dp", "head"),
            P(None, "dp", "head"),
            P(None, "dp", "head"),
            P(None, "dp", "head"),
            P(None, "dp", "head"),
            P(("dp", "head")),
            P(("dp", "head")),
            P(("dp", "head")),
            P(),
            P(),
        ),
        check_vma=False,
    )
```
